256 devices in a mesh: bx: 4 (over x), by: 4 (over y), vert: 16 (over z, core).
Axes of the slice: x: 4, y: 4, z: 8, core: 2. Of those that a mesh axis runs over, the one named last changes fastest.
Arguments:
- estimate: float32 [128, 128, 512], P('bx', 'by', 'vert'), may hold values from 0.5 to 1.5
- view_tiles: bfloat16 [4, 4, 16, 64, 64, 128], P('bx', 'by', 'vert'), may hold values from 0.19921875 to 2
- slot_view: int32 [4, 4, 4], P('bx', 'by'), may hold values from 0 to 3, each once within a row
- psf_taps: float32 [4, 3, 3, 33], replicated, may hold values from 0.05 to 1
Outputs:
- refined: float32 [128, 128, 512], P('bx', 'by', 'vert')
The draws below stay inside these ranges and needn't reach their ends.
Inputs may be any that keep to these rules, and one draw needn't show every extreme that they name: `slot_view`: each block's list names every view once.
All inputs are finite; a program needn't handle non-finite values.
Results may differ from the reference program's by a relative error of at most 0.0003.
Values may be sent and summed in bfloat16 or wider, within the bound.
A program may use at most 128 MiB of HBM per device.

```python
import math
import jax
import jax.numpy as jnp
from jax import lax

X_DEV = 32
Y_DEV = 32
NZ = 512
VIEWS = 4
RANK = 3
RAD = 16
ITERS = 1
TAPS = 33
ZPARTS = 4
Z_DEV = 128
NX = 128
NY = 128
N_BX = 4
N_BY = 4
N_VERT = 16


def levels(own_key, extent, pieces, low, high):
    def one(dim, shards_of):
        steps = jax.random.uniform(jax.random.fold_in(jax.random.fold_in(own_key, 6), dim), (shards_of,), jnp.float32, low / len(pieces), high / len(pieces))
        return jnp.repeat(jnp.exp(steps), extent[dim] // shards_of).reshape((-1,) + (1,) * (len(extent) - dim - 1))

    gain = one(*pieces[0])
    for cut in pieces[1:]:
        gain = gain * one(*cut)
    return gain


def setup_inputs(seed: int = 0) -> dict:
    splits = jax.random.split(jax.random.key(seed), 5)
    return {
        "estimate": jnp.clip(0.5 + 1.0 * jax.random.uniform(splits[0], (NX, NY, NZ), jnp.float32) ** levels(splits[0], (NX, NY, NZ), ((0, 4), (1, 4), (2, 16)), -0.2, 0.2), 0.5, 1.5),
        "view_tiles": jnp.clip(0.19921875 + 1.8007812 * jax.random.uniform(splits[1], (N_BX, N_BY, N_VERT, X_DEV + 2 * RAD, Y_DEV + 2 * RAD, Z_DEV), jnp.float32) ** levels(splits[1], (N_BX, N_BY, N_VERT, X_DEV + 2 * RAD, Y_DEV + 2 * RAD, Z_DEV), ((0, 4), (1, 4), (2, 16)), -0.2, 0.2), 0.19921875, 2.0).astype(jnp.bfloat16),
        "slot_view": jax.vmap(lambda own: jax.random.permutation(own, VIEWS))(jax.random.split(splits[2], N_BX * N_BY)).reshape((N_BX, N_BY, VIEWS)).astype(jnp.int32),
        "psf_taps": jnp.clip(jnp.exp(jax.random.uniform(splits[3], (VIEWS, 3, RANK, TAPS), jnp.float32, math.log(0.05), math.log(1.0))), 0.05, 1.0),
    }


BACKGROUND = 0.1


def as_stored(values):
    return lax.optimization_barrier(values.astype(jnp.bfloat16)).astype(jnp.float32)


def forward_pass(volume, kernel, along):
    padding = [(0, 0)] * volume.ndim
    padding[along] = (RAD, RAD)
    padded = jnp.pad(volume, padding)
    length = volume.shape[along]
    result = jnp.zeros(volume.shape, jnp.float32)
    for tap_index in range(TAPS):
        result = result + kernel[tap_index] * lax.slice_in_dim(padded, tap_index, tap_index + length, axis=along)
    return result


def back_pass(volume, kernel, along, extend):
    padded = volume
    if extend:
        padding = [(0, 0)] * volume.ndim
        padding[along] = (RAD, RAD)
        padded = jnp.pad(volume, padding)
    length = padded.shape[along] - 2 * RAD
    out_shape = list(padded.shape)
    out_shape[along] = length
    result = jnp.zeros(tuple(out_shape), jnp.float32)
    for tap_index in range(TAPS):
        begin = 2 * RAD - tap_index
        result = result + kernel[tap_index] * lax.slice_in_dim(padded, begin, begin + length, axis=along)
    return result


def reference(estimate, view_tiles, slot_view, psf_taps):
    kernels = as_stored(psf_taps / jnp.sum(psf_taps, axis=-1, keepdims=True))
    current = estimate
    zero_index = jnp.int32(0)
    frame_x = X_DEV + 2 * RAD
    frame_y = Y_DEV + 2 * RAD
    for sweep in range(ITERS):
        sharp = as_stored(current)

        def blur_view(view_kernels):
            summed = jnp.zeros(sharp.shape, jnp.float32)
            for rank_index in range(RANK):
                along_x = as_stored(forward_pass(sharp, view_kernels[0, rank_index], 0))
                along_y = as_stored(forward_pass(along_x, view_kernels[1, rank_index], 1))
                summed = summed + forward_pass(along_y, view_kernels[2, rank_index], 2)
            return summed / RANK

        blurred = lax.map(blur_view, kernels)
        framed = jnp.pad(blurred, ((0, 0), (RAD, RAD), (RAD, RAD), (0, 0)))

        def update_block(block_index):
            row_block = (block_index // N_BY).astype(jnp.int32)
            col_block = (block_index % N_BY).astype(jnp.int32)
            tile_row = lax.dynamic_index_in_dim(view_tiles, row_block, 0, False)
            tile_set = lax.dynamic_index_in_dim(tile_row, col_block, 0, False)
            grouped = tile_set.reshape(ZPARTS, VIEWS, frame_x, frame_y, Z_DEV)
            label_row = lax.dynamic_index_in_dim(slot_view, row_block, 0, False)
            labels = lax.dynamic_index_in_dim(label_row, col_block, 0, False)
            row_start = (row_block * X_DEV).astype(jnp.int32)
            col_start = (col_block * Y_DEV).astype(jnp.int32)
            block_now = lax.dynamic_slice(current, (row_start, col_start, zero_index), (X_DEV, Y_DEV, NZ))
            grid_x = row_start - RAD + jnp.arange(frame_x, dtype=jnp.int32)
            grid_y = col_start - RAD + jnp.arange(frame_y, dtype=jnp.int32)
            inside_x = ((grid_x >= 0) & (grid_x < NX)).astype(jnp.float32)
            inside_y = ((grid_y >= 0) & (grid_y < NY)).astype(jnp.float32)
            inside = inside_x[:, None, None] * inside_y[None, :, None]
            summed_corr = jnp.zeros((X_DEV, Y_DEV, NZ), jnp.float32)
            for slot_index in range(VIEWS):
                view_index = labels[slot_index].astype(jnp.int32)
                tile = grouped[:, slot_index].transpose(1, 2, 0, 3).reshape(frame_x, frame_y, NZ).astype(jnp.float32)
                view_kernels = lax.dynamic_index_in_dim(kernels, view_index, 0, False)
                view_blur = lax.dynamic_index_in_dim(framed, view_index, 0, False)
                blur_frame = lax.dynamic_slice(view_blur, (row_start, col_start, zero_index), (frame_x, frame_y, NZ))
                quotient = as_stored(tile / (blur_frame + BACKGROUND) * inside)
                correction = jnp.zeros((X_DEV, Y_DEV, NZ), jnp.float32)
                for rank_index in range(RANK):
                    back_x = as_stored(back_pass(quotient, view_kernels[0, rank_index], 0, False))
                    back_y = as_stored(back_pass(back_x, view_kernels[1, rank_index], 1, False))
                    correction = correction + back_pass(back_y, view_kernels[2, rank_index], 2, True)
                summed_corr = summed_corr + correction / RANK
            return block_now * summed_corr / VIEWS

        updated = lax.map(update_block, jnp.arange(N_BX * N_BY, dtype=jnp.int32))
        current = updated.reshape(N_BX, N_BY, X_DEV, Y_DEV, NZ).transpose(0, 2, 1, 3, 4).reshape(NX, NY, NZ)
    return current
```

```python
import jax
import jax.numpy as jnp
from jax import lax
from jax.experimental import pallas as pl
from jax.experimental.pallas import tpu as pltpu
from jax.sharding import PartitionSpec as P

BACKGROUND = 0.1
MESH = pl.DeviceIdType.MESH
F32, BF16 = jnp.float32, jnp.bfloat16
BLOCK = 32
RAD = 16
TAPS = 33
RANK = 3
VIEWS = 4
GROUPS = 4
LANES = 128


def iota(shape, axis):
    return lax.broadcasted_iota(jnp.int32, shape, axis)


def dot(a, b):
    return jnp.dot(a, b, preferred_element_type=F32)


def build_tables(psf, slot_view, slot, bx, by, q, taps, tx, ty, wz, tyb, txb, wb):
    view = slot_view[0, 0, slot]
    held = iota((3, RANK, VIEWS, TAPS), 2) == view
    mine = jnp.sum(jnp.where(held, psf[...], 0.0), axis=2)
    mine = (mine / jnp.sum(mine, axis=-1, keepdims=True)).astype(BF16).astype(F32)
    taps[...] = jnp.zeros_like(taps)
    for a in range(3):
        taps[0, 8 * a : 8 * a + RANK, :TAPS] = mine[a]
    flip = (iota((LANES, LANES), 0) + iota((LANES, LANES), 1) == TAPS - 1).astype(BF16)
    taps[1] = dot(taps[0].astype(BF16), flip)

    def band(flipped, axis, r, rows, start):
        line = taps[flipped, 8 * axis + r : 8 * axis + r + 1, :]
        line = jnp.broadcast_to(line, (rows, LANES))
        return pltpu.roll(line, start % LANES, 1, stride=1, stride_axis=0)

    def inside(rows, first, index):
        place = index * BLOCK - first + iota((rows, LANES), 1)
        return (place >= 0) & (place < 4 * BLOCK)

    lane64 = iota((64, LANES), 1)
    for r in range(RANK):
        m = jnp.where(inside(64, 2 * RAD, bx), band(0, 0, r, 64, 0), 0.0)
        tx[r * 64 : r * 64 + 64, :] = m.astype(BF16)
        m = jnp.where(inside(BLOCK, RAD, bx), band(1, 0, r, BLOCK, 0), 0.0)
        txb[r * BLOCK : (r + 1) * BLOCK, :] = m.astype(BF16)
        m = jnp.where(inside(BLOCK, RAD, by), band(1, 1, r, BLOCK, 0), 0.0)
        tyb[r * BLOCK : (r + 1) * BLOCK, :] = m.astype(BF16)
    y0, y1, y2 = [
        jnp.where(inside(64, 2 * RAD, by), band(0, 1, r, 64, 0), 0.0) for r in range(RANK)
    ]
    y1, y2 = pltpu.roll(y1, 96, 1), pltpu.roll(y2, 64, 1)
    ty[:, 0:128] = jnp.where(lane64 < 96, y0, y1).astype(BF16)
    ty[:, 128:256] = jnp.where(lane64 < 64, y1, y2).astype(BF16)
    ty[:, 256:384] = jnp.where(lane64 < 32, y2, 0.0).astype(BF16)

    z_in, z_out = iota((LANES, LANES), 0), iota((LANES, LANES), 1)
    near = jnp.abs(z_in - z_out) <= RAD
    rim, out = iota((32, LANES), 0), iota((32, LANES), 1)
    rim_ok = ((rim < RAD) & (out <= rim) & (q > 0)) | ((rim >= RAD) & (out >= rim + 96) & (q < 3))
    row16, lane16 = iota((16, LANES), 0), iota((16, LANES), 1)
    for r in range(RANK):
        main = jnp.where(near, band(1, 2, r, LANES, -RAD), 0.0).astype(BF16)
        edge = jnp.where(rim_ok, band(1, 2, r, 32, 96), 0.0).astype(BF16)
        for g in range(GROUPS):
            wz[r, g, 0:128, :] = main
            wz[r, g, 128:256, :] = jnp.zeros((128, LANES), BF16)
            wz[r, g, 128 + 32 * g : 160 + 32 * g, :] = edge
        main = jnp.where(near, band(0, 2, r, LANES, -RAD), 0.0)
        low = jnp.where((lane16 < RAD) & (q > 0), band(0, 2, r, 16, 0), 0.0)
        high = jnp.where((lane16 < RAD) & (q < 3), band(0, 2, r, 16, 96), 0.0)
        high = pltpu.roll(high, RAD, 1)
        for g in range(GROUPS):
            rows = pl.ds(r * 128, 128)
            wb[g, rows, 0:128] = (pltpu.roll(main, 32 * g, 1) if g else main).astype(BF16)
            wb[g, rows, 128:256] = jnp.zeros((128, LANES), BF16)
            lo, hi = (pltpu.roll(m, 32 * g, 1) if g else m for m in (low, high))
            wb[g, r * 128 : r * 128 + 16, 128:256] = lo.astype(BF16)
            wb[g, r * 128 + 112 : r * 128 + 128, 128:256] = hi.astype(BF16)


def kernel(
    est, tile, psf, slot_view, total,
    packed, parts, field, along_x, along_z, back_y, back_x, sums, rims,
    got_core, got_rim, got_chip, got_edge, wide,
    taps, tx, ty, wz, tyb, txb, wb,
    part_send, part_recv, face_send, face_recv, core_send, core_recv, sum_send, sum_recv,
):
    bx, by, vert = lax.axis_index("bx"), lax.axis_index("by"), lax.axis_index("vert")
    q, slot = vert // VIEWS, vert % VIEWS
    core, chip = slot % 2, slot // 2
    q_up, q_down = (q + 1) % 4, (q + 3) % 4

    def at_vert(index):
        return {"vert": index}

    partner = at_vert(q * 4 + chip * 2 + 1 - core)
    x_up, x_down = {"bx": (bx + 1) % 4}, {"bx": (bx + 3) % 4}
    y_up, y_down = {"by": (by + 1) % 4}, {"by": (by + 3) % 4}
    first, last = slot == 0, slot == VIEWS - 1
    is_edge = first | last

    got_edge[...] = jnp.zeros_like(got_edge)
    barrier = pltpu.get_barrier_semaphore()

    def greet(device):
        pl.semaphore_signal(barrier, inc=1, device_id=device, device_id_type=MESH)

    for k in range(1, VIEWS):
        greet(at_vert(q * 4 + (slot + k) % VIEWS))
    for device in (x_up, x_down, y_up, y_down):
        greet(device)
    greet(at_vert(q_down * 4 + 3))
    greet(at_vert(q_up * 4))

    @pl.when(first)
    def _():
        greet(at_vert(q_down * 4 + 1))

    @pl.when(last)
    def _():
        greet(at_vert(q_up * 4 + 2))

    wide[:, 0:BLOCK] = est[...].reshape(BLOCK * BLOCK, BLOCK)
    for t in range(8):
        rows = [wide[pl.ds(g * 8 + t, BLOCK, stride=BLOCK), :][:, :BLOCK] for g in range(GROUPS)]
        line = pltpu.roll(jnp.concatenate(rows, axis=1), slot * 32, 1)
        packed[t * BLOCK : (t + 1) * BLOCK, :] = line.astype(BF16)

    pl.semaphore_wait(barrier, jnp.where(is_edge, 11, 8))

    def part_copy(dst_index, send, device, half):
        return pltpu.make_async_remote_copy(
            src_ref=packed.at[pl.ds(half * 128, 128), :], dst_ref=parts.at[dst_index],
            send_sem=part_send.at[send], recv_sem=part_recv.at[dst_index],
            device_id=device, device_id_type=MESH,
        )

    for k in range(1, VIEWS):
        other = (slot + k) % VIEWS
        part_copy(slot, k - 1, at_vert(q * 4 + other), other % 2).start()

    @pl.when(last)
    def _():
        for k in range(VIEWS):
            part_copy(4, 3 + k, at_vert(q_up * 4 + k), k % 2).start()

    @pl.when(first)
    def _():
        for k in range(VIEWS):
            part_copy(5, 3 + k, at_vert(q_down * 4 + k), k % 2).start()

    parts[slot] = packed[pl.ds(core * 128, 128), :]
    build_tables(psf, slot_view, slot, bx, by, q, taps, tx, ty, wz, tyb, txb, wb)

    for k in range(1, VIEWS):
        part_copy((slot + k) % VIEWS, 0, partner, 0).wait_recv()
    for k in (4, 5):
        part_copy(k, 0, partner, 0).wait_recv()

    lane = iota((BLOCK, LANES), 1)
    chunk = lane // 32
    for t in range(4):
        rows = pl.ds(t * BLOCK, BLOCK)
        have = [parts[k, rows, :].astype(F32) for k in range(6)]
        for g in range(GROUPS):
            line = have[(3 - g) % 4]
            for at in range(3):
                line = jnp.where(chunk == at, have[(at - g) % 4], line)
            if g:
                line = pltpu.roll(line, LANES - 32 * g, 1)
            field[1, core * 4 + t, g, BLOCK : 2 * BLOCK, :] = line.astype(BF16)
        line = pltpu.roll(jnp.where(lane % 32 < RAD, have[5], have[4]), RAD, 1)
        field[1, core * 4 + t, 4, BLOCK : 2 * BLOCK, :] = line.astype(BF16)

    def piece(jy, jx, tp, owner):
        t = owner * 4 + tp * 2
        return field.at[jy, pl.ds(t, 2), :, pl.ds(jx * BLOCK, BLOCK), :]

    def number(jy, jx, tp):
        return (jy * 3 + jx) * 2 + tp

    def face_copy(source, target, tp, send, device):
        return pltpu.make_async_remote_copy(
            src_ref=piece(*source, tp, core), dst_ref=piece(*target, tp, core),
            send_sem=face_send.at[send], recv_sem=face_recv.at[number(*target, tp)],
            device_id=device, device_id_type=MESH,
        )

    def core_copy(jy, jx, tp, owner):
        return pltpu.make_async_remote_copy(
            src_ref=piece(jy, jx, tp, owner), dst_ref=piece(jy, jx, tp, owner),
            send_sem=core_send.at[number(jy, jx, tp)], recv_sem=core_recv.at[number(jy, jx, tp)],
            device_id=partner, device_id_type=MESH,
        )

    faces = []

    def send_face(source, target, tp, device):
        copy = face_copy(source, target, tp, len(faces), device)
        copy.start()
        faces.append(copy)

    def arrived(jy, jx, tp):
        face_copy((jy, jx), (jy, jx), tp, 0, partner).wait_recv()
        core_copy(jy, jx, tp, core).start()

    for first_tp in (0, 1):
        send_face((1, 1), (1, 0), first_tp, x_up)
        send_face((1, 1), (1, 2), first_tp, x_down)
        send_face((1, 1), (0, 1), 1 - first_tp, y_up)
        send_face((1, 1), (2, 1), 1 - first_tp, y_down)
    for tp in (0, 1):
        core_copy(1, 1, tp, core).start()
    for side in (0, 2):
        arrived(1, side, 0)
        send_face((1, side), (0, side), 0, y_up)
        send_face((1, side), (2, side), 0, y_down)
        arrived(side, 1, 1)
        send_face((side, 1), (side, 0), 1, x_up)
        send_face((side, 1), (side, 2), 1, x_down)
    for side in (0, 2):
        arrived(1, side, 1)
        arrived(side, 1, 0)

    def forward_x(jy):
        def body(pair, carry):
            for m in range(GROUPS + 1):
                both = jnp.concatenate([field[jy, 2 * pair + k, m] for k in range(2)], axis=1)
                done = dot(tx[:, 0:96], both).astype(BF16)
                for k in range(2):
                    along_x[jy, 2 * pair + k, m] = done[:, k * LANES : (k + 1) * LANES]
            return carry

        lax.fori_loop(0, 4, body, 0)

    for jx in range(3):
        for tp in range(2):
            core_copy(1, jx, tp, 1 - core).wait_recv()
    forward_x(1)
    for jy in (0, 2):
        for jx in (0, 2):
            for tp in range(2):
                arrived(jy, jx, tp)
    for jy in (0, 2):
        for jx in range(3):
            for tp in range(2):
                core_copy(jy, jx, tp, 1 - core).wait_recv()
        forward_x(jy)

    def forward_z(step, carry):
        jy, g = step // GROUPS, step % GROUPS
        for r in range(RANK):
            rows = slice(r * 64, (r + 1) * 64)
            main = along_x[jy, :, g, rows, :].reshape(512, LANES)
            rim = along_x[jy, :, 4, rows, :].reshape(512, LANES)
            done = dot(jnp.concatenate([main, rim], axis=1), wz[r, g])
            along_z[r, pl.ds((jy * 32 + g * 8) * 64, 512), :] = done
        return carry

    lax.fori_loop(0, 3 * GROUPS, forward_z, 0)

    def along_y(pair, carry):
        stacks = []
        for r in range(RANK):
            pieces = [along_z[r, pl.ds(2 * pair + k, 96, stride=64), :] for k in range(2)]
            stacks.append(jnp.concatenate(pieces, axis=1).astype(BF16))
        blurred = dot(ty[:, 0:288], jnp.concatenate(stacks, axis=0)) / RANK
        seen = jnp.concatenate([tile[2 * pair + k] for k in range(2)], axis=1).astype(F32)
        quotient = (seen / (blurred + BACKGROUND)).astype(BF16)
        done = dot(tyb[:, 0:64], quotient)
        for k in range(2):
            back_y[pl.ds((2 * pair + k) * 96, 96), :] = done[:, k * LANES : (k + 1) * LANES]
        return carry

    lax.fori_loop(0, 32, along_y, 0)

    def backward_x(pair, carry):
        for r in range(RANK):
            pieces = [
                back_y[pl.ds(r * BLOCK + 2 * pair + k, 64, stride=96), :] for k in range(2)
            ]
            both = jnp.concatenate(pieces, axis=1).astype(BF16)
            done = dot(txb[r * BLOCK : (r + 1) * BLOCK, 0:64], both).astype(BF16)
            for k in range(2):
                back_x[pl.ds((2 * pair + k) * BLOCK, BLOCK), r * LANES : (r + 1) * LANES] = done[
                    :, k * LANES : (k + 1) * LANES
                ]
        return carry

    lax.fori_loop(0, BLOCK // 2, backward_x, 0)

    lane256 = iota((256, LANES), 1)
    chunk256 = lane256 // 32
    rim_sum = None
    for g in range(GROUPS):
        done = dot(back_x[g * 256 : (g + 1) * 256, :], wb[g])
        for c in range(4):
            at = (g + c) % 4
            sums[c, :, at * 32 : at * 32 + 32] = done[:, at * 32 : at * 32 + 32]
        rim_sum = done[:, LANES:] if rim_sum is None else rim_sum + done[:, LANES:]
    top, bottom = rim_sum[0:128], rim_sum[128:256]
    is_low = iota((128, LANES), 1) % 32 < RAD
    rims[0] = jnp.where(is_low, top, pltpu.roll(bottom, RAD, 1))
    rims[1] = jnp.where(is_low, pltpu.roll(top, LANES - RAD, 1), bottom)

    def sum_copy(source, target, index, device):
        return pltpu.make_async_remote_copy(
            src_ref=source, dst_ref=target, send_sem=sum_send.at[index],
            recv_sem=sum_recv.at[index], device_id=device, device_id_type=MESH,
        )

    swaps = [
        sum_copy(sums.at[(1 - chip) * 2 + 1 - core], got_core.at[0], 0, partner),
        sum_copy(rims.at[1 - core], got_rim, 1, partner),
        sum_copy(sums.at[chip * 2 + 1 - core], got_core.at[1], 2, partner),
    ]
    for copy in swaps:
        copy.start()
    far = (1 - chip) * 2 + core
    swaps[0].wait_recv()
    sums[far] = sums[far] + got_core[0]
    over = sum_copy(sums.at[far], got_chip, 3, at_vert(q * 4 + far))
    over.start()
    swaps[1].wait_recv()
    rims[core] = rims[core] + got_rim[...]
    edge_home = jnp.where(core == 0, q_down * 4 + 3, q_up * 4)

    def edge_copy(which):
        return pltpu.make_async_remote_copy(
            src_ref=rims.at[core], dst_ref=got_edge.at[which], send_sem=sum_send.at[4],
            recv_sem=sum_recv.at[4 + which], device_id=at_vert(edge_home), device_id_type=MESH,
        )

    edge_copy(chip).start()
    swaps[2].wait_recv()
    sums[slot] = sums[slot] + got_core[1]
    over.wait_recv()

    @pl.when(is_edge)
    def _():
        edge_copy(0).wait_recv()
        edge_copy(1).wait_recv()

    edge = got_edge[0] + got_edge[1]
    mine = sums[slot] + got_chip[...]
    start = jnp.where(last, RAD, 0)
    lane128 = iota((128, LANES), 1)
    keep = is_edge & (lane128 >= start) & (lane128 < start + RAD)
    for g in range(GROUPS):
        own = pltpu.roll(mine, (8 - g - slot) % 4 * 32, 1)
        top = pltpu.roll(edge, (start + LANES - 32 * g) % LANES, 1)
        bottom = pltpu.roll(edge, (start + 2 * LANES - RAD - 32 * g) % LANES, 1)
        wide[g * 256 : g * 256 + 128, :] = own[0:128] + jnp.where(keep, top, 0.0)
        wide[g * 256 + 128 : g * 256 + 256, :] = own[128:256] + jnp.where(keep, bottom, 0.0)
    for x in range(BLOCK):
        total[x] = wide[pl.ds(x, BLOCK, stride=BLOCK), :][:, 0:BLOCK]

    for k in range(1, VIEWS):
        part_copy(slot, k - 1, partner, 0).wait_send()

    @pl.when(is_edge)
    def _():
        for k in range(VIEWS):
            part_copy(4, 3 + k, partner, 0).wait_send()

    for copy in faces:
        copy.wait_send()
    for jy in range(3):
        for jx in range(3):
            for tp in range(2):
                core_copy(jy, jx, tp, core).wait_send()
    for copy in swaps:
        copy.wait_send()
    over.wait_send()
    edge_copy(0).wait_send()


def local(estimate, view_tiles, slot_view, psf_taps):
    vmem = pl.BlockSpec(memory_space=pltpu.VMEM)
    scratch = [
        pltpu.VMEM((256, LANES), BF16),
        pltpu.VMEM((6, 128, LANES), BF16),
        pltpu.VMEM((3, 8, 5, 96, LANES), BF16),
        pltpu.VMEM((3, 8, 5, 192, LANES), BF16),
        pltpu.VMEM((RANK, 96 * 64, LANES), F32),
        pltpu.VMEM((64 * 96, LANES), F32),
        pltpu.VMEM((1024, RANK * LANES), BF16),
        pltpu.VMEM((4, 256, LANES), F32),
        pltpu.VMEM((2, 128, LANES), F32),
        pltpu.VMEM((2, 256, LANES), F32),
        pltpu.VMEM((128, LANES), F32),
        pltpu.VMEM((256, LANES), F32),
        pltpu.VMEM((2, 128, LANES), F32),
        pltpu.VMEM((1024, LANES), F32),
        pltpu.VMEM((2, 24, LANES), F32),
        pltpu.VMEM((192, LANES), BF16),
        pltpu.VMEM((64, 384), BF16),
        pltpu.VMEM((RANK, GROUPS, 256, LANES), BF16),
        pltpu.VMEM((96, LANES), BF16),
        pltpu.VMEM((96, LANES), BF16),
        pltpu.VMEM((GROUPS, RANK * LANES, 256), BF16),
        pltpu.SemaphoreType.DMA((7,)),
        pltpu.SemaphoreType.DMA((6,)),
        pltpu.SemaphoreType.DMA((16,)),
        pltpu.SemaphoreType.DMA((18,)),
        pltpu.SemaphoreType.DMA((18,)),
        pltpu.SemaphoreType.DMA((18,)),
        pltpu.SemaphoreType.DMA((5,)),
        pltpu.SemaphoreType.DMA((6,)),
    ]
    total = pl.pallas_call(
        kernel,
        out_shape=jax.ShapeDtypeStruct(estimate.shape, F32),
        in_specs=[vmem, vmem, vmem, pl.BlockSpec(memory_space=pltpu.SMEM)],
        out_specs=vmem,
        scratch_shapes=scratch,
        compiler_params=pltpu.CompilerParams(
            collective_id=0, has_side_effects=True, vmem_limit_bytes=48 * 1024 * 1024
        ),
    )(estimate, view_tiles[0, 0, 0], jnp.transpose(psf_taps, (1, 2, 0, 3)), slot_view)
    return estimate * total * (1.0 / (RANK * VIEWS))


def solution(mesh):
    placed = (
        P("bx", "by", "vert"),
        P("bx", "by", "vert", None, None, None),
        P("bx", "by", None),
        P(),
    )
    return jax.shard_map(
        local, mesh=mesh, in_specs=placed, out_specs=P("bx", "by", "vert"), check_vma=False
    )
```

```python
import jax
import jax.numpy as jnp
from jax import lax
from jax.experimental import pallas as pl
from jax.experimental.pallas import tpu as pltpu
from jax.sharding import PartitionSpec as P

BACKGROUND = 0.1
MESH = pl.DeviceIdType.MESH
F32, BF16 = jnp.float32, jnp.bfloat16
BLOCK = 32
RAD = 16
TAPS = 33
RANK = 3
VIEWS = 4
GROUPS = 4
LANES = 128


def iota(shape, axis):
    return lax.broadcasted_iota(jnp.int32, shape, axis)


def dot(a, b):
    return jnp.dot(a, b, preferred_element_type=F32)


def build_taps(psf, slot_view, slot, taps):
    listed = slot_view[...]
    view = jnp.sum(jnp.where(iota(listed.shape, 2) == slot, listed, 0), axis=2, keepdims=True)
    held = iota((VIEWS, TAPS), 0) == view[0]
    mine = jnp.sum(jnp.where(held[None, None], psf[...], 0.0), axis=2)
    mine = (mine / jnp.sum(mine, axis=-1, keepdims=True)).astype(BF16).astype(F32)
    taps[...] = jnp.zeros_like(taps)
    for a in range(3):
        taps[0, 8 * a : 8 * a + RANK, :TAPS] = mine[a]
    flip = (iota((LANES, LANES), 0) + iota((LANES, LANES), 1) == TAPS - 1).astype(BF16)
    taps[1] = dot(taps[0].astype(BF16), flip)


def band(line, rows, start):
    line = jnp.broadcast_to(line, (rows, LANES))
    return pltpu.roll(line, start % LANES, 1, stride=1, stride_axis=0)


def build_z(taps, q, wz, wb):
    z_in, z_out = iota((LANES, LANES), 0), iota((LANES, LANES), 1)
    near = jnp.abs(z_in - z_out) <= RAD
    rim, out = iota((32, LANES), 0), iota((32, LANES), 1)
    rim_ok = ((rim < RAD) & (out <= rim) & (q > 0)) | ((rim >= RAD) & (out >= rim + 96) & (q < 3))
    lane16 = iota((16, LANES), 1)
    for r in range(RANK):
        forward, backward = taps[1, 16 + r : 17 + r, :], taps[0, 16 + r : 17 + r, :]
        columns = slice(r * LANES, (r + 1) * LANES)
        wz[0:128, columns] = jnp.where(near, band(forward, LANES, -RAD), 0.0).astype(BF16)
        wz[128:160, columns] = jnp.where(rim_ok, band(forward, 32, 96), 0.0).astype(BF16)
        wz[160:256, columns] = jnp.zeros((96, LANES), BF16)
        main = jnp.where(near, band(backward, LANES, -RAD), 0.0)
        low = jnp.where((lane16 < RAD) & (q > 0), band(backward, 16, 0), 0.0)
        high = jnp.where((lane16 < RAD) & (q < 3), band(backward, 16, 96), 0.0)
        high = pltpu.roll(high, RAD, 1)
        for g in range(GROUPS):
            wb[g, r * 128 : r * 128 + 128, 0:128] = (
                pltpu.roll(main, 32 * g, 1) if g else main
            ).astype(BF16)
            wb[g, r * 128 : r * 128 + 128, 128:256] = jnp.zeros((128, LANES), BF16)
            lo, hi = (pltpu.roll(m, 32 * g, 1) if g else m for m in (low, high))
            wb[g, r * 128 : r * 128 + 16, 128:256] = lo.astype(BF16)
            wb[g, r * 128 + 112 : r * 128 + 128, 128:256] = hi.astype(BF16)


def build_x(taps, bx, tx, txb):
    spread = (iota((LANES, 384), 1) == 8 * iota((LANES, 384), 0)).astype(BF16)
    past = iota((LANES, LANES), 1) >= iota((LANES, LANES), 0)
    none = jnp.zeros((LANES, LANES), BF16)
    low, high = bx > 0, bx < 3

    def tiles(line):
        turned = [band(line[:, i * LANES : (i + 1) * LANES], LANES, 0) for i in range(3)]
        before = [0.0, turned[0], turned[1]]
        return [jnp.where(past, turned[i], before[i]) for i in range(3)]

    def put(ref, kept):
        for half in range(2):
            for at in range(4):
                here = none
                if 0 <= at - half < 3:
                    here = jnp.where(kept[at], kept_tiles[at - half], 0.0).astype(BF16)
                ref[half * 128 : half * 128 + 128, at * 128 : at * 128 + 128] = here

    wide = [dot(taps[k, 0:8, :].astype(BF16), spread) for k in range(2)]
    for r in range(RANK):
        kept_tiles = tiles(wide[0][r : r + 1])
        put(tx.at[0, r], (low, low, True, True))
        put(tx.at[1, r], (True, True, high, high))
        kept_tiles = tiles(wide[1][r : r + 1])
        put(txb.at[r], (low, True, True, high))


def build_y(taps, by, ty, tyb):
    def inside(rows, first):
        place = by * BLOCK - first + iota((rows, LANES), 1)
        return (place >= 0) & (place < 4 * BLOCK)

    plain = [
        jnp.where(inside(64, 2 * RAD), band(taps[0, 8 + r : 9 + r, :], 64, 0), 0.0) for r in range(RANK)
    ] + [
        jnp.where(inside(32, RAD), band(taps[1, 8 + r : 9 + r, :], 32, 0), 0.0) for r in range(RANK)
    ]
    plain = jnp.concatenate(plain, axis=0).astype(BF16)
    y, column = iota((LANES, 256), 0), iota((LANES, 256), 1)
    parts = [
        dot(plain, (column == 16 * (y // 8) + 8 * k + y % 8).astype(BF16)).reshape(36, 8, 256)
        for k in range(2)
    ]
    both = jnp.stack(parts, axis=1).reshape(36 * 16, 256).astype(BF16)
    for r in range(RANK):
        ty[r] = both[r * 128 : (r + 1) * 128]
    tyb[...] = both[384:576, 0:128]


def kernel(
    est_hbm, tile_hbm, psf_hbm, slot_view_hbm, total,
    est, tile, psf, slot_view,
    packed, parts, field, after_z, after_x, back_y, back_x, sums, rims,
    got_core, got_rim, got_chip, got_edge,
    taps, tx, ty, wz, tyb, txb, wb,
    load_sem, part_send, part_recv, face_send, face_recv, core_send, core_recv, sum_send, sum_recv,
):
    bx, by, vert = lax.axis_index("bx"), lax.axis_index("by"), lax.axis_index("vert")
    q, slot = vert // VIEWS, vert % VIEWS
    core, chip = slot % 2, slot // 2
    q_up, q_down = (q + 1) % 4, (q + 3) % 4

    loads = [
        pltpu.make_async_copy(source, target, load_sem.at[i])
        for i, (source, target) in enumerate(
            ((est_hbm, est), (psf_hbm, psf), (slot_view_hbm, slot_view), (tile_hbm, tile))
        )
    ]
    for copy in loads:
        copy.start()

    def at_vert(index):
        return {"vert": index}

    partner = at_vert(q * 4 + chip * 2 + 1 - core)
    x_up, x_down = {"bx": (bx + 1) % 4}, {"bx": (bx + 3) % 4}
    y_up, y_down = {"by": (by + 1) % 4}, {"by": (by + 3) % 4}
    first, last = slot == 0, slot == VIEWS - 1
    is_edge = first | last

    got_edge[...] = jnp.zeros_like(got_edge)
    barrier = pltpu.get_barrier_semaphore()

    def greet(device):
        pl.semaphore_signal(barrier, inc=1, device_id=device, device_id_type=MESH)

    for k in range(1, VIEWS):
        greet(at_vert(q * 4 + (slot + k) % VIEWS))
    for device in (x_up, x_down, y_up, y_down):
        greet(device)
    greet(at_vert(q_down * 4 + 3))
    greet(at_vert(q_up * 4))

    @pl.when(first)
    def _():
        greet(at_vert(q_down * 4 + 1))

    @pl.when(last)
    def _():
        greet(at_vert(q_up * 4 + 2))

    loads[0].wait()
    groups = est[...].reshape(BLOCK, GROUPS, 8, BLOCK)
    line = jnp.concatenate([groups[:, g].reshape(256, BLOCK) for g in range(GROUPS)], axis=1)
    packed[...] = pltpu.roll(line, slot * 32, 1).astype(BF16)

    pl.semaphore_wait(barrier, jnp.where(is_edge, 11, 8))

    def part_copy(dst_index, send, device, half):
        return pltpu.make_async_remote_copy(
            src_ref=packed.at[pl.ds(half * 128, 128), :], dst_ref=parts.at[dst_index],
            send_sem=part_send.at[send], recv_sem=part_recv.at[dst_index],
            device_id=device, device_id_type=MESH,
        )

    for k in range(1, VIEWS):
        other = (slot + k) % VIEWS
        part_copy(slot, k - 1, at_vert(q * 4 + other), other % 2).start()

    @pl.when(last)
    def _():
        for k in range(VIEWS):
            part_copy(4, 3 + k, at_vert(q_up * 4 + k), k % 2).start()

    @pl.when(first)
    def _():
        for k in range(VIEWS):
            part_copy(5, 3 + k, at_vert(q_down * 4 + k), k % 2).start()

    parts[slot] = packed[pl.ds(core * 128, 128), :]
    loads[1].wait()
    loads[2].wait()
    build_taps(psf, slot_view, slot, taps)
    build_z(taps, q, wz, wb)

    for k in range(1, VIEWS):
        part_copy((slot + k) % VIEWS, 0, partner, 0).wait_recv()
    for k in (4, 5):
        part_copy(k, 0, partner, 0).wait_recv()

    chunk = iota((128, LANES), 1) // 32
    own_rows = pl.ds(256 + core * 128, 128)
    have = [parts[k].astype(F32) for k in range(6)]
    for g in range(GROUPS):
        line = have[(3 - g) % 4]
        for at in range(3):
            line = jnp.where(chunk == at, have[(at - g) % 4], line)
        if g:
            line = pltpu.roll(line, LANES - 32 * g, 1)
        field[1, g, own_rows, :] = line.astype(BF16)
    is_high = iota((128, LANES), 1) % 32 < RAD
    line = pltpu.roll(jnp.where(is_high, have[5], have[4]), RAD, 1)
    field[1, 4, own_rows, :] = line.astype(BF16)

    def piece(jy, jx, tp, owner):
        return field.at[jy, :, pl.ds(jx * 256 + owner * 128 + tp * 64, 64), :]

    def number(jy, jx, tp):
        return (jy * 3 + jx) * 2 + tp

    def face_copy(source, target, tp, send, device):
        return pltpu.make_async_remote_copy(
            src_ref=piece(*source, tp, core), dst_ref=piece(*target, tp, core),
            send_sem=face_send.at[send], recv_sem=face_recv.at[number(*target, tp)],
            device_id=device, device_id_type=MESH,
        )

    def core_copy(jy, jx, tp, owner):
        return pltpu.make_async_remote_copy(
            src_ref=piece(jy, jx, tp, owner), dst_ref=piece(jy, jx, tp, owner),
            send_sem=core_send.at[number(jy, jx, tp)], recv_sem=core_recv.at[number(jy, jx, tp)],
            device_id=partner, device_id_type=MESH,
        )

    faces = []

    def send_face(source, target, tp, device):
        copy = face_copy(source, target, tp, len(faces), device)
        copy.start()
        faces.append(copy)

    def arrived(jy, jx, tp):
        face_copy((jy, jx), (jy, jx), tp, 0, partner).wait_recv()
        core_copy(jy, jx, tp, core).start()

    def swapped(jy, jx):
        for tp in range(2):
            core_copy(jy, jx, tp, 1 - core).wait_recv()

    def forward_z(jy, jx):
        rows = pl.ds(jx * 256, 256)
        rim = field[jy, 4, rows, :]
        for g in range(GROUPS):
            turned = pltpu.roll(rim, LANES - 32 * g, 1) if g else rim
            done = dot(jnp.concatenate([field[jy, g, rows, :], turned], axis=1), wz[...])
            for r in range(RANK):
                after_z[r, jy * GROUPS + g, rows, :] = done[:, r * 128 : (r + 1) * 128].astype(BF16)

    def forward_x(jy):
        def body(step, carry):
            r, group = step // 2, jy * GROUPS + step % 2 * 2
            for b in range(2):
                rows = pl.ds(b * 256, 512)
                both = jnp.concatenate([after_z[r, group + k, rows, :] for k in range(2)], axis=1)
                done = dot(tx[b, r], both).astype(BF16)
                for k in range(2):
                    after_x[r, group + k, b * 256 : b * 256 + 256, :] = done[:, k * 128 : k * 128 + 128]
            return carry

        lax.fori_loop(0, 2 * RANK, body, 0)

    for first_tp in (0, 1):
        send_face((1, 1), (1, 0), first_tp, x_up)
        send_face((1, 1), (1, 2), first_tp, x_down)
        send_face((1, 1), (0, 1), 1 - first_tp, y_up)
        send_face((1, 1), (2, 1), 1 - first_tp, y_down)
    for tp in (0, 1):
        core_copy(1, 1, tp, core).start()
    build_x(taps, bx, tx, txb)
    for side in (0, 2):
        arrived(1, side, 0)
        send_face((1, side), (0, side), 0, y_up)
        send_face((1, side), (2, side), 0, y_down)
        arrived(side, 1, 1)
        send_face((side, 1), (side, 0), 1, x_up)
        send_face((side, 1), (side, 2), 1, x_down)
    build_y(taps, by, ty, tyb)
    swapped(1, 1)
    forward_z(1, 1)
    for side in (0, 2):
        arrived(1, side, 1)
        arrived(side, 1, 0)
    for side in (0, 2):
        swapped(1, side)
        forward_z(1, side)
        swapped(side, 1)
        forward_z(side, 1)
    forward_x(1)
    for jy in (0, 2):
        for jx in (0, 2):
            for tp in range(2):
                arrived(jy, jx, tp)
    for jy in (0, 2):
        for jx in (0, 2):
            swapped(jy, jx)
            forward_z(jy, jx)
        forward_x(jy)

    loads[3].wait()

    def along_y(step, carry):
        blurred = None
        for r in range(RANK):
            both = [
                after_x[r, :, pl.ds(32 * step + 16 * k, 16), :].reshape(192, LANES) for k in range(2)
            ]
            part = dot(ty[r, :, 0:192], jnp.concatenate(both, axis=1))
            blurred = part if blurred is None else blurred + part
        seen = []
        for k in range(2):
            pair = [tile[4 * step + 2 * k + i].astype(F32).reshape(8, 8, LANES) for i in range(2)]
            seen.append(jnp.stack(pair, axis=1).reshape(128, LANES))
        seen = jnp.concatenate(seen, axis=1)
        quotient = (seen / (blurred / RANK + BACKGROUND)).astype(BF16)
        done = dot(tyb[...], quotient).astype(BF16)
        for k in range(2):
            back_y[:, pl.ds(32 * step + 16 * k, 16), :] = done[:, k * 128 : k * 128 + 128].reshape(
                12, 16, LANES
            )
        return carry

    lax.fori_loop(0, 16, along_y, 0)

    for r in range(RANK):
        for pair in range(2):
            at = r * GROUPS + 2 * pair
            both = jnp.concatenate([back_y[at], back_y[at + 1]], axis=1)
            done = dot(txb[r], both).astype(BF16)
            for k in range(2):
                back_x[2 * pair + k, :, r * 128 : (r + 1) * 128] = done[:, k * 128 : k * 128 + 128]

    rim_sum = None
    for g in range(GROUPS):
        done = dot(back_x[g], wb[g])
        for c in range(4):
            at = (g + c) % 4
            sums[c, :, at * 32 : at * 32 + 32] = done[:, at * 32 : at * 32 + 32]
        rim_sum = done[:, LANES:] if rim_sum is None else rim_sum + done[:, LANES:]
    top, bottom = rim_sum[0:128], rim_sum[128:256]
    is_low = iota((128, LANES), 1) % 32 < RAD
    rims[0] = jnp.where(is_low, top, pltpu.roll(bottom, RAD, 1))
    rims[1] = jnp.where(is_low, pltpu.roll(top, LANES - RAD, 1), bottom)

    def sum_copy(source, target, index, device):
        return pltpu.make_async_remote_copy(
            src_ref=source, dst_ref=target, send_sem=sum_send.at[index],
            recv_sem=sum_recv.at[index], device_id=device, device_id_type=MESH,
        )

    swaps = [
        sum_copy(sums.at[(1 - chip) * 2 + 1 - core], got_core.at[0], 0, partner),
        sum_copy(rims.at[1 - core], got_rim, 1, partner),
        sum_copy(sums.at[chip * 2 + 1 - core], got_core.at[1], 2, partner),
    ]
    for copy in swaps:
        copy.start()
    far = (1 - chip) * 2 + core
    swaps[0].wait_recv()
    sums[far] = sums[far] + got_core[0]
    over = sum_copy(sums.at[far], got_chip, 3, at_vert(q * 4 + far))
    over.start()
    swaps[1].wait_recv()
    rims[core] = rims[core] + got_rim[...]
    edge_home = jnp.where(core == 0, q_down * 4 + 3, q_up * 4)

    def edge_copy(which):
        return pltpu.make_async_remote_copy(
            src_ref=rims.at[core], dst_ref=got_edge.at[which], send_sem=sum_send.at[4],
            recv_sem=sum_recv.at[4 + which], device_id=at_vert(edge_home), device_id_type=MESH,
        )

    edge_copy(chip).start()
    swaps[2].wait_recv()
    sums[slot] = sums[slot] + got_core[1]
    over.wait_recv()

    @pl.when(is_edge)
    def _():
        edge_copy(0).wait_recv()
        edge_copy(1).wait_recv()

    edge = got_edge[0] + got_edge[1]
    mine = sums[slot] + got_chip[...]
    start = jnp.where(last, RAD, 0)
    lane128 = iota((128, LANES), 1)
    keep = is_edge & (lane128 >= start) & (lane128 < start + RAD)
    for g in range(GROUPS):
        own = pltpu.roll(mine, (8 - g - slot) % 4 * 32, 1)
        top = pltpu.roll(edge, (start + LANES - 32 * g) % LANES, 1)
        bottom = pltpu.roll(edge, (start + 2 * LANES - RAD - 32 * g) % LANES, 1)
        halves = (own[0:128] + jnp.where(keep, top, 0.0), own[128:256] + jnp.where(keep, bottom, 0.0))
        for half in range(2):
            total[16 * half : 16 * half + 16, g * 8 : g * 8 + 8, :] = halves[half][:, 0:BLOCK].reshape(
                16, 8, BLOCK
            )

    for k in range(1, VIEWS):
        part_copy(slot, k - 1, partner, 0).wait_send()

    @pl.when(is_edge)
    def _():
        for k in range(VIEWS):
            part_copy(4, 3 + k, partner, 0).wait_send()

    for copy in faces:
        copy.wait_send()
    for jy in range(3):
        for jx in range(3):
            for tp in range(2):
                core_copy(jy, jx, tp, core).wait_send()
    for copy in swaps:
        copy.wait_send()
    over.wait_send()
    edge_copy(0).wait_send()


def local(estimate, view_tiles, slot_view, psf_taps):
    vmem = pl.BlockSpec(memory_space=pltpu.VMEM)
    hbm = pl.BlockSpec(memory_space=pltpu.HBM)
    tile = view_tiles[0, 0, 0]
    psf = jnp.transpose(psf_taps, (1, 2, 0, 3))
    scratch = [
        pltpu.VMEM(estimate.shape, F32),
        pltpu.VMEM(tile.shape, BF16),
        pltpu.VMEM(psf.shape, F32),
        pltpu.VMEM(slot_view.shape, jnp.int32),
        pltpu.VMEM((256, LANES), BF16),
        pltpu.VMEM((6, 128, LANES), BF16),
        pltpu.VMEM((3, 5, 768, LANES), BF16),
        pltpu.VMEM((RANK, 12, 768, LANES), BF16),
        pltpu.VMEM((RANK, 12, 512, LANES), BF16),
        pltpu.VMEM((12, 512, LANES), BF16),
        pltpu.VMEM((GROUPS, 256, RANK * LANES), BF16),
        pltpu.VMEM((4, 256, LANES), F32),
        pltpu.VMEM((2, 128, LANES), F32),
        pltpu.VMEM((2, 256, LANES), F32),
        pltpu.VMEM((128, LANES), F32),
        pltpu.VMEM((256, LANES), F32),
        pltpu.VMEM((2, 128, LANES), F32),
        pltpu.VMEM((2, 24, LANES), F32),
        pltpu.VMEM((2, RANK, 256, 512), BF16),
        pltpu.VMEM((RANK, 128, 256), BF16),
        pltpu.VMEM((256, RANK * LANES), BF16),
        pltpu.VMEM((192, LANES), BF16),
        pltpu.VMEM((RANK, 256, 512), BF16),
        pltpu.VMEM((GROUPS, RANK * LANES, 256), BF16),
        pltpu.SemaphoreType.DMA((4,)),
        pltpu.SemaphoreType.DMA((7,)),
        pltpu.SemaphoreType.DMA((6,)),
        pltpu.SemaphoreType.DMA((16,)),
        pltpu.SemaphoreType.DMA((18,)),
        pltpu.SemaphoreType.DMA((18,)),
        pltpu.SemaphoreType.DMA((18,)),
        pltpu.SemaphoreType.DMA((5,)),
        pltpu.SemaphoreType.DMA((6,)),
    ]
    total = pl.pallas_call(
        kernel,
        out_shape=jax.ShapeDtypeStruct(estimate.shape, F32),
        in_specs=[hbm] * 4,
        out_specs=vmem,
        scratch_shapes=scratch,
        compiler_params=pltpu.CompilerParams(
            collective_id=0, has_side_effects=True, vmem_limit_bytes=64 * 1024 * 1024
        ),
    )(estimate, tile, psf, slot_view)
    return estimate * total * (1.0 / (RANK * VIEWS))


def solution(mesh):
    placed = (
        P("bx", "by", "vert"),
        P("bx", "by", "vert", None, None, None),
        P("bx", "by", None),
        P(),
    )
    return jax.shard_map(
        local, mesh=mesh, in_specs=placed, out_specs=P("bx", "by", "vert"), check_vma=False
    )
```

```python
import jax
import jax.numpy as jnp
from jax import lax
from jax.experimental import pallas as pl
from jax.experimental.pallas import tpu as pltpu
from jax.sharding import PartitionSpec as P

BACKGROUND = 0.1
MESH = pl.DeviceIdType.MESH
F32, BF16 = jnp.float32, jnp.bfloat16
BLOCK = 32
RAD = 16
TAPS = 33
RANK = 3
VIEWS = 4
GROUPS = 4
LANES = 128


def iota(shape, axis):
    return lax.broadcasted_iota(jnp.int32, shape, axis)


def dot(a, b):
    return jnp.dot(a, b, preferred_element_type=F32)


def build_taps(psf, slot_view, slot, taps):
    listed = slot_view[...]
    view = jnp.sum(jnp.where(iota(listed.shape, 2) == slot, listed, 0), axis=2, keepdims=True)
    held = iota((VIEWS, TAPS), 0) == view[0]
    mine = jnp.sum(jnp.where(held[None, None], psf[...], 0.0), axis=2)
    mine = (mine / jnp.sum(mine, axis=-1, keepdims=True)).astype(BF16).astype(F32)
    taps[...] = jnp.zeros_like(taps)
    for a in range(3):
        taps[0, 8 * a : 8 * a + RANK, :TAPS] = mine[a]
    flip = (iota((LANES, LANES), 0) + iota((LANES, LANES), 1) == TAPS - 1).astype(BF16)
    taps[1] = dot(taps[0].astype(BF16), flip)


def band(line, rows, start):
    line = jnp.broadcast_to(line, (rows, LANES))
    return pltpu.roll(line, start % LANES, 1, stride=1, stride_axis=0)


def build_z(taps, q, wz, wb):
    z_in, z_out = iota((LANES, LANES), 0), iota((LANES, LANES), 1)
    near = jnp.abs(z_in - z_out) <= RAD
    rim, out = iota((32, LANES), 0), iota((32, LANES), 1)
    rim_ok = ((rim < RAD) & (out <= rim) & (q > 0)) | ((rim >= RAD) & (out >= rim + 96) & (q < 3))
    lane16 = iota((16, LANES), 1)
    for r in range(RANK):
        forward, backward = taps[1, 16 + r : 17 + r, :], taps[0, 16 + r : 17 + r, :]
        columns = slice(r * LANES, (r + 1) * LANES)
        wz[0:128, columns] = jnp.where(near, band(forward, LANES, -RAD), 0.0).astype(BF16)
        wz[128:160, columns] = jnp.where(rim_ok, band(forward, 32, 96), 0.0).astype(BF16)
        wz[160:256, columns] = jnp.zeros((96, LANES), BF16)
        main = jnp.where(near, band(backward, LANES, -RAD), 0.0)
        low = jnp.where((lane16 < RAD) & (q > 0), band(backward, 16, 0), 0.0)
        high = jnp.where((lane16 < RAD) & (q < 3), band(backward, 16, 96), 0.0)
        high = pltpu.roll(high, RAD, 1)
        for g in range(GROUPS):
            wb[g, r * 128 : r * 128 + 128, 0:128] = (
                pltpu.roll(main, 32 * g, 1) if g else main
            ).astype(BF16)
            wb[g, r * 128 : r * 128 + 128, 128:256] = jnp.zeros((128, LANES), BF16)
            lo, hi = (pltpu.roll(m, 32 * g, 1) if g else m for m in (low, high))
            wb[g, r * 128 : r * 128 + 16, 128:256] = lo.astype(BF16)
            wb[g, r * 128 + 112 : r * 128 + 128, 128:256] = hi.astype(BF16)


def build_x(taps, bx, tx, txb):
    spread = (iota((LANES, 384), 1) == 8 * iota((LANES, 384), 0)).astype(BF16)
    past = iota((LANES, LANES), 1) >= iota((LANES, LANES), 0)
    none = jnp.zeros((LANES, LANES), BF16)
    low, high = bx > 0, bx < 3

    def tiles(line):
        turned = [band(line[:, i * LANES : (i + 1) * LANES], LANES, 0) for i in range(3)]
        before = [0.0, turned[0], turned[1]]
        return [jnp.where(past, turned[i], before[i]) for i in range(3)]

    def put(ref, kept):
        for half in range(2):
            for at in range(4):
                here = none
                if 0 <= at - half < 3:
                    here = jnp.where(kept[at], kept_tiles[at - half], 0.0).astype(BF16)
                ref[half * 128 : half * 128 + 128, at * 128 : at * 128 + 128] = here

    wide = [dot(taps[k, 0:8, :].astype(BF16), spread) for k in range(2)]
    for r in range(RANK):
        kept_tiles = tiles(wide[0][r : r + 1])
        put(tx.at[0, r], (low, low, True, True))
        put(tx.at[1, r], (True, True, high, high))
        kept_tiles = tiles(wide[1][r : r + 1])
        put(txb.at[r], (low, True, True, high))


def build_y(taps, by, ty, tyb):
    def inside(rows, first):
        place = by * BLOCK - first + iota((rows, LANES), 1)
        return (place >= 0) & (place < 4 * BLOCK)

    plain = [
        jnp.where(inside(64, 2 * RAD), band(taps[0, 8 + r : 9 + r, :], 64, 0), 0.0) for r in range(RANK)
    ] + [
        jnp.where(inside(32, RAD), band(taps[1, 8 + r : 9 + r, :], 32, 0), 0.0) for r in range(RANK)
    ]
    plain = jnp.concatenate(plain, axis=0).astype(BF16)
    y, column = iota((LANES, 256), 0), iota((LANES, 256), 1)
    parts = [
        dot(plain, (column == 16 * (y // 8) + 8 * k + y % 8).astype(BF16)).reshape(36, 8, 256)
        for k in range(2)
    ]
    both = jnp.stack(parts, axis=1).reshape(36 * 16, 256).astype(BF16)
    for r in range(RANK):
        ty[r] = both[r * 128 : (r + 1) * 128]
    tyb[...] = both[384:576, 0:128]


def kernel(
    est_hbm, tile_hbm, psf_hbm, slot_view_hbm, total,
    est, tile, psf, slot_view,
    packed, parts, field, after_z, after_x, back_y, back_x, sums, rims,
    got_core, got_rim, got_chip, got_edge,
    taps, tx, ty, wz, tyb, txb, wb,
    load_sem, part_send, part_recv, face_send, face_recv, core_send, core_recv, sum_send, sum_recv,
):
    bx, by, vert = lax.axis_index("bx"), lax.axis_index("by"), lax.axis_index("vert")
    q, slot = vert // VIEWS, vert % VIEWS
    core, chip = slot % 2, slot // 2
    q_up, q_down = (q + 1) % 4, (q + 3) % 4

    loads = [
        pltpu.make_async_copy(source, target, load_sem.at[i])
        for i, (source, target) in enumerate(
            ((est_hbm, est), (psf_hbm, psf), (slot_view_hbm, slot_view), (tile_hbm, tile))
        )
    ]
    for copy in loads:
        copy.start()

    def at_vert(index):
        return {"vert": index}

    partner = at_vert(q * 4 + chip * 2 + 1 - core)
    x_up, x_down = {"bx": (bx + 1) % 4}, {"bx": (bx + 3) % 4}
    y_up, y_down = {"by": (by + 1) % 4}, {"by": (by + 3) % 4}
    first, last = slot == 0, slot == VIEWS - 1
    is_edge = first | last

    got_edge[...] = jnp.zeros_like(got_edge)
    barrier = pltpu.get_barrier_semaphore()

    def greet(device):
        pl.semaphore_signal(barrier, inc=1, device_id=device, device_id_type=MESH)

    for k in range(1, VIEWS):
        greet(at_vert(q * 4 + (slot + k) % VIEWS))
    for device in (x_up, x_down, y_up, y_down):
        greet(device)
    greet(at_vert(q_down * 4 + 3))
    greet(at_vert(q_up * 4))

    @pl.when(first)
    def _():
        greet(at_vert(q_down * 4 + 1))

    @pl.when(last)
    def _():
        greet(at_vert(q_up * 4 + 2))

    loads[0].wait()
    groups = est[...].reshape(BLOCK, GROUPS, 8, BLOCK)
    line = jnp.concatenate([groups[:, g].reshape(256, BLOCK) for g in range(GROUPS)], axis=1)
    packed[...] = pltpu.roll(line, slot * 32, 1).astype(BF16)

    pl.semaphore_wait(barrier, jnp.where(is_edge, 11, 8))

    def part_copy(dst_index, send, device, half):
        return pltpu.make_async_remote_copy(
            src_ref=packed.at[pl.ds(half * 128, 128), :], dst_ref=parts.at[dst_index],
            send_sem=part_send.at[send], recv_sem=part_recv.at[dst_index],
            device_id=device, device_id_type=MESH,
        )

    for k in range(1, VIEWS):
        other = (slot + k) % VIEWS
        part_copy(slot, k - 1, at_vert(q * 4 + other), other % 2).start()

    @pl.when(last)
    def _():
        for k in range(VIEWS):
            part_copy(4, 3 + k, at_vert(q_up * 4 + k), k % 2).start()

    @pl.when(first)
    def _():
        for k in range(VIEWS):
            part_copy(5, 3 + k, at_vert(q_down * 4 + k), k % 2).start()

    parts[slot] = packed[pl.ds(core * 128, 128), :]
    loads[1].wait()
    loads[2].wait()
    build_taps(psf, slot_view, slot, taps)
    build_z(taps, q, wz, wb)

    for k in range(1, VIEWS):
        part_copy((slot + k) % VIEWS, 0, partner, 0).wait_recv()
    for k in (4, 5):
        part_copy(k, 0, partner, 0).wait_recv()

    chunk = iota((128, LANES), 1) // 32
    own_rows = pl.ds(256 + core * 128, 128)
    have = [parts[k].astype(F32) for k in range(6)]
    for g in range(GROUPS):
        line = have[(3 - g) % 4]
        for at in range(3):
            line = jnp.where(chunk == at, have[(at - g) % 4], line)
        if g:
            line = pltpu.roll(line, LANES - 32 * g, 1)
        field[1, g, own_rows, :] = line.astype(BF16)
    is_high = iota((128, LANES), 1) % 32 < RAD
    line = pltpu.roll(jnp.where(is_high, have[5], have[4]), RAD, 1)
    field[1, 4, own_rows, :] = line.astype(BF16)

    def piece(jy, jx, tp, owner):
        return field.at[jy, :, pl.ds(jx * 256 + owner * 128 + tp * 64, 64), :]

    def number(jy, jx, tp):
        return (jy * 3 + jx) * 2 + tp

    def face_copy(source, target, tp, send, device):
        return pltpu.make_async_remote_copy(
            src_ref=piece(*source, tp, core), dst_ref=piece(*target, tp, core),
            send_sem=face_send.at[send], recv_sem=face_recv.at[number(*target, tp)],
            device_id=device, device_id_type=MESH,
        )

    def core_copy(jy, jx, tp, owner):
        return pltpu.make_async_remote_copy(
            src_ref=piece(jy, jx, tp, owner), dst_ref=piece(jy, jx, tp, owner),
            send_sem=core_send.at[number(jy, jx, tp)], recv_sem=core_recv.at[number(jy, jx, tp)],
            device_id=partner, device_id_type=MESH,
        )

    faces = []

    def send_face(source, target, tp, device):
        copy = face_copy(source, target, tp, len(faces), device)
        copy.start()
        faces.append(copy)

    def arrived(jy, jx, tp):
        face_copy((jy, jx), (jy, jx), tp, 0, partner).wait_recv()
        core_copy(jy, jx, tp, core).start()

    def swapped(jy, jx):
        for tp in range(2):
            core_copy(jy, jx, tp, 1 - core).wait_recv()

    def forward_z(jy, jx):
        rows = pl.ds(jx * 256, 256)
        rim = field[jy, 4, rows, :]
        for g in range(GROUPS):
            turned = pltpu.roll(rim, LANES - 32 * g, 1) if g else rim
            done = dot(jnp.concatenate([field[jy, g, rows, :], turned], axis=1), wz[...])
            for r in range(RANK):
                after_z[r, jy * GROUPS + g, rows, :] = done[:, r * 128 : (r + 1) * 128].astype(BF16)

    def forward_x(jy):
        def body(step, carry):
            r, group = step // 2, jy * GROUPS + step % 2 * 2
            for b in range(2):
                rows = pl.ds(b * 256, 512)
                both = jnp.concatenate([after_z[r, group + k, rows, :] for k in range(2)], axis=1)
                done = dot(tx[b, r], both).astype(BF16)
                for k in range(2):
                    after_x[r, group + k, b * 256 : b * 256 + 256, :] = done[:, k * 128 : k * 128 + 128]
            return carry

        lax.fori_loop(0, 2 * RANK, body, 0, unroll=True)

    for first_tp in (0, 1):
        send_face((1, 1), (1, 0), first_tp, x_up)
        send_face((1, 1), (1, 2), first_tp, x_down)
        send_face((1, 1), (0, 1), 1 - first_tp, y_up)
        send_face((1, 1), (2, 1), 1 - first_tp, y_down)
    for tp in (0, 1):
        core_copy(1, 1, tp, core).start()
    build_x(taps, bx, tx, txb)
    for side in (0, 2):
        arrived(1, side, 0)
        send_face((1, side), (0, side), 0, y_up)
        send_face((1, side), (2, side), 0, y_down)
        arrived(side, 1, 1)
        send_face((side, 1), (side, 0), 1, x_up)
        send_face((side, 1), (side, 2), 1, x_down)
    build_y(taps, by, ty, tyb)
    swapped(1, 1)
    forward_z(1, 1)
    for side in (0, 2):
        arrived(1, side, 1)
        arrived(side, 1, 0)
    for side in (0, 2):
        swapped(1, side)
        forward_z(1, side)
        swapped(side, 1)
        forward_z(side, 1)
    forward_x(1)
    for jy in (0, 2):
        for jx in (0, 2):
            for tp in range(2):
                arrived(jy, jx, tp)
    for jy in (0, 2):
        for jx in (0, 2):
            swapped(jy, jx)
            forward_z(jy, jx)
        forward_x(jy)

    loads[3].wait()

    def along_y(step, carry):
        blurred = None
        for r in range(RANK):
            both = [
                after_x[r, :, pl.ds(32 * step + 16 * k, 16), :].reshape(192, LANES) for k in range(2)
            ]
            part = dot(ty[r, :, 0:192], jnp.concatenate(both, axis=1))
            blurred = part if blurred is None else blurred + part
        seen = []
        for k in range(2):
            pair = [tile[4 * step + 2 * k + i].astype(F32).reshape(8, 8, LANES) for i in range(2)]
            seen.append(jnp.stack(pair, axis=1).reshape(128, LANES))
        seen = jnp.concatenate(seen, axis=1)
        quotient = (RANK * seen / (blurred + RANK * BACKGROUND)).astype(BF16)
        done = dot(tyb[...], quotient).astype(BF16)
        for k in range(2):
            back_y[:, pl.ds(32 * step + 16 * k, 16), :] = done[:, k * 128 : k * 128 + 128].reshape(
                12, 16, LANES
            )
        return carry

    lax.fori_loop(0, 16, along_y, 0, unroll=4)

    for r in range(RANK):
        for pair in range(2):
            at = r * GROUPS + 2 * pair
            both = jnp.concatenate([back_y[at], back_y[at + 1]], axis=1)
            done = dot(txb[r], both).astype(BF16)
            for k in range(2):
                back_x[2 * pair + k, :, r * 128 : (r + 1) * 128] = done[:, k * 128 : k * 128 + 128]

    rim_sum = None
    for g in range(GROUPS):
        done = dot(back_x[g], wb[g])
        for c in range(4):
            at = (g + c) % 4
            sums[c, :, at * 32 : at * 32 + 32] = done[:, at * 32 : at * 32 + 32]
        rim_sum = done[:, LANES:] if rim_sum is None else rim_sum + done[:, LANES:]
    top, bottom = rim_sum[0:128], rim_sum[128:256]
    is_low = iota((128, LANES), 1) % 32 < RAD
    rims[0] = jnp.where(is_low, top, pltpu.roll(bottom, RAD, 1))
    rims[1] = jnp.where(is_low, pltpu.roll(top, LANES - RAD, 1), bottom)

    def sum_copy(source, target, index, device):
        return pltpu.make_async_remote_copy(
            src_ref=source, dst_ref=target, send_sem=sum_send.at[index],
            recv_sem=sum_recv.at[index], device_id=device, device_id_type=MESH,
        )

    swaps = [
        sum_copy(sums.at[(1 - chip) * 2 + 1 - core], got_core.at[0], 0, partner),
        sum_copy(rims.at[1 - core], got_rim, 1, partner),
        sum_copy(sums.at[chip * 2 + 1 - core], got_core.at[1], 2, partner),
    ]
    for copy in swaps:
        copy.start()
    far = (1 - chip) * 2 + core
    swaps[0].wait_recv()
    sums[far] = sums[far] + got_core[0]
    over = sum_copy(sums.at[far], got_chip, 3, at_vert(q * 4 + far))
    over.start()
    swaps[1].wait_recv()
    rims[core] = rims[core] + got_rim[...]
    edge_home = jnp.where(core == 0, q_down * 4 + 3, q_up * 4)

    def edge_copy(which):
        return pltpu.make_async_remote_copy(
            src_ref=rims.at[core], dst_ref=got_edge.at[which], send_sem=sum_send.at[4],
            recv_sem=sum_recv.at[4 + which], device_id=at_vert(edge_home), device_id_type=MESH,
        )

    edge_copy(chip).start()
    swaps[2].wait_recv()
    sums[slot] = sums[slot] + got_core[1]
    over.wait_recv()

    @pl.when(is_edge)
    def _():
        edge_copy(0).wait_recv()
        edge_copy(1).wait_recv()

    edge = got_edge[0] + got_edge[1]
    mine = sums[slot] + got_chip[...]
    start = jnp.where(last, RAD, 0)
    lane128 = iota((128, LANES), 1)
    keep = is_edge & (lane128 >= start) & (lane128 < start + RAD)
    for g in range(GROUPS):
        own = pltpu.roll(mine, (8 - g - slot) % 4 * 32, 1)
        top = pltpu.roll(edge, (start + LANES - 32 * g) % LANES, 1)
        bottom = pltpu.roll(edge, (start + 2 * LANES - RAD - 32 * g) % LANES, 1)
        halves = (own[0:128] + jnp.where(keep, top, 0.0), own[128:256] + jnp.where(keep, bottom, 0.0))
        for half in range(2):
            total[16 * half : 16 * half + 16, g * 8 : g * 8 + 8, :] = halves[half][:, 0:BLOCK].reshape(
                16, 8, BLOCK
            )

    for k in range(1, VIEWS):
        part_copy(slot, k - 1, partner, 0).wait_send()

    @pl.when(is_edge)
    def _():
        for k in range(VIEWS):
            part_copy(4, 3 + k, partner, 0).wait_send()

    for copy in faces:
        copy.wait_send()
    for jy in range(3):
        for jx in range(3):
            for tp in range(2):
                core_copy(jy, jx, tp, core).wait_send()
    for copy in swaps:
        copy.wait_send()
    over.wait_send()
    edge_copy(0).wait_send()


def local(estimate, view_tiles, slot_view, psf_taps):
    vmem = pl.BlockSpec(memory_space=pltpu.VMEM)
    hbm = pl.BlockSpec(memory_space=pltpu.HBM)
    tile = view_tiles[0, 0, 0]
    psf = jnp.transpose(psf_taps, (1, 2, 0, 3))
    scratch = [
        pltpu.VMEM(estimate.shape, F32),
        pltpu.VMEM(tile.shape, BF16),
        pltpu.VMEM(psf.shape, F32),
        pltpu.VMEM(slot_view.shape, jnp.int32),
        pltpu.VMEM((256, LANES), BF16),
        pltpu.VMEM((6, 128, LANES), BF16),
        pltpu.VMEM((3, 5, 768, LANES), BF16),
        pltpu.VMEM((RANK, 12, 768, LANES), BF16),
        pltpu.VMEM((RANK, 12, 512, LANES), BF16),
        pltpu.VMEM((12, 512, LANES), BF16),
        pltpu.VMEM((GROUPS, 256, RANK * LANES), BF16),
        pltpu.VMEM((4, 256, LANES), F32),
        pltpu.VMEM((2, 128, LANES), F32),
        pltpu.VMEM((2, 256, LANES), F32),
        pltpu.VMEM((128, LANES), F32),
        pltpu.VMEM((256, LANES), F32),
        pltpu.VMEM((2, 128, LANES), F32),
        pltpu.VMEM((2, 24, LANES), F32),
        pltpu.VMEM((2, RANK, 256, 512), BF16),
        pltpu.VMEM((RANK, 128, 256), BF16),
        pltpu.VMEM((256, RANK * LANES), BF16),
        pltpu.VMEM((192, LANES), BF16),
        pltpu.VMEM((RANK, 256, 512), BF16),
        pltpu.VMEM((GROUPS, RANK * LANES, 256), BF16),
        pltpu.SemaphoreType.DMA((4,)),
        pltpu.SemaphoreType.DMA((7,)),
        pltpu.SemaphoreType.DMA((6,)),
        pltpu.SemaphoreType.DMA((16,)),
        pltpu.SemaphoreType.DMA((18,)),
        pltpu.SemaphoreType.DMA((18,)),
        pltpu.SemaphoreType.DMA((18,)),
        pltpu.SemaphoreType.DMA((5,)),
        pltpu.SemaphoreType.DMA((6,)),
    ]
    total = pl.pallas_call(
        kernel,
        out_shape=jax.ShapeDtypeStruct(estimate.shape, F32),
        in_specs=[hbm] * 4,
        out_specs=vmem,
        scratch_shapes=scratch,
        compiler_params=pltpu.CompilerParams(
            collective_id=0, has_side_effects=True, vmem_limit_bytes=64 * 1024 * 1024
        ),
    )(estimate, tile, psf, slot_view)
    return estimate * total * (1.0 / (RANK * VIEWS))


def solution(mesh):
    placed = (
        P("bx", "by", "vert"),
        P("bx", "by", "vert", None, None, None),
        P("bx", "by", None),
        P(),
    )
    return jax.shard_map(
        local, mesh=mesh, in_specs=placed, out_specs=P("bx", "by", "vert"), check_vma=False
    )
```

```python
import jax
import jax.numpy as jnp
from jax import lax
from jax.experimental import pallas as pl
from jax.experimental.pallas import tpu as pltpu
from jax.sharding import PartitionSpec as P

BACKGROUND = 0.1
MESH = pl.DeviceIdType.MESH
F32, BF16 = jnp.float32, jnp.bfloat16
BLOCK = 32
RAD = 16
TAPS = 33
RANK = 3
VIEWS = 4
GROUPS = 4
LANES = 128


def iota(shape, axis):
    return lax.broadcasted_iota(jnp.int32, shape, axis)


def dot(a, b):
    return jnp.dot(a, b, preferred_element_type=F32)


def build_taps(psf, slot_view, slot, taps):
    listed = slot_view[...]
    view = jnp.sum(jnp.where(iota(listed.shape, 2) == slot, listed, 0), axis=2, keepdims=True)
    held = iota((VIEWS, TAPS), 0) == view[0]
    mine = jnp.sum(jnp.where(held[None, None], psf[...], 0.0), axis=2)
    mine = (mine / jnp.sum(mine, axis=-1, keepdims=True)).astype(BF16).astype(F32)
    taps[...] = jnp.zeros_like(taps)
    for a in range(3):
        taps[0, 8 * a : 8 * a + RANK, :TAPS] = mine[a]
    flip = (iota((LANES, LANES), 0) + iota((LANES, LANES), 1) == TAPS - 1).astype(BF16)
    taps[1] = dot(taps[0].astype(BF16), flip)


def band(line, rows, start):
    line = jnp.broadcast_to(line, (rows, LANES))
    return pltpu.roll(line, start % LANES, 1, stride=1, stride_axis=0)


def build_z(taps, q, wz, wb):
    z_in, z_out = iota((LANES, LANES), 0), iota((LANES, LANES), 1)
    near = jnp.abs(z_in - z_out) <= RAD
    rim, out = iota((32, LANES), 0), iota((32, LANES), 1)
    rim_ok = ((rim < RAD) & (out <= rim) & (q > 0)) | ((rim >= RAD) & (out >= rim + 96) & (q < 3))
    lane16 = iota((16, LANES), 1)
    for r in range(RANK):
        forward, backward = taps[1, 16 + r : 17 + r, :], taps[0, 16 + r : 17 + r, :]
        columns = slice(r * LANES, (r + 1) * LANES)
        wz[0:128, columns] = jnp.where(near, band(forward, LANES, -RAD), 0.0).astype(BF16)
        wz[128:160, columns] = jnp.where(rim_ok, band(forward, 32, 96), 0.0).astype(BF16)
        wz[160:256, columns] = jnp.zeros((96, LANES), BF16)
        main = jnp.where(near, band(backward, LANES, -RAD), 0.0)
        low = jnp.where((lane16 < RAD) & (q > 0), band(backward, 16, 0), 0.0)
        high = jnp.where((lane16 < RAD) & (q < 3), band(backward, 16, 96), 0.0)
        high = pltpu.roll(high, RAD, 1)
        for g in range(GROUPS):
            wb[g, r * 128 : r * 128 + 128, 0:128] = (
                pltpu.roll(main, 32 * g, 1) if g else main
            ).astype(BF16)
            wb[g, r * 128 : r * 128 + 128, 128:256] = jnp.zeros((128, LANES), BF16)
            lo, hi = (pltpu.roll(m, 32 * g, 1) if g else m for m in (low, high))
            wb[g, r * 128 : r * 128 + 16, 128:256] = lo.astype(BF16)
            wb[g, r * 128 + 112 : r * 128 + 128, 128:256] = hi.astype(BF16)


def build_x(taps, bx, tx, txb):
    spread = (iota((LANES, 384), 1) == 8 * iota((LANES, 384), 0)).astype(BF16)
    past = iota((LANES, LANES), 1) >= iota((LANES, LANES), 0)
    none = jnp.zeros((LANES, LANES), BF16)
    low, high = bx > 0, bx < 3

    def tiles(line):
        turned = [band(line[:, i * LANES : (i + 1) * LANES], LANES, 0) for i in range(3)]
        before = [0.0, turned[0], turned[1]]
        return [jnp.where(past, turned[i], before[i]) for i in range(3)]

    def put(ref, kept):
        for half in range(2):
            for at in range(4):
                here = none
                if 0 <= at - half < 3:
                    here = jnp.where(kept[at], kept_tiles[at - half], 0.0).astype(BF16)
                ref[half * 128 : half * 128 + 128, at * 128 : at * 128 + 128] = here

    wide = [dot(taps[k, 0:8, :].astype(BF16), spread) for k in range(2)]
    for r in range(RANK):
        kept_tiles = tiles(wide[0][r : r + 1])
        put(tx.at[r], (True, True, True, True))
        kept_tiles = tiles(wide[1][r : r + 1])
        put(txb.at[r], (low, True, True, high))


def build_y(taps, by, ty, tyb):
    def inside(rows, first):
        place = by * BLOCK - first + iota((rows, LANES), 1)
        return (place >= 0) & (place < 4 * BLOCK)

    plain = [
        jnp.where(inside(64, 2 * RAD), band(taps[0, 8 + r : 9 + r, :], 64, 0), 0.0) for r in range(RANK)
    ] + [
        jnp.where(inside(32, RAD), band(taps[1, 8 + r : 9 + r, :], 32, 0), 0.0) for r in range(RANK)
    ]
    plain = jnp.concatenate(plain, axis=0).astype(BF16)
    y, column = iota((LANES, 256), 0), iota((LANES, 256), 1)
    parts = [
        dot(plain, (column == 16 * (y // 8) + 8 * k + y % 8).astype(BF16)).reshape(36, 8, 256)
        for k in range(2)
    ]
    both = jnp.stack(parts, axis=1).reshape(36 * 16, 256).astype(BF16)
    for r in range(RANK):
        ty[r] = both[r * 128 : (r + 1) * 128]
    tyb[...] = both[384:576, 0:128]


def kernel(
    est_hbm, tile_hbm, psf_hbm, slot_view_hbm, refined,
    est, tile, psf, slot_view,
    packed, parts, field, after_z, after_x, back_y, back_x, sums, rims,
    got_core, got_rim, got_chip, got_edge,
    taps, tx, ty, wz, tyb, txb, wb,
    load_sem, part_send, part_recv, face_send, face_recv, core_send, core_recv, sum_send, sum_recv,
):
    bx, by, vert = lax.axis_index("bx"), lax.axis_index("by"), lax.axis_index("vert")
    q, slot = vert // VIEWS, vert % VIEWS
    core, chip = slot % 2, slot // 2

    loads = [
        pltpu.make_async_copy(source, target, load_sem.at[i])
        for i, (source, target) in enumerate(
            ((est_hbm, est), (psf_hbm, psf), (slot_view_hbm, slot_view), (tile_hbm, tile))
        )
    ]
    for copy in loads:
        copy.start()

    def at_vert(index):
        return {"vert": index}

    partner = at_vert(q * 4 + chip * 2 + 1 - core)
    x_up, x_down = ({"bx": bx + 1}, bx < 3), ({"bx": bx - 1}, bx > 0)
    y_up, y_down = ({"by": by + 1}, by < 3), ({"by": by - 1}, by > 0)
    above, below = q < 3, q > 0
    first, last = slot == 0, slot == VIEWS - 1
    is_edge = (first & below) | (last & above)

    def exists(jy, jx):
        here = jy == jy
        for index, j in ((by, jy), (bx, jx)):
            if j != 1:
                here = (index > 0 if j == 0 else index < 3) & here
        return here

    got_edge[...] = jnp.zeros_like(got_edge)
    barrier = pltpu.get_barrier_semaphore()

    def greet(device):
        pl.semaphore_signal(barrier, inc=1, device_id=device, device_id_type=MESH)

    for k in range(1, VIEWS):
        greet(at_vert(q * 4 + (slot + k) % VIEWS))
    for device, there in (x_up, x_down, y_up, y_down):
        pl.when(there)(lambda device=device: greet(device))

    @pl.when(below)
    def _():
        greet(at_vert(vert - slot - 1))
        pl.when(first)(lambda: greet(at_vert(vert - 3)))

    @pl.when(above)
    def _():
        greet(at_vert(vert - slot + 4))
        pl.when(last)(lambda: greet(at_vert(vert + 3)))

    loads[0].wait()
    groups = est[...].reshape(BLOCK, GROUPS, 8, BLOCK)
    line = jnp.concatenate([groups[:, g].reshape(256, BLOCK) for g in range(GROUPS)], axis=1)
    packed[...] = pltpu.roll(line, slot * 32, 1).astype(BF16)

    beside = [(there, 1) for _, there in (x_up, x_down, y_up, y_down)] + [(is_edge, 4)]
    beside += [((slot == 1) & above, 1), ((slot == 2) & below, 1)]
    pl.semaphore_wait(barrier, 3 + sum(jnp.where(there, n, 0) for there, n in beside))

    def part_copy(dst_index, send, device, half):
        return pltpu.make_async_remote_copy(
            src_ref=packed.at[pl.ds(half * 128, 128), :], dst_ref=parts.at[dst_index],
            send_sem=part_send.at[send], recv_sem=part_recv.at[dst_index],
            device_id=device, device_id_type=MESH,
        )

    for k in range(1, VIEWS):
        other = (slot + k) % VIEWS
        part_copy(slot, k - 1, at_vert(q * 4 + other), other % 2).start()

    @pl.when(last & above)
    def _():
        for k in range(VIEWS):
            part_copy(4, 3 + k, at_vert(vert + 1 + k), k % 2).start()

    @pl.when(first & below)
    def _():
        for k in range(VIEWS):
            part_copy(5, 3 + k, at_vert(vert - 4 + k), k % 2).start()

    parts[slot] = packed[pl.ds(core * 128, 128), :]

    def clear(ref):
        ref[...] = jnp.zeros(ref.shape, BF16)

    pl.when(~below)(lambda: clear(parts.at[4]))
    pl.when(~above)(lambda: clear(parts.at[5]))
    pl.when(bx == 0)(lambda: clear(field.at[:, :, 0:256, :]))
    pl.when(bx == 3)(lambda: clear(field.at[:, :, 512:768, :]))
    pl.when(by == 0)(lambda: clear(field.at[0]))
    pl.when(by == 3)(lambda: clear(field.at[2]))
    loads[1].wait()
    loads[2].wait()
    build_taps(psf, slot_view, slot, taps)
    build_z(taps, q, wz, wb)

    for k in range(1, VIEWS):
        part_copy((slot + k) % VIEWS, 0, partner, 0).wait_recv()
    for k, there in ((4, below), (5, above)):
        pl.when(there)(lambda k=k: part_copy(k, 0, partner, 0).wait_recv())

    chunk = iota((128, LANES), 1) // 32
    own_rows = pl.ds(256 + core * 128, 128)
    have = [parts[k].astype(F32) for k in range(6)]
    for g in range(GROUPS):
        line = have[(3 - g) % 4]
        for at in range(3):
            line = jnp.where(chunk == at, have[(at - g) % 4], line)
        if g:
            line = pltpu.roll(line, LANES - 32 * g, 1)
        field[1, g, own_rows, :] = line.astype(BF16)
    is_high = iota((128, LANES), 1) % 32 < RAD
    line = pltpu.roll(jnp.where(is_high, have[5], have[4]), RAD, 1)
    field[1, 4, own_rows, :] = line.astype(BF16)

    def piece(jy, jx, tp, owner):
        return field.at[jy, :, pl.ds(jx * 256 + owner * 128 + tp * 64, 64), :]

    def number(jy, jx, tp):
        return (jy * 3 + jx) * 2 + tp

    def face_copy(source, target, tp, send, device):
        return pltpu.make_async_remote_copy(
            src_ref=piece(*source, tp, core), dst_ref=piece(*target, tp, core),
            send_sem=face_send.at[send], recv_sem=face_recv.at[number(*target, tp)],
            device_id=device, device_id_type=MESH,
        )

    def core_copy(jy, jx, tp, owner):
        return pltpu.make_async_remote_copy(
            src_ref=piece(jy, jx, tp, owner), dst_ref=piece(jy, jx, tp, owner),
            send_sem=core_send.at[number(jy, jx, tp)], recv_sem=core_recv.at[number(jy, jx, tp)],
            device_id=partner, device_id_type=MESH,
        )

    faces = []

    def send_face(source, target, tp, way):
        device, there = way
        copy = face_copy(source, target, tp, len(faces), device)
        there = there & exists(*source)
        pl.when(there)(copy.start)
        faces.append((copy, there))

    def arrived(jy, jx, tp):
        @pl.when(exists(jy, jx))
        def _():
            face_copy((jy, jx), (jy, jx), tp, 0, partner).wait_recv()
            core_copy(jy, jx, tp, core).start()

    def swapped(jy, jx):
        @pl.when(exists(jy, jx))
        def _():
            for tp in range(2):
                core_copy(jy, jx, tp, 1 - core).wait_recv()

    def forward_z(jy, jx):
        rows = pl.ds(jx * 256, 256)
        rim = field[jy, 4, rows, :]
        for g in range(GROUPS):
            turned = pltpu.roll(rim, LANES - 32 * g, 1) if g else rim
            done = dot(jnp.concatenate([field[jy, g, rows, :], turned], axis=1), wz[...])
            for r in range(RANK):
                after_z[r, jy * GROUPS + g, rows, :] = done[:, r * 128 : (r + 1) * 128].astype(BF16)

    def forward_x(jy):
        def body(step, carry):
            r, group = step // 2, jy * GROUPS + step % 2 * 2
            for b in range(2):
                rows = pl.ds(b * 256, 512)
                both = jnp.concatenate([after_z[r, group + k, rows, :] for k in range(2)], axis=1)
                done = dot(tx[r], both).astype(BF16)
                for k in range(2):
                    after_x[r, group + k, b * 256 : b * 256 + 256, :] = done[:, k * 128 : k * 128 + 128]
            return carry

        lax.fori_loop(0, 2 * RANK, body, 0, unroll=True)

    for first_tp in (0, 1):
        send_face((1, 1), (1, 0), first_tp, x_up)
        send_face((1, 1), (1, 2), first_tp, x_down)
        send_face((1, 1), (0, 1), 1 - first_tp, y_up)
        send_face((1, 1), (2, 1), 1 - first_tp, y_down)
    for tp in (0, 1):
        core_copy(1, 1, tp, core).start()
    build_x(taps, bx, tx, txb)
    for side in (0, 2):
        arrived(1, side, 0)
        send_face((1, side), (0, side), 0, y_up)
        send_face((1, side), (2, side), 0, y_down)
        arrived(side, 1, 1)
        send_face((side, 1), (side, 0), 1, x_up)
        send_face((side, 1), (side, 2), 1, x_down)
    build_y(taps, by, ty, tyb)
    swapped(1, 1)
    forward_z(1, 1)
    for side in (0, 2):
        arrived(1, side, 1)
        arrived(side, 1, 0)
    for side in (0, 2):
        swapped(1, side)
        forward_z(1, side)
        swapped(side, 1)
        forward_z(side, 1)
    forward_x(1)
    for jy in (0, 2):
        for jx in (0, 2):
            for tp in range(2):
                arrived(jy, jx, tp)
    for jy in (0, 2):
        for jx in (0, 2):
            swapped(jy, jx)
            forward_z(jy, jx)
        forward_x(jy)

    loads[3].wait()

    def along_y(step, carry):
        blurred = None
        for r in range(RANK):
            both = [
                after_x[r, :, pl.ds(32 * step + 16 * k, 16), :].reshape(192, LANES) for k in range(2)
            ]
            part = dot(ty[r, :, 0:192], jnp.concatenate(both, axis=1))
            blurred = part if blurred is None else blurred + part
        seen = []
        for k in range(2):
            pair = [tile[4 * step + 2 * k + i].astype(F32).reshape(8, 8, LANES) for i in range(2)]
            seen.append(jnp.stack(pair, axis=1).reshape(128, LANES))
        seen = jnp.concatenate(seen, axis=1)
        quotient = (RANK * seen / (blurred + RANK * BACKGROUND)).astype(BF16)
        done = dot(tyb[...], quotient).astype(BF16)
        for k in range(2):
            back_y[:, pl.ds(32 * step + 16 * k, 16), :] = done[:, k * 128 : k * 128 + 128].reshape(
                12, 16, LANES
            )
        return carry

    def backward(half):
        rows, within = slice(half * 128, half * 128 + 128), slice(half * 128, half * 128 + 384)
        rim_sum = None
        for pair in range(2):
            for r in range(RANK):
                at = r * GROUPS + 2 * pair
                both = jnp.concatenate([back_y[at, within, :], back_y[at + 1, within, :]], axis=1)
                done = dot(txb[r, rows, within], both).astype(BF16)
                for k in range(2):
                    back_x[2 * pair + k, rows, r * 128 : (r + 1) * 128] = done[:, k * 128 : k * 128 + 128]
            for g in (2 * pair, 2 * pair + 1):
                done = dot(back_x[g, rows, :], wb[g])
                for c in range(4):
                    at = (g + c) % 4
                    sums[half, c, :, at * 32 : at * 32 + 32] = done[:, at * 32 : at * 32 + 32]
                rim_sum = done[:, LANES:] if rim_sum is None else rim_sum + done[:, LANES:]
        return rim_sum

    far = (1 - chip) * 2 + core

    def sum_copy(source, target, index, device):
        return pltpu.make_async_remote_copy(
            src_ref=source, dst_ref=target, send_sem=sum_send.at[index],
            recv_sem=sum_recv.at[index], device_id=device, device_id_type=MESH,
        )

    far_swap = [
        sum_copy(sums.at[h, (1 - chip) * 2 + 1 - core], got_core.at[h, 0], h, partner) for h in range(2)
    ]
    near_swap = [
        sum_copy(sums.at[h, chip * 2 + 1 - core], got_core.at[h, 1], 2 + h, partner) for h in range(2)
    ]
    over = [sum_copy(sums.at[h, far], got_chip.at[h], 4 + h, at_vert(q * 4 + far)) for h in range(2)]
    rim_swap = sum_copy(rims.at[1 - core], got_rim, 6, partner)
    edge_home = jnp.where(core == 0, vert - slot - 1, vert - slot + 4)
    edge_there = jnp.where(core == 0, q, 3 - q) > 0

    def edge_copy(which):
        return pltpu.make_async_remote_copy(
            src_ref=rims.at[core], dst_ref=got_edge.at[which], send_sem=sum_send.at[7],
            recv_sem=sum_recv.at[7 + which], device_id=at_vert(edge_home), device_id_type=MESH,
        )

    def pass_over(h):
        far_swap[h].wait_recv()
        sums[h, far] = sums[h, far] + got_core[h, 0]
        over[h].start()

    lax.fori_loop(0, 12, along_y, 0, unroll=4)
    top = backward(0)
    far_swap[0].start()
    near_swap[0].start()
    lax.fori_loop(12, 16, along_y, 0, unroll=4)
    pass_over(0)
    bottom = backward(1)
    far_swap[1].start()
    is_low = iota((128, LANES), 1) % 32 < RAD
    rims[0] = jnp.where(is_low, top, pltpu.roll(bottom, RAD, 1))
    rims[1] = jnp.where(is_low, pltpu.roll(top, LANES - RAD, 1), bottom)
    rim_swap.start()
    near_swap[1].start()
    pass_over(1)
    rim_swap.wait_recv()
    rims[core] = rims[core] + got_rim[...]
    pl.when(edge_there)(lambda: edge_copy(chip).start())

    mine = []
    for h in range(2):
        near_swap[h].wait_recv()
        mine.append(sums[h, slot] + got_core[h, 1])
    for h in range(2):
        over[h].wait_recv()
        mine[h] = mine[h] + got_chip[h]

    @pl.when(is_edge)
    def _():
        edge_copy(0).wait_recv()
        edge_copy(1).wait_recv()

    edge = got_edge[0] + got_edge[1]
    start = jnp.where(last, RAD, 0)
    lane = iota((128, LANES), 1)
    keep = is_edge & (lane >= start) & (lane < start + RAD)
    for g in range(GROUPS):
        for h in range(2):
            rim = pltpu.roll(edge, (start + 2 * LANES - RAD * h - 32 * g) % LANES, 1)
            own = pltpu.roll(mine[h], (8 - g - slot) % 4 * 32, 1) + jnp.where(keep, rim, 0.0)
            at = (slice(16 * h, 16 * h + 16), slice(g * 8, g * 8 + 8))
            refined[at] = est[at] * (own[:, 0:BLOCK].reshape(16, 8, BLOCK) * (1.0 / (RANK * VIEWS)))

    for k in range(1, VIEWS):
        part_copy(slot, k - 1, partner, 0).wait_send()

    @pl.when(is_edge)
    def _():
        for k in range(VIEWS):
            part_copy(4, 3 + k, partner, 0).wait_send()

    for copy, there in faces:
        pl.when(there)(copy.wait_send)
    for jy in range(3):
        for jx in range(3):

            @pl.when(exists(jy, jx))
            def _():
                for tp in range(2):
                    core_copy(jy, jx, tp, core).wait_send()

    for copy in far_swap + near_swap + over + [rim_swap]:
        copy.wait_send()
    pl.when(edge_there)(lambda: edge_copy(0).wait_send())


def local(estimate, view_tiles, slot_view, psf_taps):
    vmem = pl.BlockSpec(memory_space=pltpu.VMEM)
    hbm = pl.BlockSpec(memory_space=pltpu.HBM)
    tile = view_tiles[0, 0, 0]
    psf = jnp.transpose(psf_taps, (1, 2, 0, 3))
    scratch = [
        pltpu.VMEM(estimate.shape, F32),
        pltpu.VMEM(tile.shape, BF16),
        pltpu.VMEM(psf.shape, F32),
        pltpu.VMEM(slot_view.shape, jnp.int32),
        pltpu.VMEM((256, LANES), BF16),
        pltpu.VMEM((6, 128, LANES), BF16),
        pltpu.VMEM((3, 5, 768, LANES), BF16),
        pltpu.VMEM((RANK, 12, 768, LANES), BF16),
        pltpu.VMEM((RANK, 12, 512, LANES), BF16),
        pltpu.VMEM((12, 512, LANES), BF16),
        pltpu.VMEM((GROUPS, 256, RANK * LANES), BF16),
        pltpu.VMEM((2, 4, 128, LANES), F32),
        pltpu.VMEM((2, 128, LANES), F32),
        pltpu.VMEM((2, 2, 128, LANES), F32),
        pltpu.VMEM((128, LANES), F32),
        pltpu.VMEM((2, 128, LANES), F32),
        pltpu.VMEM((2, 128, LANES), F32),
        pltpu.VMEM((2, 24, LANES), F32),
        pltpu.VMEM((RANK, 256, 512), BF16),
        pltpu.VMEM((RANK, 128, 256), BF16),
        pltpu.VMEM((256, RANK * LANES), BF16),
        pltpu.VMEM((192, LANES), BF16),
        pltpu.VMEM((RANK, 256, 512), BF16),
        pltpu.VMEM((GROUPS, RANK * LANES, 256), BF16),
        pltpu.SemaphoreType.DMA((4,)),
        pltpu.SemaphoreType.DMA((7,)),
        pltpu.SemaphoreType.DMA((6,)),
        pltpu.SemaphoreType.DMA((16,)),
        pltpu.SemaphoreType.DMA((18,)),
        pltpu.SemaphoreType.DMA((18,)),
        pltpu.SemaphoreType.DMA((18,)),
        pltpu.SemaphoreType.DMA((8,)),
        pltpu.SemaphoreType.DMA((9,)),
    ]
    return pl.pallas_call(
        kernel,
        out_shape=jax.ShapeDtypeStruct(estimate.shape, F32),
        in_specs=[hbm] * 4,
        out_specs=vmem,
        scratch_shapes=scratch,
        compiler_params=pltpu.CompilerParams(
            collective_id=0, has_side_effects=True, vmem_limit_bytes=64 * 1024 * 1024
        ),
    )(estimate, tile, psf, slot_view)


def solution(mesh):
    placed = (
        P("bx", "by", "vert"),
        P("bx", "by", "vert", None, None, None),
        P("bx", "by", None),
        P(),
    )
    return jax.shard_map(
        local, mesh=mesh, in_specs=placed, out_specs=P("bx", "by", "vert"), check_vma=False
    )
```

```python
import jax
import jax.numpy as jnp
from jax import lax
from jax.experimental import pallas as pl
from jax.experimental.pallas import tpu as pltpu
from jax.sharding import PartitionSpec as P

BACKGROUND = 0.1
MESH = pl.DeviceIdType.MESH
F32, BF16 = jnp.float32, jnp.bfloat16
BLOCK = 32
RAD = 16
TAPS = 33
RANK = 3
VIEWS = 4
GROUPS = 4
LANES = 128


def iota(shape, axis):
    return lax.broadcasted_iota(jnp.int32, shape, axis)


def dot(a, b):
    return jnp.dot(a, b, preferred_element_type=F32)


def build_taps(psf, slot_view, slot, taps):
    listed = slot_view[...]
    view = jnp.sum(jnp.where(iota(listed.shape, 2) == slot, listed, 0), axis=2, keepdims=True)
    held = iota((VIEWS, TAPS), 0) == view[0]
    mine = jnp.sum(jnp.where(held[None, None], psf[...], 0.0), axis=2)
    mine = (mine / jnp.sum(mine, axis=-1, keepdims=True)).astype(BF16).astype(F32)
    taps[...] = jnp.zeros_like(taps)
    for a in range(3):
        taps[0, 8 * a : 8 * a + RANK, :TAPS] = mine[a]
    flip = (iota((LANES, LANES), 0) + iota((LANES, LANES), 1) == TAPS - 1).astype(BF16)
    taps[1] = dot(taps[0].astype(BF16), flip)


def band(line, rows, start):
    line = jnp.broadcast_to(line, (rows, LANES))
    return pltpu.roll(line, start % LANES, 1, stride=1, stride_axis=0)


def build_z(taps, q, wz, wb):
    z_in, z_out = iota((LANES, LANES), 0), iota((LANES, LANES), 1)
    near = jnp.abs(z_in - z_out) <= RAD
    rim, out = iota((32, LANES), 0), iota((32, LANES), 1)
    rim_ok = ((rim < RAD) & (out <= rim) & (q > 0)) | ((rim >= RAD) & (out >= rim + 96) & (q < 3))
    lane16 = iota((16, LANES), 1)
    for r in range(RANK):
        forward, backward = taps[1, 16 + r : 17 + r, :], taps[0, 16 + r : 17 + r, :]
        columns = slice(r * LANES, (r + 1) * LANES)
        wz[0:128, columns] = jnp.where(near, band(forward, LANES, -RAD), 0.0).astype(BF16)
        wz[128:160, columns] = jnp.where(rim_ok, band(forward, 32, 96), 0.0).astype(BF16)
        wz[160:256, columns] = jnp.zeros((96, LANES), BF16)
        main = jnp.where(near, band(backward, LANES, -RAD), 0.0)
        low = jnp.where((lane16 < RAD) & (q > 0), band(backward, 16, 0), 0.0)
        high = jnp.where((lane16 < RAD) & (q < 3), band(backward, 16, 96), 0.0)
        for g in range(GROUPS):
            wb[g, r * 128 : r * 128 + 128, 0:128] = (
                pltpu.roll(main, 32 * g, 1) if g else main
            ).astype(BF16)
            wb[g, r * 128 : r * 128 + 128, 128:256] = jnp.zeros((128, LANES), BF16)
            lo, hi = pltpu.roll(low, RAD * g, 1) if g else low, pltpu.roll(high, 64 + RAD * g, 1)
            wb[g, r * 128 : r * 128 + 16, 128:256] = lo.astype(BF16)
            wb[g, r * 128 + 112 : r * 128 + 128, 128:256] = hi.astype(BF16)


def build_x(taps, bx, tx, txb):
    spread = (iota((LANES, 384), 1) == 8 * iota((LANES, 384), 0)).astype(BF16)
    past = iota((LANES, LANES), 1) >= iota((LANES, LANES), 0)
    none = jnp.zeros((LANES, LANES), BF16)
    low, high = bx > 0, bx < 3

    def tiles(line):
        turned = [band(line[:, i * LANES : (i + 1) * LANES], LANES, 0) for i in range(3)]
        before = [0.0, turned[0], turned[1]]
        return [jnp.where(past, turned[i], before[i]) for i in range(3)]

    def put(ref, kept):
        for half in range(2):
            for at in range(4):
                here = none
                if 0 <= at - half < 3:
                    here = jnp.where(kept[at], kept_tiles[at - half], 0.0).astype(BF16)
                ref[half * 128 : half * 128 + 128, at * 128 : at * 128 + 128] = here

    wide = [dot(taps[k, 0:8, :].astype(BF16), spread) for k in range(2)]
    for r in range(RANK):
        kept_tiles = tiles(wide[0][r : r + 1])
        put(tx.at[r], (True, True, True, True))
        kept_tiles = tiles(wide[1][r : r + 1])
        put(txb.at[r], (low, True, True, high))


def build_y(taps, by, ty, tyb):
    def inside(rows, first):
        place = by * BLOCK - first + iota((rows, LANES), 1)
        return (place >= 0) & (place < 4 * BLOCK)

    plain = [
        jnp.where(inside(64, 2 * RAD), band(taps[0, 8 + r : 9 + r, :], 64, 0), 0.0) for r in range(RANK)
    ] + [
        jnp.where(inside(32, RAD), band(taps[1, 8 + r : 9 + r, :], 32, 0), 0.0) for r in range(RANK)
    ]
    plain = jnp.concatenate(plain, axis=0).astype(BF16)
    y, column = iota((LANES, 256), 0), iota((LANES, 256), 1)
    parts = [
        dot(plain, (column == 16 * (y // 8) + 8 * k + y % 8).astype(BF16)).reshape(36, 8, 256)
        for k in range(2)
    ]
    both = jnp.stack(parts, axis=1).reshape(36 * 16, 256).astype(BF16)
    for r in range(RANK):
        ty[r] = both[r * 128 : (r + 1) * 128]
    tyb[...] = both[384:576, 0:128]


def kernel(
    est_hbm, tile_hbm, psf_hbm, slot_view_hbm, refined,
    est, tile, psf, slot_view,
    packed, parts, field, after_z, after_x, back_y, back_x, sums, rims,
    got_core, got_rim, got_chip, got_edge,
    taps, tx, ty, wz, tyb, txb, wb,
    load_sem, part_send, part_recv, face_send, face_recv, core_send, core_recv, sum_send, sum_recv,
):
    bx, by, vert = lax.axis_index("bx"), lax.axis_index("by"), lax.axis_index("vert")
    q, slot = vert // VIEWS, vert % VIEWS
    core, chip = slot % 2, slot // 2

    loads = [
        pltpu.make_async_copy(source, target, load_sem.at[i])
        for i, (source, target) in enumerate(
            ((est_hbm, est), (psf_hbm, psf), (slot_view_hbm, slot_view), (tile_hbm, tile))
        )
    ]
    for copy in loads:
        copy.start()

    def at_vert(index):
        return {"vert": index}

    partner = at_vert(q * 4 + chip * 2 + 1 - core)
    x_up, x_down = ({"bx": bx + 1}, bx < 3), ({"bx": bx - 1}, bx > 0)
    y_up, y_down = ({"by": by + 1}, by < 3), ({"by": by - 1}, by > 0)
    above, below = q < 3, q > 0
    first, last = slot == 0, slot == VIEWS - 1
    is_edge = (first & below) | (last & above)

    def exists(jy, jx):
        here = jy == jy
        for index, j in ((by, jy), (bx, jx)):
            if j != 1:
                here = (index > 0 if j == 0 else index < 3) & here
        return here

    got_edge[...] = jnp.zeros_like(got_edge)
    barrier = pltpu.get_barrier_semaphore()

    def greet(device):
        pl.semaphore_signal(barrier, inc=1, device_id=device, device_id_type=MESH)

    for k in range(1, VIEWS):
        greet(at_vert(q * 4 + (slot + k) % VIEWS))
    for device, there in (x_up, x_down, y_up, y_down):
        pl.when(there)(lambda device=device: greet(device))

    @pl.when(below)
    def _():
        greet(at_vert(vert - slot - 1))
        pl.when(first)(lambda: greet(at_vert(vert - 3)))

    @pl.when(above)
    def _():
        greet(at_vert(vert - slot + 4))
        pl.when(last)(lambda: greet(at_vert(vert + 3)))

    loads[0].wait()
    groups = est[...].reshape(BLOCK, GROUPS, 8, BLOCK)
    line = jnp.concatenate([groups[:, g].reshape(256, BLOCK) for g in range(GROUPS)], axis=1)
    packed[...] = pltpu.roll(line, slot * 32, 1).astype(BF16)

    beside = [(there, 1) for _, there in (x_up, x_down, y_up, y_down)] + [(is_edge, 4)]
    beside += [((slot == 1) & above, 1), ((slot == 2) & below, 1)]
    pl.semaphore_wait(barrier, 3 + sum(jnp.where(there, n, 0) for there, n in beside))

    def part_copy(dst_index, send, device, half):
        return pltpu.make_async_remote_copy(
            src_ref=packed.at[pl.ds(half * 128, 128), :], dst_ref=parts.at[dst_index],
            send_sem=part_send.at[send], recv_sem=part_recv.at[dst_index],
            device_id=device, device_id_type=MESH,
        )

    for k in range(1, VIEWS):
        other = (slot + k) % VIEWS
        part_copy(slot, k - 1, at_vert(q * 4 + other), other % 2).start()

    @pl.when(last & above)
    def _():
        for k in range(VIEWS):
            part_copy(4, 3 + k, at_vert(vert + 1 + k), k % 2).start()

    @pl.when(first & below)
    def _():
        for k in range(VIEWS):
            part_copy(5, 3 + k, at_vert(vert - 4 + k), k % 2).start()

    parts[slot] = packed[pl.ds(core * 128, 128), :]

    def clear(ref):
        ref[...] = jnp.zeros(ref.shape, BF16)

    pl.when(~below)(lambda: clear(parts.at[4]))
    pl.when(~above)(lambda: clear(parts.at[5]))
    pl.when(bx == 0)(lambda: clear(field.at[:, :, 0:256, :]))
    pl.when(bx == 3)(lambda: clear(field.at[:, :, 512:768, :]))
    pl.when(by == 0)(lambda: clear(field.at[0]))
    pl.when(by == 3)(lambda: clear(field.at[2]))
    loads[1].wait()
    loads[2].wait()
    build_taps(psf, slot_view, slot, taps)
    build_z(taps, q, wz, wb)

    for k in range(1, VIEWS):
        part_copy((slot + k) % VIEWS, 0, partner, 0).wait_recv()
    for k, there in ((4, below), (5, above)):
        pl.when(there)(lambda k=k: part_copy(k, 0, partner, 0).wait_recv())

    chunk = iota((128, LANES), 1) // 32
    own_rows = pl.ds(256 + core * 128, 128)
    have = [parts[k].astype(F32) for k in range(6)]
    for g in range(GROUPS):
        line = have[(3 - g) % 4]
        for at in range(3):
            line = jnp.where(chunk == at, have[(at - g) % 4], line)
        if g:
            line = pltpu.roll(line, LANES - 32 * g, 1)
        field[1, g, own_rows, :] = line.astype(BF16)
    is_high = iota((128, LANES), 1) % 32 < RAD
    line = pltpu.roll(jnp.where(is_high, have[5], have[4]), RAD, 1)
    field[1, 4, own_rows, :] = line.astype(BF16)

    def piece(jy, jx, tp, owner):
        return field.at[jy, :, pl.ds(jx * 256 + owner * 128 + tp * 64, 64), :]

    def number(jy, jx, tp):
        return (jy * 3 + jx) * 2 + tp

    def face_copy(source, target, tp, send, device):
        return pltpu.make_async_remote_copy(
            src_ref=piece(*source, tp, core), dst_ref=piece(*target, tp, core),
            send_sem=face_send.at[send], recv_sem=face_recv.at[number(*target, tp)],
            device_id=device, device_id_type=MESH,
        )

    def core_copy(jy, jx, tp, owner):
        return pltpu.make_async_remote_copy(
            src_ref=piece(jy, jx, tp, owner), dst_ref=piece(jy, jx, tp, owner),
            send_sem=core_send.at[number(jy, jx, tp)], recv_sem=core_recv.at[number(jy, jx, tp)],
            device_id=partner, device_id_type=MESH,
        )

    faces = []

    def send_face(source, target, tp, way):
        device, there = way
        copy = face_copy(source, target, tp, len(faces), device)
        there = there & exists(*source)
        pl.when(there)(copy.start)
        faces.append((copy, there))

    def arrived(jy, jx, tp):
        @pl.when(exists(jy, jx))
        def _():
            face_copy((jy, jx), (jy, jx), tp, 0, partner).wait_recv()
            core_copy(jy, jx, tp, core).start()

    def swapped(jy, jx):
        @pl.when(exists(jy, jx))
        def _():
            for tp in range(2):
                core_copy(jy, jx, tp, 1 - core).wait_recv()

    def forward_z(jy, jx):
        rows = pl.ds(jx * 256, 256)
        rim = field[jy, 4, rows, :]
        for g in range(GROUPS):
            turned = pltpu.roll(rim, LANES - 32 * g, 1) if g else rim
            done = dot(jnp.concatenate([field[jy, g, rows, :], turned], axis=1), wz[...])
            for r in range(RANK):
                after_z[r, jy * GROUPS + g, rows, :] = done[:, r * 128 : (r + 1) * 128].astype(BF16)

    def forward_x(jy):
        def body(step, carry):
            r, group = step // 2, jy * GROUPS + step % 2 * 2
            for b in range(2):
                rows = pl.ds(b * 256, 512)
                both = jnp.concatenate([after_z[r, group + k, rows, :] for k in range(2)], axis=1)
                done = dot(tx[r], both).astype(BF16)
                for k in range(2):
                    after_x[r, group + k, b * 256 : b * 256 + 256, :] = done[:, k * 128 : k * 128 + 128]
            return carry

        lax.fori_loop(0, 2 * RANK, body, 0, unroll=True)

    for first_tp in (0, 1):
        send_face((1, 1), (1, 0), first_tp, x_up)
        send_face((1, 1), (1, 2), first_tp, x_down)
        send_face((1, 1), (0, 1), 1 - first_tp, y_up)
        send_face((1, 1), (2, 1), 1 - first_tp, y_down)
    for tp in (0, 1):
        core_copy(1, 1, tp, core).start()
    build_x(taps, bx, tx, txb)
    for side in (0, 2):
        arrived(1, side, 0)
        send_face((1, side), (0, side), 0, y_up)
        send_face((1, side), (2, side), 0, y_down)
        arrived(side, 1, 1)
        send_face((side, 1), (side, 0), 1, x_up)
        send_face((side, 1), (side, 2), 1, x_down)
    build_y(taps, by, ty, tyb)
    swapped(1, 1)
    forward_z(1, 1)
    for side in (0, 2):
        arrived(1, side, 1)
        arrived(side, 1, 0)
    for side in (0, 2):
        swapped(1, side)
        forward_z(1, side)
        swapped(side, 1)
        forward_z(side, 1)
    forward_x(1)
    for jy in (0, 2):
        for jx in (0, 2):
            for tp in range(2):
                arrived(jy, jx, tp)
    for jy in (0, 2):
        for jx in (0, 2):
            swapped(jy, jx)
            forward_z(jy, jx)
        forward_x(jy)

    loads[3].wait()

    def along_y(step, carry):
        blurred = None
        for r in range(RANK):
            both = [
                after_x[r, :, pl.ds(32 * step + 16 * k, 16), :].reshape(192, LANES) for k in range(2)
            ]
            part = dot(ty[r, :, 0:192], jnp.concatenate(both, axis=1))
            blurred = part if blurred is None else blurred + part
        seen = []
        for k in range(2):
            pair = [tile[4 * step + 2 * k + i].astype(F32).reshape(8, 8, LANES) for i in range(2)]
            seen.append(jnp.stack(pair, axis=1).reshape(128, LANES))
        seen = jnp.concatenate(seen, axis=1)
        quotient = (RANK * seen / (blurred + RANK * BACKGROUND)).astype(BF16)
        done = dot(tyb[...], quotient).astype(BF16)
        for k in range(2):
            back_y[:, pl.ds(32 * step + 16 * k, 16), :] = done[:, k * 128 : k * 128 + 128].reshape(
                12, 16, LANES
            )
        return carry

    def backward_x(half):
        rows, within = slice(half * 128, half * 128 + 128), slice(half * 128, half * 128 + 384)
        for pair in range(2):
            for r in range(RANK):
                at = r * GROUPS + 2 * pair
                both = jnp.concatenate([back_y[at, within, :], back_y[at + 1, within, :]], axis=1)
                done = dot(txb[r, rows, within], both).astype(BF16)
                for k in range(2):
                    back_x[2 * pair + k, rows, r * 128 : (r + 1) * 128] = done[:, k * 128 : k * 128 + 128]

    def backward_rims(half):
        rows = slice(half * 128, half * 128 + 128)
        both = dot(back_x[0, rows, :], wb[0, :, LANES:])
        for g in range(1, GROUPS):
            both = both + dot(back_x[g, rows, :], wb[g, :, LANES:])
        is_low = iota((64, LANES), 1) < 64
        rims[half, 0] = jnp.where(is_low, both[0:64], pltpu.roll(both[64:128], 64, 1))
        rims[half, 1] = jnp.where(is_low, pltpu.roll(both[0:64], 64, 1), both[64:128])

    def backward_z(half):
        rows = slice(half * 128, half * 128 + 128)
        for g in range(GROUPS):
            done = dot(back_x[g, rows, :], wb[g, :, :LANES])
            for c in range(4):
                at = (g + c) % 4
                sums[half, c, :, at * 32 : at * 32 + 32] = done[:, at * 32 : at * 32 + 32]

    far = (1 - chip) * 2 + core

    def sum_copy(source, target, index, device):
        return pltpu.make_async_remote_copy(
            src_ref=source, dst_ref=target, send_sem=sum_send.at[index],
            recv_sem=sum_recv.at[index], device_id=device, device_id_type=MESH,
        )

    far_swap = [
        sum_copy(sums.at[h, (1 - chip) * 2 + 1 - core], got_core.at[h, 0], h, partner) for h in range(2)
    ]
    near_swap = [
        sum_copy(sums.at[h, chip * 2 + 1 - core], got_core.at[h, 1], 2 + h, partner) for h in range(2)
    ]
    over = [sum_copy(sums.at[h, far], got_chip.at[h], 4 + h, at_vert(q * 4 + far)) for h in range(2)]
    rim_swap = [sum_copy(rims.at[h, 1 - core], got_rim.at[h], 6 + h, partner) for h in range(2)]
    edge_home = jnp.where(core == 0, vert - slot - 1, vert - slot + 4)
    edge_there = jnp.where(core == 0, q, 3 - q) > 0

    def edge_copy(h, which):
        return pltpu.make_async_remote_copy(
            src_ref=rims.at[h, core], dst_ref=got_edge.at[which, h], send_sem=sum_send.at[8 + h],
            recv_sem=sum_recv.at[8 + 2 * h + which], device_id=at_vert(edge_home), device_id_type=MESH,
        )

    def backward(h):
        backward_x(h)
        backward_rims(h)
        rim_swap[h].start()
        backward_z(h)
        far_swap[h].start()
        near_swap[h].start()

    def pass_over(h):
        rim_swap[h].wait_recv()
        rims[h, core] = rims[h, core] + got_rim[h]
        pl.when(edge_there)(lambda: edge_copy(h, chip).start())
        far_swap[h].wait_recv()
        sums[h, far] = sums[h, far] + got_core[h, 0]
        over[h].start()

    lax.fori_loop(0, 12, along_y, 0, unroll=4)
    backward(0)
    lax.fori_loop(12, 16, along_y, 0, unroll=4)
    pass_over(0)
    backward(1)
    pass_over(1)

    mine = []
    for h in range(2):
        near_swap[h].wait_recv()
        mine.append(sums[h, slot] + got_core[h, 1])
    for h in range(2):
        over[h].wait_recv()
        mine[h] = mine[h] + got_chip[h]

    @pl.when(is_edge)
    def _():
        for h in range(2):
            edge_copy(h, 0).wait_recv()
            edge_copy(h, 1).wait_recv()

    start = jnp.where(last, RAD, 0)
    lane = iota((64, LANES), 1)
    keep = is_edge & (lane >= start) & (lane < start + RAD)
    for h in range(2):
        edge = got_edge[0, h] + got_edge[1, h]
        for g in range(GROUPS):
            own = pltpu.roll(mine[h], (8 - g - slot) % 4 * 32, 1)
            for k in range(2):
                rim = pltpu.roll(edge, (start + LANES - 64 * k - RAD * g) % LANES, 1)
                part = own[64 * k : 64 * k + 64] + jnp.where(keep, rim, 0.0)
                part = part[:, 0:BLOCK].reshape(8, 8, BLOCK) * (1.0 / (RANK * VIEWS))
                at = (slice(16 * h + 8 * k, 16 * h + 8 * k + 8), slice(g * 8, g * 8 + 8))
                refined[at] = est[at] * part

    for k in range(1, VIEWS):
        part_copy(slot, k - 1, partner, 0).wait_send()

    @pl.when(is_edge)
    def _():
        for k in range(VIEWS):
            part_copy(4, 3 + k, partner, 0).wait_send()

    for copy, there in faces:
        pl.when(there)(copy.wait_send)
    for jy in range(3):
        for jx in range(3):

            @pl.when(exists(jy, jx))
            def _():
                for tp in range(2):
                    core_copy(jy, jx, tp, core).wait_send()

    for copy in far_swap + near_swap + over + rim_swap:
        copy.wait_send()

    @pl.when(edge_there)
    def _():
        for h in range(2):
            edge_copy(h, 0).wait_send()


def local(estimate, view_tiles, slot_view, psf_taps):
    vmem = pl.BlockSpec(memory_space=pltpu.VMEM)
    hbm = pl.BlockSpec(memory_space=pltpu.HBM)
    tile = view_tiles[0, 0, 0]
    psf = jnp.transpose(psf_taps, (1, 2, 0, 3))
    scratch = [
        pltpu.VMEM(estimate.shape, F32),
        pltpu.VMEM(tile.shape, BF16),
        pltpu.VMEM(psf.shape, F32),
        pltpu.VMEM(slot_view.shape, jnp.int32),
        pltpu.VMEM((256, LANES), BF16),
        pltpu.VMEM((6, 128, LANES), BF16),
        pltpu.VMEM((3, 5, 768, LANES), BF16),
        pltpu.VMEM((RANK, 12, 768, LANES), BF16),
        pltpu.VMEM((RANK, 12, 512, LANES), BF16),
        pltpu.VMEM((12, 512, LANES), BF16),
        pltpu.VMEM((GROUPS, 256, RANK * LANES), BF16),
        pltpu.VMEM((2, 4, 128, LANES), F32),
        pltpu.VMEM((2, 2, 64, LANES), F32),
        pltpu.VMEM((2, 2, 128, LANES), F32),
        pltpu.VMEM((2, 64, LANES), F32),
        pltpu.VMEM((2, 128, LANES), F32),
        pltpu.VMEM((2, 2, 64, LANES), F32),
        pltpu.VMEM((2, 24, LANES), F32),
        pltpu.VMEM((RANK, 256, 512), BF16),
        pltpu.VMEM((RANK, 128, 256), BF16),
        pltpu.VMEM((256, RANK * LANES), BF16),
        pltpu.VMEM((192, LANES), BF16),
        pltpu.VMEM((RANK, 256, 512), BF16),
        pltpu.VMEM((GROUPS, RANK * LANES, 256), BF16),
        pltpu.SemaphoreType.DMA((4,)),
        pltpu.SemaphoreType.DMA((7,)),
        pltpu.SemaphoreType.DMA((6,)),
        pltpu.SemaphoreType.DMA((16,)),
        pltpu.SemaphoreType.DMA((18,)),
        pltpu.SemaphoreType.DMA((18,)),
        pltpu.SemaphoreType.DMA((18,)),
        pltpu.SemaphoreType.DMA((10,)),
        pltpu.SemaphoreType.DMA((12,)),
    ]
    return pl.pallas_call(
        kernel,
        out_shape=pltpu.VMEM(estimate.shape, F32),
        in_specs=[hbm] * 4,
        out_specs=vmem,
        scratch_shapes=scratch,
        compiler_params=pltpu.CompilerParams(
            collective_id=0, has_side_effects=True, vmem_limit_bytes=56 * 1024 * 1024
        ),
    )(*(pltpu.with_memory_space_constraint(a, pltpu.HBM) for a in (estimate, tile, psf, slot_view)))


def solution(mesh):
    placed = (
        P("bx", "by", "vert"),
        P("bx", "by", "vert", None, None, None),
        P("bx", "by", None),
        P(),
    )
    return jax.shard_map(
        local, mesh=mesh, in_specs=placed, out_specs=P("bx", "by", "vert"), check_vma=False
    )
```

```python
import jax
import jax.numpy as jnp
from jax import lax
from jax.experimental import pallas as pl
from jax.experimental.pallas import tpu as pltpu
from jax.sharding import PartitionSpec as P

BACKGROUND = 0.1
MESH = pl.DeviceIdType.MESH
F32, BF16 = jnp.float32, jnp.bfloat16
BLOCK = 32
RAD = 16
TAPS = 33
RANK = 3
VIEWS = 4
GROUPS = 4
LANES = 128


def iota(shape, axis):
    return lax.broadcasted_iota(jnp.int32, shape, axis)


def dot(a, b):
    return jnp.dot(a, b, preferred_element_type=F32)


def band(line, rows, start):
    line = jnp.broadcast_to(line, (rows, LANES))
    return pltpu.roll(line, start % LANES, 1, stride=1, stride_axis=0)


def swap_quads(a, b):
    low, axis = iota(a.shape, a.ndim - 2) < 4, a.ndim - 2
    return jnp.where(low, a, pltpu.roll(b, 4, axis)), jnp.where(low, pltpu.roll(a, 4, axis), b)


def build_taps(psf, slot_view, slot, taps):
    listed = slot_view[...]
    view = jnp.sum(jnp.where(iota(listed.shape, 2) == slot, listed, 0), axis=2, keepdims=True)
    held = iota((VIEWS, TAPS), 0) == view[0]
    mine = jnp.sum(jnp.where(held[None, None], psf[...], 0.0), axis=2)
    mine = (mine / jnp.sum(mine, axis=-1, keepdims=True)).astype(BF16).astype(F32)
    taps[...] = jnp.zeros_like(taps)
    for a in range(3):
        taps[0, 8 * a : 8 * a + RANK, :TAPS] = mine[a]
    flip = (iota((LANES, LANES), 0) + iota((LANES, LANES), 1) == TAPS - 1).astype(BF16)
    taps[1] = dot(taps[0].astype(BF16), flip)


def build_z(taps, wz, wb):
    z_in, z_out = iota((LANES, LANES), 0), iota((LANES, LANES), 1)
    near = jnp.abs(z_in - z_out) <= RAD
    rim, out = iota((32, LANES), 0), iota((32, LANES), 1)
    rim_ok = ((rim < RAD) & (out <= rim)) | ((rim >= RAD) & (out >= rim + 96))
    lane16 = iota((16, LANES), 1)
    for r in range(RANK):
        forward, backward = taps[1, 16 + r : 17 + r, :], taps[0, 16 + r : 17 + r, :]
        columns = slice(r * LANES, (r + 1) * LANES)
        wz[0:128, columns] = jnp.where(near, band(forward, LANES, -RAD), 0.0).astype(BF16)
        wz[128:160, columns] = jnp.where(rim_ok, band(forward, 32, 96), 0.0).astype(BF16)
        wz[160:256, columns] = jnp.zeros((96, LANES), BF16)
        main = jnp.where(near, band(backward, LANES, -RAD), 0.0)
        low = jnp.where(lane16 < RAD, band(backward, 16, 0), 0.0)
        high = jnp.where(lane16 < RAD, band(backward, 16, 96), 0.0)
        for g in range(GROUPS):
            wb[g, r * 128 : r * 128 + 128, 0:128] = (
                pltpu.roll(main, 32 * g, 1) if g else main
            ).astype(BF16)
            wb[g, r * 128 : r * 128 + 128, 128:256] = jnp.zeros((128, LANES), BF16)
            lo, hi = pltpu.roll(low, RAD * g, 1) if g else low, pltpu.roll(high, 64 + RAD * g, 1)
            wb[g, r * 128 : r * 128 + 16, 128:256] = lo.astype(BF16)
            wb[g, r * 128 + 112 : r * 128 + 128, 128:256] = hi.astype(BF16)


def build_x(taps, bx, tx, txb):
    spread = (iota((LANES, 256), 1) == 4 * iota((LANES, 256), 0)).astype(BF16)
    lane, row = iota((LANES, LANES), 1), iota((LANES, LANES), 0)
    low, high = bx > 0, bx < 3

    def tiles(line):
        turned = [band(line[:, i * LANES : (i + 1) * LANES], LANES, 0) for i in range(2)]
        return jnp.where(lane >= row, turned[0], 0.0), jnp.where(lane >= row, turned[1], turned[0])

    wide = [dot(taps[k, 0:8, :].astype(BF16), spread) for k in range(2)]
    for r in range(RANK):
        left, right = tiles(wide[0][r : r + 1])
        tx[r, :, 0:128] = left.astype(BF16)
        tx[r, :, 128:256] = right.astype(BF16)
        left, right = [m[0:64] for m in tiles(wide[1][r : r + 1])]
        txb[0, r, :, 0:128] = jnp.where((lane[0:64] >= 64) | low, left, 0.0).astype(BF16)
        txb[0, r, :, 128:256] = right.astype(BF16)
        txb[1, r, :, 0:128] = left.astype(BF16)
        txb[1, r, :, 128:256] = jnp.where(high, right, 0.0).astype(BF16)


def build_y(taps, by, ty, tyb):
    place = by * BLOCK - RAD + iota((BLOCK, LANES), 1)
    inside = (place >= 0) & (place < 4 * BLOCK)
    plain = [band(taps[0, 8 + r : 9 + r, :], BLOCK, 0) for r in range(RANK)]
    plain += [
        jnp.where(inside, band(taps[1, 8 + r : 9 + r, :], BLOCK, 0), 0.0) for r in range(RANK)
    ]
    plain = jnp.concatenate(plain, axis=0).astype(BF16)
    y, column = iota((LANES, 256), 0), iota((LANES, 256), 1)
    wide = [
        dot(plain, (column == 16 * (y // 4) + 4 * x + y % 4).astype(BF16)).astype(BF16)
        for x in range(4)
    ]
    row, source = iota((LANES, LANES), 0), iota((LANES, LANES), 1)
    order = (row == 16 * (source % 32 // 4) + 4 * (source // 32) + source % 4).astype(BF16)
    for i in range(2 * RANK):
        done = dot(order, jnp.concatenate([m[i * 32 : i * 32 + 32] for m in wide], axis=0)).astype(BF16)
        if i < RANK:
            ty[i] = done
        else:
            tyb[(i - RANK) * 128 : (i - RANK + 1) * 128, :] = done


def kernel(
    est_hbm, tile_hbm, psf_hbm, slot_view_hbm, refined,
    est, tile, psf, slot_view,
    packed, parts, field, after_z, after_x, seen, back_y, back_x, sums, rims,
    got_core, got_rim, got_chip, got_edge,
    taps, tx, ty, wz, tyb, txb, wb,
    load_sem, part_send, part_recv, face_send, face_recv, core_send, core_recv, sum_send, sum_recv,
):
    bx, by, vert = lax.axis_index("bx"), lax.axis_index("by"), lax.axis_index("vert")
    q, slot = vert // VIEWS, vert % VIEWS
    core, chip = slot % 2, slot // 2

    loads = [
        pltpu.make_async_copy(source, target, load_sem.at[i])
        for i, (source, target) in enumerate(
            ((est_hbm, est), (psf_hbm, psf), (slot_view_hbm, slot_view), (tile_hbm, tile))
        )
    ]
    for copy in loads:
        copy.start()

    def at_vert(index):
        return {"vert": index}

    partner = at_vert(q * 4 + chip * 2 + 1 - core)
    x_up, x_down = ({"bx": bx + 1}, bx < 3), ({"bx": bx - 1}, bx > 0)
    y_up, y_down = ({"by": by + 1}, by < 3), ({"by": by - 1}, by > 0)
    above, below = q < 3, q > 0
    first, last = slot == 0, slot == VIEWS - 1
    is_edge = (first & below) | (last & above)

    def exists(jy, jx):
        here = jy == jy
        for index, j in ((by, jy), (bx, jx)):
            if j != 1:
                here = (index > 0 if j == 0 else index < 3) & here
        return here

    got_edge[...] = jnp.zeros_like(got_edge)
    barrier = pltpu.get_barrier_semaphore()

    def greet(device):
        pl.semaphore_signal(barrier, inc=1, device_id=device, device_id_type=MESH)

    for k in range(1, VIEWS):
        greet(at_vert(q * 4 + (slot + k) % VIEWS))
    for device, there in (x_up, x_down, y_up, y_down):
        pl.when(there)(lambda device=device: greet(device))

    @pl.when(below)
    def _():
        greet(at_vert(vert - slot - 1))
        pl.when(first)(lambda: greet(at_vert(vert - 3)))

    @pl.when(above)
    def _():
        greet(at_vert(vert - slot + 4))
        pl.when(last)(lambda: greet(at_vert(vert + 3)))

    loads[0].wait()
    groups = est[...].reshape(BLOCK, GROUPS, 8, BLOCK)
    line = jnp.concatenate([groups[:, g].reshape(256, BLOCK) for g in range(GROUPS)], axis=1)
    line = pltpu.roll(line, slot * 32, 1).reshape(16, 2, 8, LANES)
    for side, quads in enumerate(swap_quads(line[:, 0], line[:, 1])):
        packed[side * 128 : side * 128 + 128, :] = quads.reshape(128, LANES).astype(BF16)

    beside = [(there, 1) for _, there in (x_up, x_down, y_up, y_down)] + [(is_edge, 4)]
    beside += [((slot == 1) & above, 1), ((slot == 2) & below, 1)]
    pl.semaphore_wait(barrier, 3 + sum(jnp.where(there, n, 0) for there, n in beside))

    def part_copy(source, tp, send, device, side):
        return pltpu.make_async_remote_copy(
            src_ref=packed.at[pl.ds(side * 128 + tp * 64, 64), :], dst_ref=parts.at[source, tp],
            send_sem=part_send.at[send * 2 + tp], recv_sem=part_recv.at[source * 2 + tp],
            device_id=device, device_id_type=MESH,
        )

    for tp in range(2):
        for k in range(1, VIEWS):
            other = (slot + k) % VIEWS
            part_copy(slot, tp, k - 1, at_vert(q * 4 + other), other % 2).start()

        @pl.when(last & above)
        def _():
            for k in range(VIEWS):
                part_copy(4, tp, 3 + k, at_vert(vert + 1 + k), k % 2).start()

        @pl.when(first & below)
        def _():
            for k in range(VIEWS):
                part_copy(5, tp, 3 + k, at_vert(vert - 4 + k), k % 2).start()

    parts[slot] = packed[pl.ds(core * 128, 128), :].reshape(2, 64, LANES)

    def clear(ref):
        ref[...] = jnp.zeros(ref.shape, BF16)

    pl.when(~below)(lambda: clear(parts.at[4]))
    pl.when(~above)(lambda: clear(parts.at[5]))
    pl.when(bx == 0)(lambda: clear(field.at[:, :, :, 0:128, :]))
    pl.when(bx == 3)(lambda: clear(field.at[:, :, :, 256:384, :]))
    pl.when(by == 0)(lambda: clear(field.at[0]))
    pl.when(by == 3)(lambda: clear(field.at[2]))
    loads[1].wait()
    loads[2].wait()
    build_taps(psf, slot_view, slot, taps)
    build_z(taps, wz, wb)

    def assemble(tp):
        for k in range(1, VIEWS):
            part_copy((slot + k) % VIEWS, tp, 0, partner, 0).wait_recv()
        for k, there in ((4, below), (5, above)):
            pl.when(there)(lambda k=k: part_copy(k, tp, 0, partner, 0).wait_recv())
        lane = iota((64, LANES), 1)
        rows = slice(128 + tp * 64, 192 + tp * 64)
        have = [parts[k, tp].astype(F32) for k in range(6)]
        for g in range(GROUPS):
            line = have[(3 - g) % 4]
            for at in range(3):
                line = jnp.where(lane // 32 == at, have[(at - g) % 4], line)
            if g:
                line = pltpu.roll(line, LANES - 32 * g, 1)
            field[1, g, core, rows, :] = line.astype(BF16)
        line = pltpu.roll(jnp.where(lane % 32 < RAD, have[5], have[4]), RAD, 1)
        field[1, 4, core, rows, :] = line.astype(BF16)

    def piece(jy, jx, tp, side):
        return field.at[jy, :, side, pl.ds(jx * 128 + tp * 64, 64), :]

    def number(jy, jx, tp):
        return (jy * 3 + jx) * 2 + tp

    def face_copy(source, target, tp, send, device):
        return pltpu.make_async_remote_copy(
            src_ref=piece(*source, tp, core), dst_ref=piece(*target, tp, core),
            send_sem=face_send.at[send], recv_sem=face_recv.at[number(*target, tp)],
            device_id=device, device_id_type=MESH,
        )

    def core_copy(jy, jx, tp, side):
        return pltpu.make_async_remote_copy(
            src_ref=piece(jy, jx, tp, side), dst_ref=piece(jy, jx, tp, side),
            send_sem=core_send.at[number(jy, jx, tp)], recv_sem=core_recv.at[number(jy, jx, tp)],
            device_id=partner, device_id_type=MESH,
        )

    faces = []

    def send_face(source, target, tp, way):
        device, there = way
        copy = face_copy(source, target, tp, len(faces), device)
        there = there & exists(*source)
        pl.when(there)(copy.start)
        faces.append((copy, there))

    def arrived(jy, jx, tp):
        @pl.when(exists(jy, jx))
        def _():
            face_copy((jy, jx), (jy, jx), tp, 0, partner).wait_recv()
            core_copy(jy, jx, tp, core).start()

    def swapped(jy, jx):
        @pl.when(exists(jy, jx))
        def _():
            for tp in range(2):
                core_copy(jy, jx, tp, 1 - core).wait_recv()

    def forward_z(jy, jx):
        rows = slice(jx * 128, jx * 128 + 128)
        rim = field[jy, 4, :, rows, :].reshape(256, LANES)
        for g in range(GROUPS):
            turned = pltpu.roll(rim, LANES - 32 * g, 1) if g else rim
            main = field[jy, g, :, rows, :].reshape(256, LANES)
            done = dot(jnp.concatenate([main, turned], axis=1), wz[...]).astype(BF16)
            for r in range(RANK):
                after_z[r, jy * GROUPS + g, :, rows, :] = done[:, r * 128 : (r + 1) * 128].reshape(
                    2, 128, LANES
                )

    def forward_x(jy):
        def body(step, carry):
            r, group = step // GROUPS, jy * GROUPS + step % GROUPS
            for b in range(2):
                rows = pl.ds(b * 128, 256)
                both = jnp.concatenate([after_z[r, group, k, rows, :] for k in range(2)], axis=1)
                done = dot(tx[r], both).astype(BF16)
                for k in range(2):
                    after_x[r, group, k, b * 128 : b * 128 + 128, :] = done[:, k * 128 : k * 128 + 128]
            return carry

        lax.fori_loop(0, GROUPS * RANK, body, 0, unroll=True)

    for tp in (0, 1):
        assemble(tp)
        send_face((1, 1), (1, 0), tp, x_up)
        send_face((1, 1), (1, 2), tp, x_down)
        send_face((1, 1), (0, 1), tp, y_up)
        send_face((1, 1), (2, 1), tp, y_down)
        core_copy(1, 1, tp, core).start()
    build_x(taps, bx, tx, txb)
    for side in (0, 2):
        arrived(1, side, 0)
        send_face((1, side), (0, side), 0, y_up)
        send_face((1, side), (2, side), 0, y_down)
    for side in (0, 2):
        arrived(side, 1, 1)
        send_face((side, 1), (side, 0), 1, x_up)
        send_face((side, 1), (side, 2), 1, x_down)
    build_y(taps, by, ty, tyb)
    loads[3].wait()

    def order_tile(i, carry):
        quad = tile[pl.ds(4 * i, 4)].astype(F32).reshape(2, 2, 8, 8, LANES)
        sides = swap_quads(quad[:, 0], quad[:, 1])
        rows = jnp.stack([m[x] for m in sides for x in range(2)], axis=1)
        seen[i] = rows.reshape(256, LANES).astype(BF16)
        return carry

    lax.fori_loop(0, 16, order_tile, 0)
    swapped(1, 1)
    forward_z(1, 1)
    for side in (0, 2):
        arrived(1, side, 1)
        arrived(side, 1, 0)
    for side in (0, 2):
        swapped(1, side)
        forward_z(1, side)
        swapped(side, 1)
        forward_z(side, 1)
    forward_x(1)
    for jy in (0, 2):
        for jx in (0, 2):
            for tp in range(2):
                arrived(jy, jx, tp)
    for jy in (0, 2):
        for jx in (0, 2):
            swapped(jy, jx)
            forward_z(jy, jx)
        forward_x(jy)

    def along_y(step, carry):
        quotient = []
        for b in range(2):
            blurred = None
            for r in range(RANK):
                both = [
                    after_x[r, 4 * b : 4 * b + 8, :, pl.ds(32 * step + 16 * k, 16), :].reshape(256, LANES)
                    for k in range(2)
                ]
                part = dot(ty[r], jnp.concatenate(both, axis=1))
                blurred = part if blurred is None else blurred + part
            rows = slice(128 * b, 128 * b + 128)
            both = jnp.concatenate([seen[2 * step + k, rows, :] for k in range(2)], axis=1).astype(F32)
            quotient.append((RANK * both / (blurred + RANK * BACKGROUND)).astype(BF16))
        done = dot(tyb[...], jnp.concatenate(quotient, axis=0)).astype(BF16)
        for k in range(2):
            back_y[:, pl.ds(32 * step + 16 * k, 16), :] = done[:, k * 128 : k * 128 + 128].reshape(
                24, 16, LANES
            )
        return carry

    def backward_x(half):
        within = slice(half * 64, half * 64 + 192)
        for g in range(GROUPS):
            for r in range(RANK):
                at = (r * GROUPS + g) * 2
                both = jnp.concatenate([back_y[at, within, :], back_y[at + 1, within, :]], axis=1)
                done = dot(txb[half, r, :, 0:192], both).astype(BF16)
                for k in range(2):
                    back_x[g, half, k * 64 : k * 64 + 64, r * 128 : (r + 1) * 128] = done[
                        :, k * 128 : k * 128 + 128
                    ]

    def backward_rims(half):
        both = dot(back_x[0, half], wb[0, :, LANES:])
        for g in range(1, GROUPS):
            both = both + dot(back_x[g, half], wb[g, :, LANES:])
        is_low = iota((64, LANES), 1) < 64
        rims[half, 0] = jnp.where(is_low, both[0:64], pltpu.roll(both[64:128], 64, 1))
        rims[half, 1] = jnp.where(is_low, pltpu.roll(both[0:64], 64, 1), both[64:128])

    def backward_z(half):
        for g in range(GROUPS):
            done = dot(back_x[g, half], wb[g, :, :LANES])
            for c in range(4):
                at = (g + c) % 4
                sums[half, c, :, at * 32 : at * 32 + 32] = done[:, at * 32 : at * 32 + 32]

    far = (1 - chip) * 2 + core

    def sum_copy(source, target, index, device):
        return pltpu.make_async_remote_copy(
            src_ref=source, dst_ref=target, send_sem=sum_send.at[index],
            recv_sem=sum_recv.at[index], device_id=device, device_id_type=MESH,
        )

    far_swap = [
        sum_copy(sums.at[h, (1 - chip) * 2 + 1 - core], got_core.at[h, 0], h, partner) for h in range(2)
    ]
    near_swap = [
        sum_copy(sums.at[h, chip * 2 + 1 - core], got_core.at[h, 1], 2 + h, partner) for h in range(2)
    ]
    over = [sum_copy(sums.at[h, far], got_chip.at[h], 4 + h, at_vert(q * 4 + far)) for h in range(2)]
    rim_swap = [sum_copy(rims.at[h, 1 - core], got_rim.at[h], 6 + h, partner) for h in range(2)]
    edge_home = jnp.where(core == 0, vert - slot - 1, vert - slot + 4)
    edge_there = jnp.where(core == 0, q, 3 - q) > 0

    def edge_copy(h, which):
        return pltpu.make_async_remote_copy(
            src_ref=rims.at[h, core], dst_ref=got_edge.at[which, h], send_sem=sum_send.at[8 + h],
            recv_sem=sum_recv.at[8 + 2 * h + which], device_id=at_vert(edge_home), device_id_type=MESH,
        )

    def backward(h):
        backward_x(h)
        backward_rims(h)
        rim_swap[h].start()
        backward_z(h)
        far_swap[h].start()
        near_swap[h].start()

    def pass_over(h):
        rim_swap[h].wait_recv()
        rims[h, core] = rims[h, core] + got_rim[h]
        pl.when(edge_there)(lambda: edge_copy(h, chip).start())
        far_swap[h].wait_recv()
        sums[h, far] = sums[h, far] + got_core[h, 0]
        over[h].start()

    lax.fori_loop(0, 6, along_y, 0, unroll=2)
    backward(0)
    lax.fori_loop(6, 8, along_y, 0, unroll=2)
    pass_over(0)
    backward(1)
    pass_over(1)

    mine = []
    for h in range(2):
        near_swap[h].wait_recv()
        mine.append(sums[h, slot] + got_core[h, 1])
    for h in range(2):
        over[h].wait_recv()
        mine[h] = mine[h] + got_chip[h]

    @pl.when(is_edge)
    def _():
        for h in range(2):
            edge_copy(h, 0).wait_recv()
            edge_copy(h, 1).wait_recv()

    start = jnp.where(last, RAD, 0)
    lane = iota((64, LANES), 1)
    keep = is_edge & (lane >= start) & (lane < start + RAD)
    for h in range(2):
        edge = got_edge[0, h] + got_edge[1, h]
        for g in range(GROUPS):
            own = pltpu.roll(mine[h], (8 - g - slot) % 4 * 32, 1)
            sides = []
            for k in range(2):
                rim = pltpu.roll(edge, (start + LANES - 64 * k - RAD * g) % LANES, 1)
                part = own[64 * k : 64 * k + 64] + jnp.where(keep, rim, 0.0)
                sides.append(part.reshape(8, 8, LANES) * (1.0 / (RANK * VIEWS)))
            part = jnp.stack(swap_quads(*sides), axis=1).reshape(16, 8, LANES)
            at = (slice(16 * h, 16 * h + 16), slice(g * 8, g * 8 + 8))
            refined[at] = est[at] * part[:, :, 0:BLOCK]

    for tp in range(2):
        for k in range(1, VIEWS):
            part_copy(slot, tp, k - 1, partner, 0).wait_send()

        @pl.when(is_edge)
        def _():
            for k in range(VIEWS):
                part_copy(4, tp, 3 + k, partner, 0).wait_send()

    for copy, there in faces:
        pl.when(there)(copy.wait_send)
    for jy in range(3):
        for jx in range(3):

            @pl.when(exists(jy, jx))
            def _():
                for tp in range(2):
                    core_copy(jy, jx, tp, core).wait_send()

    for copy in far_swap + near_swap + over + rim_swap:
        copy.wait_send()

    @pl.when(edge_there)
    def _():
        for h in range(2):
            edge_copy(h, 0).wait_send()


def local(estimate, view_tiles, slot_view, psf_taps):
    vmem = pl.BlockSpec(memory_space=pltpu.VMEM)
    hbm = pl.BlockSpec(memory_space=pltpu.HBM)
    tile = view_tiles[0, 0, 0]
    psf = jnp.transpose(psf_taps, (1, 2, 0, 3))
    scratch = [
        pltpu.VMEM(estimate.shape, F32),
        pltpu.VMEM(tile.shape, BF16),
        pltpu.VMEM(psf.shape, F32),
        pltpu.VMEM(slot_view.shape, jnp.int32),
        pltpu.VMEM((256, LANES), BF16),
        pltpu.VMEM((6, 2, 64, LANES), BF16),
        pltpu.VMEM((3, 5, 2, 384, LANES), BF16),
        pltpu.VMEM((RANK, 12, 2, 384, LANES), BF16),
        pltpu.VMEM((RANK, 12, 2, 256, LANES), BF16),
        pltpu.VMEM((16, 256, LANES), BF16),
        pltpu.VMEM((24, 256, LANES), BF16),
        pltpu.VMEM((GROUPS, 2, 128, RANK * LANES), BF16),
        pltpu.VMEM((2, 4, 128, LANES), F32),
        pltpu.VMEM((2, 2, 64, LANES), F32),
        pltpu.VMEM((2, 2, 128, LANES), F32),
        pltpu.VMEM((2, 64, LANES), F32),
        pltpu.VMEM((2, 128, LANES), F32),
        pltpu.VMEM((2, 2, 64, LANES), F32),
        pltpu.VMEM((2, 24, LANES), F32),
        pltpu.VMEM((RANK, 128, 256), BF16),
        pltpu.VMEM((RANK, 128, 256), BF16),
        pltpu.VMEM((256, RANK * LANES), BF16),
        pltpu.VMEM((RANK * 128, 256), BF16),
        pltpu.VMEM((2, RANK, 64, 256), BF16),
        pltpu.VMEM((GROUPS, RANK * LANES, 256), BF16),
        pltpu.SemaphoreType.DMA((4,)),
        pltpu.SemaphoreType.DMA((14,)),
        pltpu.SemaphoreType.DMA((12,)),
        pltpu.SemaphoreType.DMA((16,)),
        pltpu.SemaphoreType.DMA((18,)),
        pltpu.SemaphoreType.DMA((18,)),
        pltpu.SemaphoreType.DMA((18,)),
        pltpu.SemaphoreType.DMA((10,)),
        pltpu.SemaphoreType.DMA((12,)),
    ]
    return pl.pallas_call(
        kernel,
        out_shape=pltpu.VMEM(estimate.shape, F32),
        in_specs=[hbm] * 4,
        out_specs=vmem,
        scratch_shapes=scratch,
        compiler_params=pltpu.CompilerParams(
            collective_id=0, has_side_effects=True, vmem_limit_bytes=56 * 1024 * 1024
        ),
    )(*(pltpu.with_memory_space_constraint(a, pltpu.HBM) for a in (estimate, tile, psf, slot_view)))


def solution(mesh):
    placed = (
        P("bx", "by", "vert"),
        P("bx", "by", "vert", None, None, None),
        P("bx", "by", None),
        P(),
    )
    return jax.shard_map(
        local, mesh=mesh, in_specs=placed, out_specs=P("bx", "by", "vert"), check_vma=False
    )
```

```python
import jax
import jax.numpy as jnp
from jax import lax
from jax.experimental import pallas as pl
from jax.experimental.pallas import tpu as pltpu
from jax.sharding import PartitionSpec as P

BACKGROUND = 0.1
MESH = pl.DeviceIdType.MESH
F32, BF16 = jnp.float32, jnp.bfloat16
BLOCK = 32
RAD = 16
TAPS = 33
RANK = 3
VIEWS = 4
GROUPS = 4
LANES = 128


def iota(shape, axis):
    return lax.broadcasted_iota(jnp.int32, shape, axis)


def dot(a, b):
    return jnp.dot(a, b, preferred_element_type=F32)


def band(line, rows, start):
    line = jnp.broadcast_to(line, (rows, LANES))
    return pltpu.roll(line, start % LANES, 1, stride=1, stride_axis=0)


def swap_quads(a, b):
    low, axis = iota(a.shape, a.ndim - 2) < 4, a.ndim - 2
    return jnp.where(low, a, pltpu.roll(b, 4, axis)), jnp.where(low, pltpu.roll(a, 4, axis), b)


def build_taps(psf, slot_view, slot, taps):
    listed = slot_view[...]
    view = jnp.sum(jnp.where(iota(listed.shape, 2) == slot, listed, 0), axis=2, keepdims=True)
    held = iota((VIEWS, TAPS), 0) == view[0]
    mine = jnp.sum(jnp.where(held[None, None], psf[...], 0.0), axis=2)
    mine = (mine / jnp.sum(mine, axis=-1, keepdims=True)).astype(BF16).astype(F32)
    taps[...] = jnp.zeros_like(taps)
    for a in range(3):
        taps[0, 8 * a : 8 * a + RANK, :TAPS] = mine[a]
    flip = (iota((LANES, LANES), 0) + iota((LANES, LANES), 1) == TAPS - 1).astype(BF16)
    taps[1] = dot(taps[0].astype(BF16), flip)


def build_z(taps, wz, wb):
    z_in, z_out = iota((LANES, LANES), 0), iota((LANES, LANES), 1)
    near = jnp.abs(z_in - z_out) <= RAD
    rim, out = iota((32, LANES), 0), iota((32, LANES), 1)
    rim_ok = ((rim < RAD) & (out <= rim)) | ((rim >= RAD) & (out >= rim + 96))
    lane16 = iota((16, LANES), 1)
    for r in range(RANK):
        forward, backward = taps[1, 16 + r : 17 + r, :], taps[0, 16 + r : 17 + r, :]
        columns = slice(r * LANES, (r + 1) * LANES)
        wz[0:128, columns] = jnp.where(near, band(forward, LANES, -RAD), 0.0).astype(BF16)
        wz[128:160, columns] = jnp.where(rim_ok, band(forward, 32, 96), 0.0).astype(BF16)
        wz[160:256, columns] = jnp.zeros((96, LANES), BF16)
        main = jnp.where(near, band(backward, LANES, -RAD), 0.0)
        low = jnp.where(lane16 < RAD, band(backward, 16, 0), 0.0)
        high = jnp.where(lane16 < RAD, band(backward, 16, 96), 0.0)
        for g in range(GROUPS):
            wb[g, r * 128 : r * 128 + 128, 0:128] = (
                pltpu.roll(main, 32 * g, 1) if g else main
            ).astype(BF16)
            wb[g, r * 128 : r * 128 + 128, 128:256] = jnp.zeros((128, LANES), BF16)
            lo, hi = pltpu.roll(low, RAD * g, 1) if g else low, pltpu.roll(high, 64 + RAD * g, 1)
            wb[g, r * 128 : r * 128 + 16, 128:256] = lo.astype(BF16)
            wb[g, r * 128 + 112 : r * 128 + 128, 128:256] = hi.astype(BF16)


def build_x(taps, bx, tx, txb):
    spread = (iota((LANES, 256), 1) == 4 * iota((LANES, 256), 0)).astype(BF16)
    lane, row = iota((LANES, LANES), 1), iota((LANES, LANES), 0)
    low, high = bx > 0, bx < 3

    def tiles(line):
        turned = [band(line[:, i * LANES : (i + 1) * LANES], LANES, 0) for i in range(2)]
        return jnp.where(lane >= row, turned[0], 0.0), jnp.where(lane >= row, turned[1], turned[0])

    wide = [dot(taps[k, 0:8, :].astype(BF16), spread) for k in range(2)]
    for r in range(RANK):
        left, right = tiles(wide[0][r : r + 1])
        tx[r, :, 0:128] = left.astype(BF16)
        tx[r, :, 128:256] = right.astype(BF16)
        left, right = [m[0:64] for m in tiles(wide[1][r : r + 1])]
        txb[0, r, :, 0:128] = jnp.where((lane[0:64] >= 64) | low, left, 0.0).astype(BF16)
        txb[0, r, :, 128:256] = right.astype(BF16)
        txb[1, r, :, 0:128] = left.astype(BF16)
        txb[1, r, :, 128:256] = jnp.where(high, right, 0.0).astype(BF16)


def build_y(taps, by, ty, tyb):
    place = by * BLOCK - RAD + iota((BLOCK, LANES), 1)
    inside = (place >= 0) & (place < 4 * BLOCK)
    plain = [band(taps[0, 8 + r : 9 + r, :], BLOCK, 0) for r in range(RANK)]
    plain += [
        jnp.where(inside, band(taps[1, 8 + r : 9 + r, :], BLOCK, 0), 0.0) for r in range(RANK)
    ]
    plain = jnp.concatenate(plain, axis=0).astype(BF16)
    y, column = iota((LANES, 256), 0), iota((LANES, 256), 1)
    wide = [
        dot(plain, (column == 16 * (y // 4) + 4 * x + y % 4).astype(BF16)).astype(BF16)
        for x in range(4)
    ]
    row, source = iota((LANES, LANES), 0), iota((LANES, LANES), 1)
    order = (row == 16 * (source % 32 // 4) + 4 * (source // 32) + source % 4).astype(BF16)
    for i in range(2 * RANK):
        done = dot(order, jnp.concatenate([m[i * 32 : i * 32 + 32] for m in wide], axis=0)).astype(BF16)
        if i < RANK:
            ty[i] = done
        else:
            tyb[(i - RANK) * 128 : (i - RANK + 1) * 128, :] = done


def kernel(
    est_hbm, tile_hbm, psf_hbm, slot_view_hbm, refined,
    est, tile, psf, slot_view,
    packed, parts, field, after_z, after_x, seen, back_y, back_x, sums, rims,
    got_core, got_rim, got_chip, got_edge,
    taps, tx, ty, wz, tyb, txb, wb,
    load_sem, part_send, part_recv, face_send, face_recv, core_send, core_recv, sum_send, sum_recv,
):
    bx, by, vert = lax.axis_index("bx"), lax.axis_index("by"), lax.axis_index("vert")
    q, slot = vert // VIEWS, vert % VIEWS
    core, chip = slot % 2, slot // 2

    loads = [
        pltpu.make_async_copy(source, target, load_sem.at[i])
        for i, (source, target) in enumerate(
            ((est_hbm, est), (psf_hbm, psf), (slot_view_hbm, slot_view), (tile_hbm, tile))
        )
    ]
    for copy in loads:
        copy.start()

    def at_vert(index):
        return {"vert": index}

    partner = at_vert(q * 4 + chip * 2 + 1 - core)
    x_up, x_down = ({"bx": bx + 1}, bx < 3), ({"bx": bx - 1}, bx > 0)
    y_up, y_down = ({"by": by + 1}, by < 3), ({"by": by - 1}, by > 0)
    above, below = q < 3, q > 0
    first, last = slot == 0, slot == VIEWS - 1
    is_edge = (first & below) | (last & above)

    def exists(jy, jx):
        here = jy == jy
        for index, j in ((by, jy), (bx, jx)):
            if j != 1:
                here = (index > 0 if j == 0 else index < 3) & here
        return here

    got_edge[...] = jnp.zeros_like(got_edge)
    barrier = pltpu.get_barrier_semaphore()

    def greet(device):
        pl.semaphore_signal(barrier, inc=1, device_id=device, device_id_type=MESH)

    for k in range(1, VIEWS):
        greet(at_vert(q * 4 + (slot + k) % VIEWS))
    for device, there in (x_up, x_down, y_up, y_down):
        pl.when(there)(lambda device=device: greet(device))

    @pl.when(below)
    def _():
        greet(at_vert(vert - slot - 1))
        pl.when(first)(lambda: greet(at_vert(vert - 3)))

    @pl.when(above)
    def _():
        greet(at_vert(vert - slot + 4))
        pl.when(last)(lambda: greet(at_vert(vert + 3)))

    loads[0].wait()
    groups = est[...].reshape(BLOCK, GROUPS, 8, BLOCK)
    line = jnp.concatenate([groups[:, g].reshape(256, BLOCK) for g in range(GROUPS)], axis=1)
    line = pltpu.roll(line, slot * 32, 1).reshape(16, 2, 8, LANES)
    for side, quads in enumerate(swap_quads(line[:, 0], line[:, 1])):
        packed[side * 128 : side * 128 + 128, :] = quads.reshape(128, LANES).astype(BF16)

    beside = [(there, 1) for _, there in (x_up, x_down, y_up, y_down)] + [(is_edge, 4)]
    beside += [((slot == 1) & above, 1), ((slot == 2) & below, 1)]
    pl.semaphore_wait(barrier, 3 + sum(jnp.where(there, n, 0) for there, n in beside))

    def part_copy(source, tp, send, device, side):
        return pltpu.make_async_remote_copy(
            src_ref=packed.at[pl.ds(side * 128 + tp * 64, 64), :], dst_ref=parts.at[source, tp],
            send_sem=part_send.at[send * 2 + tp], recv_sem=part_recv.at[source * 2 + tp],
            device_id=device, device_id_type=MESH,
        )

    for tp in range(2):
        for k in range(1, VIEWS):
            other = (slot + k) % VIEWS
            part_copy(slot, tp, k - 1, at_vert(q * 4 + other), other % 2).start()

        @pl.when(last & above)
        def _():
            for k in range(VIEWS):
                part_copy(4, tp, 3 + k, at_vert(vert + 1 + k), k % 2).start()

        @pl.when(first & below)
        def _():
            for k in range(VIEWS):
                part_copy(5, tp, 3 + k, at_vert(vert - 4 + k), k % 2).start()

    parts[slot] = packed[pl.ds(core * 128, 128), :].reshape(2, 64, LANES)

    def clear(ref):
        ref[...] = jnp.zeros(ref.shape, BF16)

    pl.when(~below)(lambda: clear(parts.at[4]))
    pl.when(~above)(lambda: clear(parts.at[5]))
    pl.when(bx == 0)(lambda: clear(field.at[:, :, :, 0:128, :]))
    pl.when(bx == 3)(lambda: clear(field.at[:, :, :, 256:384, :]))
    pl.when(by == 0)(lambda: clear(field.at[0]))
    pl.when(by == 3)(lambda: clear(field.at[2]))
    loads[1].wait()
    loads[2].wait()
    build_taps(psf, slot_view, slot, taps)
    build_z(taps, wz, wb)

    def assemble(tp):
        for k in range(1, VIEWS):
            part_copy((slot + k) % VIEWS, tp, 0, partner, 0).wait_recv()
        for k, there in ((4, below), (5, above)):
            pl.when(there)(lambda k=k: part_copy(k, tp, 0, partner, 0).wait_recv())
        lane = iota((64, LANES), 1)
        rows = slice(128 + tp * 64, 192 + tp * 64)
        have = [parts[k, tp].astype(F32) for k in range(6)]
        for g in range(GROUPS):
            line = have[(3 - g) % 4]
            for at in range(3):
                line = jnp.where(lane // 32 == at, have[(at - g) % 4], line)
            if g:
                line = pltpu.roll(line, LANES - 32 * g, 1)
            field[1, g, core, rows, :] = line.astype(BF16)
        line = pltpu.roll(jnp.where(lane % 32 < RAD, have[5], have[4]), RAD, 1)
        field[1, 4, core, rows, :] = line.astype(BF16)

    def piece(jy, jx, tp, side):
        return field.at[jy, :, side, pl.ds(jx * 128 + tp * 64, 64), :]

    def number(jy, jx, tp):
        return (jy * 3 + jx) * 2 + tp

    def face_copy(source, target, tp, send, device):
        return pltpu.make_async_remote_copy(
            src_ref=piece(*source, tp, core), dst_ref=piece(*target, tp, core),
            send_sem=face_send.at[send], recv_sem=face_recv.at[number(*target, tp)],
            device_id=device, device_id_type=MESH,
        )

    def core_copy(jy, jx, tp, side):
        return pltpu.make_async_remote_copy(
            src_ref=piece(jy, jx, tp, side), dst_ref=piece(jy, jx, tp, side),
            send_sem=core_send.at[number(jy, jx, tp)], recv_sem=core_recv.at[number(jy, jx, tp)],
            device_id=partner, device_id_type=MESH,
        )

    faces = []

    def send_face(source, target, tp, way):
        device, there = way
        copy = face_copy(source, target, tp, len(faces), device)
        there = there & exists(*source)
        pl.when(there)(copy.start)
        faces.append((copy, there))

    def arrived(jy, jx, tp):
        @pl.when(exists(jy, jx))
        def _():
            face_copy((jy, jx), (jy, jx), tp, 0, partner).wait_recv()
            core_copy(jy, jx, tp, core).start()

    def swapped(jy, jx):
        @pl.when(exists(jy, jx))
        def _():
            for tp in range(2):
                core_copy(jy, jx, tp, 1 - core).wait_recv()

    def forward_z(jy, jx):
        rows = slice(jx * 128, jx * 128 + 128)
        rim = field[jy, 4, :, rows, :].reshape(256, LANES)
        for g in range(GROUPS):
            turned = pltpu.roll(rim, LANES - 32 * g, 1) if g else rim
            main = field[jy, g, :, rows, :].reshape(256, LANES)
            done = dot(jnp.concatenate([main, turned], axis=1), wz[...]).astype(BF16)
            for r in range(RANK):
                after_z[r, jy * GROUPS + g, :, rows, :] = done[:, r * 128 : (r + 1) * 128].reshape(
                    2, 128, LANES
                )

    def forward_x(jy):
        def body(step, carry):
            r, group = step // GROUPS, jy * GROUPS + step % GROUPS
            for b in range(2):
                rows = pl.ds(b * 128, 256)
                both = jnp.concatenate([after_z[r, group, k, rows, :] for k in range(2)], axis=1)
                done = dot(tx[r], both).astype(BF16)
                for k in range(2):
                    after_x[r, group, k, b * 128 : b * 128 + 128, :] = done[:, k * 128 : k * 128 + 128]
            return carry

        lax.fori_loop(0, GROUPS * RANK, body, 0, unroll=True)

    for tp in (0, 1):
        assemble(tp)
        send_face((1, 1), (1, 0), tp, x_up)
        send_face((1, 1), (1, 2), tp, x_down)
        send_face((1, 1), (0, 1), tp, y_up)
        send_face((1, 1), (2, 1), tp, y_down)
        core_copy(1, 1, tp, core).start()
    build_x(taps, bx, tx, txb)
    for side in (0, 2):
        arrived(1, side, 0)
        send_face((1, side), (0, side), 0, y_up)
        send_face((1, side), (2, side), 0, y_down)
    for side in (0, 2):
        arrived(side, 1, 1)
        send_face((side, 1), (side, 0), 1, x_up)
        send_face((side, 1), (side, 2), 1, x_down)
    build_y(taps, by, ty, tyb)
    loads[3].wait()

    def order_tile(i, carry):
        quad = tile[pl.ds(4 * i, 4)].astype(F32).reshape(2, 2, 8, 8, LANES)
        sides = swap_quads(quad[:, 0], quad[:, 1])
        rows = jnp.stack([m[x] for m in sides for x in range(2)], axis=1)
        seen[i] = rows.reshape(256, LANES).astype(BF16)
        return carry

    lax.fori_loop(0, 16, order_tile, 0, unroll=4)
    swapped(1, 1)
    forward_z(1, 1)
    for side in (0, 2):
        arrived(1, side, 1)
        arrived(side, 1, 0)
    for side in (0, 2):
        swapped(1, side)
        swapped(side, 1)
    for side in (0, 2):
        forward_z(1, side)
        forward_z(side, 1)
    forward_x(1)
    for jy in (0, 2):
        for jx in (0, 2):
            for tp in range(2):
                arrived(jy, jx, tp)
    for jy in (0, 2):
        for jx in (0, 2):
            swapped(jy, jx)
    for jy in (0, 2):
        for jx in (0, 2):
            forward_z(jy, jx)
        forward_x(jy)

    def along_y(step):
        quotient = []
        for b in range(2):
            blurred = None
            for r in range(RANK):
                both = [
                    after_x[r, 4 * b : 4 * b + 8, :, pl.ds(32 * step + 16 * k, 16), :].reshape(256, LANES)
                    for k in range(2)
                ]
                part = dot(ty[r], jnp.concatenate(both, axis=1))
                blurred = part if blurred is None else blurred + part
            rows = slice(128 * b, 128 * b + 128)
            both = jnp.concatenate([seen[2 * step + k, rows, :] for k in range(2)], axis=1).astype(F32)
            quotient.append((RANK * both / (blurred + RANK * BACKGROUND)).astype(BF16))
        quotient = jnp.concatenate(quotient, axis=0)
        for r in range(RANK):
            done = dot(tyb[r * 128 : r * 128 + 128, :], quotient).astype(BF16)
            for k in range(2):
                back_y[r * 8 : r * 8 + 8, pl.ds(32 * step + 16 * k, 16), :] = done[
                    :, k * 128 : k * 128 + 128
                ].reshape(8, 16, LANES)

    def backward_x(half):
        within = slice(half * 64, half * 64 + 192)
        for g in range(GROUPS):
            for r in range(RANK):
                at = (r * GROUPS + g) * 2
                both = jnp.concatenate([back_y[at, within, :], back_y[at + 1, within, :]], axis=1)
                done = dot(txb[half, r, :, 0:192], both).astype(BF16)
                for k in range(2):
                    back_x[g, half, k * 64 : k * 64 + 64, r * 128 : (r + 1) * 128] = done[
                        :, k * 128 : k * 128 + 128
                    ]

    def backward_rims(half):
        both = dot(back_x[0, half], wb[0, :, LANES:])
        for g in range(1, GROUPS):
            both = both + dot(back_x[g, half], wb[g, :, LANES:])
        is_low = iota((64, LANES), 1) < 64
        rims[half, 0] = jnp.where(is_low, both[0:64], pltpu.roll(both[64:128], 64, 1))
        rims[half, 1] = jnp.where(is_low, pltpu.roll(both[0:64], 64, 1), both[64:128])

    def backward_z(half):
        for g in range(GROUPS):
            done = dot(back_x[g, half], wb[g, :, :LANES])
            for c in range(4):
                at = (g + c) % 4
                sums[half, c, :, at * 32 : at * 32 + 32] = done[:, at * 32 : at * 32 + 32]

    far = (1 - chip) * 2 + core

    def sum_copy(source, target, index, device):
        return pltpu.make_async_remote_copy(
            src_ref=source, dst_ref=target, send_sem=sum_send.at[index],
            recv_sem=sum_recv.at[index], device_id=device, device_id_type=MESH,
        )

    far_swap = [
        sum_copy(sums.at[h, (1 - chip) * 2 + 1 - core], got_core.at[h, 0], h, partner) for h in range(2)
    ]
    near_swap = [
        sum_copy(sums.at[h, chip * 2 + 1 - core], got_core.at[h, 1], 2 + h, partner) for h in range(2)
    ]
    over = [sum_copy(sums.at[h, far], got_chip.at[h], 4 + h, at_vert(q * 4 + far)) for h in range(2)]
    rim_swap = [sum_copy(rims.at[h, 1 - core], got_rim.at[h], 6 + h, partner) for h in range(2)]
    edge_home = jnp.where(core == 0, vert - slot - 1, vert - slot + 4)
    edge_there = jnp.where(core == 0, q, 3 - q) > 0

    def edge_copy(h, which):
        return pltpu.make_async_remote_copy(
            src_ref=rims.at[h, core], dst_ref=got_edge.at[which, h], send_sem=sum_send.at[8 + h],
            recv_sem=sum_recv.at[8 + 2 * h + which], device_id=at_vert(edge_home), device_id_type=MESH,
        )

    def backward(h):
        backward_x(h)
        backward_rims(h)
        rim_swap[h].start()
        backward_z(h)
        far_swap[h].start()
        near_swap[h].start()

    def pass_over(h):
        rim_swap[h].wait_recv()
        rims[h, core] = rims[h, core] + got_rim[h]
        pl.when(edge_there)(lambda: edge_copy(h, chip).start())
        far_swap[h].wait_recv()
        sums[h, far] = sums[h, far] + got_core[h, 0]
        over[h].start()

    for step in range(6):
        along_y(step)
    backward(0)
    for step in range(6, 8):
        along_y(step)
    pass_over(0)
    backward(1)
    pass_over(1)

    mine = []
    for h in range(2):
        near_swap[h].wait_recv()
        mine.append(sums[h, slot] + got_core[h, 1])
    for h in range(2):
        over[h].wait_recv()
        mine[h] = mine[h] + got_chip[h]

    @pl.when(is_edge)
    def _():
        for h in range(2):
            edge_copy(h, 0).wait_recv()
            edge_copy(h, 1).wait_recv()

    start = jnp.where(last, RAD, 0)
    lane = iota((64, LANES), 1)
    keep = is_edge & (lane >= start) & (lane < start + RAD)
    for h in range(2):
        edge = got_edge[0, h] + got_edge[1, h]
        for g in range(GROUPS):
            own = pltpu.roll(mine[h], (8 - g - slot) % 4 * 32, 1)
            sides = []
            for k in range(2):
                rim = pltpu.roll(edge, (start + LANES - 64 * k - RAD * g) % LANES, 1)
                part = own[64 * k : 64 * k + 64] + jnp.where(keep, rim, 0.0)
                sides.append(part.reshape(8, 8, LANES) * (1.0 / (RANK * VIEWS)))
            part = jnp.stack(swap_quads(*sides), axis=1).reshape(16, 8, LANES)
            at = (slice(16 * h, 16 * h + 16), slice(g * 8, g * 8 + 8))
            refined[at] = est[at] * part[:, :, 0:BLOCK]

    for tp in range(2):
        for k in range(1, VIEWS):
            part_copy(slot, tp, k - 1, partner, 0).wait_send()

        @pl.when(is_edge)
        def _():
            for k in range(VIEWS):
                part_copy(4, tp, 3 + k, partner, 0).wait_send()

    for copy, there in faces:
        pl.when(there)(copy.wait_send)
    for jy in range(3):
        for jx in range(3):

            @pl.when(exists(jy, jx))
            def _():
                for tp in range(2):
                    core_copy(jy, jx, tp, core).wait_send()

    for copy in far_swap + near_swap + over + rim_swap:
        copy.wait_send()

    @pl.when(edge_there)
    def _():
        for h in range(2):
            edge_copy(h, 0).wait_send()


def local(estimate, view_tiles, slot_view, psf_taps):
    vmem = pl.BlockSpec(memory_space=pltpu.VMEM)
    hbm = pl.BlockSpec(memory_space=pltpu.HBM)
    tile = view_tiles[0, 0, 0]
    psf = jnp.transpose(psf_taps, (1, 2, 0, 3))
    scratch = [
        pltpu.VMEM(estimate.shape, F32),
        pltpu.VMEM(tile.shape, BF16),
        pltpu.VMEM(psf.shape, F32),
        pltpu.VMEM(slot_view.shape, jnp.int32),
        pltpu.VMEM((256, LANES), BF16),
        pltpu.VMEM((6, 2, 64, LANES), BF16),
        pltpu.VMEM((3, 5, 2, 384, LANES), BF16),
        pltpu.VMEM((RANK, 12, 2, 384, LANES), BF16),
        pltpu.VMEM((RANK, 12, 2, 256, LANES), BF16),
        pltpu.VMEM((16, 256, LANES), BF16),
        pltpu.VMEM((24, 256, LANES), BF16),
        pltpu.VMEM((GROUPS, 2, 128, RANK * LANES), BF16),
        pltpu.VMEM((2, 4, 128, LANES), F32),
        pltpu.VMEM((2, 2, 64, LANES), F32),
        pltpu.VMEM((2, 2, 128, LANES), F32),
        pltpu.VMEM((2, 64, LANES), F32),
        pltpu.VMEM((2, 128, LANES), F32),
        pltpu.VMEM((2, 2, 64, LANES), F32),
        pltpu.VMEM((2, 24, LANES), F32),
        pltpu.VMEM((RANK, 128, 256), BF16),
        pltpu.VMEM((RANK, 128, 256), BF16),
        pltpu.VMEM((256, RANK * LANES), BF16),
        pltpu.VMEM((RANK * 128, 256), BF16),
        pltpu.VMEM((2, RANK, 64, 256), BF16),
        pltpu.VMEM((GROUPS, RANK * LANES, 256), BF16),
        pltpu.SemaphoreType.DMA((4,)),
        pltpu.SemaphoreType.DMA((14,)),
        pltpu.SemaphoreType.DMA((12,)),
        pltpu.SemaphoreType.DMA((16,)),
        pltpu.SemaphoreType.DMA((18,)),
        pltpu.SemaphoreType.DMA((18,)),
        pltpu.SemaphoreType.DMA((18,)),
        pltpu.SemaphoreType.DMA((10,)),
        pltpu.SemaphoreType.DMA((12,)),
    ]
    return pl.pallas_call(
        kernel,
        out_shape=pltpu.VMEM(estimate.shape, F32),
        in_specs=[hbm] * 4,
        out_specs=vmem,
        scratch_shapes=scratch,
        compiler_params=pltpu.CompilerParams(
            collective_id=0, has_side_effects=True, vmem_limit_bytes=56 * 1024 * 1024
        ),
    )(*(pltpu.with_memory_space_constraint(a, pltpu.HBM) for a in (estimate, tile, psf, slot_view)))


def solution(mesh):
    placed = (
        P("bx", "by", "vert"),
        P("bx", "by", "vert", None, None, None),
        P("bx", "by", None),
        P(),
    )
    return jax.shard_map(
        local, mesh=mesh, in_specs=placed, out_specs=P("bx", "by", "vert"), check_vma=False
    )
```

```python
import jax
import jax.numpy as jnp
from jax import lax
from jax.experimental import pallas as pl
from jax.experimental.pallas import tpu as pltpu
from jax.sharding import PartitionSpec as P

BACKGROUND = 0.1
MESH = pl.DeviceIdType.MESH
F32, BF16 = jnp.float32, jnp.bfloat16
BLOCK = 32
RAD = 16
TAPS = 33
RANK = 3
VIEWS = 4
GROUPS = 4
LANES = 128


def iota(shape, axis):
    return lax.broadcasted_iota(jnp.int32, shape, axis)


def dot(a, b):
    return jnp.dot(a, b, preferred_element_type=F32)


def band(line, rows, start):
    line = jnp.broadcast_to(line, (rows, LANES))
    return pltpu.roll(line, start % LANES, 1, stride=1, stride_axis=0)


def swap_quads(a, b):
    low, axis = iota(a.shape, a.ndim - 2) < 4, a.ndim - 2
    return jnp.where(low, a, pltpu.roll(b, 4, axis)), jnp.where(low, pltpu.roll(a, 4, axis), b)


def build_taps(psf, slot_view, slot, taps):
    listed = slot_view[...]
    view = jnp.sum(jnp.where(iota(listed.shape, 2) == slot, listed, 0), axis=2, keepdims=True)
    held = iota((VIEWS, TAPS), 0) == view[0]
    mine = jnp.sum(jnp.where(held[None, None], psf[...], 0.0), axis=2)
    mine = (mine / jnp.sum(mine, axis=-1, keepdims=True)).astype(BF16).astype(F32)
    taps[...] = jnp.zeros_like(taps)
    for a in range(3):
        taps[0, 8 * a : 8 * a + RANK, :TAPS] = mine[a]
    flip = (iota((LANES, LANES), 0) + iota((LANES, LANES), 1) == TAPS - 1).astype(BF16)
    taps[1] = dot(taps[0].astype(BF16), flip)


def build_z(taps, wz, wb):
    z_in, z_out = iota((LANES, LANES), 0), iota((LANES, LANES), 1)
    near = jnp.abs(z_in - z_out) <= RAD
    rim, out = iota((32, LANES), 0), iota((32, LANES), 1)
    rim_ok = ((rim < RAD) & (out <= rim)) | ((rim >= RAD) & (out >= rim + 96))
    lane16 = iota((16, LANES), 1)
    for r in range(RANK):
        forward, backward = taps[1, 16 + r : 17 + r, :], taps[0, 16 + r : 17 + r, :]
        columns = slice(r * LANES, (r + 1) * LANES)
        wz[0:128, columns] = jnp.where(near, band(forward, LANES, -RAD), 0.0).astype(BF16)
        wz[128:160, columns] = jnp.where(rim_ok, band(forward, 32, 96), 0.0).astype(BF16)
        wz[160:256, columns] = jnp.zeros((96, LANES), BF16)
        main = jnp.where(near, band(backward, LANES, -RAD), 0.0)
        low = jnp.where(lane16 < RAD, band(backward, 16, 0), 0.0)
        high = jnp.where(lane16 < RAD, band(backward, 16, 96), 0.0)
        for g in range(GROUPS):
            wb[g, r * 128 : r * 128 + 128, 0:128] = (
                pltpu.roll(main, 32 * g, 1) if g else main
            ).astype(BF16)
            wb[g, r * 128 : r * 128 + 128, 128:256] = jnp.zeros((128, LANES), BF16)
            lo, hi = pltpu.roll(low, RAD * g, 1) if g else low, pltpu.roll(high, 64 + RAD * g, 1)
            wb[g, r * 128 : r * 128 + 16, 128:256] = lo.astype(BF16)
            wb[g, r * 128 + 112 : r * 128 + 128, 128:256] = hi.astype(BF16)


def build_x(taps, bx, tx, txb):
    spread = (iota((LANES, 256), 1) == 4 * iota((LANES, 256), 0)).astype(BF16)
    lane, row = iota((LANES, LANES), 1), iota((LANES, LANES), 0)
    low, high = bx > 0, bx < 3

    def tiles(line):
        turned = [band(line[:, i * LANES : (i + 1) * LANES], LANES, 0) for i in range(2)]
        return jnp.where(lane >= row, turned[0], 0.0), jnp.where(lane >= row, turned[1], turned[0])

    wide = [dot(taps[k, 0:8, :].astype(BF16), spread) for k in range(2)]
    for r in range(RANK):
        left, right = tiles(wide[0][r : r + 1])
        tx[r, :, 0:128] = left.astype(BF16)
        tx[r, :, 128:256] = right.astype(BF16)
        left, right = [m[0:64] for m in tiles(wide[1][r : r + 1])]
        txb[0, r, :, 0:128] = jnp.where((lane[0:64] >= 64) | low, left, 0.0).astype(BF16)
        txb[0, r, :, 128:256] = right.astype(BF16)
        txb[1, r, :, 0:128] = left.astype(BF16)
        txb[1, r, :, 128:256] = jnp.where(high, right, 0.0).astype(BF16)


def build_y(taps, by, ty, tyb):
    place = by * BLOCK - RAD + iota((BLOCK, LANES), 1)
    inside = (place >= 0) & (place < 4 * BLOCK)
    plain = [band(taps[0, 8 + r : 9 + r, :], BLOCK, 0) for r in range(RANK)]
    plain += [
        jnp.where(inside, band(taps[1, 8 + r : 9 + r, :], BLOCK, 0), 0.0) for r in range(RANK)
    ]
    plain = jnp.concatenate(plain, axis=0).astype(BF16)
    y, column = iota((LANES, 256), 0), iota((LANES, 256), 1)
    wide = [
        dot(plain, (column == 16 * (y // 4) + 4 * x + y % 4).astype(BF16)).astype(BF16)
        for x in range(4)
    ]
    row, source = iota((LANES, LANES), 0), iota((LANES, LANES), 1)
    order = (row == 16 * (source % 32 // 4) + 4 * (source // 32) + source % 4).astype(BF16)
    for i in range(2 * RANK):
        done = dot(order, jnp.concatenate([m[i * 32 : i * 32 + 32] for m in wide], axis=0)).astype(BF16)
        if i < RANK:
            ty[i] = done
        else:
            tyb[(i - RANK) * 128 : (i - RANK + 1) * 128, :] = done


def kernel(
    est_hbm, tile_hbm, psf_hbm, slot_view_hbm, refined,
    est, tile, psf, slot_view,
    packed, parts, field, after_z, after_x, seen, back_y, back_x, sums, rims,
    got_core, got_rim, got_chip, got_edge,
    taps, tx, ty, wz, tyb, txb, wb,
    load_sem, part_send, part_recv, face_send, face_recv, core_send, core_recv, sum_send, sum_recv,
):
    bx, by, vert = lax.axis_index("bx"), lax.axis_index("by"), lax.axis_index("vert")
    q, slot = vert // VIEWS, vert % VIEWS
    core, chip = slot % 2, slot // 2

    loads = [
        pltpu.make_async_copy(source, target, load_sem.at[i])
        for i, (source, target) in enumerate(
            ((est_hbm, est), (psf_hbm, psf), (slot_view_hbm, slot_view), (tile_hbm, tile))
        )
    ]
    for copy in loads:
        copy.start()

    def at_vert(index):
        return {"vert": index}

    partner = at_vert(q * 4 + chip * 2 + 1 - core)
    x_up, x_down = ({"bx": bx + 1}, bx < 3), ({"bx": bx - 1}, bx > 0)
    y_up, y_down = ({"by": by + 1}, by < 3), ({"by": by - 1}, by > 0)
    above, below = q < 3, q > 0
    first, last = slot == 0, slot == VIEWS - 1
    is_edge = (first & below) | (last & above)

    def exists(jy, jx):
        here = jy == jy
        for index, j in ((by, jy), (bx, jx)):
            if j != 1:
                here = (index > 0 if j == 0 else index < 3) & here
        return here

    got_edge[...] = jnp.zeros_like(got_edge)
    barrier = pltpu.get_barrier_semaphore()

    def greet(device):
        pl.semaphore_signal(barrier, inc=1, device_id=device, device_id_type=MESH)

    for k in range(1, VIEWS):
        greet(at_vert(q * 4 + (slot + k) % VIEWS))
    for device, there in (x_up, x_down, y_up, y_down):
        pl.when(there)(lambda device=device: greet(device))

    @pl.when(below)
    def _():
        greet(at_vert(vert - slot - 1))
        pl.when(first)(lambda: greet(at_vert(vert - 3)))

    @pl.when(above)
    def _():
        greet(at_vert(vert - slot + 4))
        pl.when(last)(lambda: greet(at_vert(vert + 3)))

    loads[0].wait()
    groups = est[...].reshape(BLOCK, GROUPS, 8, BLOCK)
    line = jnp.concatenate([groups[:, g].reshape(256, BLOCK) for g in range(GROUPS)], axis=1)
    line = pltpu.roll(line, slot * 32, 1).reshape(16, 2, 8, LANES)
    for side, quads in enumerate(swap_quads(line[:, 0], line[:, 1])):
        packed[side * 128 : side * 128 + 128, :] = quads.reshape(128, LANES).astype(BF16)

    beside = [(there, 1) for _, there in (x_up, x_down, y_up, y_down)] + [(is_edge, 4)]
    beside += [((slot == 1) & above, 1), ((slot == 2) & below, 1)]
    pl.semaphore_wait(barrier, 3 + sum(jnp.where(there, n, 0) for there, n in beside))

    def part_copy(source, tp, send, device, side):
        return pltpu.make_async_remote_copy(
            src_ref=packed.at[pl.ds(side * 128 + tp * 64, 64), :], dst_ref=parts.at[source, tp],
            send_sem=part_send.at[send * 2 + tp], recv_sem=part_recv.at[source * 2 + tp],
            device_id=device, device_id_type=MESH,
        )

    for tp in range(2):
        for k in range(1, VIEWS):
            other = (slot + k) % VIEWS
            part_copy(slot, tp, k - 1, at_vert(q * 4 + other), other % 2).start()

        @pl.when(last & above)
        def _():
            for k in range(VIEWS):
                part_copy(4, tp, 3 + k, at_vert(vert + 1 + k), k % 2).start()

        @pl.when(first & below)
        def _():
            for k in range(VIEWS):
                part_copy(5, tp, 3 + k, at_vert(vert - 4 + k), k % 2).start()

    parts[slot] = packed[pl.ds(core * 128, 128), :].reshape(2, 64, LANES)

    def clear(ref):
        ref[...] = jnp.zeros(ref.shape, BF16)

    pl.when(~below)(lambda: clear(parts.at[4]))
    pl.when(~above)(lambda: clear(parts.at[5]))
    pl.when(bx == 0)(lambda: clear(field.at[:, :, :, 0:128, :]))
    pl.when(bx == 3)(lambda: clear(field.at[:, :, :, 256:384, :]))
    pl.when(by == 0)(lambda: clear(field.at[0]))
    pl.when(by == 3)(lambda: clear(field.at[2]))
    loads[1].wait()
    loads[2].wait()
    build_taps(psf, slot_view, slot, taps)
    build_z(taps, wz, wb)

    def assemble(tp):
        for k in range(1, VIEWS):
            part_copy((slot + k) % VIEWS, tp, 0, partner, 0).wait_recv()
        for k, there in ((4, below), (5, above)):
            pl.when(there)(lambda k=k: part_copy(k, tp, 0, partner, 0).wait_recv())
        lane = iota((64, LANES), 1)
        rows = slice(128 + tp * 64, 192 + tp * 64)
        have = [parts[k, tp].astype(F32) for k in range(6)]
        for g in range(GROUPS):
            line = have[(3 - g) % 4]
            for at in range(3):
                line = jnp.where(lane // 32 == at, have[(at - g) % 4], line)
            if g:
                line = pltpu.roll(line, LANES - 32 * g, 1)
            field[1, g, core, rows, :] = line.astype(BF16)
        line = pltpu.roll(jnp.where(lane % 32 < RAD, have[5], have[4]), RAD, 1)
        field[1, 4, core, rows, :] = line.astype(BF16)

    def piece(jy, jx, tp, side):
        return field.at[jy, :, side, pl.ds(jx * 128 + tp * 64, 64), :]

    def number(jy, jx, tp):
        return (jy * 3 + jx) * 2 + tp

    def face_copy(source, target, tp, send, device):
        return pltpu.make_async_remote_copy(
            src_ref=piece(*source, tp, core), dst_ref=piece(*target, tp, core),
            send_sem=face_send.at[send], recv_sem=face_recv.at[number(*target, tp)],
            device_id=device, device_id_type=MESH,
        )

    def core_copy(jy, jx, tp, side):
        return pltpu.make_async_remote_copy(
            src_ref=piece(jy, jx, tp, side), dst_ref=piece(jy, jx, tp, side),
            send_sem=core_send.at[number(jy, jx, tp)], recv_sem=core_recv.at[number(jy, jx, tp)],
            device_id=partner, device_id_type=MESH,
        )

    faces = []

    def send_face(source, target, tp, way):
        device, there = way
        copy = face_copy(source, target, tp, len(faces), device)
        there = there & exists(*source)
        pl.when(there)(copy.start)
        faces.append((copy, there))

    def arrived(jy, jx, tp):
        @pl.when(exists(jy, jx))
        def _():
            face_copy((jy, jx), (jy, jx), tp, 0, partner).wait_recv()
            core_copy(jy, jx, tp, core).start()

    def swapped(jy, jx):
        @pl.when(exists(jy, jx))
        def _():
            for tp in range(2):
                core_copy(jy, jx, tp, 1 - core).wait_recv()

    def forward_z(jy, jx):
        rows = slice(jx * 128, jx * 128 + 128)
        rim = field[jy, 4, :, rows, :].reshape(256, LANES)
        for g in range(GROUPS):
            turned = pltpu.roll(rim, LANES - 32 * g, 1) if g else rim
            main = field[jy, g, :, rows, :].reshape(256, LANES)
            done = dot(jnp.concatenate([main, turned], axis=1), wz[...]).astype(BF16)
            for r in range(RANK):
                after_z[r, jy * GROUPS + g, :, rows, :] = done[:, r * 128 : (r + 1) * 128].reshape(
                    2, 128, LANES
                )

    def forward_x(jy):
        def body(step, carry):
            r, group = step // GROUPS, jy * GROUPS + step % GROUPS
            for b in range(2):
                rows = pl.ds(b * 128, 256)
                both = jnp.concatenate([after_z[r, group, k, rows, :] for k in range(2)], axis=1)
                done = dot(tx[r], both).astype(BF16)
                for k in range(2):
                    after_x[r, group, k, b * 128 : b * 128 + 128, :] = done[:, k * 128 : k * 128 + 128]
            return carry

        lax.fori_loop(0, GROUPS * RANK, body, 0, unroll=True)

    def send_faces(tp, ways):
        for target, way in ways:
            send_face((1, 1), target, tp, way)

    along_x_links = (((1, 0), x_up), ((1, 2), x_down))
    along_y_links = (((0, 1), y_up), ((2, 1), y_down))
    assemble(0)
    send_faces(0, along_x_links)
    core_copy(1, 1, 0, core).start()
    assemble(1)
    send_faces(1, along_y_links)
    send_faces(1, along_x_links)
    send_faces(0, along_y_links)
    core_copy(1, 1, 1, core).start()
    build_x(taps, bx, tx, txb)
    for side in (0, 2):
        arrived(1, side, 0)
    for one, other in ((0, 2), (2, 0)):
        send_face((1, one), (0, one), 0, y_up)
        send_face((1, other), (2, other), 0, y_down)
    for side in (0, 2):
        arrived(side, 1, 1)
    for one, other in ((0, 2), (2, 0)):
        send_face((one, 1), (one, 0), 1, x_up)
        send_face((other, 1), (other, 2), 1, x_down)
    build_y(taps, by, ty, tyb)
    loads[3].wait()

    def order_tile(i, carry):
        quad = tile[pl.ds(4 * i, 4)].astype(F32).reshape(2, 2, 8, 8, LANES)
        sides = swap_quads(quad[:, 0], quad[:, 1])
        rows = jnp.stack([m[x] for m in sides for x in range(2)], axis=1)
        seen[i] = rows.reshape(256, LANES).astype(BF16)
        return carry

    lax.fori_loop(0, 16, order_tile, 0, unroll=4)
    swapped(1, 1)
    forward_z(1, 1)
    for side in (0, 2):
        arrived(1, side, 1)
        arrived(side, 1, 0)
    for side in (0, 2):
        swapped(1, side)
        swapped(side, 1)
    for side in (0, 2):
        forward_z(1, side)
        forward_z(side, 1)
    waves = (((0, 0), (2, 2)), ((0, 2), (2, 0)))
    for corner in waves[0]:
        for tp in range(2):
            arrived(*corner, tp)
    forward_x(1)
    for corner in waves[1]:
        for tp in range(2):
            arrived(*corner, tp)
    for wave in waves:
        for corner in wave:
            swapped(*corner)
        for corner in wave:
            forward_z(*corner)
    for jy in (0, 2):
        forward_x(jy)

    def along_y(step):
        quotient = []
        for b in range(2):
            blurred = None
            for r in range(RANK):
                both = [
                    after_x[r, 4 * b : 4 * b + 8, :, pl.ds(32 * step + 16 * k, 16), :].reshape(256, LANES)
                    for k in range(2)
                ]
                part = dot(ty[r], jnp.concatenate(both, axis=1))
                blurred = part if blurred is None else blurred + part
            rows = slice(128 * b, 128 * b + 128)
            both = jnp.concatenate([seen[2 * step + k, rows, :] for k in range(2)], axis=1).astype(F32)
            quotient.append((RANK * both / (blurred + RANK * BACKGROUND)).astype(BF16))
        quotient = jnp.concatenate(quotient, axis=0)
        for r in range(RANK):
            done = dot(tyb[r * 128 : r * 128 + 128, :], quotient).astype(BF16)
            for k in range(2):
                back_y[r * 8 : r * 8 + 8, pl.ds(32 * step + 16 * k, 16), :] = done[
                    :, k * 128 : k * 128 + 128
                ].reshape(8, 16, LANES)

    def backward_x(half):
        within = slice(half * 64, half * 64 + 192)
        for g in range(GROUPS):
            for r in range(RANK):
                at = (r * GROUPS + g) * 2
                both = jnp.concatenate([back_y[at, within, :], back_y[at + 1, within, :]], axis=1)
                done = dot(txb[half, r, :, 0:192], both).astype(BF16)
                for k in range(2):
                    back_x[g, half, k * 64 : k * 64 + 64, r * 128 : (r + 1) * 128] = done[
                        :, k * 128 : k * 128 + 128
                    ]

    def backward_rims(half):
        both = dot(back_x[0, half], wb[0, :, LANES:])
        for g in range(1, GROUPS):
            both = both + dot(back_x[g, half], wb[g, :, LANES:])
        is_low = iota((64, LANES), 1) < 64
        rims[half, 0] = jnp.where(is_low, both[0:64], pltpu.roll(both[64:128], 64, 1))
        rims[half, 1] = jnp.where(is_low, pltpu.roll(both[0:64], 64, 1), both[64:128])

    def backward_z(half):
        for g in range(GROUPS):
            done = dot(back_x[g, half], wb[g, :, :LANES])
            for c in range(4):
                at = (g + c) % 4
                sums[half, c, :, at * 32 : at * 32 + 32] = done[:, at * 32 : at * 32 + 32]

    far = (1 - chip) * 2 + core

    def sum_copy(source, target, index, device):
        return pltpu.make_async_remote_copy(
            src_ref=source, dst_ref=target, send_sem=sum_send.at[index],
            recv_sem=sum_recv.at[index], device_id=device, device_id_type=MESH,
        )

    far_swap = [
        sum_copy(sums.at[h, (1 - chip) * 2 + 1 - core], got_core.at[h, 0], h, partner) for h in range(2)
    ]
    near_swap = [
        sum_copy(sums.at[h, chip * 2 + 1 - core], got_core.at[h, 1], 2 + h, partner) for h in range(2)
    ]
    over = [sum_copy(sums.at[h, far], got_chip.at[h], 4 + h, at_vert(q * 4 + far)) for h in range(2)]
    rim_swap = [sum_copy(rims.at[h, 1 - core], got_rim.at[h], 6 + h, partner) for h in range(2)]
    edge_home = jnp.where(core == 0, vert - slot - 1, vert - slot + 4)
    edge_there = jnp.where(core == 0, q, 3 - q) > 0

    def edge_copy(h, which):
        return pltpu.make_async_remote_copy(
            src_ref=rims.at[h, core], dst_ref=got_edge.at[which, h], send_sem=sum_send.at[8 + h],
            recv_sem=sum_recv.at[8 + 2 * h + which], device_id=at_vert(edge_home), device_id_type=MESH,
        )

    def backward(h):
        backward_x(h)
        backward_rims(h)
        rim_swap[h].start()
        backward_z(h)
        far_swap[h].start()
        near_swap[h].start()

    def pass_over(h):
        rim_swap[h].wait_recv()
        rims[h, core] = rims[h, core] + got_rim[h]
        pl.when(edge_there)(lambda: edge_copy(h, chip).start())
        far_swap[h].wait_recv()
        sums[h, far] = sums[h, far] + got_core[h, 0]
        over[h].start()

    for step in range(6):
        along_y(step)
    backward(0)
    for step in range(6, 8):
        along_y(step)
    pass_over(0)
    backward(1)
    pass_over(1)

    mine = []
    for h in range(2):
        near_swap[h].wait_recv()
        mine.append(sums[h, slot] + got_core[h, 1])
    for h in range(2):
        over[h].wait_recv()
        mine[h] = mine[h] + got_chip[h]

    @pl.when(is_edge)
    def _():
        for h in range(2):
            edge_copy(h, 0).wait_recv()
            edge_copy(h, 1).wait_recv()

    start = jnp.where(last, RAD, 0)
    lane = iota((64, LANES), 1)
    keep = is_edge & (lane >= start) & (lane < start + RAD)
    for h in range(2):
        edge = got_edge[0, h] + got_edge[1, h]
        for g in range(GROUPS):
            own = pltpu.roll(mine[h], (8 - g - slot) % 4 * 32, 1)
            sides = []
            for k in range(2):
                rim = pltpu.roll(edge, (start + LANES - 64 * k - RAD * g) % LANES, 1)
                part = own[64 * k : 64 * k + 64] + jnp.where(keep, rim, 0.0)
                sides.append(part.reshape(8, 8, LANES) * (1.0 / (RANK * VIEWS)))
            part = jnp.stack(swap_quads(*sides), axis=1).reshape(16, 8, LANES)
            at = (slice(16 * h, 16 * h + 16), slice(g * 8, g * 8 + 8))
            refined[at] = est[at] * part[:, :, 0:BLOCK]

    for tp in range(2):
        for k in range(1, VIEWS):
            part_copy(slot, tp, k - 1, partner, 0).wait_send()

        @pl.when(is_edge)
        def _():
            for k in range(VIEWS):
                part_copy(4, tp, 3 + k, partner, 0).wait_send()

    for copy, there in faces:
        pl.when(there)(copy.wait_send)
    for jy in range(3):
        for jx in range(3):

            @pl.when(exists(jy, jx))
            def _():
                for tp in range(2):
                    core_copy(jy, jx, tp, core).wait_send()

    for copy in far_swap + near_swap + over + rim_swap:
        copy.wait_send()

    @pl.when(edge_there)
    def _():
        for h in range(2):
            edge_copy(h, 0).wait_send()


def local(estimate, view_tiles, slot_view, psf_taps):
    vmem = pl.BlockSpec(memory_space=pltpu.VMEM)
    hbm = pl.BlockSpec(memory_space=pltpu.HBM)
    tile = view_tiles[0, 0, 0]
    psf = jnp.transpose(psf_taps, (1, 2, 0, 3))
    scratch = [
        pltpu.VMEM(estimate.shape, F32),
        pltpu.VMEM(tile.shape, BF16),
        pltpu.VMEM(psf.shape, F32),
        pltpu.VMEM(slot_view.shape, jnp.int32),
        pltpu.VMEM((256, LANES), BF16),
        pltpu.VMEM((6, 2, 64, LANES), BF16),
        pltpu.VMEM((3, 5, 2, 384, LANES), BF16),
        pltpu.VMEM((RANK, 12, 2, 384, LANES), BF16),
        pltpu.VMEM((RANK, 12, 2, 256, LANES), BF16),
        pltpu.VMEM((16, 256, LANES), BF16),
        pltpu.VMEM((24, 256, LANES), BF16),
        pltpu.VMEM((GROUPS, 2, 128, RANK * LANES), BF16),
        pltpu.VMEM((2, 4, 128, LANES), F32),
        pltpu.VMEM((2, 2, 64, LANES), F32),
        pltpu.VMEM((2, 2, 128, LANES), F32),
        pltpu.VMEM((2, 64, LANES), F32),
        pltpu.VMEM((2, 128, LANES), F32),
        pltpu.VMEM((2, 2, 64, LANES), F32),
        pltpu.VMEM((2, 24, LANES), F32),
        pltpu.VMEM((RANK, 128, 256), BF16),
        pltpu.VMEM((RANK, 128, 256), BF16),
        pltpu.VMEM((256, RANK * LANES), BF16),
        pltpu.VMEM((RANK * 128, 256), BF16),
        pltpu.VMEM((2, RANK, 64, 256), BF16),
        pltpu.VMEM((GROUPS, RANK * LANES, 256), BF16),
        pltpu.SemaphoreType.DMA((4,)),
        pltpu.SemaphoreType.DMA((14,)),
        pltpu.SemaphoreType.DMA((12,)),
        pltpu.SemaphoreType.DMA((16,)),
        pltpu.SemaphoreType.DMA((18,)),
        pltpu.SemaphoreType.DMA((18,)),
        pltpu.SemaphoreType.DMA((18,)),
        pltpu.SemaphoreType.DMA((10,)),
        pltpu.SemaphoreType.DMA((12,)),
    ]
    return pl.pallas_call(
        kernel,
        out_shape=pltpu.VMEM(estimate.shape, F32),
        in_specs=[hbm] * 4,
        out_specs=vmem,
        scratch_shapes=scratch,
        compiler_params=pltpu.CompilerParams(
            collective_id=0, has_side_effects=True, vmem_limit_bytes=56 * 1024 * 1024
        ),
    )(*(pltpu.with_memory_space_constraint(a, pltpu.HBM) for a in (estimate, tile, psf, slot_view)))


def solution(mesh):
    placed = (
        P("bx", "by", "vert"),
        P("bx", "by", "vert", None, None, None),
        P("bx", "by", None),
        P(),
    )
    return jax.shard_map(
        local, mesh=mesh, in_specs=placed, out_specs=P("bx", "by", "vert"), check_vma=False
    )
```

```python
import jax
import jax.numpy as jnp
from jax import lax
from jax.experimental import pallas as pl
from jax.experimental.pallas import tpu as pltpu
from jax.sharding import PartitionSpec as P

BACKGROUND = 0.1
MESH = pl.DeviceIdType.MESH
F32, BF16 = jnp.float32, jnp.bfloat16
BLOCK = 32
RAD = 16
TAPS = 33
RANK = 3
VIEWS = 4
GROUPS = 4
LANES = 128


def iota(shape, axis):
    return lax.broadcasted_iota(jnp.int32, shape, axis)


def dot(a, b):
    return jnp.dot(a, b, preferred_element_type=F32)


def band(line, rows, start):
    line = jnp.broadcast_to(line, (rows, LANES))
    return pltpu.roll(line, start % LANES, 1, stride=1, stride_axis=0)


def swap_quads(a, b):
    low, axis = iota(a.shape, a.ndim - 2) < 4, a.ndim - 2
    return jnp.where(low, a, pltpu.roll(b, 4, axis)), jnp.where(low, pltpu.roll(a, 4, axis), b)


def build_taps(psf, slot_view, slot, taps):
    listed = slot_view[...]
    view = jnp.sum(jnp.where(iota(listed.shape, 2) == slot, listed, 0), axis=2, keepdims=True)
    held = iota((VIEWS, TAPS), 0) == view[0]
    mine = jnp.sum(jnp.where(held[None, None], psf[...], 0.0), axis=2)
    mine = (mine / jnp.sum(mine, axis=-1, keepdims=True)).astype(BF16).astype(F32)
    taps[...] = jnp.zeros_like(taps)
    for a in range(3):
        taps[0, 8 * a : 8 * a + RANK, :TAPS] = mine[a]
    flip = (iota((LANES, LANES), 0) + iota((LANES, LANES), 1) == TAPS - 1).astype(BF16)
    taps[1] = dot(taps[0].astype(BF16), flip)


def build_z(taps, wz, wb):
    z_in, z_out = iota((LANES, LANES), 0), iota((LANES, LANES), 1)
    near = jnp.abs(z_in - z_out) <= RAD
    rim, out = iota((32, LANES), 0), iota((32, LANES), 1)
    rim_ok = ((rim < RAD) & (out <= rim)) | ((rim >= RAD) & (out >= rim + 96))
    lane16 = iota((16, LANES), 1)
    for r in range(RANK):
        forward, backward = taps[1, 16 + r : 17 + r, :], taps[0, 16 + r : 17 + r, :]
        columns = slice(r * LANES, (r + 1) * LANES)
        wz[0:128, columns] = jnp.where(near, band(forward, LANES, -RAD), 0.0).astype(BF16)
        wz[128:160, columns] = jnp.where(rim_ok, band(forward, 32, 96), 0.0).astype(BF16)
        wz[160:256, columns] = jnp.zeros((96, LANES), BF16)
        main = jnp.where(near, band(backward, LANES, -RAD), 0.0)
        low = jnp.where(lane16 < RAD, band(backward, 16, 0), 0.0)
        high = jnp.where(lane16 < RAD, band(backward, 16, 96), 0.0)
        for g in range(GROUPS):
            wb[g, r * 128 : r * 128 + 128, 0:128] = (
                pltpu.roll(main, 32 * g, 1) if g else main
            ).astype(BF16)
            wb[g, r * 128 : r * 128 + 128, 128:256] = jnp.zeros((128, LANES), BF16)
            lo, hi = pltpu.roll(low, RAD * g, 1) if g else low, pltpu.roll(high, 64 + RAD * g, 1)
            wb[g, r * 128 : r * 128 + 16, 128:256] = lo.astype(BF16)
            wb[g, r * 128 + 112 : r * 128 + 128, 128:256] = hi.astype(BF16)


def build_x(taps, bx, tx, txb):
    spread = (iota((LANES, 256), 1) == 4 * iota((LANES, 256), 0)).astype(BF16)
    lane, row = iota((LANES, LANES), 1), iota((LANES, LANES), 0)
    low, high = bx > 0, bx < 3

    def tiles(line):
        turned = [band(line[:, i * LANES : (i + 1) * LANES], LANES, 0) for i in range(2)]
        return jnp.where(lane >= row, turned[0], 0.0), jnp.where(lane >= row, turned[1], turned[0])

    wide = [dot(taps[k, 0:8, :].astype(BF16), spread) for k in range(2)]
    for r in range(RANK):
        left, right = tiles(wide[0][r : r + 1])
        tx[r, :, 0:128] = left.astype(BF16)
        tx[r, :, 128:256] = right.astype(BF16)
        left, right = [m[0:64] for m in tiles(wide[1][r : r + 1])]
        txb[0, r, :, 0:128] = jnp.where((lane[0:64] >= 64) | low, left, 0.0).astype(BF16)
        txb[0, r, :, 128:256] = right.astype(BF16)
        txb[1, r, :, 0:128] = left.astype(BF16)
        txb[1, r, :, 128:256] = jnp.where(high, right, 0.0).astype(BF16)


def build_y(taps, by, ty, tyb):
    place = by * BLOCK - RAD + iota((BLOCK, LANES), 1)
    inside = (place >= 0) & (place < 4 * BLOCK)
    plain = [band(taps[0, 8 + r : 9 + r, :], BLOCK, 0) for r in range(RANK)]
    plain += [
        jnp.where(inside, band(taps[1, 8 + r : 9 + r, :], BLOCK, 0), 0.0) for r in range(RANK)
    ]
    plain = jnp.concatenate(plain, axis=0).astype(BF16)
    y, column = iota((LANES, 256), 0), iota((LANES, 256), 1)
    wide = [
        dot(plain, (column == 16 * (y // 4) + 4 * x + y % 4).astype(BF16)).astype(BF16)
        for x in range(4)
    ]
    row, source = iota((LANES, LANES), 0), iota((LANES, LANES), 1)
    order = (row == 16 * (source % 32 // 4) + 4 * (source // 32) + source % 4).astype(BF16)
    for i in range(2 * RANK):
        done = dot(order, jnp.concatenate([m[i * 32 : i * 32 + 32] for m in wide], axis=0)).astype(BF16)
        if i < RANK:
            ty[i] = done
        else:
            tyb[(i - RANK) * 128 : (i - RANK + 1) * 128, :] = done


def kernel(
    est_hbm, tile_hbm, psf_hbm, slot_view_hbm, refined,
    est, tile, psf, slot_view,
    packed, parts, outer, field, after_z, after_x, seen, back_y, back_x, sums, rims,
    got_core, got_rim, got_chip, got_edge,
    taps, tx, ty, wz, tyb, txb, wb,
    load_sem, part_send, part_recv, face_send, face_recv, core_send, core_recv, sum_send, sum_recv,
    rim_face_send, rim_face_recv, rim_core_send, rim_core_recv,
):
    bx, by, vert = lax.axis_index("bx"), lax.axis_index("by"), lax.axis_index("vert")
    q, slot = vert // VIEWS, vert % VIEWS
    core, chip = slot % 2, slot // 2

    loads = [
        pltpu.make_async_copy(source, target, load_sem.at[i])
        for i, (source, target) in enumerate(
            ((est_hbm, est), (psf_hbm, psf), (slot_view_hbm, slot_view), (tile_hbm, tile))
        )
    ]
    for copy in loads:
        copy.start()

    def at_vert(index):
        return {"vert": index}

    partner = at_vert(q * 4 + chip * 2 + 1 - core)
    x_up, x_down = ({"bx": bx + 1}, bx < 3), ({"bx": bx - 1}, bx > 0)
    y_up, y_down = ({"by": by + 1}, by < 3), ({"by": by - 1}, by > 0)
    above, below = q < 3, q > 0
    first, last = slot == 0, slot == VIEWS - 1
    is_edge = (first & below) | (last & above)

    def exists(jy, jx):
        here = jy == jy
        for index, j in ((by, jy), (bx, jx)):
            if j != 1:
                here = (index > 0 if j == 0 else index < 3) & here
        return here

    got_edge[...] = jnp.zeros_like(got_edge)
    barrier = pltpu.get_barrier_semaphore()

    def greet(device):
        pl.semaphore_signal(barrier, inc=1, device_id=device, device_id_type=MESH)

    for k in range(1, VIEWS):
        greet(at_vert(q * 4 + (slot + k) % VIEWS))
    for device, there in (x_up, x_down, y_up, y_down):
        pl.when(there)(lambda device=device: greet(device))

    @pl.when(below)
    def _():
        greet(at_vert(vert - slot - 1))
        pl.when(first)(lambda: greet(at_vert(vert - 3)))

    @pl.when(above)
    def _():
        greet(at_vert(vert - slot + 4))
        pl.when(last)(lambda: greet(at_vert(vert + 3)))

    loads[0].wait()
    groups = est[...].reshape(BLOCK, GROUPS, 8, BLOCK)
    line = jnp.concatenate([groups[:, g].reshape(256, BLOCK) for g in range(GROUPS)], axis=1)
    line = pltpu.roll(line, slot * 32, 1).reshape(16, 2, 8, LANES)
    for side, quads in enumerate(swap_quads(line[:, 0], line[:, 1])):
        packed[side * 128 : side * 128 + 128, :] = quads.reshape(128, LANES).astype(BF16)

    beside = [(there, 1) for _, there in (x_up, x_down, y_up, y_down)] + [(is_edge, 4)]
    beside += [((slot == 1) & above, 1), ((slot == 2) & below, 1)]
    pl.semaphore_wait(barrier, 3 + sum(jnp.where(there, n, 0) for there, n in beside))

    def part_copy(source, tp, send, device, side):
        return pltpu.make_async_remote_copy(
            src_ref=packed.at[pl.ds(side * 128 + tp * 64, 64), :], dst_ref=parts.at[source, tp],
            send_sem=part_send.at[send * 2 + tp], recv_sem=part_recv.at[source * 2 + tp],
            device_id=device, device_id_type=MESH,
        )

    for tp in range(2):
        for k in range(1, VIEWS):
            other = (slot + k) % VIEWS
            part_copy(slot, tp, k - 1, at_vert(q * 4 + other), other % 2).start()

    def outer_copy(which, send, device, side):
        return pltpu.make_async_remote_copy(
            src_ref=packed.at[pl.ds(side * 128, 128), :], dst_ref=outer.at[which],
            send_sem=part_send.at[6 + send], recv_sem=part_recv.at[8 + which],
            device_id=device, device_id_type=MESH,
        )

    @pl.when(last & above)
    def _():
        for k in range(VIEWS):
            outer_copy(0, k, at_vert(vert + 1 + k), k % 2).start()

    @pl.when(first & below)
    def _():
        for k in range(VIEWS):
            outer_copy(1, k, at_vert(vert - 4 + k), k % 2).start()

    parts[slot] = packed[pl.ds(core * 128, 128), :].reshape(2, 64, LANES)

    def clear(ref):
        ref[...] = jnp.zeros(ref.shape, BF16)

    pl.when(~below)(lambda: clear(outer.at[0]))
    pl.when(~above)(lambda: clear(outer.at[1]))
    pl.when(bx == 0)(lambda: clear(field.at[:, :, :, 0:128, :]))
    pl.when(bx == 3)(lambda: clear(field.at[:, :, :, 256:384, :]))
    pl.when(by == 0)(lambda: clear(field.at[0]))
    pl.when(by == 3)(lambda: clear(field.at[2]))
    loads[1].wait()
    loads[2].wait()
    build_taps(psf, slot_view, slot, taps)
    build_z(taps, wz, wb)

    def assemble(tp):
        for k in range(1, VIEWS):
            part_copy((slot + k) % VIEWS, tp, 0, partner, 0).wait_recv()
        lane = iota((64, LANES), 1)
        rows = slice(128 + tp * 64, 192 + tp * 64)
        have = [parts[k, tp].astype(F32) for k in range(VIEWS)]
        for g in range(GROUPS):
            line = have[(3 - g) % 4]
            for at in range(3):
                line = jnp.where(lane // 32 == at, have[(at - g) % 4], line)
            if g:
                line = pltpu.roll(line, LANES - 32 * g, 1)
            field[1, g, core, rows, :] = line.astype(BF16)

    def assemble_rims():
        for k, there in enumerate((below, above)):
            pl.when(there)(lambda k=k: outer_copy(k, 0, partner, 0).wait_recv())
        is_above = iota((128, LANES), 1) % 32 < RAD
        line = jnp.where(is_above, outer[1].astype(F32), outer[0].astype(F32))
        field[1, 4, core, 128:256, :] = pltpu.roll(line, RAD, 1).astype(BF16)

    def piece(jy, jx, tp, side):
        return field.at[jy, 0:4, side, pl.ds(jx * 128 + tp * 64, 64), :]

    def number(jy, jx, tp):
        return (jy * 3 + jx) * 2 + tp

    def face_copy(source, target, tp, send, device):
        return pltpu.make_async_remote_copy(
            src_ref=piece(*source, tp, core), dst_ref=piece(*target, tp, core),
            send_sem=face_send.at[send], recv_sem=face_recv.at[number(*target, tp)],
            device_id=device, device_id_type=MESH,
        )

    def core_copy(jy, jx, tp, side):
        return pltpu.make_async_remote_copy(
            src_ref=piece(jy, jx, tp, side), dst_ref=piece(jy, jx, tp, side),
            send_sem=core_send.at[number(jy, jx, tp)], recv_sem=core_recv.at[number(jy, jx, tp)],
            device_id=partner, device_id_type=MESH,
        )

    faces = []

    def send_face(source, target, tp, way):
        device, there = way
        copy = face_copy(source, target, tp, len(faces), device)
        there = there & exists(*source)
        pl.when(there)(copy.start)
        faces.append((copy, there))

    def arrived(jy, jx, tp):
        @pl.when(exists(jy, jx))
        def _():
            face_copy((jy, jx), (jy, jx), tp, 0, partner).wait_recv()
            core_copy(jy, jx, tp, core).start()

    def rim_piece(jy, jx, side):
        return field.at[jy, 4, side, pl.ds(jx * 128, 128), :]

    def rim_face_copy(source, target, send, device):
        return pltpu.make_async_remote_copy(
            src_ref=rim_piece(*source, core), dst_ref=rim_piece(*target, core),
            send_sem=rim_face_send.at[send], recv_sem=rim_face_recv.at[target[0] * 3 + target[1]],
            device_id=device, device_id_type=MESH,
        )

    def rim_core_copy(jy, jx, side):
        return pltpu.make_async_remote_copy(
            src_ref=rim_piece(jy, jx, side), dst_ref=rim_piece(jy, jx, side),
            send_sem=rim_core_send.at[jy * 3 + jx], recv_sem=rim_core_recv.at[jy * 3 + jx],
            device_id=partner, device_id_type=MESH,
        )

    rim_faces = []

    def send_rim(source, target, way, wanted):
        device, there = way
        copy = rim_face_copy(source, target, len(rim_faces), device)
        there = there & exists(*source) & wanted
        pl.when(there)(copy.start)
        rim_faces.append((copy, there))

    def rim_arrived(jy, jx, wanted):
        @pl.when(exists(jy, jx) & wanted)
        def _():
            rim_face_copy((jy, jx), (jy, jx), 0, partner).wait_recv()
            rim_core_copy(jy, jx, core).start()

    def swapped(jy, jx):
        @pl.when(exists(jy, jx))
        def _():
            for tp in range(2):
                core_copy(jy, jx, tp, 1 - core).wait_recv()
            rim_core_copy(jy, jx, 1 - core).wait_recv()

    def forward_z(jy, jx):
        rows = slice(jx * 128, jx * 128 + 128)
        rim = field[jy, 4, :, rows, :].reshape(256, LANES)
        for g in range(GROUPS):
            turned = pltpu.roll(rim, LANES - 32 * g, 1) if g else rim
            main = field[jy, g, :, rows, :].reshape(256, LANES)
            done = dot(jnp.concatenate([main, turned], axis=1), wz[...]).astype(BF16)
            for r in range(RANK):
                after_z[r, jy * GROUPS + g, :, rows, :] = done[:, r * 128 : (r + 1) * 128].reshape(
                    2, 128, LANES
                )

    def forward_x(jy):
        def body(step, carry):
            r, group = step // GROUPS, jy * GROUPS + step % GROUPS
            for b in range(2):
                rows = pl.ds(b * 128, 256)
                both = jnp.concatenate([after_z[r, group, k, rows, :] for k in range(2)], axis=1)
                done = dot(tx[r], both).astype(BF16)
                for k in range(2):
                    after_x[r, group, k, b * 128 : b * 128 + 128, :] = done[:, k * 128 : k * 128 + 128]
            return carry

        lax.fori_loop(0, GROUPS * RANK, body, 0, unroll=True)

    def send_faces(tp, ways):
        for target, way in ways:
            send_face((1, 1), target, tp, way)

    along_x_links = (((1, 0), x_up), ((1, 2), x_down))
    along_y_links = (((0, 1), y_up), ((2, 1), y_down))
    assemble(0)
    send_faces(0, along_x_links)
    core_copy(1, 1, 0, core).start()
    assemble(1)
    send_faces(1, along_y_links)
    send_faces(1, along_x_links)
    send_faces(0, along_y_links)
    core_copy(1, 1, 1, core).start()
    build_x(taps, bx, tx, txb)
    assemble_rims()
    always, own_first = slot == slot, core == 0
    for target, way in along_x_links + along_y_links:
        send_rim((1, 1), target, way, always)
    rim_core_copy(1, 1, core).start()
    for side in (0, 2):
        arrived(1, side, 0)
    for one, other in ((0, 2), (2, 0)):
        send_face((1, one), (0, one), 0, y_up)
        send_face((1, other), (2, other), 0, y_down)
    for side in (0, 2):
        arrived(side, 1, 1)
    for one, other in ((0, 2), (2, 0)):
        send_face((one, 1), (one, 0), 1, x_up)
        send_face((other, 1), (other, 2), 1, x_down)
    for side in (0, 2):
        rim_arrived(1, side, own_first)
        rim_arrived(side, 1, ~own_first)
    for side in (0, 2):
        send_rim((1, side), (0, side), y_up, own_first)
        send_rim((1, side), (2, side), y_down, own_first)
        send_rim((side, 1), (side, 0), x_up, ~own_first)
        send_rim((side, 1), (side, 2), x_down, ~own_first)
    build_y(taps, by, ty, tyb)
    loads[3].wait()

    def order_tile(i, carry):
        quad = tile[pl.ds(4 * i, 4)].astype(F32).reshape(2, 2, 8, 8, LANES)
        sides = swap_quads(quad[:, 0], quad[:, 1])
        rows = jnp.stack([m[x] for m in sides for x in range(2)], axis=1)
        seen[i] = rows.reshape(256, LANES).astype(BF16)
        return carry

    lax.fori_loop(0, 16, order_tile, 0, unroll=4)
    swapped(1, 1)
    forward_z(1, 1)
    for side in (0, 2):
        arrived(1, side, 1)
        arrived(side, 1, 0)
        rim_arrived(1, side, ~own_first)
        rim_arrived(side, 1, own_first)
    for side in (0, 2):
        swapped(1, side)
        swapped(side, 1)
    for side in (0, 2):
        forward_z(1, side)
        forward_z(side, 1)
    waves = (((0, 0), (2, 2)), ((0, 2), (2, 0)))
    for corner in waves[0]:
        for tp in range(2):
            arrived(*corner, tp)
        rim_arrived(*corner, always)
    forward_x(1)
    for corner in waves[1]:
        for tp in range(2):
            arrived(*corner, tp)
        rim_arrived(*corner, always)
    for wave in waves:
        for corner in wave:
            swapped(*corner)
        for corner in wave:
            forward_z(*corner)
    for jy in (0, 2):
        forward_x(jy)

    def along_y(step):
        quotient = []
        for b in range(2):
            blurred = None
            for r in range(RANK):
                both = [
                    after_x[r, 4 * b : 4 * b + 8, :, pl.ds(32 * step + 16 * k, 16), :].reshape(256, LANES)
                    for k in range(2)
                ]
                part = dot(ty[r], jnp.concatenate(both, axis=1))
                blurred = part if blurred is None else blurred + part
            rows = slice(128 * b, 128 * b + 128)
            both = jnp.concatenate([seen[2 * step + k, rows, :] for k in range(2)], axis=1).astype(F32)
            quotient.append((RANK * both / (blurred + RANK * BACKGROUND)).astype(BF16))
        quotient = jnp.concatenate(quotient, axis=0)
        for r in range(RANK):
            done = dot(tyb[r * 128 : r * 128 + 128, :], quotient).astype(BF16)
            for k in range(2):
                back_y[r * 8 : r * 8 + 8, pl.ds(32 * step + 16 * k, 16), :] = done[
                    :, k * 128 : k * 128 + 128
                ].reshape(8, 16, LANES)

    def backward_x(half):
        within = slice(half * 64, half * 64 + 192)
        for g in range(GROUPS):
            for r in range(RANK):
                at = (r * GROUPS + g) * 2
                both = jnp.concatenate([back_y[at, within, :], back_y[at + 1, within, :]], axis=1)
                done = dot(txb[half, r, :, 0:192], both).astype(BF16)
                for k in range(2):
                    back_x[g, half, k * 64 : k * 64 + 64, r * 128 : (r + 1) * 128] = done[
                        :, k * 128 : k * 128 + 128
                    ]

    def backward_rims(half):
        both = dot(back_x[0, half], wb[0, :, LANES:])
        for g in range(1, GROUPS):
            both = both + dot(back_x[g, half], wb[g, :, LANES:])
        is_low = iota((64, LANES), 1) < 64
        rims[half, 0] = jnp.where(is_low, both[0:64], pltpu.roll(both[64:128], 64, 1))
        rims[half, 1] = jnp.where(is_low, pltpu.roll(both[0:64], 64, 1), both[64:128])

    def backward_z(half):
        for g in range(GROUPS):
            done = dot(back_x[g, half], wb[g, :, :LANES])
            for c in range(4):
                at = (g + c) % 4
                sums[half, c, :, at * 32 : at * 32 + 32] = done[:, at * 32 : at * 32 + 32]

    far = (1 - chip) * 2 + core

    def sum_copy(source, target, index, device):
        return pltpu.make_async_remote_copy(
            src_ref=source, dst_ref=target, send_sem=sum_send.at[index],
            recv_sem=sum_recv.at[index], device_id=device, device_id_type=MESH,
        )

    far_swap = [
        sum_copy(sums.at[h, (1 - chip) * 2 + 1 - core], got_core.at[h, 0], h, partner) for h in range(2)
    ]
    near_swap = [
        sum_copy(sums.at[h, chip * 2 + 1 - core], got_core.at[h, 1], 2 + h, partner) for h in range(2)
    ]
    over = [sum_copy(sums.at[h, far], got_chip.at[h], 4 + h, at_vert(q * 4 + far)) for h in range(2)]
    rim_swap = [sum_copy(rims.at[h, 1 - core], got_rim.at[h], 6 + h, partner) for h in range(2)]
    edge_home = jnp.where(core == 0, vert - slot - 1, vert - slot + 4)
    edge_there = jnp.where(core == 0, q, 3 - q) > 0

    def edge_copy(h, which):
        return pltpu.make_async_remote_copy(
            src_ref=rims.at[h, core], dst_ref=got_edge.at[which, h], send_sem=sum_send.at[8 + h],
            recv_sem=sum_recv.at[8 + 2 * h + which], device_id=at_vert(edge_home), device_id_type=MESH,
        )

    def backward(h):
        backward_x(h)
        backward_rims(h)
        rim_swap[h].start()
        backward_z(h)
        far_swap[h].start()
        near_swap[h].start()

    def pass_over(h):
        rim_swap[h].wait_recv()
        rims[h, core] = rims[h, core] + got_rim[h]
        pl.when(edge_there)(lambda: edge_copy(h, chip).start())
        far_swap[h].wait_recv()
        sums[h, far] = sums[h, far] + got_core[h, 0]
        over[h].start()

    for step in range(6):
        along_y(step)
    backward(0)
    for step in range(6, 8):
        along_y(step)
    pass_over(0)
    backward(1)
    pass_over(1)

    for tp in range(2):
        for k in range(1, VIEWS):
            part_copy(slot, tp, k - 1, partner, 0).wait_send()

    @pl.when(is_edge)
    def _():
        for k in range(VIEWS):
            outer_copy(0, k, partner, 0).wait_send()

    for copy, there in faces + rim_faces:
        pl.when(there)(copy.wait_send)
    for jy in range(3):
        for jx in range(3):

            @pl.when(exists(jy, jx))
            def _():
                for tp in range(2):
                    core_copy(jy, jx, tp, core).wait_send()
                rim_core_copy(jy, jx, core).wait_send()

    start = jnp.where(last, RAD, 0)
    lane = iota((64, LANES), 1)
    keep = is_edge & (lane >= start) & (lane < start + RAD)
    for h in range(2):
        near_swap[h].wait_recv()
        mine = sums[h, slot] + got_core[h, 1]
        over[h].wait_recv()
        mine = mine + got_chip[h]

        @pl.when(is_edge)
        def _():
            edge_copy(h, 0).wait_recv()
            edge_copy(h, 1).wait_recv()

        edge = got_edge[0, h] + got_edge[1, h]
        for g in range(GROUPS):
            own = pltpu.roll(mine, (8 - g - slot) % 4 * 32, 1)
            sides = []
            for k in range(2):
                rim = pltpu.roll(edge, (start + LANES - 64 * k - RAD * g) % LANES, 1)
                part = own[64 * k : 64 * k + 64] + jnp.where(keep, rim, 0.0)
                sides.append(part.reshape(8, 8, LANES) * (1.0 / (RANK * VIEWS)))
            part = jnp.stack(swap_quads(*sides), axis=1).reshape(16, 8, LANES)
            at = (slice(16 * h, 16 * h + 16), slice(g * 8, g * 8 + 8))
            refined[at] = est[at] * part[:, :, 0:BLOCK]

    for copy in far_swap + near_swap + over + rim_swap:
        copy.wait_send()

    @pl.when(edge_there)
    def _():
        for h in range(2):
            edge_copy(h, 0).wait_send()


def local(estimate, view_tiles, slot_view, psf_taps):
    vmem = pl.BlockSpec(memory_space=pltpu.VMEM)
    hbm = pl.BlockSpec(memory_space=pltpu.HBM)
    tile = view_tiles[0, 0, 0]
    psf = jnp.transpose(psf_taps, (1, 2, 0, 3))
    scratch = [
        pltpu.VMEM(estimate.shape, F32),
        pltpu.VMEM(tile.shape, BF16),
        pltpu.VMEM(psf.shape, F32),
        pltpu.VMEM(slot_view.shape, jnp.int32),
        pltpu.VMEM((256, LANES), BF16),
        pltpu.VMEM((VIEWS, 2, 64, LANES), BF16),
        pltpu.VMEM((2, 128, LANES), BF16),
        pltpu.VMEM((3, 5, 2, 384, LANES), BF16),
        pltpu.VMEM((RANK, 12, 2, 384, LANES), BF16),
        pltpu.VMEM((RANK, 12, 2, 256, LANES), BF16),
        pltpu.VMEM((16, 256, LANES), BF16),
        pltpu.VMEM((24, 256, LANES), BF16),
        pltpu.VMEM((GROUPS, 2, 128, RANK * LANES), BF16),
        pltpu.VMEM((2, 4, 128, LANES), F32),
        pltpu.VMEM((2, 2, 64, LANES), F32),
        pltpu.VMEM((2, 2, 128, LANES), F32),
        pltpu.VMEM((2, 64, LANES), F32),
        pltpu.VMEM((2, 128, LANES), F32),
        pltpu.VMEM((2, 2, 64, LANES), F32),
        pltpu.VMEM((2, 24, LANES), F32),
        pltpu.VMEM((RANK, 128, 256), BF16),
        pltpu.VMEM((RANK, 128, 256), BF16),
        pltpu.VMEM((256, RANK * LANES), BF16),
        pltpu.VMEM((RANK * 128, 256), BF16),
        pltpu.VMEM((2, RANK, 64, 256), BF16),
        pltpu.VMEM((GROUPS, RANK * LANES, 256), BF16),
        pltpu.SemaphoreType.DMA((4,)),
        pltpu.SemaphoreType.DMA((10,)),
        pltpu.SemaphoreType.DMA((10,)),
        pltpu.SemaphoreType.DMA((16,)),
        pltpu.SemaphoreType.DMA((18,)),
        pltpu.SemaphoreType.DMA((18,)),
        pltpu.SemaphoreType.DMA((18,)),
        pltpu.SemaphoreType.DMA((10,)),
        pltpu.SemaphoreType.DMA((12,)),
        pltpu.SemaphoreType.DMA((12,)),
        pltpu.SemaphoreType.DMA((9,)),
        pltpu.SemaphoreType.DMA((9,)),
        pltpu.SemaphoreType.DMA((9,)),
    ]
    return pl.pallas_call(
        kernel,
        out_shape=pltpu.VMEM(estimate.shape, F32),
        in_specs=[hbm] * 4,
        out_specs=vmem,
        scratch_shapes=scratch,
        compiler_params=pltpu.CompilerParams(
            collective_id=0, has_side_effects=True, vmem_limit_bytes=56 * 1024 * 1024
        ),
    )(*(pltpu.with_memory_space_constraint(a, pltpu.HBM) for a in (estimate, tile, psf, slot_view)))


def solution(mesh):
    placed = (
        P("bx", "by", "vert"),
        P("bx", "by", "vert", None, None, None),
        P("bx", "by", None),
        P(),
    )
    return jax.shard_map(
        local, mesh=mesh, in_specs=placed, out_specs=P("bx", "by", "vert"), check_vma=False
    )
```

```python
import jax
import jax.numpy as jnp
from jax import lax
from jax.experimental import pallas as pl
from jax.experimental.pallas import tpu as pltpu
from jax.sharding import PartitionSpec as P

BACKGROUND = 0.1
MESH = pl.DeviceIdType.MESH
F32, BF16 = jnp.float32, jnp.bfloat16
BLOCK = 32
RAD = 16
TAPS = 33
RANK = 3
VIEWS = 4
GROUPS = 4
LANES = 128


def iota(shape, axis):
    return lax.broadcasted_iota(jnp.int32, shape, axis)


def dot(a, b):
    return jnp.dot(a, b, preferred_element_type=F32)


def band(line, rows, start):
    line = jnp.broadcast_to(line, (rows, LANES))
    return pltpu.roll(line, start % LANES, 1, stride=1, stride_axis=0)


def swap_quads(a, b):
    low, axis = iota(a.shape, a.ndim - 2) < 4, a.ndim - 2
    return jnp.where(low, a, pltpu.roll(b, 4, axis)), jnp.where(low, pltpu.roll(a, 4, axis), b)


def build_taps(psf, slot_view, slot, taps):
    listed = slot_view[...]
    view = jnp.sum(jnp.where(iota(listed.shape, 2) == slot, listed, 0), axis=2, keepdims=True)
    held = iota((VIEWS, TAPS), 0) == view[0]
    mine = jnp.sum(jnp.where(held[None, None], psf[...], 0.0), axis=2)
    mine = (mine / jnp.sum(mine, axis=-1, keepdims=True)).astype(BF16).astype(F32)
    taps[...] = jnp.zeros_like(taps)
    for a in range(3):
        taps[0, 8 * a : 8 * a + RANK, :TAPS] = mine[a]
    flip = (iota((LANES, LANES), 0) + iota((LANES, LANES), 1) == TAPS - 1).astype(BF16)
    taps[1] = dot(taps[0].astype(BF16), flip)


def build_z(taps, wz, wb):
    z_in, z_out = iota((LANES, LANES), 0), iota((LANES, LANES), 1)
    near = jnp.abs(z_in - z_out) <= RAD
    rim, out = iota((32, LANES), 0), iota((32, LANES), 1)
    rim_ok = ((rim < RAD) & (out <= rim)) | ((rim >= RAD) & (out >= rim + 96))
    lane16 = iota((16, LANES), 1)
    for r in range(RANK):
        forward, backward = taps[1, 16 + r : 17 + r, :], taps[0, 16 + r : 17 + r, :]
        columns = slice(r * LANES, (r + 1) * LANES)
        wz[0:128, columns] = jnp.where(near, band(forward, LANES, -RAD), 0.0).astype(BF16)
        wz[128:160, columns] = jnp.where(rim_ok, band(forward, 32, 96), 0.0).astype(BF16)
        wz[160:256, columns] = jnp.zeros((96, LANES), BF16)
        main = jnp.where(near, band(backward, LANES, -RAD), 0.0)
        low = jnp.where(lane16 < RAD, band(backward, 16, 0), 0.0)
        high = jnp.where(lane16 < RAD, band(backward, 16, 96), 0.0)
        for g in range(GROUPS):
            wb[g, r * 128 : r * 128 + 128, 0:128] = (
                pltpu.roll(main, 32 * g, 1) if g else main
            ).astype(BF16)
            wb[g, r * 128 : r * 128 + 128, 128:256] = jnp.zeros((128, LANES), BF16)
            lo, hi = pltpu.roll(low, RAD * g, 1) if g else low, pltpu.roll(high, 64 + RAD * g, 1)
            wb[g, r * 128 : r * 128 + 16, 128:256] = lo.astype(BF16)
            wb[g, r * 128 + 112 : r * 128 + 128, 128:256] = hi.astype(BF16)


def build_x(taps, bx, tx, txb):
    spread = (iota((LANES, 256), 1) == 4 * iota((LANES, 256), 0)).astype(BF16)
    lane, row = iota((LANES, LANES), 1), iota((LANES, LANES), 0)
    low, high = bx > 0, bx < 3

    def tiles(line):
        turned = [band(line[:, i * LANES : (i + 1) * LANES], LANES, 0) for i in range(2)]
        return jnp.where(lane >= row, turned[0], 0.0), jnp.where(lane >= row, turned[1], turned[0])

    wide = [dot(taps[k, 0:8, :].astype(BF16), spread) for k in range(2)]
    for r in range(RANK):
        left, right = tiles(wide[0][r : r + 1])
        tx[r, :, 0:128] = left.astype(BF16)
        tx[r, :, 128:256] = right.astype(BF16)
        left, right = [m[0:64] for m in tiles(wide[1][r : r + 1])]
        txb[0, r, :, 0:128] = jnp.where((lane[0:64] >= 64) | low, left, 0.0).astype(BF16)
        txb[0, r, :, 128:256] = right.astype(BF16)
        txb[1, r, :, 0:128] = left.astype(BF16)
        txb[1, r, :, 128:256] = jnp.where(high, right, 0.0).astype(BF16)


def build_y(taps, by, ty, tyb):
    place = by * BLOCK - RAD + iota((BLOCK, LANES), 1)
    inside = (place >= 0) & (place < 4 * BLOCK)
    plain = [band(taps[0, 8 + r : 9 + r, :], BLOCK, 0) for r in range(RANK)]
    plain += [
        jnp.where(inside, band(taps[1, 8 + r : 9 + r, :], BLOCK, 0), 0.0) for r in range(RANK)
    ]
    plain = jnp.concatenate(plain, axis=0).astype(BF16)
    y, column = iota((LANES, 256), 0), iota((LANES, 256), 1)
    wide = [
        dot(plain, (column == 16 * (y // 4) + 4 * x + y % 4).astype(BF16)).astype(BF16)
        for x in range(4)
    ]
    row, source = iota((LANES, LANES), 0), iota((LANES, LANES), 1)
    order = (row == 16 * (source % 32 // 4) + 4 * (source // 32) + source % 4).astype(BF16)
    for i in range(2 * RANK):
        done = dot(order, jnp.concatenate([m[i * 32 : i * 32 + 32] for m in wide], axis=0)).astype(BF16)
        if i < RANK:
            ty[i] = done
        else:
            tyb[(i - RANK) * 128 : (i - RANK + 1) * 128, :] = done


def kernel(
    est_hbm, tile_hbm, psf_hbm, slot_view_hbm, refined,
    est, tile, psf, slot_view,
    packed, parts, outer, field, after_z, after_x, seen, back_y, back_x, sums, rims,
    got_core, got_rim, got_chip, got_edge,
    taps, tx, ty, wz, tyb, txb, wb,
    load_sem, part_send, part_recv, face_send, face_recv, core_send, core_recv, sum_send, sum_recv,
):
    bx, by, vert = lax.axis_index("bx"), lax.axis_index("by"), lax.axis_index("vert")
    q, slot = vert // VIEWS, vert % VIEWS
    core, chip = slot % 2, slot // 2

    loads = [
        pltpu.make_async_copy(source, target, load_sem.at[i])
        for i, (source, target) in enumerate(
            ((est_hbm, est), (psf_hbm, psf), (slot_view_hbm, slot_view), (tile_hbm, tile))
        )
    ]
    for copy in loads:
        copy.start()

    def at_vert(index):
        return {"vert": index}

    partner = at_vert(q * 4 + chip * 2 + 1 - core)
    above, below = q < 3, q > 0
    first, last = slot == 0, slot == VIEWS - 1
    is_edge = (first & below) | (last & above)

    straight = core == 0

    def block(ju, jv):
        return jnp.where(straight, jv, ju), jnp.where(straight, ju, jv)

    def link(along_u, step):
        x_step = jnp.where(straight == along_u, step, 0)
        x, y = bx + x_step, by + step - x_step
        return {"bx": x, "by": y}, (x >= 0) & (x < 4) & (y >= 0) & (y < 4)

    u_up, u_down, v_up, v_down = link(True, 1), link(True, -1), link(False, 1), link(False, -1)

    def clear(ref):
        ref[...] = jnp.zeros(ref.shape, BF16)

    pl.when(bx == 0)(lambda: clear(field.at[:, 0, core]))
    pl.when(bx == 3)(lambda: clear(field.at[:, 2, core]))
    pl.when(by == 0)(lambda: clear(field.at[0, :, core]))
    pl.when(by == 3)(lambda: clear(field.at[2, :, core]))
    pl.when(~below)(lambda: clear(outer.at[0]))
    pl.when(~above)(lambda: clear(outer.at[1]))

    got_edge[...] = jnp.zeros_like(got_edge)
    barrier = pltpu.get_barrier_semaphore()

    def greet(device):
        pl.semaphore_signal(barrier, inc=1, device_id=device, device_id_type=MESH)

    for k in range(1, VIEWS):
        greet(at_vert(q * 4 + (slot + k) % VIEWS))
    for device, there in (u_up, u_down, v_up, v_down):
        pl.when(there)(lambda device=device: greet(device))

    @pl.when(below)
    def _():
        greet(at_vert(vert - slot - 1))
        pl.when(first)(lambda: greet(at_vert(vert - 3)))

    @pl.when(above)
    def _():
        greet(at_vert(vert - slot + 4))
        pl.when(last)(lambda: greet(at_vert(vert + 3)))

    loads[0].wait()
    groups = est[...].reshape(BLOCK, GROUPS, 8, BLOCK)
    line = jnp.concatenate([groups[:, g].reshape(256, BLOCK) for g in range(GROUPS)], axis=1)
    line = pltpu.roll(line, slot * 32, 1).reshape(16, 2, 8, LANES)
    for side, quads in enumerate(swap_quads(line[:, 0], line[:, 1])):
        packed[side * 128 : side * 128 + 128, :] = quads.reshape(128, LANES).astype(BF16)

    beside = [(there, 1) for _, there in (u_up, u_down, v_up, v_down)] + [(is_edge, 4)]
    beside += [((slot == 1) & above, 1), ((slot == 2) & below, 1)]
    pl.semaphore_wait(barrier, 3 + sum(jnp.where(there, n, 0) for there, n in beside))

    def part_copy(source, send, device, side):
        return pltpu.make_async_remote_copy(
            src_ref=packed.at[pl.ds(side * 128, 128), :], dst_ref=parts.at[source],
            send_sem=part_send.at[send], recv_sem=part_recv.at[source],
            device_id=device, device_id_type=MESH,
        )

    for k in range(1, VIEWS):
        other = (slot + k) % VIEWS
        part_copy(slot, k - 1, at_vert(q * 4 + other), other % 2).start()

    def outer_copy(which, send, device, side):
        return pltpu.make_async_remote_copy(
            src_ref=packed.at[pl.ds(side * 128, 128), :], dst_ref=outer.at[which],
            send_sem=part_send.at[3 + send], recv_sem=part_recv.at[4 + which],
            device_id=device, device_id_type=MESH,
        )

    @pl.when(last & above)
    def _():
        for k in range(VIEWS):
            outer_copy(0, k, at_vert(vert + 1 + k), k % 2).start()

    @pl.when(first & below)
    def _():
        for k in range(VIEWS):
            outer_copy(1, k, at_vert(vert - 4 + k), k % 2).start()

    parts[slot] = packed[pl.ds(core * 128, 128), :]
    loads[1].wait()
    loads[2].wait()
    build_taps(psf, slot_view, slot, taps)
    build_z(taps, wz, wb)

    def assemble():
        for k in range(1, VIEWS):
            part_copy((slot + k) % VIEWS, 0, partner, 0).wait_recv()
        chunk = iota((128, LANES), 1) // 32
        have = [parts[k].astype(F32) for k in range(VIEWS)]
        for g in range(GROUPS):
            line = have[(3 - g) % 4]
            for at in range(3):
                line = jnp.where(chunk == at, have[(at - g) % 4], line)
            if g:
                line = pltpu.roll(line, LANES - 32 * g, 1)
            for tp in range(2):
                field[1, 1, core, 6 * tp + g] = line[64 * tp : 64 * tp + 64].astype(BF16)

    def assemble_rims():
        for k, there in enumerate((below, above)):
            pl.when(there)(lambda k=k: outer_copy(k, 0, partner, 0).wait_recv())
        is_above = iota((128, LANES), 1) % 32 < RAD
        line = jnp.where(is_above, outer[1].astype(F32), outer[0].astype(F32))
        field[1, 1, core, 4:6] = pltpu.roll(line, RAD, 1).astype(BF16).reshape(2, 64, LANES)

    def message(ju, jv, which):
        return field.at[(*block(ju, jv), core, slice(4, 10) if which else slice(0, 4))]

    def face_copy(source, target, which, send, device):
        return pltpu.make_async_remote_copy(
            src_ref=message(*source, which), dst_ref=message(*target, which),
            send_sem=face_send.at[send],
            recv_sem=face_recv.at[which * 9 + target[0] * 3 + target[1]],
            device_id=device, device_id_type=MESH,
        )

    ways = {"u_up": (0, u_up, (0, 1)), "u_down": (1, u_down, (2, 1)), "v_up": (2, v_up, (1, 0)), "v_down": (3, v_down, (1, 2))}

    def send_own(name, which):
        index, (device, there), target = ways[name]
        pl.when(there)(face_copy((1, 1), target, which, index, device).start)

    def relay(name, along, which):
        index, (device, there), target = ways[name]
        source = (along, 1) if name[0] == "v" else (1, along)
        target = (along, target[1]) if name[0] == "v" else (target[0], along)
        pl.when(there)(face_copy(source, target, which, 4 + index, device).start)

    def came(ju, jv, which, over):
        there = ways[f"{over}_{'down' if (jv if over == 'v' else ju) == 0 else 'up'}"][1][1]
        copy = face_copy((ju, jv), (ju, jv), which, 0, partner)
        pl.when(there)(copy.wait_recv)

    def core_copy(jy, jx, side):
        return pltpu.make_async_remote_copy(
            src_ref=field.at[jy, jx, side], dst_ref=field.at[jy, jx, side],
            send_sem=core_send.at[0], recv_sem=core_recv.at[jy * 3 + jx],
            device_id=partner, device_id_type=MESH,
        )

    def pass_on(ju, jv):
        core_copy(*block(ju, jv), core).start()

    def swapped(jy, jx):
        core_copy(jy, jx, 1 - core).wait_recv()

    def forward_z(jy, jx):
        rows = slice(jx * 128, jx * 128 + 128)
        rim = field[jy, jx, :, 4:6].reshape(256, LANES)
        for g in range(GROUPS):
            turned = pltpu.roll(rim, LANES - 32 * g, 1) if g else rim
            main = jnp.concatenate(
                [field[jy, jx, side, 6 * tp + g] for side in range(2) for tp in range(2)], axis=0
            )
            done = dot(jnp.concatenate([main, turned], axis=1), wz[...]).astype(BF16)
            for r in range(RANK):
                after_z[r, jy * GROUPS + g, :, rows, :] = done[:, r * 128 : (r + 1) * 128].reshape(
                    2, 128, LANES
                )

    def forward_x(jy):
        def body(step, carry):
            r, group = step // GROUPS, jy * GROUPS + step % GROUPS
            for b in range(2):
                rows = pl.ds(b * 128, 256)
                both = jnp.concatenate([after_z[r, group, k, rows, :] for k in range(2)], axis=1)
                done = dot(tx[r], both).astype(BF16)
                for k in range(2):
                    after_x[r, group, k, b * 128 : b * 128 + 128, :] = done[:, k * 128 : k * 128 + 128]
            return carry

        lax.fori_loop(0, GROUPS * RANK, body, 0, unroll=True)

    assemble()
    for name in ("u_up", "u_down", "v_up", "v_down"):
        send_own(name, 0)
    assemble_rims()
    for name in ("v_up", "v_down", "u_up", "u_down"):
        send_own(name, 1)
    pass_on(1, 1)
    build_x(taps, bx, tx, txb)
    for side in (0, 2):
        came(side, 1, 0, "u")
    for one, other in ((0, 2), (2, 0)):
        relay("v_up", one, 0)
        relay("v_down", other, 0)
    for side in (0, 2):
        came(1, side, 1, "v")
    for one, other in ((0, 2), (2, 0)):
        relay("u_up", one, 1)
        relay("u_down", other, 1)
    build_y(taps, by, ty, tyb)
    loads[3].wait()

    def order_tile(i, carry):
        quad = tile[pl.ds(4 * i, 4)].astype(F32).reshape(2, 2, 8, 8, LANES)
        sides = swap_quads(quad[:, 0], quad[:, 1])
        rows = jnp.stack([m[x] for m in sides for x in range(2)], axis=1)
        seen[i] = rows.reshape(256, LANES).astype(BF16)
        return carry

    lax.fori_loop(0, 16, order_tile, 0, unroll=4)
    swapped(1, 1)
    forward_z(1, 1)
    for side in (0, 2):
        came(side, 1, 1, "u")
        pass_on(side, 1)
        came(1, side, 0, "v")
        pass_on(1, side)
    for side in (0, 2):
        swapped(1, side)
        swapped(side, 1)
    for side in (0, 2):
        forward_z(1, side)
        forward_z(side, 1)
    waves = (((0, 0), (2, 2)), ((0, 2), (2, 0)))
    for corner in waves[0]:
        came(*corner, 0, "v")
        came(*corner, 1, "u")
        pass_on(*corner)
    forward_x(1)
    for corner in waves[1]:
        came(*corner, 0, "v")
        came(*corner, 1, "u")
        pass_on(*corner)
    for wave in waves:
        for corner in wave:
            swapped(*corner)
        for corner in wave:
            forward_z(*corner)
    for jy in (0, 2):
        forward_x(jy)

    def along_y(step):
        quotient = []
        for b in range(2):
            blurred = None
            for r in range(RANK):
                both = [
                    after_x[r, 4 * b : 4 * b + 8, :, pl.ds(32 * step + 16 * k, 16), :].reshape(256, LANES)
                    for k in range(2)
                ]
                part = dot(ty[r], jnp.concatenate(both, axis=1))
                blurred = part if blurred is None else blurred + part
            rows = slice(128 * b, 128 * b + 128)
            both = jnp.concatenate([seen[2 * step + k, rows, :] for k in range(2)], axis=1).astype(F32)
            quotient.append((RANK * both / (blurred + RANK * BACKGROUND)).astype(BF16))
        quotient = jnp.concatenate(quotient, axis=0)
        for r in range(RANK):
            done = dot(tyb[r * 128 : r * 128 + 128, :], quotient).astype(BF16)
            for k in range(2):
                back_y[r * 8 : r * 8 + 8, pl.ds(32 * step + 16 * k, 16), :] = done[
                    :, k * 128 : k * 128 + 128
                ].reshape(8, 16, LANES)

    def backward_x(half):
        within = slice(half * 64, half * 64 + 192)
        for g in range(GROUPS):
            for r in range(RANK):
                at = (r * GROUPS + g) * 2
                both = jnp.concatenate([back_y[at, within, :], back_y[at + 1, within, :]], axis=1)
                done = dot(txb[half, r, :, 0:192], both).astype(BF16)
                for k in range(2):
                    back_x[g, half, k * 64 : k * 64 + 64, r * 128 : (r + 1) * 128] = done[
                        :, k * 128 : k * 128 + 128
                    ]

    def backward_rims(half):
        both = dot(back_x[0, half], wb[0, :, LANES:])
        for g in range(1, GROUPS):
            both = both + dot(back_x[g, half], wb[g, :, LANES:])
        is_low = iota((64, LANES), 1) < 64
        rims[half, 0] = jnp.where(is_low, both[0:64], pltpu.roll(both[64:128], 64, 1))
        rims[half, 1] = jnp.where(is_low, pltpu.roll(both[0:64], 64, 1), both[64:128])

    def backward_z(half):
        for g in range(GROUPS):
            done = dot(back_x[g, half], wb[g, :, :LANES])
            for c in range(4):
                at = (g + c) % 4
                sums[half, c, :, at * 32 : at * 32 + 32] = done[:, at * 32 : at * 32 + 32]

    far = (1 - chip) * 2 + core

    def sum_copy(source, target, index, device):
        return pltpu.make_async_remote_copy(
            src_ref=source, dst_ref=target, send_sem=sum_send.at[index],
            recv_sem=sum_recv.at[index], device_id=device, device_id_type=MESH,
        )

    far_swap = [
        sum_copy(sums.at[h, (1 - chip) * 2 + 1 - core], got_core.at[h, 0], h, partner) for h in range(2)
    ]
    near_swap = [
        sum_copy(sums.at[h, chip * 2 + 1 - core], got_core.at[h, 1], 2 + h, partner) for h in range(2)
    ]
    over = [sum_copy(sums.at[h, far], got_chip.at[h], 4 + h, at_vert(q * 4 + far)) for h in range(2)]
    rim_swap = [sum_copy(rims.at[h, 1 - core], got_rim.at[h], 6 + h, partner) for h in range(2)]
    edge_home = jnp.where(core == 0, vert - slot - 1, vert - slot + 4)
    edge_there = jnp.where(core == 0, q, 3 - q) > 0

    def edge_copy(h, which):
        return pltpu.make_async_remote_copy(
            src_ref=rims.at[h, core], dst_ref=got_edge.at[which, h], send_sem=sum_send.at[8 + h],
            recv_sem=sum_recv.at[8 + 2 * h + which], device_id=at_vert(edge_home), device_id_type=MESH,
        )

    def backward(h):
        backward_x(h)
        backward_rims(h)
        rim_swap[h].start()
        backward_z(h)
        far_swap[h].start()
        near_swap[h].start()

    def pass_over(h):
        rim_swap[h].wait_recv()
        rims[h, core] = rims[h, core] + got_rim[h]
        pl.when(edge_there)(lambda: edge_copy(h, chip).start())
        far_swap[h].wait_recv()
        sums[h, far] = sums[h, far] + got_core[h, 0]
        over[h].start()

    for step in range(6):
        along_y(step)
    backward(0)
    for step in range(6, 8):
        along_y(step)
    pass_over(0)
    backward(1)
    pass_over(1)

    for k in range(1, VIEWS):
        part_copy(slot, k - 1, partner, 0).wait_send()

    @pl.when(is_edge)
    def _():
        for k in range(VIEWS):
            outer_copy(0, k, partner, 0).wait_send()

    def sent(ref, semaphore):
        pltpu.make_async_remote_copy(
            src_ref=ref, dst_ref=ref, send_sem=semaphore, recv_sem=face_recv.at[0],
            device_id=partner, device_id_type=MESH,
        ).wait_send()

    for name, (index, (_, there), _) in ways.items():
        relayed = field.at[0:2, 0:2, :, 0:1] if name[0] == "v" else field.at[0:3, 0:2, :, 0:1]

        @pl.when(there)
        def _():
            sent(field.at[1, 1, core], face_send.at[index])
            sent(relayed, face_send.at[4 + index])

    sent(field.at[:, :, core], core_send.at[0])

    start = jnp.where(last, RAD, 0)
    lane = iota((64, LANES), 1)
    keep = is_edge & (lane >= start) & (lane < start + RAD)
    for h in range(2):
        near_swap[h].wait_recv()
        mine = sums[h, slot] + got_core[h, 1]
        over[h].wait_recv()
        mine = mine + got_chip[h]

        @pl.when(is_edge)
        def _():
            edge_copy(h, 0).wait_recv()
            edge_copy(h, 1).wait_recv()

        edge = got_edge[0, h] + got_edge[1, h]
        for g in range(GROUPS):
            own = pltpu.roll(mine, (8 - g - slot) % 4 * 32, 1)
            sides = []
            for k in range(2):
                rim = pltpu.roll(edge, (start + LANES - 64 * k - RAD * g) % LANES, 1)
                part = own[64 * k : 64 * k + 64] + jnp.where(keep, rim, 0.0)
                sides.append(part.reshape(8, 8, LANES) * (1.0 / (RANK * VIEWS)))
            part = jnp.stack(swap_quads(*sides), axis=1).reshape(16, 8, LANES)
            at = (slice(16 * h, 16 * h + 16), slice(g * 8, g * 8 + 8))
            refined[at] = est[at] * part[:, :, 0:BLOCK]

    for copy in far_swap + near_swap + over + rim_swap:
        copy.wait_send()

    @pl.when(edge_there)
    def _():
        for h in range(2):
            edge_copy(h, 0).wait_send()


def local(estimate, view_tiles, slot_view, psf_taps):
    vmem = pl.BlockSpec(memory_space=pltpu.VMEM)
    hbm = pl.BlockSpec(memory_space=pltpu.HBM)
    tile = view_tiles[0, 0, 0]
    psf = jnp.transpose(psf_taps, (1, 2, 0, 3))
    scratch = [
        pltpu.VMEM(estimate.shape, F32),
        pltpu.VMEM(tile.shape, BF16),
        pltpu.VMEM(psf.shape, F32),
        pltpu.VMEM(slot_view.shape, jnp.int32),
        pltpu.VMEM((256, LANES), BF16),
        pltpu.VMEM((VIEWS, 128, LANES), BF16),
        pltpu.VMEM((2, 128, LANES), BF16),
        pltpu.VMEM((3, 3, 2, 10, 64, LANES), BF16),
        pltpu.VMEM((RANK, 12, 2, 384, LANES), BF16),
        pltpu.VMEM((RANK, 12, 2, 256, LANES), BF16),
        pltpu.VMEM((16, 256, LANES), BF16),
        pltpu.VMEM((24, 256, LANES), BF16),
        pltpu.VMEM((GROUPS, 2, 128, RANK * LANES), BF16),
        pltpu.VMEM((2, 4, 128, LANES), F32),
        pltpu.VMEM((2, 2, 64, LANES), F32),
        pltpu.VMEM((2, 2, 128, LANES), F32),
        pltpu.VMEM((2, 64, LANES), F32),
        pltpu.VMEM((2, 128, LANES), F32),
        pltpu.VMEM((2, 2, 64, LANES), F32),
        pltpu.VMEM((2, 24, LANES), F32),
        pltpu.VMEM((RANK, 128, 256), BF16),
        pltpu.VMEM((RANK, 128, 256), BF16),
        pltpu.VMEM((256, RANK * LANES), BF16),
        pltpu.VMEM((RANK * 128, 256), BF16),
        pltpu.VMEM((2, RANK, 64, 256), BF16),
        pltpu.VMEM((GROUPS, RANK * LANES, 256), BF16),
        pltpu.SemaphoreType.DMA((4,)),
        pltpu.SemaphoreType.DMA((7,)),
        pltpu.SemaphoreType.DMA((6,)),
        pltpu.SemaphoreType.DMA((8,)),
        pltpu.SemaphoreType.DMA((18,)),
        pltpu.SemaphoreType.DMA((1,)),
        pltpu.SemaphoreType.DMA((9,)),
        pltpu.SemaphoreType.DMA((10,)),
        pltpu.SemaphoreType.DMA((12,)),
    ]
    return pl.pallas_call(
        kernel,
        out_shape=pltpu.VMEM(estimate.shape, F32),
        in_specs=[hbm] * 4,
        out_specs=vmem,
        scratch_shapes=scratch,
        compiler_params=pltpu.CompilerParams(
            collective_id=0, has_side_effects=True, vmem_limit_bytes=56 * 1024 * 1024
        ),
    )(*(pltpu.with_memory_space_constraint(a, pltpu.HBM) for a in (estimate, tile, psf, slot_view)))


def solution(mesh):
    placed = (
        P("bx", "by", "vert"),
        P("bx", "by", "vert", None, None, None),
        P("bx", "by", None),
        P(),
    )
    return jax.shard_map(
        local, mesh=mesh, in_specs=placed, out_specs=P("bx", "by", "vert"), check_vma=False
    )
```

```python
import jax
import jax.numpy as jnp
from jax import lax
from jax.experimental import pallas as pl
from jax.experimental.pallas import tpu as pltpu
from jax.sharding import PartitionSpec as P

BACKGROUND = 0.1
MESH = pl.DeviceIdType.MESH
F32, BF16 = jnp.float32, jnp.bfloat16
BLOCK = 32
RAD = 16
TAPS = 33
RANK = 3
VIEWS = 4
GROUPS = 4
LANES = 128


def iota(shape, axis):
    return lax.broadcasted_iota(jnp.int32, shape, axis)


def dot(a, b):
    return jnp.dot(a, b, preferred_element_type=F32)


def band(line, rows, start):
    line = jnp.broadcast_to(line, (rows, LANES))
    return pltpu.roll(line, start % LANES, 1, stride=1, stride_axis=0)


def swap_quads(a, b):
    low, axis = iota(a.shape, a.ndim - 2) < 4, a.ndim - 2
    return jnp.where(low, a, pltpu.roll(b, 4, axis)), jnp.where(low, pltpu.roll(a, 4, axis), b)


def build_taps(psf, slot_view, slot, taps):
    listed = slot_view[...]
    view = jnp.sum(jnp.where(iota(listed.shape, 2) == slot, listed, 0), axis=2, keepdims=True)
    held = iota((VIEWS, TAPS), 0) == view[0]
    mine = jnp.sum(jnp.where(held[None, None], psf[...], 0.0), axis=2)
    mine = (mine / jnp.sum(mine, axis=-1, keepdims=True)).astype(BF16).astype(F32)
    taps[...] = jnp.zeros_like(taps)
    for a in range(3):
        taps[0, 8 * a : 8 * a + RANK, :TAPS] = mine[a]
    flip = (iota((LANES, LANES), 0) + iota((LANES, LANES), 1) == TAPS - 1).astype(BF16)
    taps[1] = dot(taps[0].astype(BF16), flip)


def build_z(taps, wz, wb):
    z_in, z_out = iota((LANES, LANES), 0), iota((LANES, LANES), 1)
    near = jnp.abs(z_in - z_out) <= RAD
    rim, out = iota((32, LANES), 0), iota((32, LANES), 1)
    rim_ok = ((rim < RAD) & (out <= rim)) | ((rim >= RAD) & (out >= rim + 96))
    lane16 = iota((16, LANES), 1)
    for r in range(RANK):
        forward, backward = taps[1, 16 + r : 17 + r, :], taps[0, 16 + r : 17 + r, :]
        columns = slice(r * LANES, (r + 1) * LANES)
        wz[0:128, columns] = jnp.where(near, band(forward, LANES, -RAD), 0.0).astype(BF16)
        wz[128:160, columns] = jnp.where(rim_ok, band(forward, 32, 96), 0.0).astype(BF16)
        wz[160:256, columns] = jnp.zeros((96, LANES), BF16)
        main = jnp.where(near, band(backward, LANES, -RAD), 0.0)
        low = jnp.where(lane16 < RAD, band(backward, 16, 0), 0.0)
        high = jnp.where(lane16 < RAD, band(backward, 16, 96), 0.0)
        for g in range(GROUPS):
            wb[g, r * 128 : r * 128 + 128, 0:128] = (
                pltpu.roll(main, 32 * g, 1) if g else main
            ).astype(BF16)
            wb[g, r * 128 : r * 128 + 128, 128:256] = jnp.zeros((128, LANES), BF16)
            lo, hi = pltpu.roll(low, RAD * g, 1) if g else low, pltpu.roll(high, 64 + RAD * g, 1)
            wb[g, r * 128 : r * 128 + 16, 128:256] = lo.astype(BF16)
            wb[g, r * 128 + 112 : r * 128 + 128, 128:256] = hi.astype(BF16)


def build_x(taps, bx, tx, txb):
    spread = (iota((LANES, 256), 1) == 4 * iota((LANES, 256), 0)).astype(BF16)
    lane, row = iota((LANES, LANES), 1), iota((LANES, LANES), 0)
    low, high = bx > 0, bx < 3

    def tiles(line):
        turned = [band(line[:, i * LANES : (i + 1) * LANES], LANES, 0) for i in range(2)]
        return jnp.where(lane >= row, turned[0], 0.0), jnp.where(lane >= row, turned[1], turned[0])

    wide = [dot(taps[k, 0:8, :].astype(BF16), spread) for k in range(2)]
    for r in range(RANK):
        left, right = tiles(wide[0][r : r + 1])
        tx[r, :, 0:128] = left.astype(BF16)
        tx[r, :, 128:256] = right.astype(BF16)
        left, right = [m[0:64] for m in tiles(wide[1][r : r + 1])]
        txb[0, r, :, 0:128] = jnp.where((lane[0:64] >= 64) | low, left, 0.0).astype(BF16)
        txb[0, r, :, 128:256] = right.astype(BF16)
        txb[1, r, :, 0:128] = left.astype(BF16)
        txb[1, r, :, 128:256] = jnp.where(high, right, 0.0).astype(BF16)


def build_y(taps, by, ty, tyb):
    place = by * BLOCK - RAD + iota((BLOCK, LANES), 1)
    inside = (place >= 0) & (place < 4 * BLOCK)
    plain = [band(taps[0, 8 + r : 9 + r, :], BLOCK, 0) for r in range(RANK)]
    plain += [
        jnp.where(inside, band(taps[1, 8 + r : 9 + r, :], BLOCK, 0), 0.0) for r in range(RANK)
    ]
    plain = jnp.concatenate(plain, axis=0).astype(BF16)
    y, column = iota((LANES, 256), 0), iota((LANES, 256), 1)
    wide = [
        dot(plain, (column == 16 * (y // 4) + 4 * x + y % 4).astype(BF16)).astype(BF16)
        for x in range(4)
    ]
    row, source = iota((LANES, LANES), 0), iota((LANES, LANES), 1)
    order = (row == 16 * (source % 32 // 4) + 4 * (source // 32) + source % 4).astype(BF16)
    for i in range(2 * RANK):
        done = dot(order, jnp.concatenate([m[i * 32 : i * 32 + 32] for m in wide], axis=0)).astype(BF16)
        if i < RANK:
            ty[i] = done
        else:
            tyb[(i - RANK) * 128 : (i - RANK + 1) * 128, :] = done


def kernel(
    est_hbm, tile_hbm, psf_hbm, slot_view_hbm, refined,
    est, tile, psf, slot_view,
    packed, parts, outer, field, after_z, after_x, seen, quotient, back_y, back_x, sums, rims,
    got_core, got_rim, got_chip, got_edge,
    taps, tx, ty, wz, tyb, txb, wb,
    load_sem, part_send, part_recv, face_send, face_recv, core_send, core_recv, sum_send, sum_recv,
):
    bx, by, vert = lax.axis_index("bx"), lax.axis_index("by"), lax.axis_index("vert")
    q, slot = vert // VIEWS, vert % VIEWS
    core, chip = slot % 2, slot // 2

    loads = [
        pltpu.make_async_copy(source, target, load_sem.at[i])
        for i, (source, target) in enumerate(
            ((est_hbm, est), (psf_hbm, psf), (slot_view_hbm, slot_view), (tile_hbm, tile))
        )
    ]
    for copy in loads:
        copy.start()

    def at_vert(index):
        return {"vert": index}

    partner = at_vert(q * 4 + chip * 2 + 1 - core)
    above, below = q < 3, q > 0
    first, last = slot == 0, slot == VIEWS - 1
    is_edge = (first & below) | (last & above)

    straight = core == 0

    def block(ju, jv):
        return jnp.where(straight, jv, ju), jnp.where(straight, ju, jv)

    def link(along_u, step):
        x_step = jnp.where(straight == along_u, step, 0)
        x, y = bx + x_step, by + step - x_step
        return {"bx": x, "by": y}, (x >= 0) & (x < 4) & (y >= 0) & (y < 4)

    u_up, u_down, v_up, v_down = link(True, 1), link(True, -1), link(False, 1), link(False, -1)

    def clear(ref):
        ref[...] = jnp.zeros(ref.shape, BF16)

    pl.when(bx == 0)(lambda: clear(field.at[:, 0, core]))
    pl.when(bx == 3)(lambda: clear(field.at[:, 2, core]))
    pl.when(by == 0)(lambda: clear(field.at[0, :, core]))
    pl.when(by == 3)(lambda: clear(field.at[2, :, core]))
    pl.when(~below)(lambda: clear(outer.at[0]))
    pl.when(~above)(lambda: clear(outer.at[1]))

    got_edge[...] = jnp.zeros_like(got_edge)
    barrier = pltpu.get_barrier_semaphore()

    def greet(device):
        pl.semaphore_signal(barrier, inc=1, device_id=device, device_id_type=MESH)

    for k in range(1, VIEWS):
        greet(at_vert(q * 4 + (slot + k) % VIEWS))
    for device, there in (u_up, u_down, v_up, v_down):
        pl.when(there)(lambda device=device: greet(device))

    @pl.when(below)
    def _():
        greet(at_vert(vert - slot - 1))
        pl.when(first)(lambda: greet(at_vert(vert - 3)))

    @pl.when(above)
    def _():
        greet(at_vert(vert - slot + 4))
        pl.when(last)(lambda: greet(at_vert(vert + 3)))

    loads[0].wait()
    groups = est[...].reshape(BLOCK, GROUPS, 8, BLOCK)
    line = jnp.concatenate([groups[:, g].reshape(256, BLOCK) for g in range(GROUPS)], axis=1)
    line = pltpu.roll(line, slot * 32, 1).reshape(16, 2, 8, LANES)
    for side, quads in enumerate(swap_quads(line[:, 0], line[:, 1])):
        packed[side * 128 : side * 128 + 128, :] = quads.reshape(128, LANES).astype(BF16)

    beside = [(there, 1) for _, there in (u_up, u_down, v_up, v_down)] + [(is_edge, 4)]
    beside += [((slot == 1) & above, 1), ((slot == 2) & below, 1)]
    pl.semaphore_wait(barrier, 3 + sum(jnp.where(there, n, 0) for there, n in beside))

    def part_copy(source, send, device, side):
        return pltpu.make_async_remote_copy(
            src_ref=packed.at[pl.ds(side * 128, 128), :], dst_ref=parts.at[source],
            send_sem=part_send.at[send], recv_sem=part_recv.at[source],
            device_id=device, device_id_type=MESH,
        )

    for k in range(1, VIEWS):
        other = (slot + k) % VIEWS
        part_copy(slot, k - 1, at_vert(q * 4 + other), other % 2).start()

    def outer_copy(which, send, device, side):
        return pltpu.make_async_remote_copy(
            src_ref=packed.at[pl.ds(side * 128, 128), :], dst_ref=outer.at[which],
            send_sem=part_send.at[3 + send], recv_sem=part_recv.at[4 + which],
            device_id=device, device_id_type=MESH,
        )

    @pl.when(last & above)
    def _():
        for k in range(VIEWS):
            outer_copy(0, k, at_vert(vert + 1 + k), k % 2).start()

    @pl.when(first & below)
    def _():
        for k in range(VIEWS):
            outer_copy(1, k, at_vert(vert - 4 + k), k % 2).start()

    parts[slot] = packed[pl.ds(core * 128, 128), :]
    loads[1].wait()
    loads[2].wait()
    build_taps(psf, slot_view, slot, taps)
    build_z(taps, wz, wb)

    def assemble():
        for k in range(1, VIEWS):
            part_copy((slot + k) % VIEWS, 0, partner, 0).wait_recv()
        chunk = iota((128, LANES), 1) // 32
        have = [parts[k].astype(F32) for k in range(VIEWS)]
        for g in range(GROUPS):
            line = have[(3 - g) % 4]
            for at in range(3):
                line = jnp.where(chunk == at, have[(at - g) % 4], line)
            if g:
                line = pltpu.roll(line, LANES - 32 * g, 1)
            for tp in range(2):
                field[1, 1, core, 6 * tp + g] = line[64 * tp : 64 * tp + 64].astype(BF16)

    def assemble_rims():
        for k, there in enumerate((below, above)):
            pl.when(there)(lambda k=k: outer_copy(k, 0, partner, 0).wait_recv())
        is_above = iota((128, LANES), 1) % 32 < RAD
        line = jnp.where(is_above, outer[1].astype(F32), outer[0].astype(F32))
        field[1, 1, core, 4:6] = pltpu.roll(line, RAD, 1).astype(BF16).reshape(2, 64, LANES)

    def message(ju, jv, which):
        return field.at[(*block(ju, jv), core, slice(4, 10) if which else slice(0, 4))]

    def face_copy(source, target, which, send, device):
        return pltpu.make_async_remote_copy(
            src_ref=message(*source, which), dst_ref=message(*target, which),
            send_sem=face_send.at[send],
            recv_sem=face_recv.at[which * 9 + target[0] * 3 + target[1]],
            device_id=device, device_id_type=MESH,
        )

    ways = {"u_up": (0, u_up, (0, 1)), "u_down": (1, u_down, (2, 1)), "v_up": (2, v_up, (1, 0)), "v_down": (3, v_down, (1, 2))}

    def send_own(name, which):
        index, (device, there), target = ways[name]
        pl.when(there)(face_copy((1, 1), target, which, index, device).start)

    def relay(name, along, which):
        index, (device, there), target = ways[name]
        source = (along, 1) if name[0] == "v" else (1, along)
        target = (along, target[1]) if name[0] == "v" else (target[0], along)
        pl.when(there)(face_copy(source, target, which, 4 + index, device).start)

    def came(ju, jv, which, over):
        there = ways[f"{over}_{'down' if (jv if over == 'v' else ju) == 0 else 'up'}"][1][1]
        copy = face_copy((ju, jv), (ju, jv), which, 0, partner)
        pl.when(there)(copy.wait_recv)

    def core_copy(jy, jx, side):
        return pltpu.make_async_remote_copy(
            src_ref=field.at[jy, jx, side], dst_ref=field.at[jy, jx, side],
            send_sem=core_send.at[0], recv_sem=core_recv.at[jy * 3 + jx],
            device_id=partner, device_id_type=MESH,
        )

    def pass_on(ju, jv):
        core_copy(*block(ju, jv), core).start()

    def swapped(jy, jx):
        core_copy(jy, jx, 1 - core).wait_recv()

    def forward_z(jy, jx):
        rows = slice(jx * 128, jx * 128 + 128)
        rim = field[jy, jx, :, 4:6].reshape(256, LANES)
        for g in range(GROUPS):
            turned = pltpu.roll(rim, LANES - 32 * g, 1) if g else rim
            main = jnp.concatenate(
                [field[jy, jx, side, 6 * tp + g] for side in range(2) for tp in range(2)], axis=0
            )
            done = dot(jnp.concatenate([main, turned], axis=1), wz[...]).astype(BF16)
            for r in range(RANK):
                after_z[r, jy * GROUPS + g, :, rows, :] = done[:, r * 128 : (r + 1) * 128].reshape(
                    2, 128, LANES
                )

    def forward_x(jy, b):
        rows = slice(b * 128, b * 128 + 256)
        for r in range(RANK):
            for group in range(jy * GROUPS, jy * GROUPS + GROUPS):
                both = jnp.concatenate([after_z[r, group, k, rows, :] for k in range(2)], axis=1)
                done = dot(tx[r], both).astype(BF16)
                for k in range(2):
                    after_x[r, group, k, b * 128 : b * 128 + 128, :] = done[:, k * 128 : k * 128 + 128]

    def forward_y(step, b):
        blurred = None
        for r in range(RANK):
            both = [
                after_x[r, 4 * b : 4 * b + 8, :, 32 * step + 16 * k : 32 * step + 16 * k + 16, :].reshape(
                    256, LANES
                )
                for k in range(2)
            ]
            part = dot(ty[r], jnp.concatenate(both, axis=1))
            blurred = part if blurred is None else blurred + part
        rows = slice(128 * b, 128 * b + 128)
        both = jnp.concatenate([seen[2 * step + k, rows, :] for k in range(2)], axis=1).astype(F32)
        quotient[step, rows, :] = (RANK * both / (blurred + RANK * BACKGROUND)).astype(BF16)

    def backward_y(step):
        for r in range(RANK):
            done = dot(tyb[r * 128 : r * 128 + 128, :], quotient[step]).astype(BF16)
            for k in range(2):
                back_y[r * 8 : r * 8 + 8, 32 * step + 16 * k : 32 * step + 16 * k + 16, :] = done[
                    :, k * 128 : k * 128 + 128
                ].reshape(8, 16, LANES)

    assemble()
    for name in ("u_up", "u_down", "v_up", "v_down"):
        send_own(name, 0)
    assemble_rims()
    for name in ("v_up", "v_down", "u_up", "u_down"):
        send_own(name, 1)
    pass_on(1, 1)
    build_x(taps, bx, tx, txb)
    for side in (0, 2):
        came(side, 1, 0, "u")
    for one, other in ((0, 2), (2, 0)):
        relay("v_up", one, 0)
        relay("v_down", other, 0)
    for side in (0, 2):
        came(1, side, 1, "v")
    for one, other in ((0, 2), (2, 0)):
        relay("u_up", one, 1)
        relay("u_down", other, 1)
    build_y(taps, by, ty, tyb)
    loads[3].wait()

    def order_tile(i, carry):
        quad = tile[pl.ds(4 * i, 4)].astype(F32).reshape(2, 2, 8, 8, LANES)
        sides = swap_quads(quad[:, 0], quad[:, 1])
        rows = jnp.stack([m[x] for m in sides for x in range(2)], axis=1)
        seen[i] = rows.reshape(256, LANES).astype(BF16)
        return carry

    lax.fori_loop(0, 16, order_tile, 0, unroll=4)
    swapped(1, 1)
    forward_z(1, 1)
    for side in (0, 2):
        came(side, 1, 1, "u")
        pass_on(side, 1)
        came(1, side, 0, "v")
        pass_on(1, side)
    for side in (0, 2):
        swapped(1, side)
        swapped(side, 1)
    for side in (0, 2):
        forward_z(1, side)
        forward_z(side, 1)
    waves = (((0, 0), (2, 2)), ((0, 2), (2, 0)))
    for corner in waves[0]:
        came(*corner, 0, "v")
        came(*corner, 1, "u")
        pass_on(*corner)
    forward_x(1, 0)
    forward_x(1, 1)
    for corner in waves[0]:
        swapped(*corner)
    for corner in waves[0]:
        forward_z(*corner)
    forward_x(0, 0)
    forward_x(2, 1)
    for corner in waves[1]:
        came(*corner, 0, "v")
        came(*corner, 1, "u")
        pass_on(*corner)
    for step in range(4):
        forward_y(step, 0)
        forward_y(step + 4, 1)
    for corner in waves[1]:
        swapped(*corner)
    for corner in waves[1]:
        forward_z(*corner)
    forward_x(2, 0)
    forward_x(0, 1)

    def backward_x(half):
        within = slice(half * 64, half * 64 + 192)
        for g in range(GROUPS):
            for r in range(RANK):
                at = (r * GROUPS + g) * 2
                both = jnp.concatenate([back_y[at, within, :], back_y[at + 1, within, :]], axis=1)
                done = dot(txb[half, r, :, 0:192], both).astype(BF16)
                for k in range(2):
                    back_x[g, half, k * 64 : k * 64 + 64, r * 128 : (r + 1) * 128] = done[
                        :, k * 128 : k * 128 + 128
                    ]

    def backward_rims(half):
        both = dot(back_x[0, half], wb[0, :, LANES:])
        for g in range(1, GROUPS):
            both = both + dot(back_x[g, half], wb[g, :, LANES:])
        is_low = iota((64, LANES), 1) < 64
        rims[half, 0] = jnp.where(is_low, both[0:64], pltpu.roll(both[64:128], 64, 1))
        rims[half, 1] = jnp.where(is_low, pltpu.roll(both[0:64], 64, 1), both[64:128])

    def backward_z(half):
        for g in range(GROUPS):
            done = dot(back_x[g, half], wb[g, :, :LANES])
            for c in range(4):
                at = (g + c) % 4
                sums[half, c, :, at * 32 : at * 32 + 32] = done[:, at * 32 : at * 32 + 32]

    far = (1 - chip) * 2 + core

    def sum_copy(source, target, index, device):
        return pltpu.make_async_remote_copy(
            src_ref=source, dst_ref=target, send_sem=sum_send.at[index],
            recv_sem=sum_recv.at[index], device_id=device, device_id_type=MESH,
        )

    far_swap = [
        sum_copy(sums.at[h, (1 - chip) * 2 + 1 - core], got_core.at[h, 0], h, partner) for h in range(2)
    ]
    near_swap = [
        sum_copy(sums.at[h, chip * 2 + 1 - core], got_core.at[h, 1], 2 + h, partner) for h in range(2)
    ]
    over = [sum_copy(sums.at[h, far], got_chip.at[h], 4 + h, at_vert(q * 4 + far)) for h in range(2)]
    rim_swap = [sum_copy(rims.at[h, 1 - core], got_rim.at[h], 6 + h, partner) for h in range(2)]
    edge_home = jnp.where(core == 0, vert - slot - 1, vert - slot + 4)
    edge_there = jnp.where(core == 0, q, 3 - q) > 0

    def edge_copy(h, which):
        return pltpu.make_async_remote_copy(
            src_ref=rims.at[h, core], dst_ref=got_edge.at[which, h], send_sem=sum_send.at[8 + h],
            recv_sem=sum_recv.at[8 + 2 * h + which], device_id=at_vert(edge_home), device_id_type=MESH,
        )

    def backward(h):
        backward_x(h)
        backward_rims(h)
        rim_swap[h].start()
        backward_z(h)
        far_swap[h].start()
        near_swap[h].start()

    def pass_over(h):
        rim_swap[h].wait_recv()
        rims[h, core] = rims[h, core] + got_rim[h]
        pl.when(edge_there)(lambda: edge_copy(h, chip).start())
        far_swap[h].wait_recv()
        sums[h, far] = sums[h, far] + got_core[h, 0]
        over[h].start()

    for step in range(4):
        forward_y(step, 1)
        backward_y(step)
    for step in range(4, 6):
        forward_y(step, 0)
        backward_y(step)
    backward(0)
    for step in range(6, 8):
        forward_y(step, 0)
        backward_y(step)
    pass_over(0)
    backward(1)
    pass_over(1)

    for k in range(1, VIEWS):
        part_copy(slot, k - 1, partner, 0).wait_send()

    @pl.when(is_edge)
    def _():
        for k in range(VIEWS):
            outer_copy(0, k, partner, 0).wait_send()

    def sent(ref, semaphore):
        pltpu.make_async_remote_copy(
            src_ref=ref, dst_ref=ref, send_sem=semaphore, recv_sem=face_recv.at[0],
            device_id=partner, device_id_type=MESH,
        ).wait_send()

    for name, (index, (_, there), _) in ways.items():
        relayed = field.at[0:2, 0:2, :, 0:1] if name[0] == "v" else field.at[0:3, 0:2, :, 0:1]

        @pl.when(there)
        def _():
            sent(field.at[1, 1, core], face_send.at[index])
            sent(relayed, face_send.at[4 + index])

    sent(field.at[:, :, core], core_send.at[0])

    start = jnp.where(last, RAD, 0)
    lane = iota((64, LANES), 1)
    keep = is_edge & (lane >= start) & (lane < start + RAD)
    for h in range(2):
        near_swap[h].wait_recv()
        mine = sums[h, slot] + got_core[h, 1]
        over[h].wait_recv()
        mine = mine + got_chip[h]

        @pl.when(is_edge)
        def _():
            edge_copy(h, 0).wait_recv()
            edge_copy(h, 1).wait_recv()

        edge = got_edge[0, h] + got_edge[1, h]
        for g in range(GROUPS):
            own = pltpu.roll(mine, (8 - g - slot) % 4 * 32, 1)
            sides = []
            for k in range(2):
                rim = pltpu.roll(edge, (start + LANES - 64 * k - RAD * g) % LANES, 1)
                part = own[64 * k : 64 * k + 64] + jnp.where(keep, rim, 0.0)
                sides.append(part.reshape(8, 8, LANES) * (1.0 / (RANK * VIEWS)))
            part = jnp.stack(swap_quads(*sides), axis=1).reshape(16, 8, LANES)
            at = (slice(16 * h, 16 * h + 16), slice(g * 8, g * 8 + 8))
            refined[at] = est[at] * part[:, :, 0:BLOCK]

    for copy in far_swap + near_swap + over + rim_swap:
        copy.wait_send()

    @pl.when(edge_there)
    def _():
        for h in range(2):
            edge_copy(h, 0).wait_send()


def local(estimate, view_tiles, slot_view, psf_taps):
    vmem = pl.BlockSpec(memory_space=pltpu.VMEM)
    hbm = pl.BlockSpec(memory_space=pltpu.HBM)
    tile = view_tiles[0, 0, 0]
    psf = jnp.transpose(psf_taps, (1, 2, 0, 3))
    scratch = [
        pltpu.VMEM(estimate.shape, F32),
        pltpu.VMEM(tile.shape, BF16),
        pltpu.VMEM(psf.shape, F32),
        pltpu.VMEM(slot_view.shape, jnp.int32),
        pltpu.VMEM((256, LANES), BF16),
        pltpu.VMEM((VIEWS, 128, LANES), BF16),
        pltpu.VMEM((2, 128, LANES), BF16),
        pltpu.VMEM((3, 3, 2, 10, 64, LANES), BF16),
        pltpu.VMEM((RANK, 12, 2, 384, LANES), BF16),
        pltpu.VMEM((RANK, 12, 2, 256, LANES), BF16),
        pltpu.VMEM((16, 256, LANES), BF16),
        pltpu.VMEM((8, 256, 2 * LANES), BF16),
        pltpu.VMEM((24, 256, LANES), BF16),
        pltpu.VMEM((GROUPS, 2, 128, RANK * LANES), BF16),
        pltpu.VMEM((2, 4, 128, LANES), F32),
        pltpu.VMEM((2, 2, 64, LANES), F32),
        pltpu.VMEM((2, 2, 128, LANES), F32),
        pltpu.VMEM((2, 64, LANES), F32),
        pltpu.VMEM((2, 128, LANES), F32),
        pltpu.VMEM((2, 2, 64, LANES), F32),
        pltpu.VMEM((2, 24, LANES), F32),
        pltpu.VMEM((RANK, 128, 256), BF16),
        pltpu.VMEM((RANK, 128, 256), BF16),
        pltpu.VMEM((256, RANK * LANES), BF16),
        pltpu.VMEM((RANK * 128, 256), BF16),
        pltpu.VMEM((2, RANK, 64, 256), BF16),
        pltpu.VMEM((GROUPS, RANK * LANES, 256), BF16),
        pltpu.SemaphoreType.DMA((4,)),
        pltpu.SemaphoreType.DMA((7,)),
        pltpu.SemaphoreType.DMA((6,)),
        pltpu.SemaphoreType.DMA((8,)),
        pltpu.SemaphoreType.DMA((18,)),
        pltpu.SemaphoreType.DMA((1,)),
        pltpu.SemaphoreType.DMA((9,)),
        pltpu.SemaphoreType.DMA((10,)),
        pltpu.SemaphoreType.DMA((12,)),
    ]
    return pl.pallas_call(
        kernel,
        out_shape=pltpu.VMEM(estimate.shape, F32),
        in_specs=[hbm] * 4,
        out_specs=vmem,
        scratch_shapes=scratch,
        compiler_params=pltpu.CompilerParams(
            collective_id=0, has_side_effects=True, vmem_limit_bytes=56 * 1024 * 1024
        ),
    )(*(pltpu.with_memory_space_constraint(a, pltpu.HBM) for a in (estimate, tile, psf, slot_view)))


def solution(mesh):
    placed = (
        P("bx", "by", "vert"),
        P("bx", "by", "vert", None, None, None),
        P("bx", "by", None),
        P(),
    )
    return jax.shard_map(
        local, mesh=mesh, in_specs=placed, out_specs=P("bx", "by", "vert"), check_vma=False
    )
```

```python
import jax
import jax.numpy as jnp
from jax import lax
from jax.experimental import pallas as pl
from jax.experimental.pallas import tpu as pltpu
from jax.sharding import PartitionSpec as P

BACKGROUND = 0.1
MESH = pl.DeviceIdType.MESH
F32, BF16 = jnp.float32, jnp.bfloat16
BLOCK = 32
RAD = 16
TAPS = 33
RANK = 3
VIEWS = 4
GROUPS = 4
LANES = 128


def iota(shape, axis):
    return lax.broadcasted_iota(jnp.int32, shape, axis)


def dot(a, b):
    return jnp.dot(a, b, preferred_element_type=F32)


def band(line, rows, start):
    line = jnp.broadcast_to(line, (rows, LANES))
    return pltpu.roll(line, start % LANES, 1, stride=1, stride_axis=0)


def swap_quads(a, b):
    low, axis = iota(a.shape, a.ndim - 2) < 4, a.ndim - 2
    return jnp.where(low, a, pltpu.roll(b, 4, axis)), jnp.where(low, pltpu.roll(a, 4, axis), b)


def build_taps(psf, slot_view, slot, taps):
    listed = slot_view[...]
    view = jnp.sum(jnp.where(iota(listed.shape, 2) == slot, listed, 0), axis=2, keepdims=True)
    held = iota((VIEWS, TAPS), 0) == view[0]
    mine = jnp.sum(jnp.where(held[None, None], psf[...], 0.0), axis=2)
    mine = (mine / jnp.sum(mine, axis=-1, keepdims=True)).astype(BF16).astype(F32)
    taps[...] = jnp.zeros_like(taps)
    for a in range(3):
        taps[0, 8 * a : 8 * a + RANK, :TAPS] = mine[a]
    flip = (iota((LANES, LANES), 0) + iota((LANES, LANES), 1) == TAPS - 1).astype(BF16)
    taps[1] = dot(taps[0].astype(BF16), flip)


def build_z(taps, wz, wb):
    z_in, z_out = iota((LANES, LANES), 0), iota((LANES, LANES), 1)
    near = jnp.abs(z_in - z_out) <= RAD
    rim, out = iota((32, LANES), 0), iota((32, LANES), 1)
    rim_ok = ((rim < RAD) & (out <= rim)) | ((rim >= RAD) & (out >= rim + 96))
    lane16 = iota((16, LANES), 1)
    for r in range(RANK):
        forward, backward = taps[1, 16 + r : 17 + r, :], taps[0, 16 + r : 17 + r, :]
        columns = slice(r * LANES, (r + 1) * LANES)
        wz[0:128, columns] = jnp.where(near, band(forward, LANES, -RAD), 0.0).astype(BF16)
        wz[128:160, columns] = jnp.where(rim_ok, band(forward, 32, 96), 0.0).astype(BF16)
        wz[160:256, columns] = jnp.zeros((96, LANES), BF16)
        main = jnp.where(near, band(backward, LANES, -RAD), 0.0)
        low = jnp.where(lane16 < RAD, band(backward, 16, 0), 0.0)
        high = jnp.where(lane16 < RAD, band(backward, 16, 96), 0.0)
        for g in range(GROUPS):
            wb[g, r * 128 : r * 128 + 128, 0:128] = (
                pltpu.roll(main, 32 * g, 1) if g else main
            ).astype(BF16)
            wb[g, r * 128 : r * 128 + 128, 128:256] = jnp.zeros((128, LANES), BF16)
            lo, hi = pltpu.roll(low, RAD * g, 1) if g else low, pltpu.roll(high, 64 + RAD * g, 1)
            wb[g, r * 128 : r * 128 + 16, 128:256] = lo.astype(BF16)
            wb[g, r * 128 + 112 : r * 128 + 128, 128:256] = hi.astype(BF16)


def build_x(taps, bx, tx, txb):
    spread = (iota((LANES, 256), 1) == 4 * iota((LANES, 256), 0)).astype(BF16)
    lane, row = iota((LANES, LANES), 1), iota((LANES, LANES), 0)
    low, high = bx > 0, bx < 3

    def tiles(line):
        turned = [band(line[:, i * LANES : (i + 1) * LANES], LANES, 0) for i in range(2)]
        return jnp.where(lane >= row, turned[0], 0.0), jnp.where(lane >= row, turned[1], turned[0])

    wide = [dot(taps[k, 0:8, :].astype(BF16), spread) for k in range(2)]
    for r in range(RANK):
        left, right = tiles(wide[0][r : r + 1])
        tx[r, :, 0:128] = left.astype(BF16)
        tx[r, :, 128:256] = right.astype(BF16)
        left, right = [m[0:64] for m in tiles(wide[1][r : r + 1])]
        txb[0, r, :, 0:128] = jnp.where((lane[0:64] >= 64) | low, left, 0.0).astype(BF16)
        txb[0, r, :, 128:256] = right.astype(BF16)
        txb[1, r, :, 0:128] = left.astype(BF16)
        txb[1, r, :, 128:256] = jnp.where(high, right, 0.0).astype(BF16)


def build_y(taps, by, ty, tyb):
    place = by * BLOCK - RAD + iota((BLOCK, LANES), 1)
    inside = (place >= 0) & (place < 4 * BLOCK)
    plain = [band(taps[0, 8 + r : 9 + r, :], BLOCK, 0) for r in range(RANK)]
    plain += [
        jnp.where(inside, band(taps[1, 8 + r : 9 + r, :], BLOCK, 0), 0.0) for r in range(RANK)
    ]
    plain = jnp.concatenate(plain, axis=0).astype(BF16)
    y, column = iota((LANES, 256), 0), iota((LANES, 256), 1)
    wide = [
        dot(plain, (column == 16 * (y // 4) + 4 * x + y % 4).astype(BF16)).astype(BF16)
        for x in range(4)
    ]
    row, source = iota((LANES, LANES), 0), iota((LANES, LANES), 1)
    order = (row == 16 * (source % 32 // 4) + 4 * (source // 32) + source % 4).astype(BF16)
    for i in range(2 * RANK):
        done = dot(order, jnp.concatenate([m[i * 32 : i * 32 + 32] for m in wide], axis=0)).astype(BF16)
        if i < RANK:
            ty[i] = done
        else:
            tyb[(i - RANK) * 128 : (i - RANK + 1) * 128, :] = done


def kernel(
    est_hbm, tile_hbm, psf_hbm, slot_view_hbm, refined,
    est, tile, psf, slot_view,
    packed, parts, outer, field, after_z, after_x, seen, back_y, back_x, sums, rims,
    got_core, got_rim, got_chip, got_edge,
    taps, tx, ty, wz, tyb, txb, wb,
    load_sem, part_send, part_recv, face_send, face_recv, core_send, core_recv, sum_send, sum_recv,
):
    bx, by, vert = lax.axis_index("bx"), lax.axis_index("by"), lax.axis_index("vert")
    q, slot = vert // VIEWS, vert % VIEWS
    core, chip = slot % 2, slot // 2

    loads = [
        pltpu.make_async_copy(source, target, load_sem.at[i])
        for i, (source, target) in enumerate(
            ((est_hbm, est), (psf_hbm, psf), (slot_view_hbm, slot_view), (tile_hbm, tile))
        )
    ]
    for copy in loads:
        copy.start()

    def at_vert(index):
        return {"vert": index}

    partner = at_vert(q * 4 + chip * 2 + 1 - core)
    above, below = q < 3, q > 0
    first, last = slot == 0, slot == VIEWS - 1
    is_edge = (first & below) | (last & above)

    straight = core == 0

    def block(ju, jv):
        return jnp.where(straight, jv, ju), jnp.where(straight, ju, jv)

    def link(along_u, step):
        x_step = jnp.where(straight == along_u, step, 0)
        x, y = bx + x_step, by + step - x_step
        return {"bx": x, "by": y}, (x >= 0) & (x < 4) & (y >= 0) & (y < 4)

    u_up, u_down, v_up, v_down = link(True, 1), link(True, -1), link(False, 1), link(False, -1)

    def clear(ref):
        ref[...] = jnp.zeros(ref.shape, BF16)

    pl.when(bx == 0)(lambda: clear(field.at[:, 0, core]))
    pl.when(bx == 3)(lambda: clear(field.at[:, 2, core]))
    pl.when(by == 0)(lambda: clear(field.at[0, :, core]))
    pl.when(by == 3)(lambda: clear(field.at[2, :, core]))
    pl.when(~below)(lambda: clear(outer.at[0]))
    pl.when(~above)(lambda: clear(outer.at[1]))

    got_edge[...] = jnp.zeros_like(got_edge)
    barrier = pltpu.get_barrier_semaphore()

    def greet(device):
        pl.semaphore_signal(barrier, inc=1, device_id=device, device_id_type=MESH)

    for k in range(1, VIEWS):
        greet(at_vert(q * 4 + (slot + k) % VIEWS))
    for device, there in (u_up, u_down, v_up, v_down):
        pl.when(there)(lambda device=device: greet(device))

    @pl.when(below)
    def _():
        greet(at_vert(vert - slot - 1))
        pl.when(first)(lambda: greet(at_vert(vert - 3)))

    @pl.when(above)
    def _():
        greet(at_vert(vert - slot + 4))
        pl.when(last)(lambda: greet(at_vert(vert + 3)))

    loads[0].wait()
    groups = est[...].reshape(BLOCK, GROUPS, 8, BLOCK)
    line = jnp.concatenate([groups[:, g].reshape(256, BLOCK) for g in range(GROUPS)], axis=1)
    line = pltpu.roll(line, slot * 32, 1).reshape(16, 2, 8, LANES)
    for side, quads in enumerate(swap_quads(line[:, 0], line[:, 1])):
        packed[side * 128 : side * 128 + 128, :] = quads.reshape(128, LANES).astype(BF16)

    beside = [(there, 1) for _, there in (u_up, u_down, v_up, v_down)] + [(is_edge, 4)]
    beside += [((slot == 1) & above, 1), ((slot == 2) & below, 1)]
    pl.semaphore_wait(barrier, 3 + sum(jnp.where(there, n, 0) for there, n in beside))

    def part_copy(source, send, device, side):
        return pltpu.make_async_remote_copy(
            src_ref=packed.at[pl.ds(side * 128, 128), :], dst_ref=parts.at[source],
            send_sem=part_send.at[send], recv_sem=part_recv.at[source],
            device_id=device, device_id_type=MESH,
        )

    for k in range(1, VIEWS):
        other = (slot + k) % VIEWS
        part_copy(slot, k - 1, at_vert(q * 4 + other), other % 2).start()

    def outer_copy(which, send, device, side):
        return pltpu.make_async_remote_copy(
            src_ref=packed.at[pl.ds(side * 128, 128), :], dst_ref=outer.at[which],
            send_sem=part_send.at[3 + send], recv_sem=part_recv.at[4 + which],
            device_id=device, device_id_type=MESH,
        )

    @pl.when(last & above)
    def _():
        for k in range(VIEWS):
            outer_copy(0, k, at_vert(vert + 1 + k), k % 2).start()

    @pl.when(first & below)
    def _():
        for k in range(VIEWS):
            outer_copy(1, k, at_vert(vert - 4 + k), k % 2).start()

    parts[slot] = packed[pl.ds(core * 128, 128), :]
    loads[1].wait()
    loads[2].wait()
    build_taps(psf, slot_view, slot, taps)
    build_z(taps, wz, wb)

    def assemble():
        for k in range(1, VIEWS):
            part_copy((slot + k) % VIEWS, 0, partner, 0).wait_recv()
        chunk = iota((128, LANES), 1) // 32
        have = [parts[k].astype(F32) for k in range(VIEWS)]
        for g in range(GROUPS):
            line = have[(3 - g) % 4]
            for at in range(3):
                line = jnp.where(chunk == at, have[(at - g) % 4], line)
            if g:
                line = pltpu.roll(line, LANES - 32 * g, 1)
            for tp in range(2):
                field[1, 1, core, 6 * tp + g] = line[64 * tp : 64 * tp + 64].astype(BF16)

    def assemble_rims():
        for k, there in enumerate((below, above)):
            pl.when(there)(lambda k=k: outer_copy(k, 0, partner, 0).wait_recv())
        is_above = iota((128, LANES), 1) % 32 < RAD
        line = jnp.where(is_above, outer[1].astype(F32), outer[0].astype(F32))
        field[1, 1, core, 4:6] = pltpu.roll(line, RAD, 1).astype(BF16).reshape(2, 64, LANES)

    def message(ju, jv, which):
        return field.at[(*block(ju, jv), core, slice(4, 10) if which else slice(0, 4))]

    def face_copy(source, target, which, send, device):
        return pltpu.make_async_remote_copy(
            src_ref=message(*source, which), dst_ref=message(*target, which),
            send_sem=face_send.at[send],
            recv_sem=face_recv.at[which * 9 + target[0] * 3 + target[1]],
            device_id=device, device_id_type=MESH,
        )

    ways = {"u_up": (0, u_up, (0, 1)), "u_down": (1, u_down, (2, 1)), "v_up": (2, v_up, (1, 0)), "v_down": (3, v_down, (1, 2))}

    def send_own(name, which):
        index, (device, there), target = ways[name]
        pl.when(there)(face_copy((1, 1), target, which, index, device).start)

    def relay(name, along, which):
        index, (device, there), target = ways[name]
        source = (along, 1) if name[0] == "v" else (1, along)
        target = (along, target[1]) if name[0] == "v" else (target[0], along)
        pl.when(there)(face_copy(source, target, which, 4 + index, device).start)

    def came(ju, jv, which, over):
        there = ways[f"{over}_{'down' if (jv if over == 'v' else ju) == 0 else 'up'}"][1][1]
        copy = face_copy((ju, jv), (ju, jv), which, 0, partner)
        pl.when(there)(copy.wait_recv)

    def core_copy(jy, jx, side):
        return pltpu.make_async_remote_copy(
            src_ref=field.at[jy, jx, side], dst_ref=field.at[jy, jx, side],
            send_sem=core_send.at[0], recv_sem=core_recv.at[jy * 3 + jx],
            device_id=partner, device_id_type=MESH,
        )

    def pass_on(ju, jv):
        core_copy(*block(ju, jv), core).start()

    def swapped(jy, jx):
        core_copy(jy, jx, 1 - core).wait_recv()

    def forward_z(jy, jx):
        rows = pl.ds(jx * 128, 128)
        rim = field[jy, jx, :, 4:6].reshape(256, LANES)
        lines = []
        for g in range(GROUPS):
            turned = pltpu.roll(rim, LANES - 32 * g, 1) if g else rim
            main = jnp.concatenate(
                [field[jy, jx, side, 6 * tp + g] for side in range(2) for tp in range(2)], axis=0
            )
            lines.append(jnp.concatenate([main, turned], axis=1))
        done = dot(jnp.concatenate(lines, axis=0), wz[...]).astype(BF16)
        for r in range(RANK):
            after_z[r, pl.ds(jy * GROUPS, GROUPS), :, rows, :] = done[
                :, r * 128 : (r + 1) * 128
            ].reshape(GROUPS, 2, 128, LANES)

    def forward_x(jy, r):
        for g in range(GROUPS):
            group = jy * GROUPS + g
            for b in range(2):
                rows = pl.ds(b * 128, 256)
                both = jnp.concatenate([after_z[r, group, k, rows, :] for k in range(2)], axis=1)
                done = dot(tx[r], both).astype(BF16)
                for k in range(2):
                    after_x[r, group, k, b * 128 : b * 128 + 128, :] = done[:, k * 128 : k * 128 + 128]

    def loop(count, body):
        def step(i, carry):
            body(i)
            return carry

        lax.fori_loop(0, count, step, 0)

    assemble()
    for name in ("u_up", "u_down", "v_up", "v_down"):
        send_own(name, 0)
    assemble_rims()
    for name in ("v_up", "v_down", "u_up", "u_down"):
        send_own(name, 1)
    pass_on(1, 1)
    build_x(taps, bx, tx, txb)
    for side in (0, 2):
        came(side, 1, 0, "u")
    for one, other in ((0, 2), (2, 0)):
        relay("v_up", one, 0)
        relay("v_down", other, 0)
    for side in (0, 2):
        came(1, side, 1, "v")
    for one, other in ((0, 2), (2, 0)):
        relay("u_up", one, 1)
        relay("u_down", other, 1)
    build_y(taps, by, ty, tyb)
    loads[3].wait()

    def order_tile(i, carry):
        quad = tile[pl.ds(4 * i, 4)].astype(F32).reshape(2, 2, 8, 8, LANES)
        sides = swap_quads(quad[:, 0], quad[:, 1])
        rows = jnp.stack([m[x] for m in sides for x in range(2)], axis=1)
        seen[i] = rows.reshape(256, LANES).astype(BF16)
        return carry

    lax.fori_loop(0, 16, order_tile, 0, unroll=4)
    swapped(1, 1)
    forward_z(1, 1)
    for side in (0, 2):
        came(side, 1, 1, "u")
        pass_on(side, 1)
        came(1, side, 0, "v")
        pass_on(1, side)
    for side in (0, 2):
        swapped(1, side)
        swapped(side, 1)
    loop(4, lambda i: forward_z(jnp.where(i % 2 == 1, i - 1, 1), jnp.where(i % 2 == 1, 1, i)))
    waves = (((0, 0), (2, 2)), ((0, 2), (2, 0)))
    for corner in waves[0]:
        came(*corner, 0, "v")
        came(*corner, 1, "u")
        pass_on(*corner)
    loop(RANK, lambda r: forward_x(1, r))
    for corner in waves[1]:
        came(*corner, 0, "v")
        came(*corner, 1, "u")
        pass_on(*corner)
    for corner in waves[0] + waves[1]:
        swapped(*corner)
    loop(4, lambda i: forward_z(i // 2 * 2, i % 2 * 2))
    loop(2 * RANK, lambda i: forward_x(i // RANK * 2, i % RANK))

    def along_y(step):
        quotient = []
        for b in range(2):
            blurred = None
            for r in range(RANK):
                both = [
                    after_x[r, 4 * b : 4 * b + 8, :, pl.ds(32 * step + 16 * k, 16), :].reshape(256, LANES)
                    for k in range(2)
                ]
                part = dot(ty[r], jnp.concatenate(both, axis=1))
                blurred = part if blurred is None else blurred + part
            rows = slice(128 * b, 128 * b + 128)
            both = jnp.concatenate([seen[2 * step + k, rows, :] for k in range(2)], axis=1).astype(F32)
            quotient.append((RANK * both / (blurred + RANK * BACKGROUND)).astype(BF16))
        quotient = jnp.concatenate(quotient, axis=0)
        for r in range(RANK):
            done = dot(tyb[r * 128 : r * 128 + 128, :], quotient).astype(BF16)
            for k in range(2):
                back_y[r * 8 : r * 8 + 8, pl.ds(32 * step + 16 * k, 16), :] = done[
                    :, k * 128 : k * 128 + 128
                ].reshape(8, 16, LANES)

    def backward_x(half):
        within = slice(half * 64, half * 64 + 192)
        for g in range(GROUPS):
            for r in range(RANK):
                at = (r * GROUPS + g) * 2
                both = jnp.concatenate([back_y[at, within, :], back_y[at + 1, within, :]], axis=1)
                done = dot(txb[half, r, :, 0:192], both).astype(BF16)
                for k in range(2):
                    back_x[g, half, k * 64 : k * 64 + 64, r * 128 : (r + 1) * 128] = done[
                        :, k * 128 : k * 128 + 128
                    ]

    def backward_rims(half):
        both = dot(back_x[0, half], wb[0, :, LANES:])
        for g in range(1, GROUPS):
            both = both + dot(back_x[g, half], wb[g, :, LANES:])
        is_low = iota((64, LANES), 1) < 64
        rims[half, 0] = jnp.where(is_low, both[0:64], pltpu.roll(both[64:128], 64, 1))
        rims[half, 1] = jnp.where(is_low, pltpu.roll(both[0:64], 64, 1), both[64:128])

    def backward_z(half):
        for g in range(GROUPS):
            done = dot(back_x[g, half], wb[g, :, :LANES])
            for c in range(4):
                at = (g + c) % 4
                sums[half, c, :, at * 32 : at * 32 + 32] = done[:, at * 32 : at * 32 + 32]

    far = (1 - chip) * 2 + core

    def sum_copy(source, target, index, device):
        return pltpu.make_async_remote_copy(
            src_ref=source, dst_ref=target, send_sem=sum_send.at[index],
            recv_sem=sum_recv.at[index], device_id=device, device_id_type=MESH,
        )

    far_swap = [
        sum_copy(sums.at[h, (1 - chip) * 2 + 1 - core], got_core.at[h, 0], h, partner) for h in range(2)
    ]
    near_swap = [
        sum_copy(sums.at[h, chip * 2 + 1 - core], got_core.at[h, 1], 2 + h, partner) for h in range(2)
    ]
    over = [sum_copy(sums.at[h, far], got_chip.at[h], 4 + h, at_vert(q * 4 + far)) for h in range(2)]
    rim_swap = [sum_copy(rims.at[h, 1 - core], got_rim.at[h], 6 + h, partner) for h in range(2)]
    edge_home = jnp.where(core == 0, vert - slot - 1, vert - slot + 4)
    edge_there = jnp.where(core == 0, q, 3 - q) > 0

    def edge_copy(h, which):
        return pltpu.make_async_remote_copy(
            src_ref=rims.at[h, core], dst_ref=got_edge.at[which, h], send_sem=sum_send.at[8 + h],
            recv_sem=sum_recv.at[8 + 2 * h + which], device_id=at_vert(edge_home), device_id_type=MESH,
        )

    def backward(h):
        backward_x(h)
        backward_rims(h)
        rim_swap[h].start()
        backward_z(h)
        far_swap[h].start()
        near_swap[h].start()

    def pass_over(h):
        rim_swap[h].wait_recv()
        rims[h, core] = rims[h, core] + got_rim[h]
        pl.when(edge_there)(lambda: edge_copy(h, chip).start())
        far_swap[h].wait_recv()
        sums[h, far] = sums[h, far] + got_core[h, 0]
        over[h].start()

    lax.fori_loop(0, 6, lambda i, c: along_y(i), None, unroll=2)
    backward(0)
    lax.fori_loop(6, 8, lambda i, c: along_y(i), None, unroll=2)
    pass_over(0)
    backward(1)
    pass_over(1)

    for k in range(1, VIEWS):
        part_copy(slot, k - 1, partner, 0).wait_send()

    @pl.when(is_edge)
    def _():
        for k in range(VIEWS):
            outer_copy(0, k, partner, 0).wait_send()

    def sent(ref, semaphore):
        pltpu.make_async_remote_copy(
            src_ref=ref, dst_ref=ref, send_sem=semaphore, recv_sem=face_recv.at[0],
            device_id=partner, device_id_type=MESH,
        ).wait_send()

    for name, (index, (_, there), _) in ways.items():
        relayed = field.at[0:2, 0:2, :, 0:1] if name[0] == "v" else field.at[0:3, 0:2, :, 0:1]

        @pl.when(there)
        def _():
            sent(field.at[1, 1, core], face_send.at[index])
            sent(relayed, face_send.at[4 + index])

    sent(field.at[:, :, core], core_send.at[0])

    start = jnp.where(last, RAD, 0)
    lane = iota((64, LANES), 1)
    keep = is_edge & (lane >= start) & (lane < start + RAD)
    for h in range(2):
        near_swap[h].wait_recv()
        mine = sums[h, slot] + got_core[h, 1]
        over[h].wait_recv()
        mine = mine + got_chip[h]

        @pl.when(is_edge)
        def _():
            edge_copy(h, 0).wait_recv()
            edge_copy(h, 1).wait_recv()

        edge = got_edge[0, h] + got_edge[1, h]
        for g in range(GROUPS):
            own = pltpu.roll(mine, (8 - g - slot) % 4 * 32, 1)
            sides = []
            for k in range(2):
                rim = pltpu.roll(edge, (start + LANES - 64 * k - RAD * g) % LANES, 1)
                part = own[64 * k : 64 * k + 64] + jnp.where(keep, rim, 0.0)
                sides.append(part.reshape(8, 8, LANES) * (1.0 / (RANK * VIEWS)))
            part = jnp.stack(swap_quads(*sides), axis=1).reshape(16, 8, LANES)
            at = (slice(16 * h, 16 * h + 16), slice(g * 8, g * 8 + 8))
            refined[at] = est[at] * part[:, :, 0:BLOCK]

    for copy in far_swap + near_swap + over + rim_swap:
        copy.wait_send()

    @pl.when(edge_there)
    def _():
        for h in range(2):
            edge_copy(h, 0).wait_send()


def local(estimate, view_tiles, slot_view, psf_taps):
    vmem = pl.BlockSpec(memory_space=pltpu.VMEM)
    hbm = pl.BlockSpec(memory_space=pltpu.HBM)
    tile = view_tiles[0, 0, 0]
    psf = jnp.transpose(psf_taps, (1, 2, 0, 3))
    scratch = [
        pltpu.VMEM(estimate.shape, F32),
        pltpu.VMEM(tile.shape, BF16),
        pltpu.VMEM(psf.shape, F32),
        pltpu.VMEM(slot_view.shape, jnp.int32),
        pltpu.VMEM((256, LANES), BF16),
        pltpu.VMEM((VIEWS, 128, LANES), BF16),
        pltpu.VMEM((2, 128, LANES), BF16),
        pltpu.VMEM((3, 3, 2, 10, 64, LANES), BF16),
        pltpu.VMEM((RANK, 12, 2, 384, LANES), BF16),
        pltpu.VMEM((RANK, 12, 2, 256, LANES), BF16),
        pltpu.VMEM((16, 256, LANES), BF16),
        pltpu.VMEM((24, 256, LANES), BF16),
        pltpu.VMEM((GROUPS, 2, 128, RANK * LANES), BF16),
        pltpu.VMEM((2, 4, 128, LANES), F32),
        pltpu.VMEM((2, 2, 64, LANES), F32),
        pltpu.VMEM((2, 2, 128, LANES), F32),
        pltpu.VMEM((2, 64, LANES), F32),
        pltpu.VMEM((2, 128, LANES), F32),
        pltpu.VMEM((2, 2, 64, LANES), F32),
        pltpu.VMEM((2, 24, LANES), F32),
        pltpu.VMEM((RANK, 128, 256), BF16),
        pltpu.VMEM((RANK, 128, 256), BF16),
        pltpu.VMEM((256, RANK * LANES), BF16),
        pltpu.VMEM((RANK * 128, 256), BF16),
        pltpu.VMEM((2, RANK, 64, 256), BF16),
        pltpu.VMEM((GROUPS, RANK * LANES, 256), BF16),
        pltpu.SemaphoreType.DMA((4,)),
        pltpu.SemaphoreType.DMA((7,)),
        pltpu.SemaphoreType.DMA((6,)),
        pltpu.SemaphoreType.DMA((8,)),
        pltpu.SemaphoreType.DMA((18,)),
        pltpu.SemaphoreType.DMA((1,)),
        pltpu.SemaphoreType.DMA((9,)),
        pltpu.SemaphoreType.DMA((10,)),
        pltpu.SemaphoreType.DMA((12,)),
    ]
    return pl.pallas_call(
        kernel,
        out_shape=pltpu.VMEM(estimate.shape, F32),
        in_specs=[hbm] * 4,
        out_specs=vmem,
        scratch_shapes=scratch,
        compiler_params=pltpu.CompilerParams(
            collective_id=0, has_side_effects=True, vmem_limit_bytes=56 * 1024 * 1024
        ),
    )(*(pltpu.with_memory_space_constraint(a, pltpu.HBM) for a in (estimate, tile, psf, slot_view)))


def solution(mesh):
    placed = (
        P("bx", "by", "vert"),
        P("bx", "by", "vert", None, None, None),
        P("bx", "by", None),
        P(),
    )
    return jax.shard_map(
        local, mesh=mesh, in_specs=placed, out_specs=P("bx", "by", "vert"), check_vma=False
    )
```

```python
import jax
import jax.numpy as jnp
from jax import lax
from jax.experimental import pallas as pl
from jax.experimental.pallas import tpu as pltpu
from jax.sharding import PartitionSpec as P

BACKGROUND = 0.1
MESH = pl.DeviceIdType.MESH
F32, BF16 = jnp.float32, jnp.bfloat16
BLOCK = 32
RAD = 16
TAPS = 33
RANK = 3
VIEWS = 4
GROUPS = 4
LANES = 128


def iota(shape, axis):
    return lax.broadcasted_iota(jnp.int32, shape, axis)


def dot(a, b):
    return jnp.dot(a, b, preferred_element_type=F32)


def band(line, rows, start):
    line = jnp.broadcast_to(line, (rows, LANES))
    return pltpu.roll(line, start % LANES, 1, stride=1, stride_axis=0)


def swap_quads(a, b):
    low, axis = iota(a.shape, a.ndim - 2) < 4, a.ndim - 2
    return jnp.where(low, a, pltpu.roll(b, 4, axis)), jnp.where(low, pltpu.roll(a, 4, axis), b)


def build_taps(psf, slot_view, slot, taps):
    listed = slot_view[...]
    view = jnp.sum(jnp.where(iota(listed.shape, 2) == slot, listed, 0), axis=2, keepdims=True)
    held = iota((VIEWS, TAPS), 0) == view[0]
    mine = jnp.sum(jnp.where(held[None, None], psf[...], 0.0), axis=2)
    mine = (mine / jnp.sum(mine, axis=-1, keepdims=True)).astype(BF16).astype(F32)
    taps[...] = jnp.zeros_like(taps)
    for a in range(3):
        taps[0, 8 * a : 8 * a + RANK, :TAPS] = mine[a]
    flip = (iota((LANES, LANES), 0) + iota((LANES, LANES), 1) == TAPS - 1).astype(BF16)
    taps[1] = dot(taps[0].astype(BF16), flip)


def build_z(taps, wz, wb):
    z_in, z_out = iota((LANES, LANES), 0), iota((LANES, LANES), 1)
    near = jnp.abs(z_in - z_out) <= RAD
    rim, out = iota((32, LANES), 0), iota((32, LANES), 1)
    rim_ok = ((rim < RAD) & (out <= rim)) | ((rim >= RAD) & (out >= rim + 96))
    lane16 = iota((16, LANES), 1)
    for r in range(RANK):
        forward, backward = taps[1, 16 + r : 17 + r, :], taps[0, 16 + r : 17 + r, :]
        columns = slice(r * LANES, (r + 1) * LANES)
        wz[0:128, columns] = jnp.where(near, band(forward, LANES, -RAD), 0.0).astype(BF16)
        wz[128:160, columns] = jnp.where(rim_ok, band(forward, 32, 96), 0.0).astype(BF16)
        wz[160:256, columns] = jnp.zeros((96, LANES), BF16)
        main = jnp.where(near, band(backward, LANES, -RAD), 0.0)
        low = jnp.where(lane16 < RAD, band(backward, 16, 0), 0.0)
        high = jnp.where(lane16 < RAD, band(backward, 16, 96), 0.0)
        for g in range(GROUPS):
            wb[g, r * 128 : r * 128 + 128, 0:128] = (
                pltpu.roll(main, 32 * g, 1) if g else main
            ).astype(BF16)
            wb[g, r * 128 : r * 128 + 128, 128:256] = jnp.zeros((128, LANES), BF16)
            lo, hi = pltpu.roll(low, RAD * g, 1) if g else low, pltpu.roll(high, 64 + RAD * g, 1)
            wb[g, r * 128 : r * 128 + 16, 128:256] = lo.astype(BF16)
            wb[g, r * 128 + 112 : r * 128 + 128, 128:256] = hi.astype(BF16)


def build_x(taps, bx, tx, txb):
    spread = (iota((LANES, 256), 1) == 4 * iota((LANES, 256), 0)).astype(BF16)
    lane, row = iota((LANES, LANES), 1), iota((LANES, LANES), 0)
    low, high = bx > 0, bx < 3

    def tiles(line):
        turned = [band(line[:, i * LANES : (i + 1) * LANES], LANES, 0) for i in range(2)]
        return jnp.where(lane >= row, turned[0], 0.0), jnp.where(lane >= row, turned[1], turned[0])

    wide = [dot(taps[k, 0:8, :].astype(BF16), spread) for k in range(2)]
    for r in range(RANK):
        left, right = tiles(wide[0][r : r + 1])
        tx[r, :, 0:128] = left.astype(BF16)
        tx[r, :, 128:256] = right.astype(BF16)
        left, right = [m[0:64] for m in tiles(wide[1][r : r + 1])]
        txb[0, r, :, 0:128] = jnp.where((lane[0:64] >= 64) | low, left, 0.0).astype(BF16)
        txb[0, r, :, 128:256] = right.astype(BF16)
        txb[1, r, :, 0:128] = left.astype(BF16)
        txb[1, r, :, 128:256] = jnp.where(high, right, 0.0).astype(BF16)


def build_y(taps, by, ty, tyb):
    place = by * BLOCK - RAD + iota((BLOCK, LANES), 1)
    inside = (place >= 0) & (place < 4 * BLOCK)
    plain = [band(taps[0, 8 + r : 9 + r, :], BLOCK, 0) for r in range(RANK)]
    plain += [
        jnp.where(inside, band(taps[1, 8 + r : 9 + r, :], BLOCK, 0), 0.0) for r in range(RANK)
    ]
    plain = jnp.concatenate(plain, axis=0).astype(BF16)
    y, column = iota((LANES, 256), 0), iota((LANES, 256), 1)
    wide = [
        dot(plain, (column == 16 * (y // 4) + 4 * x + y % 4).astype(BF16)).astype(BF16)
        for x in range(4)
    ]
    row, source = iota((LANES, LANES), 0), iota((LANES, LANES), 1)
    order = (row == 16 * (source % 32 // 4) + 4 * (source // 32) + source % 4).astype(BF16)
    for i in range(2 * RANK):
        done = dot(order, jnp.concatenate([m[i * 32 : i * 32 + 32] for m in wide], axis=0)).astype(BF16)
        if i < RANK:
            ty[i] = done
        else:
            tyb[(i - RANK) * 128 : (i - RANK + 1) * 128, :] = done


def kernel(
    est_hbm, tile_hbm, psf_hbm, slot_view_hbm, refined,
    est, tile, psf, slot_view,
    packed, parts, outer, field, after_z, after_x, seen, back_y, back_x, sums, rims,
    got_core, got_rim, got_chip, got_edge,
    taps, tx, ty, wz, tyb, txb, wb,
    load_sem, part_send, part_recv, face_send, face_recv, core_send, core_recv, sum_send, sum_recv,
):
    bx, by, vert = lax.axis_index("bx"), lax.axis_index("by"), lax.axis_index("vert")
    q, slot = vert // VIEWS, vert % VIEWS
    core, chip = slot % 2, slot // 2

    loads = [
        pltpu.make_async_copy(source, target, load_sem.at[i])
        for i, (source, target) in enumerate(
            ((est_hbm, est), (psf_hbm, psf), (slot_view_hbm, slot_view), (tile_hbm, tile))
        )
    ]
    for copy in loads:
        copy.start()

    def at_vert(index):
        return {"vert": index}

    partner = at_vert(q * 4 + chip * 2 + 1 - core)
    above, below = q < 3, q > 0
    first, last = slot == 0, slot == VIEWS - 1
    is_edge = (first & below) | (last & above)

    straight = core == 0

    def block(ju, jv):
        return jnp.where(straight, jv, ju), jnp.where(straight, ju, jv)

    def link(along_u, step):
        x_step = jnp.where(straight == along_u, step, 0)
        x, y = bx + x_step, by + step - x_step
        return {"bx": x, "by": y}, (x >= 0) & (x < 4) & (y >= 0) & (y < 4)

    u_up, u_down, v_up, v_down = link(True, 1), link(True, -1), link(False, 1), link(False, -1)

    def clear(ref):
        ref[...] = jnp.zeros(ref.shape, BF16)

    pl.when(bx == 0)(lambda: clear(field.at[:, 0, core]))
    pl.when(bx == 3)(lambda: clear(field.at[:, 2, core]))
    pl.when(by == 0)(lambda: clear(field.at[0, :, core]))
    pl.when(by == 3)(lambda: clear(field.at[2, :, core]))
    pl.when(~below)(lambda: clear(outer.at[0]))
    pl.when(~above)(lambda: clear(outer.at[1]))

    got_edge[...] = jnp.zeros_like(got_edge)
    barrier = pltpu.get_barrier_semaphore()

    def greet(device):
        pl.semaphore_signal(barrier, inc=1, device_id=device, device_id_type=MESH)

    for k in range(1, VIEWS):
        greet(at_vert(q * 4 + (slot + k) % VIEWS))
    for device, there in (u_up, u_down, v_up, v_down):
        pl.when(there)(lambda device=device: greet(device))

    @pl.when(below)
    def _():
        greet(at_vert(vert - slot - 1))
        pl.when(first)(lambda: greet(at_vert(vert - 3)))

    @pl.when(above)
    def _():
        greet(at_vert(vert - slot + 4))
        pl.when(last)(lambda: greet(at_vert(vert + 3)))

    loads[0].wait()
    groups = est[...].reshape(BLOCK, GROUPS, 8, BLOCK)
    line = jnp.concatenate([groups[:, g].reshape(256, BLOCK) for g in range(GROUPS)], axis=1)
    line = pltpu.roll(line, slot * 32, 1).reshape(16, 2, 8, LANES)
    for side, quads in enumerate(swap_quads(line[:, 0], line[:, 1])):
        packed[side * 128 : side * 128 + 128, :] = quads.reshape(128, LANES).astype(BF16)

    beside = [(there, 1) for _, there in (u_up, u_down, v_up, v_down)] + [(is_edge, 4)]
    beside += [((slot == 1) & above, 1), ((slot == 2) & below, 1)]
    pl.semaphore_wait(barrier, 3 + sum(jnp.where(there, n, 0) for there, n in beside))

    def part_copy(source, send, device, side):
        return pltpu.make_async_remote_copy(
            src_ref=packed.at[pl.ds(side * 128, 128), :], dst_ref=parts.at[source],
            send_sem=part_send.at[send], recv_sem=part_recv.at[source],
            device_id=device, device_id_type=MESH,
        )

    for k in range(1, VIEWS):
        other = (slot + k) % VIEWS
        part_copy(slot, k - 1, at_vert(q * 4 + other), other % 2).start()

    def outer_copy(which, send, device, side):
        return pltpu.make_async_remote_copy(
            src_ref=packed.at[pl.ds(side * 128, 128), :], dst_ref=outer.at[which],
            send_sem=part_send.at[3 + send], recv_sem=part_recv.at[4 + which],
            device_id=device, device_id_type=MESH,
        )

    @pl.when(last & above)
    def _():
        for k in range(VIEWS):
            outer_copy(0, k, at_vert(vert + 1 + k), k % 2).start()

    @pl.when(first & below)
    def _():
        for k in range(VIEWS):
            outer_copy(1, k, at_vert(vert - 4 + k), k % 2).start()

    parts[slot] = packed[pl.ds(core * 128, 128), :]
    loads[1].wait()
    loads[2].wait()
    build_taps(psf, slot_view, slot, taps)
    build_z(taps, wz, wb)

    def assemble():
        for k in range(1, VIEWS):
            part_copy((slot + k) % VIEWS, 0, partner, 0).wait_recv()
        chunk = iota((128, LANES), 1) // 32
        have = [parts[k].astype(F32) for k in range(VIEWS)]
        for g in range(GROUPS):
            line = have[(3 - g) % 4]
            for at in range(3):
                line = jnp.where(chunk == at, have[(at - g) % 4], line)
            if g:
                line = pltpu.roll(line, LANES - 32 * g, 1)
            for tp in range(2):
                field[1, 1, core, 6 * tp + g] = line[64 * tp : 64 * tp + 64].astype(BF16)

    def assemble_rims():
        for k, there in enumerate((below, above)):
            pl.when(there)(lambda k=k: outer_copy(k, 0, partner, 0).wait_recv())
        is_above = iota((128, LANES), 1) % 32 < RAD
        line = jnp.where(is_above, outer[1].astype(F32), outer[0].astype(F32))
        field[1, 1, core, 4:6] = pltpu.roll(line, RAD, 1).astype(BF16).reshape(2, 64, LANES)

    def message(ju, jv, which):
        return field.at[(*block(ju, jv), core, slice(4, 10) if which else slice(0, 4))]

    def face_copy(source, target, which, send, device):
        return pltpu.make_async_remote_copy(
            src_ref=message(*source, which), dst_ref=message(*target, which),
            send_sem=face_send.at[send],
            recv_sem=face_recv.at[which * 9 + target[0] * 3 + target[1]],
            device_id=device, device_id_type=MESH,
        )

    ways = {"u_up": (0, u_up, (0, 1)), "u_down": (1, u_down, (2, 1)), "v_up": (2, v_up, (1, 0)), "v_down": (3, v_down, (1, 2))}

    def send_own(name, which):
        index, (device, there), target = ways[name]
        pl.when(there)(face_copy((1, 1), target, which, index, device).start)

    def relay(name, along, which):
        index, (device, there), target = ways[name]
        source = (along, 1) if name[0] == "v" else (1, along)
        target = (along, target[1]) if name[0] == "v" else (target[0], along)
        pl.when(there)(face_copy(source, target, which, 4 + index, device).start)

    def came(ju, jv, which, over):
        there = ways[f"{over}_{'down' if (jv if over == 'v' else ju) == 0 else 'up'}"][1][1]
        copy = face_copy((ju, jv), (ju, jv), which, 0, partner)
        pl.when(there)(copy.wait_recv)

    def core_copy(jy, jx, side):
        return pltpu.make_async_remote_copy(
            src_ref=field.at[jy, jx, side], dst_ref=field.at[jy, jx, side],
            send_sem=core_send.at[0], recv_sem=core_recv.at[jy * 3 + jx],
            device_id=partner, device_id_type=MESH,
        )

    def pass_on(ju, jv):
        core_copy(*block(ju, jv), core).start()

    def swapped(jy, jx):
        core_copy(jy, jx, 1 - core).wait_recv()

    def forward_z(jy, jx):
        rows = slice(jx * 128, jx * 128 + 128)
        rim = field[jy, jx, :, 4:6].reshape(256, LANES)
        for g in range(GROUPS):
            turned = pltpu.roll(rim, LANES - 32 * g, 1) if g else rim
            main = jnp.concatenate(
                [field[jy, jx, side, 6 * tp + g] for side in range(2) for tp in range(2)], axis=0
            )
            done = dot(jnp.concatenate([main, turned], axis=1), wz[...]).astype(BF16)
            for r in range(RANK):
                after_z[r, jy * GROUPS + g, :, rows, :] = done[:, r * 128 : (r + 1) * 128].reshape(
                    2, 128, LANES
                )

    def forward_x(jy):
        for r in range(RANK):
            for group in (jy * GROUPS, jy * GROUPS + 2):
                for b in range(2):
                    rows = slice(b * 128, b * 128 + 256)
                    both = [after_z[r, group + k // 2, k % 2, rows, :] for k in range(4)]
                    done = dot(tx[r], jnp.concatenate(both, axis=1)).astype(BF16)
                    for k in range(4):
                        after_x[r, group + k // 2, k % 2, b * 128 : b * 128 + 128, :] = done[
                            :, k * 128 : k * 128 + 128
                        ]

    assemble()
    for name in ("u_up", "u_down", "v_up", "v_down"):
        send_own(name, 0)
    assemble_rims()
    for name in ("v_up", "v_down", "u_up", "u_down"):
        send_own(name, 1)
    pass_on(1, 1)
    build_x(taps, bx, tx, txb)
    for side in (0, 2):
        came(side, 1, 0, "u")
    for one, other in ((0, 2), (2, 0)):
        relay("v_up", one, 0)
        relay("v_down", other, 0)
    for side in (0, 2):
        came(1, side, 1, "v")
    for one, other in ((0, 2), (2, 0)):
        relay("u_up", one, 1)
        relay("u_down", other, 1)
    build_y(taps, by, ty, tyb)
    loads[3].wait()

    def order_tile(i, carry):
        quad = tile[pl.ds(4 * i, 4)].astype(F32).reshape(2, 2, 8, 8, LANES)
        sides = swap_quads(quad[:, 0], quad[:, 1])
        rows = jnp.stack([m[x] for m in sides for x in range(2)], axis=1)
        seen[i] = rows.reshape(256, LANES).astype(BF16)
        return carry

    lax.fori_loop(0, 16, order_tile, 0, unroll=4)
    swapped(1, 1)
    forward_z(1, 1)
    for side in (0, 2):
        came(side, 1, 1, "u")
        pass_on(side, 1)
        came(1, side, 0, "v")
        pass_on(1, side)
    for side in (0, 2):
        swapped(1, side)
        swapped(side, 1)
    for side in (0, 2):
        forward_z(1, side)
        forward_z(side, 1)
    waves = (((0, 0), (2, 2)), ((0, 2), (2, 0)))
    for corner in waves[0]:
        came(*corner, 0, "v")
        came(*corner, 1, "u")
        pass_on(*corner)
    forward_x(1)
    for corner in waves[1]:
        came(*corner, 0, "v")
        came(*corner, 1, "u")
        pass_on(*corner)
    for wave in waves:
        for corner in wave:
            swapped(*corner)
        for corner in wave:
            forward_z(*corner)
    for jy in (0, 2):
        forward_x(jy)

    def along_y(step):
        quotient = []
        for b in range(2):
            blurred = None
            for r in range(RANK):
                quads = [
                    after_x[r, 4 * b : 4 * b + 8, :, 16 * i : 16 * i + 16, :].reshape(256, LANES)
                    for i in range(4 * step, 4 * step + 4)
                ]
                part = dot(ty[r], jnp.concatenate(quads, axis=1))
                blurred = part if blurred is None else blurred + part
            rows = slice(128 * b, 128 * b + 128)
            quads = [seen[i, rows, :] for i in range(4 * step, 4 * step + 4)]
            quads = jnp.concatenate(quads, axis=1).astype(F32)
            quotient.append((RANK * quads / (blurred + RANK * BACKGROUND)).astype(BF16))
        quotient = jnp.concatenate(quotient, axis=0)
        for r in range(RANK):
            done = dot(tyb[r * 128 : r * 128 + 128, :], quotient).astype(BF16)
            for k in range(4):
                i = 4 * step + k
                back_y[r * 8 : r * 8 + 8, 16 * i : 16 * i + 16, :] = done[
                    :, k * 128 : k * 128 + 128
                ].reshape(8, 16, LANES)

    def backward_x(half):
        within = slice(half * 64, half * 64 + 192)
        for g in (0, 2):
            for r in range(RANK):
                at = (r * GROUPS + g) * 2
                sides = jnp.concatenate([back_y[at + k, within, :] for k in range(4)], axis=1)
                done = dot(txb[half, r, :, 0:192], sides).astype(BF16)
                for k in range(4):
                    rows = slice(k % 2 * 64, k % 2 * 64 + 64)
                    back_x[g + k // 2, half, rows, r * 128 : (r + 1) * 128] = done[
                        :, k * 128 : k * 128 + 128
                    ]

    def backward_rims(half):
        both = dot(back_x[0, half], wb[0, :, LANES:])
        for g in range(1, GROUPS):
            both = both + dot(back_x[g, half], wb[g, :, LANES:])
        is_low = iota((64, LANES), 1) < 64
        rims[half, 0] = jnp.where(is_low, both[0:64], pltpu.roll(both[64:128], 64, 1))
        rims[half, 1] = jnp.where(is_low, pltpu.roll(both[0:64], 64, 1), both[64:128])

    def backward_z(half):
        for g in range(GROUPS):
            done = dot(back_x[g, half], wb[g, :, :LANES])
            for c in range(4):
                at = (g + c) % 4
                sums[half, c, :, at * 32 : at * 32 + 32] = done[:, at * 32 : at * 32 + 32]

    far = (1 - chip) * 2 + core

    def sum_copy(source, target, index, device):
        return pltpu.make_async_remote_copy(
            src_ref=source, dst_ref=target, send_sem=sum_send.at[index],
            recv_sem=sum_recv.at[index], device_id=device, device_id_type=MESH,
        )

    far_swap = [
        sum_copy(sums.at[h, (1 - chip) * 2 + 1 - core], got_core.at[h, 0], h, partner) for h in range(2)
    ]
    near_swap = [
        sum_copy(sums.at[h, chip * 2 + 1 - core], got_core.at[h, 1], 2 + h, partner) for h in range(2)
    ]
    over = [sum_copy(sums.at[h, far], got_chip.at[h], 4 + h, at_vert(q * 4 + far)) for h in range(2)]
    rim_swap = [sum_copy(rims.at[h, 1 - core], got_rim.at[h], 6 + h, partner) for h in range(2)]
    edge_home = jnp.where(core == 0, vert - slot - 1, vert - slot + 4)
    edge_there = jnp.where(core == 0, q, 3 - q) > 0

    def edge_copy(h, which):
        return pltpu.make_async_remote_copy(
            src_ref=rims.at[h, core], dst_ref=got_edge.at[which, h], send_sem=sum_send.at[8 + h],
            recv_sem=sum_recv.at[8 + 2 * h + which], device_id=at_vert(edge_home), device_id_type=MESH,
        )

    def backward(h):
        backward_x(h)
        backward_rims(h)
        rim_swap[h].start()
        backward_z(h)
        far_swap[h].start()
        near_swap[h].start()

    def pass_over(h):
        rim_swap[h].wait_recv()
        rims[h, core] = rims[h, core] + got_rim[h]
        pl.when(edge_there)(lambda: edge_copy(h, chip).start())
        far_swap[h].wait_recv()
        sums[h, far] = sums[h, far] + got_core[h, 0]
        over[h].start()

    for step in range(3):
        along_y(step)
    backward(0)
    along_y(3)
    pass_over(0)
    backward(1)
    pass_over(1)

    for k in range(1, VIEWS):
        part_copy(slot, k - 1, partner, 0).wait_send()

    @pl.when(is_edge)
    def _():
        for k in range(VIEWS):
            outer_copy(0, k, partner, 0).wait_send()

    def sent(ref, semaphore):
        pltpu.make_async_remote_copy(
            src_ref=ref, dst_ref=ref, send_sem=semaphore, recv_sem=face_recv.at[0],
            device_id=partner, device_id_type=MESH,
        ).wait_send()

    for name, (index, (_, there), _) in ways.items():
        relayed = field.at[0:2, 0:2, :, 0:1] if name[0] == "v" else field.at[0:3, 0:2, :, 0:1]

        @pl.when(there)
        def _():
            sent(field.at[1, 1, core], face_send.at[index])
            sent(relayed, face_send.at[4 + index])

    sent(field.at[:, :, core], core_send.at[0])

    start = jnp.where(last, RAD, 0)
    lane = iota((64, LANES), 1)
    keep = is_edge & (lane >= start) & (lane < start + RAD)
    for h in range(2):
        near_swap[h].wait_recv()
        mine = sums[h, slot] + got_core[h, 1]
        over[h].wait_recv()
        mine = mine + got_chip[h]

        @pl.when(is_edge)
        def _():
            edge_copy(h, 0).wait_recv()
            edge_copy(h, 1).wait_recv()

        edge = got_edge[0, h] + got_edge[1, h]
        for g in range(GROUPS):
            own = pltpu.roll(mine, (8 - g - slot) % 4 * 32, 1)
            sides = []
            for k in range(2):
                rim = pltpu.roll(edge, (start + LANES - 64 * k - RAD * g) % LANES, 1)
                part = own[64 * k : 64 * k + 64] + jnp.where(keep, rim, 0.0)
                sides.append(part.reshape(8, 8, LANES) * (1.0 / (RANK * VIEWS)))
            part = jnp.stack(swap_quads(*sides), axis=1).reshape(16, 8, LANES)
            at = (slice(16 * h, 16 * h + 16), slice(g * 8, g * 8 + 8))
            refined[at] = est[at] * part[:, :, 0:BLOCK]

    for copy in far_swap + near_swap + over + rim_swap:
        copy.wait_send()

    @pl.when(edge_there)
    def _():
        for h in range(2):
            edge_copy(h, 0).wait_send()


def local(estimate, view_tiles, slot_view, psf_taps):
    vmem = pl.BlockSpec(memory_space=pltpu.VMEM)
    hbm = pl.BlockSpec(memory_space=pltpu.HBM)
    tile = view_tiles[0, 0, 0]
    psf = jnp.transpose(psf_taps, (1, 2, 0, 3))
    scratch = [
        pltpu.VMEM(estimate.shape, F32),
        pltpu.VMEM(tile.shape, BF16),
        pltpu.VMEM(psf.shape, F32),
        pltpu.VMEM(slot_view.shape, jnp.int32),
        pltpu.VMEM((256, LANES), BF16),
        pltpu.VMEM((VIEWS, 128, LANES), BF16),
        pltpu.VMEM((2, 128, LANES), BF16),
        pltpu.VMEM((3, 3, 2, 10, 64, LANES), BF16),
        pltpu.VMEM((RANK, 12, 2, 384, LANES), BF16),
        pltpu.VMEM((RANK, 12, 2, 256, LANES), BF16),
        pltpu.VMEM((16, 256, LANES), BF16),
        pltpu.VMEM((24, 256, LANES), BF16),
        pltpu.VMEM((GROUPS, 2, 128, RANK * LANES), BF16),
        pltpu.VMEM((2, 4, 128, LANES), F32),
        pltpu.VMEM((2, 2, 64, LANES), F32),
        pltpu.VMEM((2, 2, 128, LANES), F32),
        pltpu.VMEM((2, 64, LANES), F32),
        pltpu.VMEM((2, 128, LANES), F32),
        pltpu.VMEM((2, 2, 64, LANES), F32),
        pltpu.VMEM((2, 24, LANES), F32),
        pltpu.VMEM((RANK, 128, 256), BF16),
        pltpu.VMEM((RANK, 128, 256), BF16),
        pltpu.VMEM((256, RANK * LANES), BF16),
        pltpu.VMEM((RANK * 128, 256), BF16),
        pltpu.VMEM((2, RANK, 64, 256), BF16),
        pltpu.VMEM((GROUPS, RANK * LANES, 256), BF16),
        pltpu.SemaphoreType.DMA((4,)),
        pltpu.SemaphoreType.DMA((7,)),
        pltpu.SemaphoreType.DMA((6,)),
        pltpu.SemaphoreType.DMA((8,)),
        pltpu.SemaphoreType.DMA((18,)),
        pltpu.SemaphoreType.DMA((1,)),
        pltpu.SemaphoreType.DMA((9,)),
        pltpu.SemaphoreType.DMA((10,)),
        pltpu.SemaphoreType.DMA((12,)),
    ]
    return pl.pallas_call(
        kernel,
        out_shape=pltpu.VMEM(estimate.shape, F32),
        in_specs=[hbm] * 4,
        out_specs=vmem,
        scratch_shapes=scratch,
        compiler_params=pltpu.CompilerParams(
            collective_id=0, has_side_effects=True, vmem_limit_bytes=56 * 1024 * 1024
        ),
    )(*(pltpu.with_memory_space_constraint(a, pltpu.HBM) for a in (estimate, tile, psf, slot_view)))


def solution(mesh):
    placed = (
        P("bx", "by", "vert"),
        P("bx", "by", "vert", None, None, None),
        P("bx", "by", None),
        P(),
    )
    return jax.shard_map(
        local, mesh=mesh, in_specs=placed, out_specs=P("bx", "by", "vert"), check_vma=False
    )
```

```python
import jax
import jax.numpy as jnp
from jax import lax
from jax.experimental import pallas as pl
from jax.experimental.pallas import tpu as pltpu
from jax.sharding import PartitionSpec as P

BACKGROUND = 0.1
MESH = pl.DeviceIdType.MESH
F32, BF16 = jnp.float32, jnp.bfloat16
BLOCK = 32
RAD = 16
TAPS = 33
RANK = 3
VIEWS = 4
GROUPS = 4
LANES = 128


def iota(shape, axis):
    return lax.broadcasted_iota(jnp.int32, shape, axis)


def dot(a, b):
    return jnp.dot(a, b, preferred_element_type=F32)


def band(line, rows, start):
    line = jnp.broadcast_to(line, (rows, LANES))
    return pltpu.roll(line, start % LANES, 1, stride=1, stride_axis=0)


def swap_quads(a, b):
    low, axis = iota(a.shape, a.ndim - 2) < 4, a.ndim - 2
    return jnp.where(low, a, pltpu.roll(b, 4, axis)), jnp.where(low, pltpu.roll(a, 4, axis), b)


def build_taps(psf, slot_view, slot, taps):
    listed = slot_view[...]
    view = jnp.sum(jnp.where(iota(listed.shape, 2) == slot, listed, 0), axis=2, keepdims=True)
    held = iota((VIEWS, TAPS), 0) == view[0]
    mine = jnp.sum(jnp.where(held[None, None], psf[...], 0.0), axis=2)
    mine = (mine / jnp.sum(mine, axis=-1, keepdims=True)).astype(BF16).astype(F32)
    taps[...] = jnp.zeros_like(taps)
    for a in range(3):
        taps[0, 8 * a : 8 * a + RANK, :TAPS] = mine[a]
    flip = (iota((LANES, LANES), 0) + iota((LANES, LANES), 1) == TAPS - 1).astype(BF16)
    taps[1] = dot(taps[0].astype(BF16), flip)


def build_z(taps, wz, wb):
    z_in, z_out = iota((LANES, LANES), 0), iota((LANES, LANES), 1)
    near = jnp.abs(z_in - z_out) <= RAD
    rim, out = iota((32, LANES), 0), iota((32, LANES), 1)
    rim_ok = ((rim < RAD) & (out <= rim)) | ((rim >= RAD) & (out >= rim + 96))
    lane16 = iota((16, LANES), 1)
    for r in range(RANK):
        forward, backward = taps[1, 16 + r : 17 + r, :], taps[0, 16 + r : 17 + r, :]
        columns = slice(r * LANES, (r + 1) * LANES)
        wz[0:128, columns] = jnp.where(near, band(forward, LANES, -RAD), 0.0).astype(BF16)
        wz[128:160, columns] = jnp.where(rim_ok, band(forward, 32, 96), 0.0).astype(BF16)
        wz[160:256, columns] = jnp.zeros((96, LANES), BF16)
        main = jnp.where(near, band(backward, LANES, -RAD), 0.0)
        low = jnp.where(lane16 < RAD, band(backward, 16, 0), 0.0)
        high = jnp.where(lane16 < RAD, band(backward, 16, 96), 0.0)
        for g in range(GROUPS):
            wb[g, r * 128 : r * 128 + 128, 0:128] = (
                pltpu.roll(main, 32 * g, 1) if g else main
            ).astype(BF16)
            wb[g, r * 128 : r * 128 + 128, 128:256] = jnp.zeros((128, LANES), BF16)
            lo, hi = pltpu.roll(low, RAD * g, 1) if g else low, pltpu.roll(high, 64 + RAD * g, 1)
            wb[g, r * 128 : r * 128 + 16, 128:256] = lo.astype(BF16)
            wb[g, r * 128 + 112 : r * 128 + 128, 128:256] = hi.astype(BF16)


def build_x(taps, bx, tx, txb):
    spread = (iota((LANES, 256), 1) == 4 * iota((LANES, 256), 0)).astype(BF16)
    lane, row = iota((LANES, LANES), 1), iota((LANES, LANES), 0)
    low, high = bx > 0, bx < 3

    def tiles(line):
        turned = [band(line[:, i * LANES : (i + 1) * LANES], LANES, 0) for i in range(2)]
        return jnp.where(lane >= row, turned[0], 0.0), jnp.where(lane >= row, turned[1], turned[0])

    wide = [dot(taps[k, 0:8, :].astype(BF16), spread) for k in range(2)]
    for r in range(RANK):
        left, right = tiles(wide[0][r : r + 1])
        tx[r, :, 0:128] = left.astype(BF16)
        tx[r, :, 128:256] = right.astype(BF16)
        left, right = [m[0:64] for m in tiles(wide[1][r : r + 1])]
        txb[0, r, :, 0:128] = jnp.where((lane[0:64] >= 64) | low, left, 0.0).astype(BF16)
        txb[0, r, :, 128:256] = right.astype(BF16)
        txb[1, r, :, 0:128] = left.astype(BF16)
        txb[1, r, :, 128:256] = jnp.where(high, right, 0.0).astype(BF16)


def build_y(taps, by, ty, tyb):
    place = by * BLOCK - RAD + iota((BLOCK, LANES), 1)
    inside = (place >= 0) & (place < 4 * BLOCK)
    plain = [band(taps[0, 8 + r : 9 + r, :], BLOCK, 0) for r in range(RANK)]
    plain += [
        jnp.where(inside, band(taps[1, 8 + r : 9 + r, :], BLOCK, 0), 0.0) for r in range(RANK)
    ]
    plain = jnp.concatenate(plain, axis=0).astype(BF16)
    y, column = iota((LANES, 256), 0), iota((LANES, 256), 1)
    wide = [
        dot(plain, (column == 16 * (y // 4) + 4 * x + y % 4).astype(BF16)).astype(BF16)
        for x in range(4)
    ]
    row, source = iota((LANES, LANES), 0), iota((LANES, LANES), 1)
    order = (row == 16 * (source % 32 // 4) + 4 * (source // 32) + source % 4).astype(BF16)
    for i in range(2 * RANK):
        done = dot(order, jnp.concatenate([m[i * 32 : i * 32 + 32] for m in wide], axis=0)).astype(BF16)
        if i < RANK:
            ty[i] = done
        else:
            tyb[(i - RANK) * 128 : (i - RANK + 1) * 128, :] = done


def kernel(
    est_hbm, tile_hbm, psf_hbm, slot_view_hbm, refined,
    est, tile, psf, slot_view,
    packed, parts, outer, field, after_z, after_x, seen, back_y, back_x, sums, rims,
    got_core, got_chip, got_edge,
    taps, tx, ty, wz, tyb, txb, wb,
    load_sem, part_send, part_recv, face_send, face_recv, core_send, core_recv, sum_send, sum_recv,
):
    bx, by, vert = lax.axis_index("bx"), lax.axis_index("by"), lax.axis_index("vert")
    q, slot = vert // VIEWS, vert % VIEWS
    core, chip = slot % 2, slot // 2

    loads = [
        pltpu.make_async_copy(source, target, load_sem.at[i])
        for i, (source, target) in enumerate(
            ((est_hbm, est), (psf_hbm, psf), (slot_view_hbm, slot_view), (tile_hbm, tile))
        )
    ]
    for copy in loads:
        copy.start()

    def at_vert(index):
        return {"vert": index}

    partner = at_vert(q * 4 + chip * 2 + 1 - core)
    above, below = q < 3, q > 0
    first, last = slot == 0, slot == VIEWS - 1
    is_edge = (first & below) | (last & above)

    straight = core == 0

    def block(ju, jv):
        return jnp.where(straight, jv, ju), jnp.where(straight, ju, jv)

    def link(along_u, step):
        x_step = jnp.where(straight == along_u, step, 0)
        x, y = bx + x_step, by + step - x_step
        return {"bx": x, "by": y}, (x >= 0) & (x < 4) & (y >= 0) & (y < 4)

    u_up, u_down, v_up, v_down = link(True, 1), link(True, -1), link(False, 1), link(False, -1)

    def clear(ref):
        ref[...] = jnp.zeros(ref.shape, BF16)

    pl.when(bx == 0)(lambda: clear(field.at[:, 0, core]))
    pl.when(bx == 3)(lambda: clear(field.at[:, 2, core]))
    pl.when(by == 0)(lambda: clear(field.at[0, :, core]))
    pl.when(by == 3)(lambda: clear(field.at[2, :, core]))
    pl.when(~below)(lambda: clear(outer.at[0]))
    pl.when(~above)(lambda: clear(outer.at[1]))

    got_edge[...] = jnp.zeros_like(got_edge)
    barrier = pltpu.get_barrier_semaphore()

    def greet(device):
        pl.semaphore_signal(barrier, inc=1, device_id=device, device_id_type=MESH)

    for k in range(1, VIEWS):
        greet(at_vert(q * 4 + (slot + k) % VIEWS))
    for device, there in (u_up, u_down, v_up, v_down):
        pl.when(there)(lambda device=device: greet(device))

    @pl.when(below)
    def _():
        greet(at_vert(vert - slot - 1))

        @pl.when(first)
        def _():
            for k in range(2, VIEWS + 1):
                greet(at_vert(vert - k))

    @pl.when(above)
    def _():
        greet(at_vert(vert - slot + 4))

        @pl.when(last)
        def _():
            for k in range(2, VIEWS + 1):
                greet(at_vert(vert + k))

    loads[0].wait()
    groups = est[...].reshape(BLOCK, GROUPS, 8, BLOCK)
    line = jnp.concatenate([groups[:, g].reshape(256, BLOCK) for g in range(GROUPS)], axis=1)
    line = pltpu.roll(line, slot * 32, 1).reshape(16, 2, 8, LANES)
    for side, quads in enumerate(swap_quads(line[:, 0], line[:, 1])):
        packed[side * 128 : side * 128 + 128, :] = quads.reshape(128, LANES).astype(BF16)

    beside = [(there, 1) for _, there in (u_up, u_down, v_up, v_down)] + [(is_edge, 4)]
    beside += [(~last & above, 1), (~first & below, 1)]
    pl.semaphore_wait(barrier, 3 + sum(jnp.where(there, n, 0) for there, n in beside))

    def part_copy(source, send, device, side):
        return pltpu.make_async_remote_copy(
            src_ref=packed.at[pl.ds(side * 128, 128), :], dst_ref=parts.at[source],
            send_sem=part_send.at[send], recv_sem=part_recv.at[source],
            device_id=device, device_id_type=MESH,
        )

    for k in range(1, VIEWS):
        other = (slot + k) % VIEWS
        part_copy(slot, k - 1, at_vert(q * 4 + other), other % 2).start()

    def outer_copy(which, send, device, side):
        return pltpu.make_async_remote_copy(
            src_ref=packed.at[pl.ds(side * 128, 128), :], dst_ref=outer.at[which],
            send_sem=part_send.at[3 + send], recv_sem=part_recv.at[4 + which],
            device_id=device, device_id_type=MESH,
        )

    @pl.when(last & above)
    def _():
        for k in range(VIEWS):
            outer_copy(0, k, at_vert(vert + 1 + k), k % 2).start()

    @pl.when(first & below)
    def _():
        for k in range(VIEWS):
            outer_copy(1, k, at_vert(vert - 4 + k), k % 2).start()

    parts[slot] = packed[pl.ds(core * 128, 128), :]
    loads[1].wait()
    loads[2].wait()
    build_taps(psf, slot_view, slot, taps)
    build_z(taps, wz, wb)

    def assemble():
        for k in range(1, VIEWS):
            part_copy((slot + k) % VIEWS, 0, partner, 0).wait_recv()
        chunk = iota((128, LANES), 1) // 32
        have = [parts[k].astype(F32) for k in range(VIEWS)]
        for g in range(GROUPS):
            line = have[(3 - g) % 4]
            for at in range(3):
                line = jnp.where(chunk == at, have[(at - g) % 4], line)
            if g:
                line = pltpu.roll(line, LANES - 32 * g, 1)
            for tp in range(2):
                field[1, 1, core, 6 * tp + g] = line[64 * tp : 64 * tp + 64].astype(BF16)

    def assemble_rims():
        for k, there in enumerate((below, above)):
            pl.when(there)(lambda k=k: outer_copy(k, 0, partner, 0).wait_recv())
        is_above = iota((128, LANES), 1) % 32 < RAD
        line = jnp.where(is_above, outer[1].astype(F32), outer[0].astype(F32))
        field[1, 1, core, 4:6] = pltpu.roll(line, RAD, 1).astype(BF16).reshape(2, 64, LANES)

    def message(ju, jv, which):
        return field.at[(*block(ju, jv), core, slice(4, 10) if which else slice(0, 4))]

    def face_copy(source, target, which, send, device):
        return pltpu.make_async_remote_copy(
            src_ref=message(*source, which), dst_ref=message(*target, which),
            send_sem=face_send.at[send],
            recv_sem=face_recv.at[which * 9 + target[0] * 3 + target[1]],
            device_id=device, device_id_type=MESH,
        )

    ways = {"u_up": (0, u_up, (0, 1)), "u_down": (1, u_down, (2, 1)), "v_up": (2, v_up, (1, 0)), "v_down": (3, v_down, (1, 2))}

    def send_own(name, which):
        index, (device, there), target = ways[name]
        pl.when(there)(face_copy((1, 1), target, which, index, device).start)

    def relay(name, along, which):
        index, (device, there), target = ways[name]
        source = (along, 1) if name[0] == "v" else (1, along)
        target = (along, target[1]) if name[0] == "v" else (target[0], along)
        pl.when(there)(face_copy(source, target, which, 4 + index, device).start)

    def came(ju, jv, which, over):
        there = ways[f"{over}_{'down' if (jv if over == 'v' else ju) == 0 else 'up'}"][1][1]
        copy = face_copy((ju, jv), (ju, jv), which, 0, partner)
        pl.when(there)(copy.wait_recv)

    def core_copy(jy, jx, side):
        return pltpu.make_async_remote_copy(
            src_ref=field.at[jy, jx, side], dst_ref=field.at[jy, jx, side],
            send_sem=core_send.at[0], recv_sem=core_recv.at[jy * 3 + jx],
            device_id=partner, device_id_type=MESH,
        )

    def pass_on(ju, jv):
        core_copy(*block(ju, jv), core).start()

    def swapped(jy, jx):
        core_copy(jy, jx, 1 - core).wait_recv()

    def forward_z(jy, jx):
        rows = slice(jx * 128, jx * 128 + 128)
        rim = field[jy, jx, :, 4:6].reshape(256, LANES)
        for g in range(GROUPS):
            turned = pltpu.roll(rim, LANES - 32 * g, 1) if g else rim
            main = jnp.concatenate(
                [field[jy, jx, side, 6 * tp + g] for side in range(2) for tp in range(2)], axis=0
            )
            done = dot(jnp.concatenate([main, turned], axis=1), wz[...]).astype(BF16)
            for r in range(RANK):
                after_z[r, jy * GROUPS + g, :, rows, :] = done[:, r * 128 : (r + 1) * 128].reshape(
                    2, 128, LANES
                )

    def forward_x(jy):
        for r in range(RANK):
            for group in (jy * GROUPS, jy * GROUPS + 2):
                for b in range(2):
                    rows = slice(b * 128, b * 128 + 256)
                    both = [after_z[r, group + k // 2, k % 2, rows, :] for k in range(4)]
                    done = dot(tx[r], jnp.concatenate(both, axis=1)).astype(BF16)
                    for k in range(4):
                        after_x[r, group + k // 2, k % 2, b * 128 : b * 128 + 128, :] = done[
                            :, k * 128 : k * 128 + 128
                        ]

    assemble()
    for name in ("u_up", "u_down", "v_up", "v_down"):
        send_own(name, 0)
    assemble_rims()
    for name in ("v_up", "v_down", "u_up", "u_down"):
        send_own(name, 1)
    pass_on(1, 1)
    build_x(taps, bx, tx, txb)
    for side in (0, 2):
        came(side, 1, 0, "u")
    for one, other in ((0, 2), (2, 0)):
        relay("v_up", one, 0)
        relay("v_down", other, 0)
    for side in (0, 2):
        came(1, side, 1, "v")
    for one, other in ((0, 2), (2, 0)):
        relay("u_up", one, 1)
        relay("u_down", other, 1)
    build_y(taps, by, ty, tyb)
    loads[3].wait()

    def order_tile(i, carry):
        quad = tile[pl.ds(4 * i, 4)].astype(F32).reshape(2, 2, 8, 8, LANES)
        sides = swap_quads(quad[:, 0], quad[:, 1])
        rows = jnp.stack([m[x] for m in sides for x in range(2)], axis=1)
        seen[i] = rows.reshape(256, LANES).astype(BF16)
        return carry

    lax.fori_loop(0, 16, order_tile, 0, unroll=4)
    swapped(1, 1)
    forward_z(1, 1)
    for side in (0, 2):
        came(side, 1, 1, "u")
        pass_on(side, 1)
        came(1, side, 0, "v")
        pass_on(1, side)
    for side in (0, 2):
        swapped(1, side)
        swapped(side, 1)
    for side in (0, 2):
        forward_z(1, side)
        forward_z(side, 1)
    waves = (((0, 0), (2, 2)), ((0, 2), (2, 0)))
    for corner in waves[0]:
        came(*corner, 0, "v")
        came(*corner, 1, "u")
        pass_on(*corner)
    forward_x(1)
    for corner in waves[1]:
        came(*corner, 0, "v")
        came(*corner, 1, "u")
        pass_on(*corner)
    for wave in waves:
        for corner in wave:
            swapped(*corner)
        for corner in wave:
            forward_z(*corner)
    for jy in (0, 2):
        forward_x(jy)

    def along_y(step):
        quotient = []
        for b in range(2):
            blurred = None
            for r in range(RANK):
                quads = [
                    after_x[r, 4 * b : 4 * b + 8, :, 16 * i : 16 * i + 16, :].reshape(256, LANES)
                    for i in range(4 * step, 4 * step + 4)
                ]
                part = dot(ty[r], jnp.concatenate(quads, axis=1))
                blurred = part if blurred is None else blurred + part
            rows = slice(128 * b, 128 * b + 128)
            quads = [seen[i, rows, :] for i in range(4 * step, 4 * step + 4)]
            quads = jnp.concatenate(quads, axis=1).astype(F32)
            quotient.append((RANK * quads / (blurred + RANK * BACKGROUND)).astype(BF16))
        quotient = jnp.concatenate(quotient, axis=0)
        for r in range(RANK):
            done = dot(tyb[r * 128 : r * 128 + 128, :], quotient).astype(BF16)
            for k in range(4):
                i = 4 * step + k
                back_y[r * 8 : r * 8 + 8, 16 * i : 16 * i + 16, :] = done[
                    :, k * 128 : k * 128 + 128
                ].reshape(8, 16, LANES)

    def backward_x(half):
        within = slice(half * 64, half * 64 + 192)
        for g in (0, 2):
            for r in range(RANK):
                at = (r * GROUPS + g) * 2
                sides = jnp.concatenate([back_y[at + k, within, :] for k in range(4)], axis=1)
                done = dot(txb[half, r, :, 0:192], sides).astype(BF16)
                for k in range(4):
                    rows = slice(k % 2 * 64, k % 2 * 64 + 64)
                    back_x[g + k // 2, half, rows, r * 128 : (r + 1) * 128] = done[
                        :, k * 128 : k * 128 + 128
                    ]

    def backward_z(half):
        parts_z = [dot(back_x[g, half], wb[g]) for g in range(GROUPS)]
        both = (parts_z[0] + parts_z[1] + (parts_z[2] + parts_z[3]))[:, LANES:]
        is_low = iota((64, LANES), 1) < 64
        rims[half, 0] = jnp.where(is_low, both[0:64], pltpu.roll(both[64:128], 64, 1))
        rims[half, 1] = jnp.where(is_low, pltpu.roll(both[0:64], 64, 1), both[64:128])
        for which in range(2):
            pl.when((below, above)[which])(rim_copy(half, which).start)
        for g in range(GROUPS):
            for c in range(4):
                at = (g + c) % 4
                sums[half, c, :, at * 32 : at * 32 + 32] = parts_z[g][:, at * 32 : at * 32 + 32]

    far = (1 - chip) * 2 + core

    def sum_copy(source, target, index, device):
        return pltpu.make_async_remote_copy(
            src_ref=source, dst_ref=target, send_sem=sum_send.at[index],
            recv_sem=sum_recv.at[index], device_id=device, device_id_type=MESH,
        )

    far_swap = [
        sum_copy(sums.at[h, (1 - chip) * 2 + 1 - core], got_core.at[h, 0], h, partner) for h in range(2)
    ]
    near_swap = [
        sum_copy(sums.at[h, chip * 2 + 1 - core], got_core.at[h, 1], 2 + h, partner) for h in range(2)
    ]
    over = [sum_copy(sums.at[h, far], got_chip.at[h], 4 + h, at_vert(q * 4 + far)) for h in range(2)]

    def rim_copy(h, which):
        home = (vert - slot - 1, vert - slot + 4)[which]
        return pltpu.make_async_remote_copy(
            src_ref=rims.at[h, which], dst_ref=got_edge.at[slot, h], send_sem=sum_send.at[6 + 2 * h + which],
            recv_sem=sum_recv.at[6 + 2 * slot + h], device_id=at_vert(home), device_id_type=MESH,
        )

    def rim_came(h):
        for k in range(VIEWS):
            pltpu.make_async_remote_copy(
                src_ref=rims.at[h, 0], dst_ref=got_edge.at[k, h], send_sem=sum_send.at[6],
                recv_sem=sum_recv.at[6 + 2 * k + h], device_id=partner, device_id_type=MESH,
            ).wait_recv()

    def backward(h):
        backward_x(h)
        backward_z(h)
        far_swap[h].start()
        near_swap[h].start()

    def pass_over(h):
        far_swap[h].wait_recv()
        sums[h, far] = sums[h, far] + got_core[h, 0]
        over[h].start()

    for step in range(3):
        along_y(step)
    backward(0)
    along_y(3)
    pass_over(0)
    backward(1)
    pass_over(1)

    for k in range(1, VIEWS):
        part_copy(slot, k - 1, partner, 0).wait_send()

    @pl.when(is_edge)
    def _():
        for k in range(VIEWS):
            outer_copy(0, k, partner, 0).wait_send()

    def sent(ref, semaphore):
        pltpu.make_async_remote_copy(
            src_ref=ref, dst_ref=ref, send_sem=semaphore, recv_sem=face_recv.at[0],
            device_id=partner, device_id_type=MESH,
        ).wait_send()

    for name, (index, (_, there), _) in ways.items():
        relayed = field.at[0:2, 0:2, :, 0:1] if name[0] == "v" else field.at[0:3, 0:2, :, 0:1]

        @pl.when(there)
        def _():
            sent(field.at[1, 1, core], face_send.at[index])
            sent(relayed, face_send.at[4 + index])

    sent(field.at[:, :, core], core_send.at[0])

    start = jnp.where(last, RAD, 0)
    lane = iota((64, LANES), 1)
    keep = is_edge & (lane >= start) & (lane < start + RAD)
    for h in range(2):
        near_swap[h].wait_recv()
        mine = sums[h, slot] + got_core[h, 1]
        over[h].wait_recv()
        mine = mine + got_chip[h]

        pl.when(is_edge)(lambda: rim_came(h))
        edge = got_edge[0, h] + got_edge[1, h] + (got_edge[2, h] + got_edge[3, h])
        for g in range(GROUPS):
            own = pltpu.roll(mine, (8 - g - slot) % 4 * 32, 1)
            sides = []
            for k in range(2):
                rim = pltpu.roll(edge, (start + LANES - 64 * k - RAD * g) % LANES, 1)
                part = own[64 * k : 64 * k + 64] + jnp.where(keep, rim, 0.0)
                sides.append(part.reshape(8, 8, LANES) * (1.0 / (RANK * VIEWS)))
            part = jnp.stack(swap_quads(*sides), axis=1).reshape(16, 8, LANES)
            at = (slice(16 * h, 16 * h + 16), slice(g * 8, g * 8 + 8))
            refined[at] = est[at] * part[:, :, 0:BLOCK]

    for copy in far_swap + near_swap + over:
        copy.wait_send()
    for which in range(2):

        @pl.when((below, above)[which])
        def _():
            for h in range(2):
                rim_copy(h, which).wait_send()


def local(estimate, view_tiles, slot_view, psf_taps):
    vmem = pl.BlockSpec(memory_space=pltpu.VMEM)
    hbm = pl.BlockSpec(memory_space=pltpu.HBM)
    tile = view_tiles[0, 0, 0]
    psf = jnp.transpose(psf_taps, (1, 2, 0, 3))
    scratch = [
        pltpu.VMEM(estimate.shape, F32),
        pltpu.VMEM(tile.shape, BF16),
        pltpu.VMEM(psf.shape, F32),
        pltpu.VMEM(slot_view.shape, jnp.int32),
        pltpu.VMEM((256, LANES), BF16),
        pltpu.VMEM((VIEWS, 128, LANES), BF16),
        pltpu.VMEM((2, 128, LANES), BF16),
        pltpu.VMEM((3, 3, 2, 10, 64, LANES), BF16),
        pltpu.VMEM((RANK, 12, 2, 384, LANES), BF16),
        pltpu.VMEM((RANK, 12, 2, 256, LANES), BF16),
        pltpu.VMEM((16, 256, LANES), BF16),
        pltpu.VMEM((24, 256, LANES), BF16),
        pltpu.VMEM((GROUPS, 2, 128, RANK * LANES), BF16),
        pltpu.VMEM((2, 4, 128, LANES), F32),
        pltpu.VMEM((2, 2, 64, LANES), F32),
        pltpu.VMEM((2, 2, 128, LANES), F32),
        pltpu.VMEM((2, 128, LANES), F32),
        pltpu.VMEM((VIEWS, 2, 64, LANES), F32),
        pltpu.VMEM((2, 24, LANES), F32),
        pltpu.VMEM((RANK, 128, 256), BF16),
        pltpu.VMEM((RANK, 128, 256), BF16),
        pltpu.VMEM((256, RANK * LANES), BF16),
        pltpu.VMEM((RANK * 128, 256), BF16),
        pltpu.VMEM((2, RANK, 64, 256), BF16),
        pltpu.VMEM((GROUPS, RANK * LANES, 256), BF16),
        pltpu.SemaphoreType.DMA((4,)),
        pltpu.SemaphoreType.DMA((7,)),
        pltpu.SemaphoreType.DMA((6,)),
        pltpu.SemaphoreType.DMA((8,)),
        pltpu.SemaphoreType.DMA((18,)),
        pltpu.SemaphoreType.DMA((1,)),
        pltpu.SemaphoreType.DMA((9,)),
        pltpu.SemaphoreType.DMA((10,)),
        pltpu.SemaphoreType.DMA((14,)),
    ]
    return pl.pallas_call(
        kernel,
        out_shape=pltpu.VMEM(estimate.shape, F32),
        in_specs=[hbm] * 4,
        out_specs=vmem,
        scratch_shapes=scratch,
        compiler_params=pltpu.CompilerParams(
            collective_id=0, has_side_effects=True, vmem_limit_bytes=56 * 1024 * 1024
        ),
    )(*(pltpu.with_memory_space_constraint(a, pltpu.HBM) for a in (estimate, tile, psf, slot_view)))


def solution(mesh):
    placed = (
        P("bx", "by", "vert"),
        P("bx", "by", "vert", None, None, None),
        P("bx", "by", None),
        P(),
    )
    return jax.shard_map(
        local, mesh=mesh, in_specs=placed, out_specs=P("bx", "by", "vert"), check_vma=False
    )
```

```python
import jax
import jax.numpy as jnp
from jax import lax
from jax.experimental import pallas as pl
from jax.experimental.pallas import tpu as pltpu
from jax.sharding import PartitionSpec as P

BACKGROUND = 0.1
MESH = pl.DeviceIdType.MESH
F32, BF16 = jnp.float32, jnp.bfloat16
BLOCK = 32
RAD = 16
TAPS = 33
RANK = 3
VIEWS = 4
GROUPS = 4
LANES = 128


def iota(shape, axis):
    return lax.broadcasted_iota(jnp.int32, shape, axis)


def dot(a, b):
    return jnp.dot(a, b, preferred_element_type=F32)


def band(line, rows, start):
    line = jnp.broadcast_to(line, (rows, LANES))
    return pltpu.roll(line, start % LANES, 1, stride=1, stride_axis=0)


def swap_quads(a, b):
    low, axis = iota(a.shape, a.ndim - 2) < 4, a.ndim - 2
    return jnp.where(low, a, pltpu.roll(b, 4, axis)), jnp.where(low, pltpu.roll(a, 4, axis), b)


def build_taps(psf, slot_view, slot, taps):
    listed = slot_view[...]
    view = jnp.sum(jnp.where(iota(listed.shape, 2) == slot, listed, 0), axis=2, keepdims=True)
    held = iota((VIEWS, TAPS), 0) == view[0]
    mine = jnp.sum(jnp.where(held[None, None], psf[...], 0.0), axis=2)
    mine = (mine / jnp.sum(mine, axis=-1, keepdims=True)).astype(BF16).astype(F32)
    taps[...] = jnp.zeros_like(taps)
    for a in range(3):
        taps[0, 8 * a : 8 * a + RANK, :TAPS] = mine[a]
    flip = (iota((LANES, LANES), 0) + iota((LANES, LANES), 1) == TAPS - 1).astype(BF16)
    taps[1] = dot(taps[0].astype(BF16), flip)


def build_z(taps, wz, wb):
    z_in, z_out = iota((LANES, LANES), 0), iota((LANES, LANES), 1)
    near = jnp.abs(z_in - z_out) <= RAD
    rim, out = iota((32, LANES), 0), iota((32, LANES), 1)
    rim_ok = ((rim < RAD) & (out <= rim)) | ((rim >= RAD) & (out >= rim + 96))
    lane16 = iota((16, LANES), 1)
    for r in range(RANK):
        forward, backward = taps[1, 16 + r : 17 + r, :], taps[0, 16 + r : 17 + r, :]
        columns = slice(r * LANES, (r + 1) * LANES)
        wz[0:128, columns] = jnp.where(near, band(forward, LANES, -RAD), 0.0).astype(BF16)
        wz[128:160, columns] = jnp.where(rim_ok, band(forward, 32, 96), 0.0).astype(BF16)
        wz[160:256, columns] = jnp.zeros((96, LANES), BF16)
        main = jnp.where(near, band(backward, LANES, -RAD), 0.0)
        low = jnp.where(lane16 < RAD, band(backward, 16, 0), 0.0)
        high = jnp.where(lane16 < RAD, band(backward, 16, 96), 0.0)
        for g in range(GROUPS):
            wb[g, r * 128 : r * 128 + 128, 0:128] = (
                pltpu.roll(main, 32 * g, 1) if g else main
            ).astype(BF16)
            wb[g, r * 128 : r * 128 + 128, 128:256] = jnp.zeros((128, LANES), BF16)
            lo, hi = pltpu.roll(low, RAD * g, 1) if g else low, pltpu.roll(high, 64 + RAD * g, 1)
            wb[g, r * 128 : r * 128 + 16, 128:256] = lo.astype(BF16)
            wb[g, r * 128 + 112 : r * 128 + 128, 128:256] = hi.astype(BF16)


def build_x(taps, bx, tx, txb):
    spread = (iota((LANES, 256), 1) == 4 * iota((LANES, 256), 0)).astype(BF16)
    lane, row = iota((LANES, LANES), 1), iota((LANES, LANES), 0)
    low, high = bx > 0, bx < 3

    def tiles(line):
        turned = [band(line[:, i * LANES : (i + 1) * LANES], LANES, 0) for i in range(2)]
        return jnp.where(lane >= row, turned[0], 0.0), jnp.where(lane >= row, turned[1], turned[0])

    wide = [dot(taps[k, 0:8, :].astype(BF16), spread) for k in range(2)]
    for r in range(RANK):
        left, right = tiles(wide[0][r : r + 1])
        tx[r, :, 0:128] = left.astype(BF16)
        tx[r, :, 128:256] = right.astype(BF16)
        left, right = [m[0:64] for m in tiles(wide[1][r : r + 1])]
        txb[0, r, :, 0:128] = jnp.where((lane[0:64] >= 64) | low, left, 0.0).astype(BF16)
        txb[0, r, :, 128:256] = right.astype(BF16)
        txb[1, r, :, 0:128] = left.astype(BF16)
        txb[1, r, :, 128:256] = jnp.where(high, right, 0.0).astype(BF16)


def build_y(taps, by, ty, tyb):
    place = by * BLOCK - RAD + iota((BLOCK, LANES), 1)
    inside = (place >= 0) & (place < 4 * BLOCK)
    plain = [band(taps[0, 8 + r : 9 + r, :], BLOCK, 0) for r in range(RANK)]
    plain += [
        jnp.where(inside, band(taps[1, 8 + r : 9 + r, :], BLOCK, 0), 0.0) for r in range(RANK)
    ]
    plain = jnp.concatenate(plain, axis=0).astype(BF16)
    y, column = iota((LANES, 256), 0), iota((LANES, 256), 1)
    wide = [
        dot(plain, (column == 16 * (y // 4) + 4 * x + y % 4).astype(BF16)).astype(BF16)
        for x in range(4)
    ]
    row, source = iota((LANES, LANES), 0), iota((LANES, LANES), 1)
    order = (row == 16 * (source % 32 // 4) + 4 * (source // 32) + source % 4).astype(BF16)
    for i in range(2 * RANK):
        done = dot(order, jnp.concatenate([m[i * 32 : i * 32 + 32] for m in wide], axis=0)).astype(BF16)
        if i < RANK:
            ty[i] = done
        else:
            tyb[(i - RANK) * 128 : (i - RANK + 1) * 128, :] = done


def kernel(
    est_hbm, tile_hbm, psf_hbm, slot_view_hbm, refined,
    est, tile, psf, slot_view,
    packed, parts, outer, field, after_z, after_x, seen, back_y, back_x, sums, rims,
    got_core, got_chip, got_edge,
    taps, tx, ty, wz, tyb, txb, wb,
    load_sem, part_send, part_recv, face_send, face_recv, core_send, core_recv, sum_send, sum_recv, ready,
):
    bx, by, vert = lax.axis_index("bx"), lax.axis_index("by"), lax.axis_index("vert")
    q, slot = vert // VIEWS, vert % VIEWS
    core, chip = slot % 2, slot // 2

    loads = [
        pltpu.make_async_copy(source, target, load_sem.at[i])
        for i, (source, target) in enumerate(
            ((est_hbm, est), (psf_hbm, psf), (slot_view_hbm, slot_view), (tile_hbm, tile))
        )
    ]
    for copy in loads:
        copy.start()

    def at_vert(index):
        return {"vert": index}

    partner = at_vert(q * 4 + chip * 2 + 1 - core)
    above, below = q < 3, q > 0
    first, last = slot == 0, slot == VIEWS - 1
    is_edge = (first & below) | (last & above)

    straight = core == 0

    def block(ju, jv):
        return jnp.where(straight, jv, ju), jnp.where(straight, ju, jv)

    def link(along_u, step):
        x_step = jnp.where(straight == along_u, step, 0)
        x, y = bx + x_step, by + step - x_step
        return {"bx": x, "by": y}, (x >= 0) & (x < 4) & (y >= 0) & (y < 4)

    u_up, u_down, v_up, v_down = link(True, 1), link(True, -1), link(False, 1), link(False, -1)

    def clear(ref):
        ref[...] = jnp.zeros(ref.shape, BF16)

    pl.when(bx == 0)(lambda: clear(field.at[:, 0, core]))
    pl.when(bx == 3)(lambda: clear(field.at[:, 2, core]))
    pl.when(by == 0)(lambda: clear(field.at[0, :, core]))
    pl.when(by == 3)(lambda: clear(field.at[2, :, core]))
    pl.when(~below)(lambda: clear(outer.at[0]))
    pl.when(~above)(lambda: clear(outer.at[1]))

    got_edge[...] = jnp.zeros_like(got_edge)
    barrier = pltpu.get_barrier_semaphore()

    def greet(device):
        pl.semaphore_signal(barrier, inc=1, device_id=device, device_id_type=MESH)

    for k in range(1, VIEWS):
        greet(at_vert(q * 4 + (slot + k) % VIEWS))
    for device, there in (u_up, u_down, v_up, v_down):
        pl.when(there)(lambda device=device: greet(device))

    @pl.when(above)
    def _():
        greet(at_vert(vert - slot + 4))

        @pl.when(last)
        def _():
            for k in range(2, VIEWS + 1):
                greet(at_vert(vert + k))

    loads[0].wait()
    groups = est[...].reshape(BLOCK, GROUPS, 8, BLOCK)
    line = jnp.concatenate([groups[:, g].reshape(256, BLOCK) for g in range(GROUPS)], axis=1)
    line = pltpu.roll(line, slot * 32, 1).reshape(16, 2, 8, LANES)
    for side, quads in enumerate(swap_quads(line[:, 0], line[:, 1])):
        packed[side * 128 : side * 128 + 128, :] = quads.reshape(128, LANES).astype(BF16)

    beside = [(there, 1) for _, there in (u_up, u_down, v_up, v_down)]
    beside += [(first & below, VIEWS), (~first & below, 1)]
    pl.semaphore_wait(barrier, 3 + sum(jnp.where(there, n, 0) for there, n in beside))

    def answer(device):
        pl.semaphore_signal(ready, inc=1, device_id=device, device_id_type=MESH)

    @pl.when(first & below)
    def _():
        for k in range(1, VIEWS + 1):
            answer(at_vert(vert - k))

    pl.when(~first & below)(lambda: answer(at_vert(vert - slot - 1)))

    def part_copy(source, send, device, side):
        return pltpu.make_async_remote_copy(
            src_ref=packed.at[pl.ds(side * 128, 128), :], dst_ref=parts.at[source],
            send_sem=part_send.at[send], recv_sem=part_recv.at[source],
            device_id=device, device_id_type=MESH,
        )

    for k in range(1, VIEWS):
        other = (slot + k) % VIEWS
        part_copy(slot, k - 1, at_vert(q * 4 + other), other % 2).start()

    def outer_copy(which, send, device, side):
        return pltpu.make_async_remote_copy(
            src_ref=packed.at[pl.ds(side * 128, 128), :], dst_ref=outer.at[which],
            send_sem=part_send.at[3 + send], recv_sem=part_recv.at[4 + which],
            device_id=device, device_id_type=MESH,
        )

    @pl.when(first & below)
    def _():
        for k in range(VIEWS):
            outer_copy(1, k, at_vert(vert - 4 + k), k % 2).start()

    parts[slot] = packed[pl.ds(core * 128, 128), :]
    loads[1].wait()
    loads[2].wait()
    build_taps(psf, slot_view, slot, taps)
    build_z(taps, wz, wb)

    def assemble():
        for k in range(1, VIEWS):
            part_copy((slot + k) % VIEWS, 0, partner, 0).wait_recv()
        chunk = iota((128, LANES), 1) // 32
        have = [parts[k].astype(F32) for k in range(VIEWS)]
        for g in range(GROUPS):
            line = have[(3 - g) % 4]
            for at in range(3):
                line = jnp.where(chunk == at, have[(at - g) % 4], line)
            if g:
                line = pltpu.roll(line, LANES - 32 * g, 1)
            for tp in range(2):
                field[1, 1, core, 6 * tp + g] = line[64 * tp : 64 * tp + 64].astype(BF16)

    def assemble_rims():
        for k, there in enumerate((below, above)):
            pl.when(there)(lambda k=k: outer_copy(k, 0, partner, 0).wait_recv())
        is_above = iota((128, LANES), 1) % 32 < RAD
        line = jnp.where(is_above, outer[1].astype(F32), outer[0].astype(F32))
        field[1, 1, core, 4:6] = pltpu.roll(line, RAD, 1).astype(BF16).reshape(2, 64, LANES)

    def message(ju, jv, which):
        return field.at[(*block(ju, jv), core, slice(4, 10) if which else slice(0, 4))]

    def face_copy(source, target, which, send, device):
        return pltpu.make_async_remote_copy(
            src_ref=message(*source, which), dst_ref=message(*target, which),
            send_sem=face_send.at[send],
            recv_sem=face_recv.at[which * 9 + target[0] * 3 + target[1]],
            device_id=device, device_id_type=MESH,
        )

    ways = {"u_up": (0, u_up, (0, 1)), "u_down": (1, u_down, (2, 1)), "v_up": (2, v_up, (1, 0)), "v_down": (3, v_down, (1, 2))}

    def send_own(name, which):
        index, (device, there), target = ways[name]
        pl.when(there)(face_copy((1, 1), target, which, index, device).start)

    def relay(name, along, which):
        index, (device, there), target = ways[name]
        source = (along, 1) if name[0] == "v" else (1, along)
        target = (along, target[1]) if name[0] == "v" else (target[0], along)
        pl.when(there)(face_copy(source, target, which, 4 + index, device).start)

    def came(ju, jv, which, over):
        there = ways[f"{over}_{'down' if (jv if over == 'v' else ju) == 0 else 'up'}"][1][1]
        copy = face_copy((ju, jv), (ju, jv), which, 0, partner)
        pl.when(there)(copy.wait_recv)

    def core_copy(jy, jx, side):
        return pltpu.make_async_remote_copy(
            src_ref=field.at[jy, jx, side], dst_ref=field.at[jy, jx, side],
            send_sem=core_send.at[0], recv_sem=core_recv.at[jy * 3 + jx],
            device_id=partner, device_id_type=MESH,
        )

    def pass_on(ju, jv):
        core_copy(*block(ju, jv), core).start()

    def swapped(jy, jx):
        core_copy(jy, jx, 1 - core).wait_recv()

    def forward_z(jy, jx):
        rows = slice(jx * 128, jx * 128 + 128)
        rim = field[jy, jx, :, 4:6].reshape(256, LANES)
        for g in range(GROUPS):
            turned = pltpu.roll(rim, LANES - 32 * g, 1) if g else rim
            main = jnp.concatenate(
                [field[jy, jx, side, 6 * tp + g] for side in range(2) for tp in range(2)], axis=0
            )
            done = dot(jnp.concatenate([main, turned], axis=1), wz[...]).astype(BF16)
            for r in range(RANK):
                after_z[r, jy * GROUPS + g, :, rows, :] = done[:, r * 128 : (r + 1) * 128].reshape(
                    2, 128, LANES
                )

    def forward_x(jy):
        for r in range(RANK):
            for group in (jy * GROUPS, jy * GROUPS + 2):
                for b in range(2):
                    rows = slice(b * 128, b * 128 + 256)
                    both = [after_z[r, group + k // 2, k % 2, rows, :] for k in range(4)]
                    done = dot(tx[r], jnp.concatenate(both, axis=1)).astype(BF16)
                    for k in range(4):
                        after_x[r, group + k // 2, k % 2, b * 128 : b * 128 + 128, :] = done[
                            :, k * 128 : k * 128 + 128
                        ]

    assemble()
    for name in ("u_up", "u_down", "v_up", "v_down"):
        send_own(name, 0)

    @pl.when(last & above)
    def _():
        pl.semaphore_wait(ready, VIEWS)
        for k in range(VIEWS):
            outer_copy(0, k, at_vert(vert + 1 + k), k % 2).start()

    assemble_rims()
    for name in ("v_up", "v_down", "u_up", "u_down"):
        send_own(name, 1)
    pass_on(1, 1)
    build_x(taps, bx, tx, txb)
    for side in (0, 2):
        came(side, 1, 0, "u")
    for one, other in ((0, 2), (2, 0)):
        relay("v_up", one, 0)
        relay("v_down", other, 0)
    for side in (0, 2):
        came(1, side, 1, "v")
    for one, other in ((0, 2), (2, 0)):
        relay("u_up", one, 1)
        relay("u_down", other, 1)
    build_y(taps, by, ty, tyb)
    loads[3].wait()

    def order_tile(i, carry):
        quad = tile[pl.ds(4 * i, 4)].astype(F32).reshape(2, 2, 8, 8, LANES)
        sides = swap_quads(quad[:, 0], quad[:, 1])
        rows = jnp.stack([m[x] for m in sides for x in range(2)], axis=1)
        seen[i] = rows.reshape(256, LANES).astype(BF16)
        return carry

    lax.fori_loop(0, 16, order_tile, 0, unroll=4)
    swapped(1, 1)
    forward_z(1, 1)
    for side in (0, 2):
        came(side, 1, 1, "u")
        pass_on(side, 1)
        came(1, side, 0, "v")
        pass_on(1, side)
    for side in (0, 2):
        swapped(1, side)
        swapped(side, 1)
    for side in (0, 2):
        forward_z(1, side)
        forward_z(side, 1)
    waves = (((0, 0), (2, 2)), ((0, 2), (2, 0)))
    for corner in waves[0]:
        came(*corner, 0, "v")
        came(*corner, 1, "u")
        pass_on(*corner)
    forward_x(1)
    for corner in waves[1]:
        came(*corner, 0, "v")
        came(*corner, 1, "u")
        pass_on(*corner)
    for wave in waves:
        for corner in wave:
            swapped(*corner)
        for corner in wave:
            forward_z(*corner)
    for jy in (0, 2):
        forward_x(jy)

    def along_y(step):
        quotient = []
        for b in range(2):
            blurred = None
            for r in range(RANK):
                quads = [
                    after_x[r, 4 * b : 4 * b + 8, :, 16 * i : 16 * i + 16, :].reshape(256, LANES)
                    for i in range(4 * step, 4 * step + 4)
                ]
                part = dot(ty[r], jnp.concatenate(quads, axis=1))
                blurred = part if blurred is None else blurred + part
            rows = slice(128 * b, 128 * b + 128)
            quads = [seen[i, rows, :] for i in range(4 * step, 4 * step + 4)]
            quads = jnp.concatenate(quads, axis=1).astype(F32)
            quotient.append((RANK * quads / (blurred + RANK * BACKGROUND)).astype(BF16))
        quotient = jnp.concatenate(quotient, axis=0)
        for r in range(RANK):
            done = dot(tyb[r * 128 : r * 128 + 128, :], quotient).astype(BF16)
            for k in range(4):
                i = 4 * step + k
                back_y[r * 8 : r * 8 + 8, 16 * i : 16 * i + 16, :] = done[
                    :, k * 128 : k * 128 + 128
                ].reshape(8, 16, LANES)

    def backward_x(half):
        within = slice(half * 64, half * 64 + 192)
        for g in (0, 2):
            for r in range(RANK):
                at = (r * GROUPS + g) * 2
                sides = jnp.concatenate([back_y[at + k, within, :] for k in range(4)], axis=1)
                done = dot(txb[half, r, :, 0:192], sides).astype(BF16)
                for k in range(4):
                    rows = slice(k % 2 * 64, k % 2 * 64 + 64)
                    back_x[g + k // 2, half, rows, r * 128 : (r + 1) * 128] = done[
                        :, k * 128 : k * 128 + 128
                    ]

    def backward_z(half):
        parts_z = [dot(back_x[g, half], wb[g]) for g in range(GROUPS)]
        both = (parts_z[0] + parts_z[1] + (parts_z[2] + parts_z[3]))[:, LANES:]
        is_low = iota((64, LANES), 1) < 64
        rims[half, 0] = jnp.where(is_low, both[0:64], pltpu.roll(both[64:128], 64, 1))
        rims[half, 1] = jnp.where(is_low, pltpu.roll(both[0:64], 64, 1), both[64:128])
        for which in range(2):
            pl.when((below, above)[which])(rim_copy(half, which).start)
        for g in range(GROUPS):
            for c in range(4):
                at = (g + c) % 4
                sums[half, c, :, at * 32 : at * 32 + 32] = parts_z[g][:, at * 32 : at * 32 + 32]

    far = (1 - chip) * 2 + core

    def sum_copy(source, target, index, device):
        return pltpu.make_async_remote_copy(
            src_ref=source, dst_ref=target, send_sem=sum_send.at[index],
            recv_sem=sum_recv.at[index], device_id=device, device_id_type=MESH,
        )

    far_swap = [
        sum_copy(sums.at[h, (1 - chip) * 2 + 1 - core], got_core.at[h, 0], h, partner) for h in range(2)
    ]
    near_swap = [
        sum_copy(sums.at[h, chip * 2 + 1 - core], got_core.at[h, 1], 2 + h, partner) for h in range(2)
    ]
    over = [sum_copy(sums.at[h, far], got_chip.at[h], 4 + h, at_vert(q * 4 + far)) for h in range(2)]

    def rim_copy(h, which):
        home = (vert - slot - 1, vert - slot + 4)[which]
        return pltpu.make_async_remote_copy(
            src_ref=rims.at[h, which], dst_ref=got_edge.at[slot, h], send_sem=sum_send.at[6 + 2 * h + which],
            recv_sem=sum_recv.at[6 + 2 * slot + h], device_id=at_vert(home), device_id_type=MESH,
        )

    def rim_came(h):
        for k in range(VIEWS):
            pltpu.make_async_remote_copy(
                src_ref=rims.at[h, 0], dst_ref=got_edge.at[k, h], send_sem=sum_send.at[6],
                recv_sem=sum_recv.at[6 + 2 * k + h], device_id=partner, device_id_type=MESH,
            ).wait_recv()

    def backward(h):
        backward_x(h)
        backward_z(h)
        far_swap[h].start()
        near_swap[h].start()

    def pass_over(h):
        far_swap[h].wait_recv()
        sums[h, far] = sums[h, far] + got_core[h, 0]
        over[h].start()

    pl.when(~last & above)(lambda: pl.semaphore_wait(ready, 1))
    for step in range(3):
        along_y(step)
    backward(0)
    along_y(3)
    pass_over(0)
    backward(1)
    pass_over(1)

    for k in range(1, VIEWS):
        part_copy(slot, k - 1, partner, 0).wait_send()

    @pl.when(is_edge)
    def _():
        for k in range(VIEWS):
            outer_copy(0, k, partner, 0).wait_send()

    def sent(ref, semaphore):
        pltpu.make_async_remote_copy(
            src_ref=ref, dst_ref=ref, send_sem=semaphore, recv_sem=face_recv.at[0],
            device_id=partner, device_id_type=MESH,
        ).wait_send()

    for name, (index, (_, there), _) in ways.items():
        relayed = field.at[0:2, 0:2, :, 0:1] if name[0] == "v" else field.at[0:3, 0:2, :, 0:1]

        @pl.when(there)
        def _():
            sent(field.at[1, 1, core], face_send.at[index])
            sent(relayed, face_send.at[4 + index])

    sent(field.at[:, :, core], core_send.at[0])

    start = jnp.where(last, RAD, 0)
    lane = iota((64, LANES), 1)
    keep = is_edge & (lane >= start) & (lane < start + RAD)
    for h in range(2):
        near_swap[h].wait_recv()
        mine = sums[h, slot] + got_core[h, 1]
        over[h].wait_recv()
        mine = mine + got_chip[h]

        pl.when(is_edge)(lambda: rim_came(h))
        edge = got_edge[0, h] + got_edge[1, h] + (got_edge[2, h] + got_edge[3, h])
        for g in range(GROUPS):
            own = pltpu.roll(mine, (8 - g - slot) % 4 * 32, 1)
            sides = []
            for k in range(2):
                rim = pltpu.roll(edge, (start + LANES - 64 * k - RAD * g) % LANES, 1)
                part = own[64 * k : 64 * k + 64] + jnp.where(keep, rim, 0.0)
                sides.append(part.reshape(8, 8, LANES) * (1.0 / (RANK * VIEWS)))
            part = jnp.stack(swap_quads(*sides), axis=1).reshape(16, 8, LANES)
            at = (slice(16 * h, 16 * h + 16), slice(g * 8, g * 8 + 8))
            refined[at] = est[at] * part[:, :, 0:BLOCK]

    for copy in far_swap + near_swap + over:
        copy.wait_send()
    for which in range(2):

        @pl.when((below, above)[which])
        def _():
            for h in range(2):
                rim_copy(h, which).wait_send()


def local(estimate, view_tiles, slot_view, psf_taps):
    vmem = pl.BlockSpec(memory_space=pltpu.VMEM)
    hbm = pl.BlockSpec(memory_space=pltpu.HBM)
    tile = view_tiles[0, 0, 0]
    psf = jnp.transpose(psf_taps, (1, 2, 0, 3))
    scratch = [
        pltpu.VMEM(estimate.shape, F32),
        pltpu.VMEM(tile.shape, BF16),
        pltpu.VMEM(psf.shape, F32),
        pltpu.VMEM(slot_view.shape, jnp.int32),
        pltpu.VMEM((256, LANES), BF16),
        pltpu.VMEM((VIEWS, 128, LANES), BF16),
        pltpu.VMEM((2, 128, LANES), BF16),
        pltpu.VMEM((3, 3, 2, 10, 64, LANES), BF16),
        pltpu.VMEM((RANK, 12, 2, 384, LANES), BF16),
        pltpu.VMEM((RANK, 12, 2, 256, LANES), BF16),
        pltpu.VMEM((16, 256, LANES), BF16),
        pltpu.VMEM((24, 256, LANES), BF16),
        pltpu.VMEM((GROUPS, 2, 128, RANK * LANES), BF16),
        pltpu.VMEM((2, 4, 128, LANES), F32),
        pltpu.VMEM((2, 2, 64, LANES), F32),
        pltpu.VMEM((2, 2, 128, LANES), F32),
        pltpu.VMEM((2, 128, LANES), F32),
        pltpu.VMEM((VIEWS, 2, 64, LANES), F32),
        pltpu.VMEM((2, 24, LANES), F32),
        pltpu.VMEM((RANK, 128, 256), BF16),
        pltpu.VMEM((RANK, 128, 256), BF16),
        pltpu.VMEM((256, RANK * LANES), BF16),
        pltpu.VMEM((RANK * 128, 256), BF16),
        pltpu.VMEM((2, RANK, 64, 256), BF16),
        pltpu.VMEM((GROUPS, RANK * LANES, 256), BF16),
        pltpu.SemaphoreType.DMA((4,)),
        pltpu.SemaphoreType.DMA((7,)),
        pltpu.SemaphoreType.DMA((6,)),
        pltpu.SemaphoreType.DMA((8,)),
        pltpu.SemaphoreType.DMA((18,)),
        pltpu.SemaphoreType.DMA((1,)),
        pltpu.SemaphoreType.DMA((9,)),
        pltpu.SemaphoreType.DMA((10,)),
        pltpu.SemaphoreType.DMA((14,)),
        pltpu.SemaphoreType.REGULAR,
    ]
    return pl.pallas_call(
        kernel,
        out_shape=pltpu.VMEM(estimate.shape, F32),
        in_specs=[hbm] * 4,
        out_specs=vmem,
        scratch_shapes=scratch,
        compiler_params=pltpu.CompilerParams(
            collective_id=0, has_side_effects=True, vmem_limit_bytes=56 * 1024 * 1024
        ),
    )(*(pltpu.with_memory_space_constraint(a, pltpu.HBM) for a in (estimate, tile, psf, slot_view)))


def solution(mesh):
    placed = (
        P("bx", "by", "vert"),
        P("bx", "by", "vert", None, None, None),
        P("bx", "by", None),
        P(),
    )
    return jax.shard_map(
        local, mesh=mesh, in_specs=placed, out_specs=P("bx", "by", "vert"), check_vma=False
    )
```

```python
import jax
import jax.numpy as jnp
from jax import lax
from jax.experimental import pallas as pl
from jax.experimental.pallas import tpu as pltpu
from jax.sharding import PartitionSpec as P

BACKGROUND = 0.1
MESH = pl.DeviceIdType.MESH
F32, BF16 = jnp.float32, jnp.bfloat16
BLOCK = 32
RAD = 16
TAPS = 33
RANK = 3
VIEWS = 4
GROUPS = 4
LANES = 128


def iota(shape, axis):
    return lax.broadcasted_iota(jnp.int32, shape, axis)


def dot(a, b):
    return jnp.dot(a, b, preferred_element_type=F32)


def band(line, rows, start):
    line = jnp.broadcast_to(line, (rows, LANES))
    return pltpu.roll(line, start % LANES, 1, stride=1, stride_axis=0)


def swap_quads(a, b):
    low, axis = iota(a.shape, a.ndim - 2) < 4, a.ndim - 2
    return jnp.where(low, a, pltpu.roll(b, 4, axis)), jnp.where(low, pltpu.roll(a, 4, axis), b)


def build_taps(psf, slot_view, slot, taps):
    listed = slot_view[...]
    view = jnp.sum(jnp.where(iota(listed.shape, 2) == slot, listed, 0), axis=2, keepdims=True)
    held = iota((VIEWS, TAPS), 0) == view[0]
    mine = jnp.sum(jnp.where(held[None, None], psf[...], 0.0), axis=2)
    mine = (mine / jnp.sum(mine, axis=-1, keepdims=True)).astype(BF16).astype(F32)
    taps[...] = jnp.zeros_like(taps)
    for a in range(3):
        taps[0, 8 * a : 8 * a + RANK, :TAPS] = mine[a]
    flip = (iota((LANES, LANES), 0) + iota((LANES, LANES), 1) == TAPS - 1).astype(BF16)
    taps[1] = dot(taps[0].astype(BF16), flip)


def build_z(taps, wz, wb):
    z_in, z_out = iota((LANES, LANES), 0), iota((LANES, LANES), 1)
    near = jnp.abs(z_in - z_out) <= RAD
    rim, out = iota((32, LANES), 0), iota((32, LANES), 1)
    rim_ok = ((rim < RAD) & (out <= rim)) | ((rim >= RAD) & (out >= rim + 96))
    lane16 = iota((16, LANES), 1)
    for r in range(RANK):
        forward, backward = taps[1, 16 + r : 17 + r, :], taps[0, 16 + r : 17 + r, :]
        columns = slice(r * LANES, (r + 1) * LANES)
        wz[0:128, columns] = jnp.where(near, band(forward, LANES, -RAD), 0.0).astype(BF16)
        wz[128:160, columns] = jnp.where(rim_ok, band(forward, 32, 96), 0.0).astype(BF16)
        wz[160:256, columns] = jnp.zeros((96, LANES), BF16)
        main = jnp.where(near, band(backward, LANES, -RAD), 0.0)
        low = jnp.where(lane16 < RAD, band(backward, 16, 0), 0.0)
        high = jnp.where(lane16 < RAD, band(backward, 16, 96), 0.0)
        for g in range(GROUPS):
            wb[g, r * 128 : r * 128 + 128, 0:128] = (
                pltpu.roll(main, 32 * g, 1) if g else main
            ).astype(BF16)
            wb[g, r * 128 : r * 128 + 128, 128:256] = jnp.zeros((128, LANES), BF16)
            lo, hi = pltpu.roll(low, RAD * g, 1) if g else low, pltpu.roll(high, 64 + RAD * g, 1)
            wb[g, r * 128 : r * 128 + 16, 128:256] = lo.astype(BF16)
            wb[g, r * 128 + 112 : r * 128 + 128, 128:256] = hi.astype(BF16)


def build_x(taps, bx, tx, txb):
    spread = (iota((LANES, 256), 1) == 4 * iota((LANES, 256), 0)).astype(BF16)
    lane, row = iota((LANES, LANES), 1), iota((LANES, LANES), 0)
    low, high = bx > 0, bx < 3

    def tiles(line):
        turned = [band(line[:, i * LANES : (i + 1) * LANES], LANES, 0) for i in range(2)]
        return jnp.where(lane >= row, turned[0], 0.0), jnp.where(lane >= row, turned[1], turned[0])

    wide = [dot(taps[k, 0:8, :].astype(BF16), spread) for k in range(2)]
    for r in range(RANK):
        left, right = tiles(wide[0][r : r + 1])
        tx[r, :, 0:128] = left.astype(BF16)
        tx[r, :, 128:256] = right.astype(BF16)
        left, right = [m[0:64] for m in tiles(wide[1][r : r + 1])]
        txb[0, r, :, 0:128] = jnp.where((lane[0:64] >= 64) | low, left, 0.0).astype(BF16)
        txb[0, r, :, 128:256] = right.astype(BF16)
        txb[1, r, :, 0:128] = left.astype(BF16)
        txb[1, r, :, 128:256] = jnp.where(high, right, 0.0).astype(BF16)


def build_y(taps, by, ty, tyb):
    place = by * BLOCK - RAD + iota((BLOCK, LANES), 1)
    inside = (place >= 0) & (place < 4 * BLOCK)
    plain = [band(taps[0, 8 + r : 9 + r, :], BLOCK, 0) for r in range(RANK)]
    plain += [
        jnp.where(inside, band(taps[1, 8 + r : 9 + r, :], BLOCK, 0), 0.0) for r in range(RANK)
    ]
    plain = jnp.concatenate(plain, axis=0).astype(BF16)
    y, column = iota((LANES, 256), 0), iota((LANES, 256), 1)
    wide = [
        dot(plain, (column == 16 * (y // 4) + 4 * x + y % 4).astype(BF16)).astype(BF16)
        for x in range(4)
    ]
    row, source = iota((LANES, LANES), 0), iota((LANES, LANES), 1)
    order = (row == 16 * (source % 32 // 4) + 4 * (source // 32) + source % 4).astype(BF16)
    for i in range(2 * RANK):
        done = dot(order, jnp.concatenate([m[i * 32 : i * 32 + 32] for m in wide], axis=0)).astype(BF16)
        if i < RANK:
            ty[i] = done
        else:
            tyb[(i - RANK) * 128 : (i - RANK + 1) * 128, :] = done


def kernel(
    est_hbm, tile_hbm, psf_hbm, slot_view_hbm, refined,
    est, tile, psf, slot_view,
    packed, parts, outer, field, after_z, after_x, seen, back_y, back_x, sums, rims,
    got_core, got_chip, got_edge,
    taps, tx, ty, wz, tyb, txb, wb,
    load_sem, part_send, part_recv, face_send, face_recv, core_send, core_recv, sum_send, sum_recv, ready,
):
    bx, by, vert = lax.axis_index("bx"), lax.axis_index("by"), lax.axis_index("vert")
    q, slot = vert // VIEWS, vert % VIEWS
    core, chip = slot % 2, slot // 2

    loads = [
        pltpu.make_async_copy(source, target, load_sem.at[i])
        for i, (source, target) in enumerate(
            ((est_hbm, est), (psf_hbm, psf), (slot_view_hbm, slot_view), (tile_hbm, tile))
        )
    ]
    for copy in loads:
        copy.start()

    def at_vert(index):
        return {"vert": index}

    partner = at_vert(q * 4 + chip * 2 + 1 - core)
    above, below = q < 3, q > 0
    first, last = slot == 0, slot == VIEWS - 1
    is_edge = (first & below) | (last & above)

    straight = core == 0

    def block(ju, jv):
        return jnp.where(straight, jv, ju), jnp.where(straight, ju, jv)

    def link(along_u, step):
        x_step = jnp.where(straight == along_u, step, 0)
        x, y = bx + x_step, by + step - x_step
        return {"bx": x, "by": y}, (x >= 0) & (x < 4) & (y >= 0) & (y < 4)

    u_up, u_down, v_up, v_down = link(True, 1), link(True, -1), link(False, 1), link(False, -1)

    def clear(ref):
        ref[...] = jnp.zeros(ref.shape, BF16)

    pl.when(bx == 0)(lambda: clear(field.at[:, 0, core]))
    pl.when(bx == 3)(lambda: clear(field.at[:, 2, core]))
    pl.when(by == 0)(lambda: clear(field.at[0, :, core]))
    pl.when(by == 3)(lambda: clear(field.at[2, :, core]))
    pl.when(~below)(lambda: clear(outer.at[0]))
    pl.when(~above)(lambda: clear(outer.at[1]))

    got_edge[...] = jnp.zeros_like(got_edge)
    barrier = pltpu.get_barrier_semaphore()

    def greet(device):
        pl.semaphore_signal(barrier, inc=1, device_id=device, device_id_type=MESH)

    for k in range(1, VIEWS):
        greet(at_vert(q * 4 + (slot + k) % VIEWS))
    for device, there in (u_up, u_down, v_up, v_down):
        pl.when(there)(lambda device=device: greet(device))

    @pl.when(above)
    def _():
        greet(at_vert(vert - slot + 4))

        @pl.when(last)
        def _():
            for k in range(2, VIEWS + 1):
                greet(at_vert(vert + k))

    beside = [(there, 1) for _, there in (u_up, u_down, v_up, v_down)]
    beside += [(first & below, VIEWS), (~first & below, 1)]
    pl.semaphore_wait(barrier, 3 + sum(jnp.where(there, n, 0) for there, n in beside))

    def answer(device):
        pl.semaphore_signal(ready, inc=1, device_id=device, device_id_type=MESH)

    @pl.when(first & below)
    def _():
        for k in range(1, VIEWS + 1):
            answer(at_vert(vert - k))

    pl.when(~first & below)(lambda: answer(at_vert(vert - slot - 1)))

    loads[0].wait()
    groups = est[...].reshape(BLOCK, GROUPS, 8, BLOCK)
    line = jnp.concatenate([groups[:, g].reshape(256, BLOCK) for g in range(GROUPS)], axis=1)
    line = pltpu.roll(line, slot * 32, 1).reshape(16, 2, 8, LANES)
    for side, quads in enumerate(swap_quads(line[:, 0], line[:, 1])):
        packed[side * 128 : side * 128 + 128, :] = quads.reshape(128, LANES).astype(BF16)

    def part_copy(source, send, device, side):
        return pltpu.make_async_remote_copy(
            src_ref=packed.at[pl.ds(side * 128, 128), :], dst_ref=parts.at[source],
            send_sem=part_send.at[send], recv_sem=part_recv.at[source],
            device_id=device, device_id_type=MESH,
        )

    for k in range(1, VIEWS):
        other = (slot + k) % VIEWS
        part_copy(slot, k - 1, at_vert(q * 4 + other), other % 2).start()

    def outer_copy(which, send, device, side):
        return pltpu.make_async_remote_copy(
            src_ref=packed.at[pl.ds(side * 128, 128), :], dst_ref=outer.at[which],
            send_sem=part_send.at[3 + send], recv_sem=part_recv.at[4 + which],
            device_id=device, device_id_type=MESH,
        )

    @pl.when(first & below)
    def _():
        for k in range(VIEWS):
            outer_copy(1, k, at_vert(vert - 4 + k), k % 2).start()

    parts[slot] = packed[pl.ds(core * 128, 128), :]
    loads[1].wait()
    loads[2].wait()
    build_taps(psf, slot_view, slot, taps)
    build_z(taps, wz, wb)

    def assemble():
        for k in range(1, VIEWS):
            part_copy((slot + k) % VIEWS, 0, partner, 0).wait_recv()
        chunk = iota((128, LANES), 1) // 32
        have = [parts[k].astype(F32) for k in range(VIEWS)]
        for g in range(GROUPS):
            line = have[(3 - g) % 4]
            for at in range(3):
                line = jnp.where(chunk == at, have[(at - g) % 4], line)
            if g:
                line = pltpu.roll(line, LANES - 32 * g, 1)
            for tp in range(2):
                field[1, 1, core, 4 * tp + g] = line[64 * tp : 64 * tp + 64].astype(BF16)

    def assemble_rims():
        for k, there in enumerate((below, above)):
            pl.when(there)(lambda k=k: outer_copy(k, 0, partner, 0).wait_recv())
        is_above = iota((128, LANES), 1) % 32 < RAD
        line = jnp.where(is_above, outer[1].astype(F32), outer[0].astype(F32))
        field[1, 1, core, 8:10] = pltpu.roll(line, RAD, 1).astype(BF16).reshape(2, 64, LANES)

    def message(ju, jv, which):
        return field.at[(*block(ju, jv), core, slice(4 * which, min(4 * which + 4, 10)))]

    def face_copy(source, target, which, send, device):
        return pltpu.make_async_remote_copy(
            src_ref=message(*source, which), dst_ref=message(*target, which),
            send_sem=face_send.at[send],
            recv_sem=face_recv.at[which * 9 + target[0] * 3 + target[1]],
            device_id=device, device_id_type=MESH,
        )

    ways = {"u_up": (0, u_up, (0, 1)), "u_down": (1, u_down, (2, 1)), "v_up": (2, v_up, (1, 0)), "v_down": (3, v_down, (1, 2))}

    def send_own(name, which):
        index, (device, there), target = ways[name]
        pl.when(there)(face_copy((1, 1), target, which, index, device).start)

    def relay(name, along, which):
        index, (device, there), target = ways[name]
        source = (along, 1) if name[0] == "v" else (1, along)
        target = (along, target[1]) if name[0] == "v" else (target[0], along)
        pl.when(there)(face_copy(source, target, which, 4 + index, device).start)

    def came(ju, jv, which, over):
        there = ways[f"{over}_{'down' if (jv if over == 'v' else ju) == 0 else 'up'}"][1][1]
        copy = face_copy((ju, jv), (ju, jv), which, 0, partner)
        pl.when(there)(copy.wait_recv)

    def core_copy(jy, jx, side):
        return pltpu.make_async_remote_copy(
            src_ref=field.at[jy, jx, side], dst_ref=field.at[jy, jx, side],
            send_sem=core_send.at[0], recv_sem=core_recv.at[jy * 3 + jx],
            device_id=partner, device_id_type=MESH,
        )

    def pass_on(ju, jv):
        core_copy(*block(ju, jv), core).start()

    def swapped(jy, jx):
        core_copy(jy, jx, 1 - core).wait_recv()

    def forward_z(jy, jx):
        rows = slice(jx * 128, jx * 128 + 128)
        rim = field[jy, jx, :, 8:10].reshape(256, LANES)
        for g in range(GROUPS):
            turned = pltpu.roll(rim, LANES - 32 * g, 1) if g else rim
            main = jnp.concatenate(
                [field[jy, jx, side, 4 * tp + g] for side in range(2) for tp in range(2)], axis=0
            )
            done = dot(jnp.concatenate([main, turned], axis=1), wz[...]).astype(BF16)
            for r in range(RANK):
                after_z[r, jy * GROUPS + g, :, rows, :] = done[:, r * 128 : (r + 1) * 128].reshape(
                    2, 128, LANES
                )

    def forward_x(jy):
        for r in range(RANK):
            for group in (jy * GROUPS, jy * GROUPS + 2):
                for b in range(2):
                    rows = slice(b * 128, b * 128 + 256)
                    both = [after_z[r, group + k // 2, k % 2, rows, :] for k in range(4)]
                    done = dot(tx[r], jnp.concatenate(both, axis=1)).astype(BF16)
                    for k in range(4):
                        after_x[r, group + k // 2, k % 2, b * 128 : b * 128 + 128, :] = done[
                            :, k * 128 : k * 128 + 128
                        ]

    assemble()
    for name in ("u_up", "u_down", "v_up", "v_down"):
        send_own(name, 0)
    for name in ("v_up", "v_down", "u_up", "u_down"):
        send_own(name, 1)

    @pl.when(last & above)
    def _():
        pl.semaphore_wait(ready, VIEWS)
        for k in range(VIEWS):
            outer_copy(0, k, at_vert(vert + 1 + k), k % 2).start()

    build_x(taps, bx, tx, txb)
    assemble_rims()
    for name in ("u_up", "u_down", "v_up", "v_down"):
        send_own(name, 2)
    pass_on(1, 1)
    for side in (0, 2):
        came(side, 1, 0, "u")
    for one, other in ((0, 2), (2, 0)):
        relay("v_up", one, 0)
        relay("v_down", other, 0)
    for side in (0, 2):
        came(1, side, 1, "v")
    for one, other in ((0, 2), (2, 0)):
        relay("u_up", one, 1)
        relay("u_down", other, 1)
    for side in (0, 2):
        came(side, 1, 2, "u")
    for one, other in ((0, 2), (2, 0)):
        relay("v_up", one, 2)
        relay("v_down", other, 2)
    build_y(taps, by, ty, tyb)
    loads[3].wait()

    def order_tile(i, carry):
        quad = tile[pl.ds(4 * i, 4)].astype(F32).reshape(2, 2, 8, 8, LANES)
        sides = swap_quads(quad[:, 0], quad[:, 1])
        rows = jnp.stack([m[x] for m in sides for x in range(2)], axis=1)
        seen[i] = rows.reshape(256, LANES).astype(BF16)
        return carry

    lax.fori_loop(0, 16, order_tile, 0, unroll=4)
    swapped(1, 1)
    forward_z(1, 1)
    for side in (0, 2):
        came(side, 1, 1, "u")
        pass_on(side, 1)
        came(1, side, 0, "v")
        came(1, side, 2, "v")
        pass_on(1, side)
    for side in (0, 2):
        swapped(1, side)
        swapped(side, 1)
    for side in (0, 2):
        forward_z(1, side)
        forward_z(side, 1)
    waves = (((0, 0), (2, 2)), ((0, 2), (2, 0)))
    for corner in waves[0]:
        came(*corner, 0, "v")
        came(*corner, 1, "u")
        came(*corner, 2, "v")
        pass_on(*corner)
    forward_x(1)
    for corner in waves[1]:
        came(*corner, 0, "v")
        came(*corner, 1, "u")
        came(*corner, 2, "v")
        pass_on(*corner)
    for wave in waves:
        for corner in wave:
            swapped(*corner)
        for corner in wave:
            forward_z(*corner)
    for jy in (0, 2):
        forward_x(jy)

    def along_y(step):
        quotient = []
        for b in range(2):
            blurred = None
            for r in range(RANK):
                quads = [
                    after_x[r, 4 * b : 4 * b + 8, :, 16 * i : 16 * i + 16, :].reshape(256, LANES)
                    for i in range(4 * step, 4 * step + 4)
                ]
                part = dot(ty[r], jnp.concatenate(quads, axis=1))
                blurred = part if blurred is None else blurred + part
            rows = slice(128 * b, 128 * b + 128)
            quads = [seen[i, rows, :] for i in range(4 * step, 4 * step + 4)]
            quads = jnp.concatenate(quads, axis=1).astype(F32)
            quotient.append((RANK * quads / (blurred + RANK * BACKGROUND)).astype(BF16))
        quotient = jnp.concatenate(quotient, axis=0)
        for r in range(RANK):
            done = dot(tyb[r * 128 : r * 128 + 128, :], quotient).astype(BF16)
            for k in range(4):
                i = 4 * step + k
                back_y[r * 8 : r * 8 + 8, 16 * i : 16 * i + 16, :] = done[
                    :, k * 128 : k * 128 + 128
                ].reshape(8, 16, LANES)

    def backward_x(half):
        within = slice(half * 64, half * 64 + 192)
        for g in (0, 2):
            for r in range(RANK):
                at = (r * GROUPS + g) * 2
                sides = jnp.concatenate([back_y[at + k, within, :] for k in range(4)], axis=1)
                done = dot(txb[half, r, :, 0:192], sides).astype(BF16)
                for k in range(4):
                    rows = slice(k % 2 * 64, k % 2 * 64 + 64)
                    back_x[g + k // 2, half, rows, r * 128 : (r + 1) * 128] = done[
                        :, k * 128 : k * 128 + 128
                    ]

    def backward_z(half):
        parts_z = [dot(back_x[g, half], wb[g]) for g in range(GROUPS)]
        both = (parts_z[0] + parts_z[1] + (parts_z[2] + parts_z[3]))[:, LANES:]
        is_low = iota((64, LANES), 1) < 64
        rims[half, 0] = jnp.where(is_low, both[0:64], pltpu.roll(both[64:128], 64, 1))
        rims[half, 1] = jnp.where(is_low, pltpu.roll(both[0:64], 64, 1), both[64:128])
        for which in range(2):
            pl.when((below, above)[which])(rim_copy(half, which).start)
        for g in range(GROUPS):
            for c in range(4):
                at = (g + c) % 4
                sums[half, c, :, at * 32 : at * 32 + 32] = parts_z[g][:, at * 32 : at * 32 + 32]

    far = (1 - chip) * 2 + core

    def sum_copy(source, target, index, device):
        return pltpu.make_async_remote_copy(
            src_ref=source, dst_ref=target, send_sem=sum_send.at[index],
            recv_sem=sum_recv.at[index], device_id=device, device_id_type=MESH,
        )

    far_swap = [
        sum_copy(sums.at[h, (1 - chip) * 2 + 1 - core], got_core.at[h, 0], h, partner) for h in range(2)
    ]
    near_swap = [
        sum_copy(sums.at[h, chip * 2 + 1 - core], got_core.at[h, 1], 2 + h, partner) for h in range(2)
    ]
    over = [sum_copy(sums.at[h, far], got_chip.at[h], 4 + h, at_vert(q * 4 + far)) for h in range(2)]

    def rim_copy(h, which):
        home = (vert - slot - 1, vert - slot + 4)[which]
        return pltpu.make_async_remote_copy(
            src_ref=rims.at[h, which], dst_ref=got_edge.at[slot, h], send_sem=sum_send.at[6 + 2 * h + which],
            recv_sem=sum_recv.at[6 + 2 * slot + h], device_id=at_vert(home), device_id_type=MESH,
        )

    def rim_came(h):
        for k in range(VIEWS):
            pltpu.make_async_remote_copy(
                src_ref=rims.at[h, 0], dst_ref=got_edge.at[k, h], send_sem=sum_send.at[6],
                recv_sem=sum_recv.at[6 + 2 * k + h], device_id=partner, device_id_type=MESH,
            ).wait_recv()

    def backward(h):
        backward_x(h)
        backward_z(h)
        far_swap[h].start()
        near_swap[h].start()

    def pass_over(h):
        far_swap[h].wait_recv()
        sums[h, far] = sums[h, far] + got_core[h, 0]
        over[h].start()

    pl.when(~last & above)(lambda: pl.semaphore_wait(ready, 1))
    for step in range(3):
        along_y(step)
    backward(0)
    along_y(3)
    pass_over(0)
    backward(1)
    pass_over(1)

    for k in range(1, VIEWS):
        part_copy(slot, k - 1, partner, 0).wait_send()

    @pl.when(is_edge)
    def _():
        for k in range(VIEWS):
            outer_copy(0, k, partner, 0).wait_send()

    def sent(ref, semaphore):
        pltpu.make_async_remote_copy(
            src_ref=ref, dst_ref=ref, send_sem=semaphore, recv_sem=face_recv.at[0],
            device_id=partner, device_id_type=MESH,
        ).wait_send()

    for name, (index, (_, there), _) in ways.items():
        relayed = field.at[0:3, 0:2, :, 0:1] if name[0] == "v" else field.at[0:2, 0:2, :, 0:1]

        @pl.when(there)
        def _():
            sent(field.at[1, 1, core], face_send.at[index])
            sent(relayed, face_send.at[4 + index])

    sent(field.at[:, :, core], core_send.at[0])

    start = jnp.where(last, RAD, 0)
    lane = iota((64, LANES), 1)
    keep = is_edge & (lane >= start) & (lane < start + RAD)
    for h in range(2):
        near_swap[h].wait_recv()
        mine = sums[h, slot] + got_core[h, 1]
        over[h].wait_recv()
        mine = mine + got_chip[h]

        pl.when(is_edge)(lambda: rim_came(h))
        edge = got_edge[0, h] + got_edge[1, h] + (got_edge[2, h] + got_edge[3, h])
        for g in range(GROUPS):
            own = pltpu.roll(mine, (8 - g - slot) % 4 * 32, 1)
            sides = []
            for k in range(2):
                rim = pltpu.roll(edge, (start + LANES - 64 * k - RAD * g) % LANES, 1)
                part = own[64 * k : 64 * k + 64] + jnp.where(keep, rim, 0.0)
                sides.append(part.reshape(8, 8, LANES) * (1.0 / (RANK * VIEWS)))
            part = jnp.stack(swap_quads(*sides), axis=1).reshape(16, 8, LANES)
            at = (slice(16 * h, 16 * h + 16), slice(g * 8, g * 8 + 8))
            refined[at] = est[at] * part[:, :, 0:BLOCK]

    for copy in far_swap + near_swap + over:
        copy.wait_send()
    for which in range(2):

        @pl.when((below, above)[which])
        def _():
            for h in range(2):
                rim_copy(h, which).wait_send()


def local(estimate, view_tiles, slot_view, psf_taps):
    vmem = pl.BlockSpec(memory_space=pltpu.VMEM)
    hbm = pl.BlockSpec(memory_space=pltpu.HBM)
    tile = view_tiles[0, 0, 0]
    psf = jnp.transpose(psf_taps, (1, 2, 0, 3))
    scratch = [
        pltpu.VMEM(estimate.shape, F32),
        pltpu.VMEM(tile.shape, BF16),
        pltpu.VMEM(psf.shape, F32),
        pltpu.VMEM(slot_view.shape, jnp.int32),
        pltpu.VMEM((256, LANES), BF16),
        pltpu.VMEM((VIEWS, 128, LANES), BF16),
        pltpu.VMEM((2, 128, LANES), BF16),
        pltpu.VMEM((3, 3, 2, 10, 64, LANES), BF16),
        pltpu.VMEM((RANK, 12, 2, 384, LANES), BF16),
        pltpu.VMEM((RANK, 12, 2, 256, LANES), BF16),
        pltpu.VMEM((16, 256, LANES), BF16),
        pltpu.VMEM((24, 256, LANES), BF16),
        pltpu.VMEM((GROUPS, 2, 128, RANK * LANES), BF16),
        pltpu.VMEM((2, 4, 128, LANES), F32),
        pltpu.VMEM((2, 2, 64, LANES), F32),
        pltpu.VMEM((2, 2, 128, LANES), F32),
        pltpu.VMEM((2, 128, LANES), F32),
        pltpu.VMEM((VIEWS, 2, 64, LANES), F32),
        pltpu.VMEM((2, 24, LANES), F32),
        pltpu.VMEM((RANK, 128, 256), BF16),
        pltpu.VMEM((RANK, 128, 256), BF16),
        pltpu.VMEM((256, RANK * LANES), BF16),
        pltpu.VMEM((RANK * 128, 256), BF16),
        pltpu.VMEM((2, RANK, 64, 256), BF16),
        pltpu.VMEM((GROUPS, RANK * LANES, 256), BF16),
        pltpu.SemaphoreType.DMA((4,)),
        pltpu.SemaphoreType.DMA((7,)),
        pltpu.SemaphoreType.DMA((6,)),
        pltpu.SemaphoreType.DMA((8,)),
        pltpu.SemaphoreType.DMA((27,)),
        pltpu.SemaphoreType.DMA((1,)),
        pltpu.SemaphoreType.DMA((9,)),
        pltpu.SemaphoreType.DMA((10,)),
        pltpu.SemaphoreType.DMA((14,)),
        pltpu.SemaphoreType.REGULAR,
    ]
    return pl.pallas_call(
        kernel,
        out_shape=pltpu.VMEM(estimate.shape, F32),
        in_specs=[hbm] * 4,
        out_specs=vmem,
        scratch_shapes=scratch,
        compiler_params=pltpu.CompilerParams(
            collective_id=0, has_side_effects=True, vmem_limit_bytes=56 * 1024 * 1024
        ),
    )(*(pltpu.with_memory_space_constraint(a, pltpu.HBM) for a in (estimate, tile, psf, slot_view)))


def solution(mesh):
    placed = (
        P("bx", "by", "vert"),
        P("bx", "by", "vert", None, None, None),
        P("bx", "by", None),
        P(),
    )
    return jax.shard_map(
        local, mesh=mesh, in_specs=placed, out_specs=P("bx", "by", "vert"), check_vma=False
    )
```

```python
import jax
import jax.numpy as jnp
from jax import lax
from jax.experimental import pallas as pl
from jax.experimental.pallas import tpu as pltpu
from jax.sharding import PartitionSpec as P

BACKGROUND = 0.1
MESH = pl.DeviceIdType.MESH
F32, BF16 = jnp.float32, jnp.bfloat16
BLOCK = 32
RAD = 16
TAPS = 33
RANK = 3
VIEWS = 4
GROUPS = 4
LANES = 128


def iota(shape, axis):
    return lax.broadcasted_iota(jnp.int32, shape, axis)


def dot(a, b):
    return jnp.dot(a, b, preferred_element_type=F32)


def band(line, rows, start):
    line = jnp.broadcast_to(line, (rows, LANES))
    return pltpu.roll(line, start % LANES, 1, stride=1, stride_axis=0)


def swap_quads(a, b):
    low, axis = iota(a.shape, a.ndim - 2) < 4, a.ndim - 2
    return jnp.where(low, a, pltpu.roll(b, 4, axis)), jnp.where(low, pltpu.roll(a, 4, axis), b)


def build_taps(psf, slot_view, slot, taps):
    listed = slot_view[...]
    view = jnp.sum(jnp.where(iota(listed.shape, 2) == slot, listed, 0), axis=2, keepdims=True)
    held = iota((VIEWS, TAPS), 0) == view[0]
    mine = jnp.sum(jnp.where(held[None, None], psf[...], 0.0), axis=2)
    mine = (mine / jnp.sum(mine, axis=-1, keepdims=True)).astype(BF16).astype(F32)
    taps[...] = jnp.zeros_like(taps)
    for a in range(3):
        taps[0, 8 * a : 8 * a + RANK, :TAPS] = mine[a]
    flip = (iota((LANES, LANES), 0) + iota((LANES, LANES), 1) == TAPS - 1).astype(BF16)
    taps[1] = dot(taps[0].astype(BF16), flip)


def build_z(taps, wz, wb):
    z_in, z_out = iota((LANES, LANES), 0), iota((LANES, LANES), 1)
    near = jnp.abs(z_in - z_out) <= RAD
    rim, out = iota((32, LANES), 0), iota((32, LANES), 1)
    rim_ok = ((rim < RAD) & (out <= rim)) | ((rim >= RAD) & (out >= rim + 96))
    lane16 = iota((16, LANES), 1)
    for r in range(RANK):
        forward, backward = taps[1, 16 + r : 17 + r, :], taps[0, 16 + r : 17 + r, :]
        columns = slice(r * LANES, (r + 1) * LANES)
        wz[0:128, columns] = jnp.where(near, band(forward, LANES, -RAD), 0.0).astype(BF16)
        wz[128:160, columns] = jnp.where(rim_ok, band(forward, 32, 96), 0.0).astype(BF16)
        wz[160:256, columns] = jnp.zeros((96, LANES), BF16)
        main = jnp.where(near, band(backward, LANES, -RAD), 0.0)
        low = jnp.where(lane16 < RAD, band(backward, 16, 0), 0.0)
        high = jnp.where(lane16 < RAD, band(backward, 16, 96), 0.0)
        for g in range(GROUPS):
            wb[g, r * 128 : r * 128 + 128, 0:128] = (
                pltpu.roll(main, 32 * g, 1) if g else main
            ).astype(BF16)
            wb[g, r * 128 : r * 128 + 128, 128:256] = jnp.zeros((128, LANES), BF16)
            lo, hi = pltpu.roll(low, RAD * g, 1) if g else low, pltpu.roll(high, 64 + RAD * g, 1)
            wb[g, r * 128 : r * 128 + 16, 128:256] = lo.astype(BF16)
            wb[g, r * 128 + 112 : r * 128 + 128, 128:256] = hi.astype(BF16)


def build_x(taps, bx, tx, txb):
    spread = (iota((LANES, 256), 1) == 4 * iota((LANES, 256), 0)).astype(BF16)
    lane, row = iota((LANES, LANES), 1), iota((LANES, LANES), 0)
    low, high = bx > 0, bx < 3

    def tiles(line):
        turned = [band(line[:, i * LANES : (i + 1) * LANES], LANES, 0) for i in range(2)]
        return jnp.where(lane >= row, turned[0], 0.0), jnp.where(lane >= row, turned[1], turned[0])

    wide = [dot(taps[k, 0:8, :].astype(BF16), spread) for k in range(2)]
    for r in range(RANK):
        left, right = tiles(wide[0][r : r + 1])
        tx[r, :, 0:128] = left.astype(BF16)
        tx[r, :, 128:256] = right.astype(BF16)
        left, right = [m[0:64] for m in tiles(wide[1][r : r + 1])]
        txb[0, r, :, 0:128] = jnp.where((lane[0:64] >= 64) | low, left, 0.0).astype(BF16)
        txb[0, r, :, 128:256] = right.astype(BF16)
        txb[1, r, :, 0:128] = left.astype(BF16)
        txb[1, r, :, 128:256] = jnp.where(high, right, 0.0).astype(BF16)


def build_y(taps, by, ty, tyb):
    place = by * BLOCK - RAD + iota((BLOCK, LANES), 1)
    inside = (place >= 0) & (place < 4 * BLOCK)
    plain = [band(taps[0, 8 + r : 9 + r, :], BLOCK, 0) for r in range(RANK)]
    plain += [
        jnp.where(inside, band(taps[1, 8 + r : 9 + r, :], BLOCK, 0), 0.0) for r in range(RANK)
    ]
    plain = jnp.concatenate(plain, axis=0).astype(BF16)
    y, column = iota((LANES, 256), 0), iota((LANES, 256), 1)
    wide = [
        dot(plain, (column == 16 * (y // 4) + 4 * x + y % 4).astype(BF16)).astype(BF16)
        for x in range(4)
    ]
    row, source = iota((LANES, LANES), 0), iota((LANES, LANES), 1)
    order = (row == 16 * (source % 32 // 4) + 4 * (source // 32) + source % 4).astype(BF16)
    for i in range(2 * RANK):
        done = dot(order, jnp.concatenate([m[i * 32 : i * 32 + 32] for m in wide], axis=0)).astype(BF16)
        if i < RANK:
            ty[i] = done
        else:
            tyb[(i - RANK) * 128 : (i - RANK + 1) * 128, :] = done


def kernel(
    est_hbm, tile_hbm, psf_hbm, slot_view_hbm, refined,
    est, tile, psf, slot_view,
    packed, parts, outer, field, after_z, after_x, seen, back_y, back_x, sums, rims,
    got_core, got_chip, got_edge,
    taps, tx, ty, wz, tyb, txb, wb,
    load_sem, part_send, part_recv, face_send, face_recv, core_send, core_recv, sum_send, sum_recv, ready,
):
    bx, by, vert = lax.axis_index("bx"), lax.axis_index("by"), lax.axis_index("vert")
    q, slot = vert // VIEWS, vert % VIEWS
    core, chip = slot % 2, slot // 2

    loads = [
        pltpu.make_async_copy(source, target, load_sem.at[i])
        for i, (source, target) in enumerate(
            ((est_hbm, est), (psf_hbm, psf), (slot_view_hbm, slot_view), (tile_hbm, tile))
        )
    ]
    for copy in loads:
        copy.start()

    def at_vert(index):
        return {"vert": index}

    partner = at_vert(q * 4 + chip * 2 + 1 - core)
    above, below = q < 3, q > 0
    first, last = slot == 0, slot == VIEWS - 1
    is_edge = (first & below) | (last & above)

    straight = core == 0

    def block(ju, jv):
        return jnp.where(straight, jv, ju), jnp.where(straight, ju, jv)

    def link(along_u, step):
        x_step = jnp.where(straight == along_u, step, 0)
        x, y = bx + x_step, by + step - x_step
        return {"bx": x, "by": y}, (x >= 0) & (x < 4) & (y >= 0) & (y < 4)

    u_up, u_down, v_up, v_down = link(True, 1), link(True, -1), link(False, 1), link(False, -1)

    def clear(ref):
        ref[...] = jnp.zeros(ref.shape, BF16)

    pl.when(bx == 0)(lambda: clear(field.at[:, 0, core]))
    pl.when(bx == 3)(lambda: clear(field.at[:, 2, core]))
    pl.when(by == 0)(lambda: clear(field.at[0, :, core]))
    pl.when(by == 3)(lambda: clear(field.at[2, :, core]))
    pl.when(~below)(lambda: clear(outer.at[0]))
    pl.when(~above)(lambda: clear(outer.at[1]))

    got_edge[...] = jnp.zeros_like(got_edge)
    barrier = pltpu.get_barrier_semaphore()

    def greet(device):
        pl.semaphore_signal(barrier, inc=1, device_id=device, device_id_type=MESH)

    for k in range(1, VIEWS):
        greet(at_vert(q * 4 + (slot + k) % VIEWS))
    for device, there in (u_up, u_down, v_up, v_down):
        pl.when(there)(lambda device=device: greet(device))

    @pl.when(above)
    def _():
        greet(at_vert(vert - slot + 4))

        @pl.when(last)
        def _():
            for k in range(2, VIEWS + 1):
                greet(at_vert(vert + k))

    beside = [(there, 1) for _, there in (u_up, u_down, v_up, v_down)]
    beside += [(first & below, VIEWS), (~first & below, 1)]
    pl.semaphore_wait(barrier, 3 + sum(jnp.where(there, n, 0) for there, n in beside))

    def answer(device):
        pl.semaphore_signal(ready, inc=1, device_id=device, device_id_type=MESH)

    @pl.when(first & below)
    def _():
        for k in range(1, VIEWS + 1):
            answer(at_vert(vert - k))

    pl.when(~first & below)(lambda: answer(at_vert(vert - slot - 1)))

    loads[0].wait()
    groups = est[...].reshape(BLOCK, GROUPS, 8, BLOCK)
    line = jnp.concatenate([groups[:, g].reshape(256, BLOCK) for g in range(GROUPS)], axis=1)
    line = pltpu.roll(line, slot * 32, 1).reshape(16, 2, 8, LANES)
    for side, quads in enumerate(swap_quads(line[:, 0], line[:, 1])):
        packed[side * 128 : side * 128 + 128, :] = quads.reshape(128, LANES).astype(BF16)

    def part_copy(source, send, device, side):
        return pltpu.make_async_remote_copy(
            src_ref=packed.at[pl.ds(side * 128, 128), :], dst_ref=parts.at[source],
            send_sem=part_send.at[send], recv_sem=part_recv.at[source],
            device_id=device, device_id_type=MESH,
        )

    for k in range(1, VIEWS):
        other = (slot + k) % VIEWS
        part_copy(slot, k - 1, at_vert(q * 4 + other), other % 2).start()

    def outer_copy(which, send, device, side):
        return pltpu.make_async_remote_copy(
            src_ref=packed.at[pl.ds(side * 128, 128), :], dst_ref=outer.at[which],
            send_sem=part_send.at[3 + send], recv_sem=part_recv.at[4 + which],
            device_id=device, device_id_type=MESH,
        )

    @pl.when(first & below)
    def _():
        for k in range(VIEWS):
            outer_copy(1, k, at_vert(vert - 4 + k), k % 2).start()

    parts[slot] = packed[pl.ds(core * 128, 128), :]
    loads[1].wait()
    loads[2].wait()
    build_taps(psf, slot_view, slot, taps)
    build_z(taps, wz, wb)

    def assemble():
        for k in range(1, VIEWS):
            part_copy((slot + k) % VIEWS, 0, partner, 0).wait_recv()
        chunk = iota((128, LANES), 1) // 32
        have = [parts[k].astype(F32) for k in range(VIEWS)]
        for g in range(GROUPS):
            line = have[(3 - g) % 4]
            for at in range(3):
                line = jnp.where(chunk == at, have[(at - g) % 4], line)
            if g:
                line = pltpu.roll(line, LANES - 32 * g, 1)
            for tp in range(2):
                field[1, 1, core, 4 * tp + g] = line[64 * tp : 64 * tp + 64].astype(BF16)

    def assemble_rims():
        for k, there in enumerate((below, above)):
            pl.when(there)(lambda k=k: outer_copy(k, 0, partner, 0).wait_recv())
        is_above = iota((128, LANES), 1) % 32 < RAD
        line = jnp.where(is_above, outer[1].astype(F32), outer[0].astype(F32))
        field[1, 1, core, 8:10] = pltpu.roll(line, RAD, 1).astype(BF16).reshape(2, 64, LANES)

    def message(ju, jv, which):
        return field.at[(*block(ju, jv), core, slice(4 * which, min(4 * which + 4, 10)))]

    def face_copy(source, target, which, send, device):
        return pltpu.make_async_remote_copy(
            src_ref=message(*source, which), dst_ref=message(*target, which),
            send_sem=face_send.at[send],
            recv_sem=face_recv.at[which * 9 + target[0] * 3 + target[1]],
            device_id=device, device_id_type=MESH,
        )

    ways = {"u_up": (0, u_up, (0, 1)), "u_down": (1, u_down, (2, 1)), "v_up": (2, v_up, (1, 0)), "v_down": (3, v_down, (1, 2))}

    def send_own(name, which):
        index, (device, there), target = ways[name]
        pl.when(there)(face_copy((1, 1), target, which, index, device).start)

    def relay(name, along, which):
        index, (device, there), target = ways[name]
        source = (along, 1) if name[0] == "v" else (1, along)
        target = (along, target[1]) if name[0] == "v" else (target[0], along)
        pl.when(there)(face_copy(source, target, which, 4 + index, device).start)

    def came(ju, jv, which, over):
        there = ways[f"{over}_{'down' if (jv if over == 'v' else ju) == 0 else 'up'}"][1][1]
        copy = face_copy((ju, jv), (ju, jv), which, 0, partner)
        pl.when(there)(copy.wait_recv)

    def core_copy(jy, jx, side):
        return pltpu.make_async_remote_copy(
            src_ref=field.at[jy, jx, side], dst_ref=field.at[jy, jx, side],
            send_sem=core_send.at[0], recv_sem=core_recv.at[jy * 3 + jx],
            device_id=partner, device_id_type=MESH,
        )

    def pass_on(ju, jv):
        core_copy(*block(ju, jv), core).start()

    def swapped(jy, jx):
        core_copy(jy, jx, 1 - core).wait_recv()

    def forward_z(jy, jx):
        rows = slice(jx * 128, jx * 128 + 128)
        rim = field[jy, jx, :, 8:10].reshape(256, LANES)
        for g in range(GROUPS):
            turned = pltpu.roll(rim, LANES - 32 * g, 1) if g else rim
            main = jnp.concatenate(
                [field[jy, jx, side, 4 * tp + g] for side in range(2) for tp in range(2)], axis=0
            )
            done = dot(jnp.concatenate([main, turned], axis=1), wz[...]).astype(BF16)
            for r in range(RANK):
                after_z[r, jy * GROUPS + g, :, rows, :] = done[:, r * 128 : (r + 1) * 128].reshape(
                    2, 128, LANES
                )

    def forward_x(jy):
        for r in range(RANK):
            for group in (jy * GROUPS, jy * GROUPS + 2):
                for b in range(2):
                    rows = slice(b * 128, b * 128 + 256)
                    both = [after_z[r, group + k // 2, k % 2, rows, :] for k in range(4)]
                    done = dot(tx[r], jnp.concatenate(both, axis=1)).astype(BF16)
                    for k in range(4):
                        after_x[r, group + k // 2, k % 2, b * 128 : b * 128 + 128, :] = done[
                            :, k * 128 : k * 128 + 128
                        ]

    assemble()
    for name in ("u_up", "u_down", "v_up", "v_down"):
        send_own(name, 0)
    for name in ("v_up", "v_down", "u_up", "u_down"):
        send_own(name, 1)

    @pl.when(last & above)
    def _():
        pl.semaphore_wait(ready, VIEWS)
        for k in range(VIEWS):
            outer_copy(0, k, at_vert(vert + 1 + k), k % 2).start()

    build_x(taps, bx, tx, txb)
    assemble_rims()
    for name in ("u_up", "u_down", "v_up", "v_down"):
        send_own(name, 2)
    pass_on(1, 1)
    for side in (0, 2):
        came(side, 1, 0, "u")
    for one, other in ((0, 2), (2, 0)):
        relay("v_up", one, 0)
        relay("v_down", other, 0)
    build_y(taps, by, ty, tyb)
    for side in (0, 2):
        came(1, side, 1, "v")
    for one, other in ((0, 2), (2, 0)):
        relay("u_up", one, 1)
        relay("u_down", other, 1)
    loads[3].wait()

    def order_tile(i, carry):
        quad = tile[pl.ds(4 * i, 4)].astype(F32).reshape(2, 2, 8, 8, LANES)
        sides = swap_quads(quad[:, 0], quad[:, 1])
        rows = jnp.stack([m[x] for m in sides for x in range(2)], axis=1)
        seen[i] = rows.reshape(256, LANES).astype(BF16)
        return carry

    lax.fori_loop(0, 16, order_tile, 0, unroll=4)
    swapped(1, 1)
    forward_z(1, 1)
    for side in (0, 2):
        came(side, 1, 2, "u")
    for one, other in ((0, 2), (2, 0)):
        relay("v_up", one, 2)
        relay("v_down", other, 2)
    for side in (0, 2):
        came(side, 1, 1, "u")
        pass_on(side, 1)
        came(1, side, 0, "v")
        came(1, side, 2, "v")
        pass_on(1, side)
    for side in (0, 2):
        swapped(1, side)
        swapped(side, 1)
    for side in (0, 2):
        forward_z(1, side)
        forward_z(side, 1)
    waves = (((0, 0), (2, 2)), ((0, 2), (2, 0)))
    for corner in waves[0]:
        came(*corner, 0, "v")
        came(*corner, 1, "u")
        came(*corner, 2, "v")
        pass_on(*corner)
    forward_x(1)
    for corner in waves[1]:
        came(*corner, 0, "v")
        came(*corner, 1, "u")
        came(*corner, 2, "v")
        pass_on(*corner)
    for wave in waves:
        for corner in wave:
            swapped(*corner)
        for corner in wave:
            forward_z(*corner)
    for jy in (0, 2):
        forward_x(jy)

    def along_y(step):
        quotient = []
        for b in range(2):
            blurred = None
            for r in range(RANK):
                quads = [
                    after_x[r, 4 * b : 4 * b + 8, :, 16 * i : 16 * i + 16, :].reshape(256, LANES)
                    for i in range(4 * step, 4 * step + 4)
                ]
                part = dot(ty[r], jnp.concatenate(quads, axis=1))
                blurred = part if blurred is None else blurred + part
            rows = slice(128 * b, 128 * b + 128)
            quads = [seen[i, rows, :] for i in range(4 * step, 4 * step + 4)]
            quads = jnp.concatenate(quads, axis=1).astype(F32)
            quotient.append((RANK * quads / (blurred + RANK * BACKGROUND)).astype(BF16))
        quotient = jnp.concatenate(quotient, axis=0)
        for r in range(RANK):
            done = dot(tyb[r * 128 : r * 128 + 128, :], quotient).astype(BF16)
            for k in range(4):
                i = 4 * step + k
                back_y[r * 8 : r * 8 + 8, 16 * i : 16 * i + 16, :] = done[
                    :, k * 128 : k * 128 + 128
                ].reshape(8, 16, LANES)

    def backward_x(half):
        within = slice(half * 64, half * 64 + 192)
        for g in (0, 2):
            for r in range(RANK):
                at = (r * GROUPS + g) * 2
                sides = jnp.concatenate([back_y[at + k, within, :] for k in range(4)], axis=1)
                done = dot(txb[half, r, :, 0:192], sides).astype(BF16)
                for k in range(4):
                    rows = slice(k % 2 * 64, k % 2 * 64 + 64)
                    back_x[g + k // 2, half, rows, r * 128 : (r + 1) * 128] = done[
                        :, k * 128 : k * 128 + 128
                    ]

    def backward_z(half):
        parts_z = [dot(back_x[g, half], wb[g]) for g in range(GROUPS)]
        both = (parts_z[0] + parts_z[1] + (parts_z[2] + parts_z[3]))[:, LANES:]
        is_low = iota((64, LANES), 1) < 64
        rims[half, 0] = jnp.where(is_low, both[0:64], pltpu.roll(both[64:128], 64, 1))
        rims[half, 1] = jnp.where(is_low, pltpu.roll(both[0:64], 64, 1), both[64:128])
        for which in range(2):
            pl.when((below, above)[which])(rim_copy(half, which).start)
        for g in range(GROUPS):
            for c in range(4):
                at = (g + c) % 4
                sums[half, c, :, at * 32 : at * 32 + 32] = parts_z[g][:, at * 32 : at * 32 + 32]

    far = (1 - chip) * 2 + core

    def sum_copy(source, target, index, device):
        return pltpu.make_async_remote_copy(
            src_ref=source, dst_ref=target, send_sem=sum_send.at[index],
            recv_sem=sum_recv.at[index], device_id=device, device_id_type=MESH,
        )

    far_swap = [
        sum_copy(sums.at[h, (1 - chip) * 2 + 1 - core], got_core.at[h, 0], h, partner) for h in range(2)
    ]
    near_swap = [
        sum_copy(sums.at[h, chip * 2 + 1 - core], got_core.at[h, 1], 2 + h, partner) for h in range(2)
    ]
    over = [sum_copy(sums.at[h, far], got_chip.at[h], 4 + h, at_vert(q * 4 + far)) for h in range(2)]

    def rim_copy(h, which):
        home = (vert - slot - 1, vert - slot + 4)[which]
        return pltpu.make_async_remote_copy(
            src_ref=rims.at[h, which], dst_ref=got_edge.at[slot, h], send_sem=sum_send.at[6 + 2 * h + which],
            recv_sem=sum_recv.at[6 + 2 * slot + h], device_id=at_vert(home), device_id_type=MESH,
        )

    def rim_came(h):
        for k in range(VIEWS):
            pltpu.make_async_remote_copy(
                src_ref=rims.at[h, 0], dst_ref=got_edge.at[k, h], send_sem=sum_send.at[6],
                recv_sem=sum_recv.at[6 + 2 * k + h], device_id=partner, device_id_type=MESH,
            ).wait_recv()

    def backward(h):
        backward_x(h)
        backward_z(h)
        far_swap[h].start()
        near_swap[h].start()

    def pass_over(h):
        far_swap[h].wait_recv()
        sums[h, far] = sums[h, far] + got_core[h, 0]
        over[h].start()

    pl.when(~last & above)(lambda: pl.semaphore_wait(ready, 1))
    for step in range(3):
        along_y(step)
    backward(0)
    along_y(3)
    pass_over(0)
    backward(1)
    pass_over(1)

    for k in range(1, VIEWS):
        part_copy(slot, k - 1, partner, 0).wait_send()

    @pl.when(is_edge)
    def _():
        for k in range(VIEWS):
            outer_copy(0, k, partner, 0).wait_send()

    def sent(ref, semaphore):
        pltpu.make_async_remote_copy(
            src_ref=ref, dst_ref=ref, send_sem=semaphore, recv_sem=face_recv.at[0],
            device_id=partner, device_id_type=MESH,
        ).wait_send()

    for name, (index, (_, there), _) in ways.items():
        relayed = field.at[0:3, 0:2, :, 0:1] if name[0] == "v" else field.at[0:2, 0:2, :, 0:1]

        @pl.when(there)
        def _():
            sent(field.at[1, 1, core], face_send.at[index])
            sent(relayed, face_send.at[4 + index])

    sent(field.at[:, :, core], core_send.at[0])

    start = jnp.where(last, RAD, 0)
    lane = iota((64, LANES), 1)
    keep = is_edge & (lane >= start) & (lane < start + RAD)
    for h in range(2):
        near_swap[h].wait_recv()
        mine = sums[h, slot] + got_core[h, 1]
        over[h].wait_recv()
        mine = mine + got_chip[h]

        pl.when(is_edge)(lambda: rim_came(h))
        edge = got_edge[0, h] + got_edge[1, h] + (got_edge[2, h] + got_edge[3, h])
        for g in range(GROUPS):
            own = pltpu.roll(mine, (8 - g - slot) % 4 * 32, 1)
            sides = []
            for k in range(2):
                rim = pltpu.roll(edge, (start + LANES - 64 * k - RAD * g) % LANES, 1)
                part = own[64 * k : 64 * k + 64] + jnp.where(keep, rim, 0.0)
                sides.append(part.reshape(8, 8, LANES) * (1.0 / (RANK * VIEWS)))
            part = jnp.stack(swap_quads(*sides), axis=1).reshape(16, 8, LANES)
            at = (slice(16 * h, 16 * h + 16), slice(g * 8, g * 8 + 8))
            refined[at] = est[at] * part[:, :, 0:BLOCK]

    for copy in far_swap + near_swap + over:
        copy.wait_send()
    for which in range(2):

        @pl.when((below, above)[which])
        def _():
            for h in range(2):
                rim_copy(h, which).wait_send()


def local(estimate, view_tiles, slot_view, psf_taps):
    vmem = pl.BlockSpec(memory_space=pltpu.VMEM)
    hbm = pl.BlockSpec(memory_space=pltpu.HBM)
    tile = view_tiles[0, 0, 0]
    psf = jnp.transpose(psf_taps, (1, 2, 0, 3))
    scratch = [
        pltpu.VMEM(estimate.shape, F32),
        pltpu.VMEM(tile.shape, BF16),
        pltpu.VMEM(psf.shape, F32),
        pltpu.VMEM(slot_view.shape, jnp.int32),
        pltpu.VMEM((256, LANES), BF16),
        pltpu.VMEM((VIEWS, 128, LANES), BF16),
        pltpu.VMEM((2, 128, LANES), BF16),
        pltpu.VMEM((3, 3, 2, 10, 64, LANES), BF16),
        pltpu.VMEM((RANK, 12, 2, 384, LANES), BF16),
        pltpu.VMEM((RANK, 12, 2, 256, LANES), BF16),
        pltpu.VMEM((16, 256, LANES), BF16),
        pltpu.VMEM((24, 256, LANES), BF16),
        pltpu.VMEM((GROUPS, 2, 128, RANK * LANES), BF16),
        pltpu.VMEM((2, 4, 128, LANES), F32),
        pltpu.VMEM((2, 2, 64, LANES), F32),
        pltpu.VMEM((2, 2, 128, LANES), F32),
        pltpu.VMEM((2, 128, LANES), F32),
        pltpu.VMEM((VIEWS, 2, 64, LANES), F32),
        pltpu.VMEM((2, 24, LANES), F32),
        pltpu.VMEM((RANK, 128, 256), BF16),
        pltpu.VMEM((RANK, 128, 256), BF16),
        pltpu.VMEM((256, RANK * LANES), BF16),
        pltpu.VMEM((RANK * 128, 256), BF16),
        pltpu.VMEM((2, RANK, 64, 256), BF16),
        pltpu.VMEM((GROUPS, RANK * LANES, 256), BF16),
        pltpu.SemaphoreType.DMA((4,)),
        pltpu.SemaphoreType.DMA((7,)),
        pltpu.SemaphoreType.DMA((6,)),
        pltpu.SemaphoreType.DMA((8,)),
        pltpu.SemaphoreType.DMA((27,)),
        pltpu.SemaphoreType.DMA((1,)),
        pltpu.SemaphoreType.DMA((9,)),
        pltpu.SemaphoreType.DMA((10,)),
        pltpu.SemaphoreType.DMA((14,)),
        pltpu.SemaphoreType.REGULAR,
    ]
    return pl.pallas_call(
        kernel,
        out_shape=pltpu.VMEM(estimate.shape, F32),
        in_specs=[hbm] * 4,
        out_specs=vmem,
        scratch_shapes=scratch,
        compiler_params=pltpu.CompilerParams(
            collective_id=0, has_side_effects=True, vmem_limit_bytes=56 * 1024 * 1024
        ),
    )(*(pltpu.with_memory_space_constraint(a, pltpu.HBM) for a in (estimate, tile, psf, slot_view)))


def solution(mesh):
    placed = (
        P("bx", "by", "vert"),
        P("bx", "by", "vert", None, None, None),
        P("bx", "by", None),
        P(),
    )
    return jax.shard_map(
        local, mesh=mesh, in_specs=placed, out_specs=P("bx", "by", "vert"), check_vma=False
    )
```

```python
import jax
import jax.numpy as jnp
from jax import lax
from jax.experimental import pallas as pl
from jax.experimental.pallas import tpu as pltpu
from jax.sharding import PartitionSpec as P

BACKGROUND = 0.1
MESH = pl.DeviceIdType.MESH
F32, BF16 = jnp.float32, jnp.bfloat16
BLOCK = 32
RAD = 16
TAPS = 33
RANK = 3
VIEWS = 4
GROUPS = 4
LANES = 128


def iota(shape, axis):
    return lax.broadcasted_iota(jnp.int32, shape, axis)


def dot(a, b):
    return jnp.dot(a, b, preferred_element_type=F32)


def band(line, rows, start):
    line = jnp.broadcast_to(line, (rows, LANES))
    return pltpu.roll(line, start % LANES, 1, stride=1, stride_axis=0)


def swap_quads(a, b):
    low, axis = iota(a.shape, a.ndim - 2) < 4, a.ndim - 2
    return jnp.where(low, a, pltpu.roll(b, 4, axis)), jnp.where(low, pltpu.roll(a, 4, axis), b)


def build_taps(psf, slot_view, slot, taps):
    listed = slot_view[...]
    view = jnp.sum(jnp.where(iota(listed.shape, 2) == slot, listed, 0), axis=2, keepdims=True)
    held = iota((VIEWS, TAPS), 0) == view[0]
    mine = jnp.sum(jnp.where(held[None, None], psf[...], 0.0), axis=2)
    mine = (mine / jnp.sum(mine, axis=-1, keepdims=True)).astype(BF16).astype(F32)
    taps[...] = jnp.zeros_like(taps)
    for a in range(3):
        taps[0, 8 * a : 8 * a + RANK, :TAPS] = mine[a]
    flip = (iota((LANES, LANES), 0) + iota((LANES, LANES), 1) == TAPS - 1).astype(BF16)
    taps[1] = dot(taps[0].astype(BF16), flip)


def build_z(taps, wz, wb):
    z_in, z_out = iota((LANES, LANES), 0), iota((LANES, LANES), 1)
    near = jnp.abs(z_in - z_out) <= RAD
    rim, out = iota((32, LANES), 0), iota((32, LANES), 1)
    rim_ok = ((rim < RAD) & (out <= rim)) | ((rim >= RAD) & (out >= rim + 96))
    lane16 = iota((16, LANES), 1)
    for r in range(RANK):
        forward, backward = taps[1, 16 + r : 17 + r, :], taps[0, 16 + r : 17 + r, :]
        columns = slice(r * LANES, (r + 1) * LANES)
        wz[0:128, columns] = jnp.where(near, band(forward, LANES, -RAD), 0.0).astype(BF16)
        wz[128:160, columns] = jnp.where(rim_ok, band(forward, 32, 96), 0.0).astype(BF16)
        wz[160:256, columns] = jnp.zeros((96, LANES), BF16)
        main = jnp.where(near, band(backward, LANES, -RAD), 0.0)
        low = jnp.where(lane16 < RAD, band(backward, 16, 0), 0.0)
        high = jnp.where(lane16 < RAD, band(backward, 16, 96), 0.0)
        for g in range(GROUPS):
            wb[g, r * 128 : r * 128 + 128, 0:128] = (
                pltpu.roll(main, 32 * g, 1) if g else main
            ).astype(BF16)
            wb[g, r * 128 : r * 128 + 128, 128:256] = jnp.zeros((128, LANES), BF16)
            lo, hi = pltpu.roll(low, RAD * g, 1) if g else low, pltpu.roll(high, 64 + RAD * g, 1)
            wb[g, r * 128 : r * 128 + 16, 128:256] = lo.astype(BF16)
            wb[g, r * 128 + 112 : r * 128 + 128, 128:256] = hi.astype(BF16)


def build_x(taps, bx, tx, txb):
    spread = (iota((LANES, 256), 1) == 4 * iota((LANES, 256), 0)).astype(BF16)
    lane, row = iota((LANES, LANES), 1), iota((LANES, LANES), 0)
    low, high = bx > 0, bx < 3

    def tiles(line):
        turned = [band(line[:, i * LANES : (i + 1) * LANES], LANES, 0) for i in range(2)]
        return jnp.where(lane >= row, turned[0], 0.0), jnp.where(lane >= row, turned[1], turned[0])

    wide = [dot(taps[k, 0:8, :].astype(BF16), spread) for k in range(2)]
    for r in range(RANK):
        left, right = tiles(wide[0][r : r + 1])
        tx[r, :, 0:128] = left.astype(BF16)
        tx[r, :, 128:256] = right.astype(BF16)
        left, right = [m[0:64] for m in tiles(wide[1][r : r + 1])]
        txb[0, r, :, 0:128] = jnp.where((lane[0:64] >= 64) | low, left, 0.0).astype(BF16)
        txb[0, r, :, 128:256] = right.astype(BF16)
        txb[1, r, :, 0:128] = left.astype(BF16)
        txb[1, r, :, 128:256] = jnp.where(high, right, 0.0).astype(BF16)


def build_y(taps, by, ty, tyb):
    place = by * BLOCK - RAD + iota((BLOCK, LANES), 1)
    inside = (place >= 0) & (place < 4 * BLOCK)
    plain = [band(taps[0, 8 + r : 9 + r, :], BLOCK, 0) for r in range(RANK)]
    plain += [
        jnp.where(inside, band(taps[1, 8 + r : 9 + r, :], BLOCK, 0), 0.0) for r in range(RANK)
    ]
    plain = jnp.concatenate(plain, axis=0).astype(BF16)
    y, column = iota((LANES, 256), 0), iota((LANES, 256), 1)
    wide = [
        dot(plain, (column == 16 * (y // 4) + 4 * x + y % 4).astype(BF16)).astype(BF16)
        for x in range(4)
    ]
    row, source = iota((LANES, LANES), 0), iota((LANES, LANES), 1)
    order = (row == 16 * (source % 32 // 4) + 4 * (source // 32) + source % 4).astype(BF16)
    for i in range(2 * RANK):
        done = dot(order, jnp.concatenate([m[i * 32 : i * 32 + 32] for m in wide], axis=0)).astype(BF16)
        if i < RANK:
            ty[i] = done
        else:
            tyb[(i - RANK) * 128 : (i - RANK + 1) * 128, :] = done


def kernel(
    est_hbm, tile_hbm, psf_hbm, slot_view_hbm, refined,
    est, tile, psf, slot_view,
    packed, parts, outer, field, after_z, after_x, seen, back_y, back_x, sums, rims,
    got_core, got_chip, got_edge,
    taps, tx, ty, wz, tyb, txb, wb,
    load_sem, part_send, part_recv, face_send, face_recv, core_send, core_recv, sum_send, sum_recv, ready,
):
    bx, by, vert = lax.axis_index("bx"), lax.axis_index("by"), lax.axis_index("vert")
    q, slot = vert // VIEWS, vert % VIEWS
    core, chip = slot % 2, slot // 2

    loads = [
        pltpu.make_async_copy(source, target, load_sem.at[i])
        for i, (source, target) in enumerate(
            ((est_hbm, est), (psf_hbm, psf), (slot_view_hbm, slot_view), (tile_hbm, tile))
        )
    ]
    for copy in loads:
        copy.start()

    def at_vert(index):
        return {"vert": index}

    partner = at_vert(q * 4 + chip * 2 + 1 - core)
    above, below = q < 3, q > 0
    first, last = slot == 0, slot == VIEWS - 1
    is_edge = (first & below) | (last & above)

    straight = core == 0

    def block(ju, jv):
        return jnp.where(straight, jv, ju), jnp.where(straight, ju, jv)

    def link(along_u, step):
        x_step = jnp.where(straight == along_u, step, 0)
        x, y = bx + x_step, by + step - x_step
        return {"bx": x, "by": y}, (x >= 0) & (x < 4) & (y >= 0) & (y < 4)

    u_up, u_down, v_up, v_down = link(True, 1), link(True, -1), link(False, 1), link(False, -1)

    def clear(ref):
        ref[...] = jnp.zeros(ref.shape, BF16)

    pl.when(bx == 0)(lambda: clear(field.at[:, 0, core]))
    pl.when(bx == 3)(lambda: clear(field.at[:, 2, core]))
    pl.when(by == 0)(lambda: clear(field.at[0, :, core]))
    pl.when(by == 3)(lambda: clear(field.at[2, :, core]))
    pl.when(~below)(lambda: clear(outer.at[0]))
    pl.when(~above)(lambda: clear(outer.at[1]))

    got_edge[...] = jnp.zeros_like(got_edge)
    barrier = pltpu.get_barrier_semaphore()

    def greet(device):
        pl.semaphore_signal(barrier, inc=1, device_id=device, device_id_type=MESH)

    for k in range(1, VIEWS):
        greet(at_vert(q * 4 + (slot + k) % VIEWS))
    for device, there in (u_up, u_down, v_up, v_down):
        pl.when(there)(lambda device=device: greet(device))

    @pl.when(above)
    def _():
        greet(at_vert(vert - slot + 4))

        @pl.when(last)
        def _():
            for k in range(2, VIEWS + 1):
                greet(at_vert(vert + k))

    beside = [(there, 1) for _, there in (u_up, u_down, v_up, v_down)]
    beside += [(first & below, VIEWS), (~first & below, 1)]
    pl.semaphore_wait(barrier, 3 + sum(jnp.where(there, n, 0) for there, n in beside))

    def answer(device):
        pl.semaphore_signal(ready, inc=1, device_id=device, device_id_type=MESH)

    @pl.when(first & below)
    def _():
        for k in range(1, VIEWS + 1):
            answer(at_vert(vert - k))

    pl.when(~first & below)(lambda: answer(at_vert(vert - slot - 1)))

    loads[0].wait()
    groups = est[...].reshape(BLOCK, GROUPS, 8, BLOCK)
    line = jnp.concatenate([groups[:, g].reshape(256, BLOCK) for g in range(GROUPS)], axis=1)
    line = pltpu.roll(line, slot * 32, 1).reshape(16, 2, 8, LANES)
    for side, quads in enumerate(swap_quads(line[:, 0], line[:, 1])):
        packed[side * 128 : side * 128 + 128, :] = quads.reshape(128, LANES).astype(BF16)

    def part_copy(source, send, device, side):
        return pltpu.make_async_remote_copy(
            src_ref=packed.at[pl.ds(side * 128, 128), :], dst_ref=parts.at[source],
            send_sem=part_send.at[send], recv_sem=part_recv.at[source],
            device_id=device, device_id_type=MESH,
        )

    for k in range(1, VIEWS):
        other = (slot + k) % VIEWS
        part_copy(slot, k - 1, at_vert(q * 4 + other), other % 2).start()

    def outer_copy(which, send, device, side):
        return pltpu.make_async_remote_copy(
            src_ref=packed.at[pl.ds(side * 128, 128), :], dst_ref=outer.at[which],
            send_sem=part_send.at[3 + send], recv_sem=part_recv.at[4 + which],
            device_id=device, device_id_type=MESH,
        )

    @pl.when(first & below)
    def _():
        for k in range(VIEWS):
            outer_copy(1, k, at_vert(vert - 4 + k), k % 2).start()

    parts[slot] = packed[pl.ds(core * 128, 128), :]
    loads[1].wait()
    loads[2].wait()
    build_taps(psf, slot_view, slot, taps)
    build_z(taps, wz, wb)

    def assemble():
        for k in range(1, VIEWS):
            part_copy((slot + k) % VIEWS, 0, partner, 0).wait_recv()
        chunk = iota((128, LANES), 1) // 32
        have = [parts[k].astype(F32) for k in range(VIEWS)]
        for g in range(GROUPS):
            line = have[(3 - g) % 4]
            for at in range(3):
                line = jnp.where(chunk == at, have[(at - g) % 4], line)
            if g:
                line = pltpu.roll(line, LANES - 32 * g, 1)
            for tp in range(2):
                field[1, 1, core, 4 * tp + g] = line[64 * tp : 64 * tp + 64].astype(BF16)

    def assemble_rims():
        for k, there in enumerate((below, above)):
            pl.when(there)(lambda k=k: outer_copy(k, 0, partner, 0).wait_recv())
        is_above = iota((128, LANES), 1) % 32 < RAD
        line = jnp.where(is_above, outer[1].astype(F32), outer[0].astype(F32))
        field[1, 1, core, 8:10] = pltpu.roll(line, RAD, 1).astype(BF16).reshape(2, 64, LANES)

    def message(ju, jv, which):
        return field.at[(*block(ju, jv), core, slice(4 * which, min(4 * which + 4, 10)))]

    def face_copy(source, target, which, send, device):
        return pltpu.make_async_remote_copy(
            src_ref=message(*source, which), dst_ref=message(*target, which),
            send_sem=face_send.at[send],
            recv_sem=face_recv.at[which * 9 + target[0] * 3 + target[1]],
            device_id=device, device_id_type=MESH,
        )

    ways = {"u_up": (0, u_up, (0, 1)), "u_down": (1, u_down, (2, 1)), "v_up": (2, v_up, (1, 0)), "v_down": (3, v_down, (1, 2))}

    def send_own(name, which):
        index, (device, there), target = ways[name]
        pl.when(there)(face_copy((1, 1), target, which, index, device).start)

    def relay(name, along, which):
        index, (device, there), target = ways[name]
        source = (along, 1) if name[0] == "v" else (1, along)
        target = (along, target[1]) if name[0] == "v" else (target[0], along)
        pl.when(there)(face_copy(source, target, which, 4 + index, device).start)

    def came(ju, jv, which, over):
        there = ways[f"{over}_{'down' if (jv if over == 'v' else ju) == 0 else 'up'}"][1][1]
        copy = face_copy((ju, jv), (ju, jv), which, 0, partner)
        pl.when(there)(copy.wait_recv)

    def core_copy(jy, jx, side):
        return pltpu.make_async_remote_copy(
            src_ref=field.at[jy, jx, side], dst_ref=field.at[jy, jx, side],
            send_sem=core_send.at[0], recv_sem=core_recv.at[jy * 3 + jx],
            device_id=partner, device_id_type=MESH,
        )

    def pass_on(ju, jv):
        core_copy(*block(ju, jv), core).start()

    def swapped(jy, jx):
        core_copy(jy, jx, 1 - core).wait_recv()

    def forward_z(*pieces):
        rim = jnp.concatenate([field[jy, jx, side, 8 + tp] for jy, jx, side in pieces for tp in range(2)])
        for g in range(GROUPS):
            turned = pltpu.roll(rim, LANES - 32 * g, 1) if g else rim
            main = jnp.concatenate(
                [field[jy, jx, side, 4 * tp + g] for jy, jx, side in pieces for tp in range(2)]
            )
            done = dot(jnp.concatenate([main, turned], axis=1), wz[...]).astype(BF16)
            for i, (jy, jx, side) in enumerate(pieces):
                for r in range(RANK):
                    after_z[r, jy * GROUPS + g, side, jx * 128 : jx * 128 + 128, :] = done[
                        i * 128 : (i + 1) * 128, r * 128 : (r + 1) * 128
                    ]

    def forward_x(jy):
        for r in range(RANK):
            for group in (jy * GROUPS, jy * GROUPS + 2):
                for b in range(2):
                    rows = slice(b * 128, b * 128 + 256)
                    both = [after_z[r, group + k // 2, k % 2, rows, :] for k in range(4)]
                    done = dot(tx[r], jnp.concatenate(both, axis=1)).astype(BF16)
                    for k in range(4):
                        after_x[r, group + k // 2, k % 2, b * 128 : b * 128 + 128, :] = done[
                            :, k * 128 : k * 128 + 128
                        ]

    assemble()
    for name in ("u_up", "u_down", "v_up", "v_down"):
        send_own(name, 0)
    for name in ("v_up", "v_down", "u_up", "u_down"):
        send_own(name, 1)

    @pl.when(last & above)
    def _():
        pl.semaphore_wait(ready, VIEWS)
        for k in range(VIEWS):
            outer_copy(0, k, at_vert(vert + 1 + k), k % 2).start()

    build_x(taps, bx, tx, txb)
    assemble_rims()
    for name in ("u_up", "u_down", "v_up", "v_down"):
        send_own(name, 2)
    pass_on(1, 1)
    for side in (0, 2):
        came(side, 1, 0, "u")
    for one, other in ((0, 2), (2, 0)):
        relay("v_up", one, 0)
        relay("v_down", other, 0)
    build_y(taps, by, ty, tyb)
    for side in (0, 2):
        came(1, side, 1, "v")
    for one, other in ((0, 2), (2, 0)):
        relay("u_up", one, 1)
        relay("u_down", other, 1)
    loads[3].wait()

    def order_tile(i, carry):
        quad = tile[pl.ds(4 * i, 4)].astype(F32).reshape(2, 2, 8, 8, LANES)
        sides = swap_quads(quad[:, 0], quad[:, 1])
        rows = jnp.stack([m[x] for m in sides for x in range(2)], axis=1)
        seen[i] = rows.reshape(256, LANES).astype(BF16)
        return carry

    lax.fori_loop(0, 16, order_tile, 0, unroll=4)
    swapped(1, 1)
    forward_z((1, 1, 0), (1, 1, 1))
    for side in (0, 2):
        came(side, 1, 2, "u")
    for one, other in ((0, 2), (2, 0)):
        relay("v_up", one, 2)
        relay("v_down", other, 2)
    for side in (0, 2):
        came(side, 1, 1, "u")
        pass_on(side, 1)
        came(1, side, 0, "v")
        came(1, side, 2, "v")
        pass_on(1, side)
    face_pairs = (((1, 0), (1, 2)), ((0, 1), (2, 1)))
    waves = (((0, 0), (2, 2)), ((0, 2), (2, 0)))

    def wave_came(wave):
        for corner in wave:
            came(*corner, 0, "v")
            came(*corner, 1, "u")
            came(*corner, 2, "v")
            pass_on(*corner)

    for one, other in face_pairs:
        forward_z((*one, core), (*other, core))
    for one, other in face_pairs:
        swapped(*one)
        swapped(*other)
    for one, other in face_pairs:
        forward_z((*one, 1 - core), (*other, 1 - core))
    wave_came(waves[0])
    forward_x(1)
    wave_came(waves[1])
    for one, other in waves:
        forward_z((*one, core), (*other, core))
    for one, other in waves:
        swapped(*one)
        swapped(*other)
    for one, other in waves:
        forward_z((*one, 1 - core), (*other, 1 - core))
    for jy in (0, 2):
        forward_x(jy)

    def along_y(step):
        quotient = []
        for b in range(2):
            blurred = None
            for r in range(RANK):
                quads = [
                    after_x[r, 4 * b : 4 * b + 8, :, 16 * i : 16 * i + 16, :].reshape(256, LANES)
                    for i in range(4 * step, 4 * step + 4)
                ]
                part = dot(ty[r], jnp.concatenate(quads, axis=1))
                blurred = part if blurred is None else blurred + part
            rows = slice(128 * b, 128 * b + 128)
            quads = [seen[i, rows, :] for i in range(4 * step, 4 * step + 4)]
            quads = jnp.concatenate(quads, axis=1).astype(F32)
            quotient.append((RANK * quads / (blurred + RANK * BACKGROUND)).astype(BF16))
        quotient = jnp.concatenate(quotient, axis=0)
        for r in range(RANK):
            done = dot(tyb[r * 128 : r * 128 + 128, :], quotient).astype(BF16)
            for k in range(4):
                i = 4 * step + k
                back_y[r * 8 : r * 8 + 8, 16 * i : 16 * i + 16, :] = done[
                    :, k * 128 : k * 128 + 128
                ].reshape(8, 16, LANES)

    def backward_x(half):
        within = slice(half * 64, half * 64 + 192)
        for g in (0, 2):
            for r in range(RANK):
                at = (r * GROUPS + g) * 2
                sides = jnp.concatenate([back_y[at + k, within, :] for k in range(4)], axis=1)
                done = dot(txb[half, r, :, 0:192], sides).astype(BF16)
                for k in range(4):
                    rows = slice(k % 2 * 64, k % 2 * 64 + 64)
                    back_x[g + k // 2, half, rows, r * 128 : (r + 1) * 128] = done[
                        :, k * 128 : k * 128 + 128
                    ]

    def backward_z(half):
        parts_z = [dot(back_x[g, half], wb[g]) for g in range(GROUPS)]
        both = (parts_z[0] + parts_z[1] + (parts_z[2] + parts_z[3]))[:, LANES:]
        is_low = iota((64, LANES), 1) < 64
        rims[half, 0] = jnp.where(is_low, both[0:64], pltpu.roll(both[64:128], 64, 1))
        rims[half, 1] = jnp.where(is_low, pltpu.roll(both[0:64], 64, 1), both[64:128])
        for which in range(2):
            pl.when((below, above)[which])(rim_copy(half, which).start)
        for g in range(GROUPS):
            for c in range(4):
                at = (g + c) % 4
                sums[half, c, :, at * 32 : at * 32 + 32] = parts_z[g][:, at * 32 : at * 32 + 32]

    far = (1 - chip) * 2 + core

    def sum_copy(source, target, index, device):
        return pltpu.make_async_remote_copy(
            src_ref=source, dst_ref=target, send_sem=sum_send.at[index],
            recv_sem=sum_recv.at[index], device_id=device, device_id_type=MESH,
        )

    far_swap = [
        sum_copy(sums.at[h, (1 - chip) * 2 + 1 - core], got_core.at[h, 0], h, partner) for h in range(2)
    ]
    near_swap = [
        sum_copy(sums.at[h, chip * 2 + 1 - core], got_core.at[h, 1], 2 + h, partner) for h in range(2)
    ]
    over = [sum_copy(sums.at[h, far], got_chip.at[h], 4 + h, at_vert(q * 4 + far)) for h in range(2)]

    def rim_copy(h, which):
        home = (vert - slot - 1, vert - slot + 4)[which]
        return pltpu.make_async_remote_copy(
            src_ref=rims.at[h, which], dst_ref=got_edge.at[slot, h], send_sem=sum_send.at[6 + 2 * h + which],
            recv_sem=sum_recv.at[6 + 2 * slot + h], device_id=at_vert(home), device_id_type=MESH,
        )

    def rim_came(h):
        for k in range(VIEWS):
            pltpu.make_async_remote_copy(
                src_ref=rims.at[h, 0], dst_ref=got_edge.at[k, h], send_sem=sum_send.at[6],
                recv_sem=sum_recv.at[6 + 2 * k + h], device_id=partner, device_id_type=MESH,
            ).wait_recv()

    def backward(h):
        backward_x(h)
        backward_z(h)
        far_swap[h].start()
        near_swap[h].start()

    def pass_over(h):
        far_swap[h].wait_recv()
        sums[h, far] = sums[h, far] + got_core[h, 0]
        over[h].start()

    pl.when(~last & above)(lambda: pl.semaphore_wait(ready, 1))
    for step in range(3):
        along_y(step)
    backward(0)
    along_y(3)
    pass_over(0)
    backward(1)
    pass_over(1)

    for k in range(1, VIEWS):
        part_copy(slot, k - 1, partner, 0).wait_send()

    @pl.when(is_edge)
    def _():
        for k in range(VIEWS):
            outer_copy(0, k, partner, 0).wait_send()

    def sent(ref, semaphore):
        pltpu.make_async_remote_copy(
            src_ref=ref, dst_ref=ref, send_sem=semaphore, recv_sem=face_recv.at[0],
            device_id=partner, device_id_type=MESH,
        ).wait_send()

    for name, (index, (_, there), _) in ways.items():
        relayed = field.at[0:3, 0:2, :, 0:1] if name[0] == "v" else field.at[0:2, 0:2, :, 0:1]

        @pl.when(there)
        def _():
            sent(field.at[1, 1, core], face_send.at[index])
            sent(relayed, face_send.at[4 + index])

    sent(field.at[:, :, core], core_send.at[0])

    start = jnp.where(last, RAD, 0)
    lane = iota((64, LANES), 1)
    keep = is_edge & (lane >= start) & (lane < start + RAD)
    for h in range(2):
        near_swap[h].wait_recv()
        mine = sums[h, slot] + got_core[h, 1]
        over[h].wait_recv()
        mine = mine + got_chip[h]

        pl.when(is_edge)(lambda: rim_came(h))
        edge = got_edge[0, h] + got_edge[1, h] + (got_edge[2, h] + got_edge[3, h])
        for g in range(GROUPS):
            own = pltpu.roll(mine, (8 - g - slot) % 4 * 32, 1)
            sides = []
            for k in range(2):
                rim = pltpu.roll(edge, (start + LANES - 64 * k - RAD * g) % LANES, 1)
                part = own[64 * k : 64 * k + 64] + jnp.where(keep, rim, 0.0)
                sides.append(part.reshape(8, 8, LANES) * (1.0 / (RANK * VIEWS)))
            part = jnp.stack(swap_quads(*sides), axis=1).reshape(16, 8, LANES)
            at = (slice(16 * h, 16 * h + 16), slice(g * 8, g * 8 + 8))
            refined[at] = est[at] * part[:, :, 0:BLOCK]

    for copy in far_swap + near_swap + over:
        copy.wait_send()
    for which in range(2):

        @pl.when((below, above)[which])
        def _():
            for h in range(2):
                rim_copy(h, which).wait_send()


def local(estimate, view_tiles, slot_view, psf_taps):
    vmem = pl.BlockSpec(memory_space=pltpu.VMEM)
    hbm = pl.BlockSpec(memory_space=pltpu.HBM)
    tile = view_tiles[0, 0, 0]
    psf = jnp.transpose(psf_taps, (1, 2, 0, 3))
    scratch = [
        pltpu.VMEM(estimate.shape, F32),
        pltpu.VMEM(tile.shape, BF16),
        pltpu.VMEM(psf.shape, F32),
        pltpu.VMEM(slot_view.shape, jnp.int32),
        pltpu.VMEM((256, LANES), BF16),
        pltpu.VMEM((VIEWS, 128, LANES), BF16),
        pltpu.VMEM((2, 128, LANES), BF16),
        pltpu.VMEM((3, 3, 2, 10, 64, LANES), BF16),
        pltpu.VMEM((RANK, 12, 2, 384, LANES), BF16),
        pltpu.VMEM((RANK, 12, 2, 256, LANES), BF16),
        pltpu.VMEM((16, 256, LANES), BF16),
        pltpu.VMEM((24, 256, LANES), BF16),
        pltpu.VMEM((GROUPS, 2, 128, RANK * LANES), BF16),
        pltpu.VMEM((2, 4, 128, LANES), F32),
        pltpu.VMEM((2, 2, 64, LANES), F32),
        pltpu.VMEM((2, 2, 128, LANES), F32),
        pltpu.VMEM((2, 128, LANES), F32),
        pltpu.VMEM((VIEWS, 2, 64, LANES), F32),
        pltpu.VMEM((2, 24, LANES), F32),
        pltpu.VMEM((RANK, 128, 256), BF16),
        pltpu.VMEM((RANK, 128, 256), BF16),
        pltpu.VMEM((256, RANK * LANES), BF16),
        pltpu.VMEM((RANK * 128, 256), BF16),
        pltpu.VMEM((2, RANK, 64, 256), BF16),
        pltpu.VMEM((GROUPS, RANK * LANES, 256), BF16),
        pltpu.SemaphoreType.DMA((4,)),
        pltpu.SemaphoreType.DMA((7,)),
        pltpu.SemaphoreType.DMA((6,)),
        pltpu.SemaphoreType.DMA((8,)),
        pltpu.SemaphoreType.DMA((27,)),
        pltpu.SemaphoreType.DMA((1,)),
        pltpu.SemaphoreType.DMA((9,)),
        pltpu.SemaphoreType.DMA((10,)),
        pltpu.SemaphoreType.DMA((14,)),
        pltpu.SemaphoreType.REGULAR,
    ]
    return pl.pallas_call(
        kernel,
        out_shape=pltpu.VMEM(estimate.shape, F32),
        in_specs=[hbm] * 4,
        out_specs=vmem,
        scratch_shapes=scratch,
        compiler_params=pltpu.CompilerParams(
            collective_id=0, has_side_effects=True, vmem_limit_bytes=56 * 1024 * 1024
        ),
    )(*(pltpu.with_memory_space_constraint(a, pltpu.HBM) for a in (estimate, tile, psf, slot_view)))


def solution(mesh):
    placed = (
        P("bx", "by", "vert"),
        P("bx", "by", "vert", None, None, None),
        P("bx", "by", None),
        P(),
    )
    return jax.shard_map(
        local, mesh=mesh, in_specs=placed, out_specs=P("bx", "by", "vert"), check_vma=False
    )
```

```python
import jax
import jax.numpy as jnp
from jax import lax
from jax.experimental import pallas as pl
from jax.experimental.pallas import tpu as pltpu
from jax.sharding import PartitionSpec as P

BACKGROUND = 0.1
MESH = pl.DeviceIdType.MESH
F32, BF16 = jnp.float32, jnp.bfloat16
BLOCK = 32
RAD = 16
TAPS = 33
RANK = 3
VIEWS = 4
GROUPS = 4
LANES = 128


def iota(shape, axis):
    return lax.broadcasted_iota(jnp.int32, shape, axis)


def dot(a, b):
    return jnp.dot(a, b, preferred_element_type=F32)


def band(line, rows, start):
    line = jnp.broadcast_to(line, (rows, LANES))
    return pltpu.roll(line, start % LANES, 1, stride=1, stride_axis=0)


def swap_quads(a, b):
    low, axis = iota(a.shape, a.ndim - 2) < 4, a.ndim - 2
    return jnp.where(low, a, pltpu.roll(b, 4, axis)), jnp.where(low, pltpu.roll(a, 4, axis), b)


def build_taps(psf, slot_view, slot, taps):
    listed = slot_view[...]
    view = jnp.sum(jnp.where(iota(listed.shape, 2) == slot, listed, 0), axis=2, keepdims=True)
    held = iota((VIEWS, TAPS), 0) == view[0]
    mine = jnp.sum(jnp.where(held[None, None], psf[...], 0.0), axis=2)
    mine = (mine / jnp.sum(mine, axis=-1, keepdims=True)).astype(BF16).astype(F32)
    taps[...] = jnp.zeros_like(taps)
    for a in range(3):
        taps[0, 8 * a : 8 * a + RANK, :TAPS] = mine[a]
    flip = (iota((LANES, LANES), 0) + iota((LANES, LANES), 1) == TAPS - 1).astype(BF16)
    taps[1] = dot(taps[0].astype(BF16), flip)


def build_z(taps, wz, wb):
    z_in, z_out = iota((LANES, LANES), 0), iota((LANES, LANES), 1)
    near = jnp.abs(z_in - z_out) <= RAD
    rim, out = iota((32, LANES), 0), iota((32, LANES), 1)
    rim_ok = ((rim < RAD) & (out <= rim)) | ((rim >= RAD) & (out >= rim + 96))
    lane16 = iota((16, LANES), 1)
    for r in range(RANK):
        forward, backward = taps[1, 16 + r : 17 + r, :], taps[0, 16 + r : 17 + r, :]
        columns = slice(r * LANES, (r + 1) * LANES)
        wz[0:128, columns] = jnp.where(near, band(forward, LANES, -RAD), 0.0).astype(BF16)
        wz[128:160, columns] = jnp.where(rim_ok, band(forward, 32, 96), 0.0).astype(BF16)
        wz[160:256, columns] = jnp.zeros((96, LANES), BF16)
        main = jnp.where(near, band(backward, LANES, -RAD), 0.0)
        low = jnp.where(lane16 < RAD, band(backward, 16, 0), 0.0)
        high = jnp.where(lane16 < RAD, band(backward, 16, 96), 0.0)
        for g in range(GROUPS):
            wb[g, r * 128 : r * 128 + 128, 0:128] = (
                pltpu.roll(main, 32 * g, 1) if g else main
            ).astype(BF16)
            wb[g, r * 128 : r * 128 + 128, 128:256] = jnp.zeros((128, LANES), BF16)
            lo, hi = pltpu.roll(low, RAD * g, 1) if g else low, pltpu.roll(high, 64 + RAD * g, 1)
            wb[g, r * 128 : r * 128 + 16, 128:256] = lo.astype(BF16)
            wb[g, r * 128 + 112 : r * 128 + 128, 128:256] = hi.astype(BF16)


def build_x(taps, bx, tx, txb):
    spread = (iota((LANES, 256), 1) == 4 * iota((LANES, 256), 0)).astype(BF16)
    lane, row = iota((LANES, LANES), 1), iota((LANES, LANES), 0)
    low, high = bx > 0, bx < 3

    def tiles(line):
        turned = [band(line[:, i * LANES : (i + 1) * LANES], LANES, 0) for i in range(2)]
        return jnp.where(lane >= row, turned[0], 0.0), jnp.where(lane >= row, turned[1], turned[0])

    wide = [dot(taps[k, 0:8, :].astype(BF16), spread) for k in range(2)]
    for r in range(RANK):
        left, right = tiles(wide[0][r : r + 1])
        tx[r, :, 0:128] = left.astype(BF16)
        tx[r, :, 128:256] = right.astype(BF16)
        left, right = [m[0:64] for m in tiles(wide[1][r : r + 1])]
        txb[0, r, :, 0:128] = jnp.where((lane[0:64] >= 64) | low, left, 0.0).astype(BF16)
        txb[0, r, :, 128:256] = right.astype(BF16)
        txb[1, r, :, 0:128] = left.astype(BF16)
        txb[1, r, :, 128:256] = jnp.where(high, right, 0.0).astype(BF16)


def build_y(taps, by, ty, tyb):
    place = by * BLOCK - RAD + iota((BLOCK, LANES), 1)
    inside = (place >= 0) & (place < 4 * BLOCK)
    plain = [band(taps[0, 8 + r : 9 + r, :], BLOCK, 0) for r in range(RANK)]
    plain += [
        jnp.where(inside, band(taps[1, 8 + r : 9 + r, :], BLOCK, 0), 0.0) for r in range(RANK)
    ]
    plain = jnp.concatenate(plain, axis=0).astype(BF16)
    y, column = iota((LANES, 256), 0), iota((LANES, 256), 1)
    wide = [
        dot(plain, (column == 16 * (y // 4) + 4 * x + y % 4).astype(BF16)).astype(BF16)
        for x in range(4)
    ]
    row, source = iota((LANES, LANES), 0), iota((LANES, LANES), 1)
    order = (row == 16 * (source % 32 // 4) + 4 * (source // 32) + source % 4).astype(BF16)
    for i in range(2 * RANK):
        done = dot(order, jnp.concatenate([m[i * 32 : i * 32 + 32] for m in wide], axis=0)).astype(BF16)
        if i < RANK:
            ty[:, i * 256 : (i + 1) * 256] = done
        else:
            tyb[(i - RANK) * 128 : (i - RANK + 1) * 128, :] = done


def kernel(
    est_hbm, tile_hbm, psf_hbm, slot_view_hbm, refined,
    est, tile, psf, slot_view,
    packed, parts, outer, field, after_z, after_x, seen, back_y, back_x, sums, rims,
    got_core, got_chip, got_edge,
    taps, tx, ty, wz, tyb, txb, wb,
    load_sem, part_send, part_recv, face_send, face_recv, core_send, core_recv, sum_send, sum_recv, ready,
):
    bx, by, vert = lax.axis_index("bx"), lax.axis_index("by"), lax.axis_index("vert")
    q, slot = vert // VIEWS, vert % VIEWS
    core, chip = slot % 2, slot // 2

    loads = [
        pltpu.make_async_copy(source, target, load_sem.at[i])
        for i, (source, target) in enumerate(
            ((est_hbm, est), (psf_hbm, psf), (slot_view_hbm, slot_view), (tile_hbm, tile))
        )
    ]
    for copy in loads:
        copy.start()

    def at_vert(index):
        return {"vert": index}

    partner = at_vert(q * 4 + chip * 2 + 1 - core)
    above, below = q < 3, q > 0
    first, last = slot == 0, slot == VIEWS - 1
    is_edge = (first & below) | (last & above)

    straight = core == 0

    def block(ju, jv):
        return jnp.where(straight, jv, ju), jnp.where(straight, ju, jv)

    def link(along_u, step):
        x_step = jnp.where(straight == along_u, step, 0)
        x, y = bx + x_step, by + step - x_step
        return {"bx": x, "by": y}, (x >= 0) & (x < 4) & (y >= 0) & (y < 4)

    u_up, u_down, v_up, v_down = link(True, 1), link(True, -1), link(False, 1), link(False, -1)

    def clear(ref):
        ref[...] = jnp.zeros(ref.shape, BF16)

    pl.when(bx == 0)(lambda: clear(field.at[:, 0, core]))
    pl.when(bx == 3)(lambda: clear(field.at[:, 2, core]))
    pl.when(by == 0)(lambda: clear(field.at[0, :, core]))
    pl.when(by == 3)(lambda: clear(field.at[2, :, core]))
    pl.when(~below)(lambda: clear(outer.at[0]))
    pl.when(~above)(lambda: clear(outer.at[1]))

    got_edge[...] = jnp.zeros_like(got_edge)
    barrier = pltpu.get_barrier_semaphore()

    def greet(device):
        pl.semaphore_signal(barrier, inc=1, device_id=device, device_id_type=MESH)

    for k in range(1, VIEWS):
        greet(at_vert(q * 4 + (slot + k) % VIEWS))
    for device, there in (u_up, u_down, v_up, v_down):
        pl.when(there)(lambda device=device: greet(device))

    @pl.when(above)
    def _():
        greet(at_vert(vert - slot + 4))

        @pl.when(last)
        def _():
            for k in range(2, VIEWS + 1):
                greet(at_vert(vert + k))

    beside = [(there, 1) for _, there in (u_up, u_down, v_up, v_down)]
    beside += [(first & below, VIEWS), (~first & below, 1)]
    pl.semaphore_wait(barrier, 3 + sum(jnp.where(there, n, 0) for there, n in beside))

    def answer(device):
        pl.semaphore_signal(ready, inc=1, device_id=device, device_id_type=MESH)

    @pl.when(first & below)
    def _():
        for k in range(1, VIEWS + 1):
            answer(at_vert(vert - k))

    pl.when(~first & below)(lambda: answer(at_vert(vert - slot - 1)))

    loads[0].wait()
    groups = est[...].reshape(BLOCK, GROUPS, 8, BLOCK)
    line = jnp.concatenate([groups[:, g].reshape(256, BLOCK) for g in range(GROUPS)], axis=1)
    line = pltpu.roll(line, slot * 32, 1).reshape(16, 2, 8, LANES)
    for side, quads in enumerate(swap_quads(line[:, 0], line[:, 1])):
        packed[side * 128 : side * 128 + 128, :] = quads.reshape(128, LANES).astype(BF16)

    def part_copy(source, send, device, side):
        return pltpu.make_async_remote_copy(
            src_ref=packed.at[pl.ds(side * 128, 128), :], dst_ref=parts.at[source],
            send_sem=part_send.at[send], recv_sem=part_recv.at[source],
            device_id=device, device_id_type=MESH,
        )

    for k in range(1, VIEWS):
        other = (slot + k) % VIEWS
        part_copy(slot, k - 1, at_vert(q * 4 + other), other % 2).start()

    def outer_copy(which, send, device, side):
        return pltpu.make_async_remote_copy(
            src_ref=packed.at[pl.ds(side * 128, 128), :], dst_ref=outer.at[which],
            send_sem=part_send.at[3 + send], recv_sem=part_recv.at[4 + which],
            device_id=device, device_id_type=MESH,
        )

    @pl.when(first & below)
    def _():
        for k in range(VIEWS):
            outer_copy(1, k, at_vert(vert - 4 + k), k % 2).start()

    parts[slot] = packed[pl.ds(core * 128, 128), :]
    loads[1].wait()
    loads[2].wait()
    build_taps(psf, slot_view, slot, taps)
    build_z(taps, wz, wb)

    def assemble():
        for k in range(1, VIEWS):
            part_copy((slot + k) % VIEWS, 0, partner, 0).wait_recv()
        chunk = iota((128, LANES), 1) // 32
        have = [parts[k].astype(F32) for k in range(VIEWS)]
        for g in range(GROUPS):
            line = have[(3 - g) % 4]
            for at in range(3):
                line = jnp.where(chunk == at, have[(at - g) % 4], line)
            if g:
                line = pltpu.roll(line, LANES - 32 * g, 1)
            for tp in range(2):
                field[1, 1, core, 4 * tp + g] = line[64 * tp : 64 * tp + 64].astype(BF16)

    def assemble_rims():
        for k, there in enumerate((below, above)):
            pl.when(there)(lambda k=k: outer_copy(k, 0, partner, 0).wait_recv())
        is_above = iota((128, LANES), 1) % 32 < RAD
        line = jnp.where(is_above, outer[1].astype(F32), outer[0].astype(F32))
        field[1, 1, core, 8:10] = pltpu.roll(line, RAD, 1).astype(BF16).reshape(2, 64, LANES)

    def message(ju, jv, which):
        return field.at[(*block(ju, jv), core, slice(4 * which, min(4 * which + 4, 10)))]

    def face_copy(source, target, which, send, device):
        return pltpu.make_async_remote_copy(
            src_ref=message(*source, which), dst_ref=message(*target, which),
            send_sem=face_send.at[send],
            recv_sem=face_recv.at[which * 9 + target[0] * 3 + target[1]],
            device_id=device, device_id_type=MESH,
        )

    ways = {"u_up": (0, u_up, (0, 1)), "u_down": (1, u_down, (2, 1)), "v_up": (2, v_up, (1, 0)), "v_down": (3, v_down, (1, 2))}

    def send_own(name, which):
        index, (device, there), target = ways[name]
        pl.when(there)(face_copy((1, 1), target, which, index, device).start)

    def relay(name, along, which):
        index, (device, there), target = ways[name]
        source = (along, 1) if name[0] == "v" else (1, along)
        target = (along, target[1]) if name[0] == "v" else (target[0], along)
        pl.when(there)(face_copy(source, target, which, 4 + index, device).start)

    def came(ju, jv, which, over):
        there = ways[f"{over}_{'down' if (jv if over == 'v' else ju) == 0 else 'up'}"][1][1]
        copy = face_copy((ju, jv), (ju, jv), which, 0, partner)
        pl.when(there)(copy.wait_recv)

    def core_copy(jy, jx, side):
        return pltpu.make_async_remote_copy(
            src_ref=field.at[jy, jx, side], dst_ref=field.at[jy, jx, side],
            send_sem=core_send.at[0], recv_sem=core_recv.at[jy * 3 + jx],
            device_id=partner, device_id_type=MESH,
        )

    def pass_on(ju, jv):
        core_copy(*block(ju, jv), core).start()

    def swapped(jy, jx):
        core_copy(jy, jx, 1 - core).wait_recv()

    def forward_z(*blocks):
        pieces = [(*b, side) for b in blocks for side in range(2)]
        rim = jnp.concatenate([field[jy, jx, side, 8 + tp] for jy, jx, side in pieces for tp in range(2)])
        for g in range(GROUPS):
            turned = pltpu.roll(rim, LANES - 32 * g, 1) if g else rim
            main = jnp.concatenate(
                [field[jy, jx, side, 4 * tp + g] for jy, jx, side in pieces for tp in range(2)]
            )
            done = dot(jnp.concatenate([main, turned], axis=1), wz[...]).astype(BF16)
            for i, (jy, jx, side) in enumerate(pieces):
                for r in range(RANK):
                    after_z[r, jy * GROUPS + g, side, jx * 128 : jx * 128 + 128, :] = done[
                        i * 128 : (i + 1) * 128, r * 128 : (r + 1) * 128
                    ]

    def forward_x(jy):
        for r in range(RANK):
            for group in (jy * GROUPS, jy * GROUPS + 2):
                for b in range(2):
                    rows = slice(b * 128, b * 128 + 256)
                    both = [after_z[r, group + k // 2, k % 2, rows, :] for k in range(4)]
                    done = dot(tx[r], jnp.concatenate(both, axis=1)).astype(BF16)
                    for k in range(4):
                        after_x[r, group + k // 2, k % 2, b * 128 : b * 128 + 128, :] = done[
                            :, k * 128 : k * 128 + 128
                        ]

    assemble()
    for name in ("u_up", "u_down", "v_up", "v_down"):
        send_own(name, 0)
    for name in ("v_up", "v_down", "u_up", "u_down"):
        send_own(name, 1)

    @pl.when(last & above)
    def _():
        pl.semaphore_wait(ready, VIEWS)
        for k in range(VIEWS):
            outer_copy(0, k, at_vert(vert + 1 + k), k % 2).start()

    build_x(taps, bx, tx, txb)
    assemble_rims()
    for name in ("u_up", "u_down", "v_up", "v_down"):
        send_own(name, 2)
    pass_on(1, 1)
    for side in (0, 2):
        came(side, 1, 0, "u")
    for one, other in ((0, 2), (2, 0)):
        relay("v_up", one, 0)
        relay("v_down", other, 0)
    build_y(taps, by, ty, tyb)
    for side in (0, 2):
        came(1, side, 1, "v")
    for one, other in ((0, 2), (2, 0)):
        relay("u_up", one, 1)
        relay("u_down", other, 1)
    loads[3].wait()

    def order_tile(i, carry):
        quad = tile[pl.ds(4 * i, 4)].astype(F32).reshape(2, 2, 8, 8, LANES)
        sides = swap_quads(quad[:, 0], quad[:, 1])
        rows = jnp.stack([m[x] for m in sides for x in range(2)], axis=1)
        seen[i] = rows.reshape(256, LANES).astype(BF16)
        return carry

    lax.fori_loop(0, 16, order_tile, 0, unroll=4)
    swapped(1, 1)
    forward_z((1, 1))
    for side in (0, 2):
        came(side, 1, 2, "u")
    for one, other in ((0, 2), (2, 0)):
        relay("v_up", one, 2)
        relay("v_down", other, 2)
    for side in (0, 2):
        came(side, 1, 1, "u")
        pass_on(side, 1)
        came(1, side, 0, "v")
        came(1, side, 2, "v")
        pass_on(1, side)
    for side in (0, 2):
        swapped(1, side)
        swapped(side, 1)
    forward_z((1, 0), (1, 2))
    forward_z((0, 1), (2, 1))
    waves = (((0, 0), (2, 2)), ((0, 2), (2, 0)))
    for corner in waves[0]:
        came(*corner, 0, "v")
        came(*corner, 1, "u")
        came(*corner, 2, "v")
        pass_on(*corner)
    forward_x(1)
    for corner in waves[1]:
        came(*corner, 0, "v")
        came(*corner, 1, "u")
        came(*corner, 2, "v")
        pass_on(*corner)
    for wave in waves:
        for corner in wave:
            swapped(*corner)
        forward_z(*wave)
    for jy in (0, 2):
        forward_x(jy)

    def along_y(step):
        quotient = []
        for b in range(2):
            terms = []
            for r in range(RANK):
                quads = [
                    after_x[r, 4 * b : 4 * b + 8, :, 16 * i : 16 * i + 16, :].reshape(256, LANES)
                    for i in range(4 * step, 4 * step + 4)
                ]
                terms.append(jnp.concatenate(quads, axis=1))
            blurred = dot(ty[...], jnp.concatenate(terms, axis=0))
            rows = slice(128 * b, 128 * b + 128)
            quads = [seen[i, rows, :] for i in range(4 * step, 4 * step + 4)]
            quads = jnp.concatenate(quads, axis=1).astype(F32)
            quotient.append((RANK * quads / (blurred + RANK * BACKGROUND)).astype(BF16))
        quotient = jnp.concatenate(quotient, axis=0)
        for r in range(RANK):
            done = dot(tyb[r * 128 : r * 128 + 128, :], quotient).astype(BF16)
            for k in range(4):
                i = 4 * step + k
                back_y[r * 8 : r * 8 + 8, 16 * i : 16 * i + 16, :] = done[
                    :, k * 128 : k * 128 + 128
                ].reshape(8, 16, LANES)

    def backward_x(half):
        within = slice(half * 64, half * 64 + 192)
        for g in (0, 2):
            for r in range(RANK):
                at = (r * GROUPS + g) * 2
                sides = jnp.concatenate([back_y[at + k, within, :] for k in range(4)], axis=1)
                done = dot(txb[half, r, :, 0:192], sides).astype(BF16)
                for k in range(4):
                    rows = slice(k % 2 * 64, k % 2 * 64 + 64)
                    back_x[g + k // 2, half, rows, r * 128 : (r + 1) * 128] = done[
                        :, k * 128 : k * 128 + 128
                    ]

    def backward_z(half):
        parts_z = [dot(back_x[g, half], wb[g]) for g in range(GROUPS)]
        both = (parts_z[0] + parts_z[1] + (parts_z[2] + parts_z[3]))[:, LANES:]
        is_low = iota((64, LANES), 1) < 64
        rims[half, 0] = jnp.where(is_low, both[0:64], pltpu.roll(both[64:128], 64, 1))
        rims[half, 1] = jnp.where(is_low, pltpu.roll(both[0:64], 64, 1), both[64:128])
        for which in range(2):
            pl.when((below, above)[which])(rim_copy(half, which).start)
        for g in range(GROUPS):
            for c in range(4):
                at = (g + c) % 4
                sums[half, c, :, at * 32 : at * 32 + 32] = parts_z[g][:, at * 32 : at * 32 + 32]

    far = (1 - chip) * 2 + core

    def sum_copy(source, target, index, device):
        return pltpu.make_async_remote_copy(
            src_ref=source, dst_ref=target, send_sem=sum_send.at[index],
            recv_sem=sum_recv.at[index], device_id=device, device_id_type=MESH,
        )

    far_swap = [
        sum_copy(sums.at[h, (1 - chip) * 2 + 1 - core], got_core.at[h, 0], h, partner) for h in range(2)
    ]
    near_swap = [
        sum_copy(sums.at[h, chip * 2 + 1 - core], got_core.at[h, 1], 2 + h, partner) for h in range(2)
    ]
    over = [sum_copy(sums.at[h, far], got_chip.at[h], 4 + h, at_vert(q * 4 + far)) for h in range(2)]

    def rim_copy(h, which):
        home = (vert - slot - 1, vert - slot + 4)[which]
        return pltpu.make_async_remote_copy(
            src_ref=rims.at[h, which], dst_ref=got_edge.at[slot, h], send_sem=sum_send.at[6 + 2 * h + which],
            recv_sem=sum_recv.at[6 + 2 * slot + h], device_id=at_vert(home), device_id_type=MESH,
        )

    def rim_came(h):
        for k in range(VIEWS):
            pltpu.make_async_remote_copy(
                src_ref=rims.at[h, 0], dst_ref=got_edge.at[k, h], send_sem=sum_send.at[6],
                recv_sem=sum_recv.at[6 + 2 * k + h], device_id=partner, device_id_type=MESH,
            ).wait_recv()

    def backward(h):
        backward_x(h)
        backward_z(h)
        far_swap[h].start()
        near_swap[h].start()

    def pass_over(h):
        far_swap[h].wait_recv()
        sums[h, far] = sums[h, far] + got_core[h, 0]
        over[h].start()

    pl.when(~last & above)(lambda: pl.semaphore_wait(ready, 1))
    for step in range(3):
        along_y(step)
    backward(0)
    along_y(3)
    pass_over(0)
    backward(1)
    pass_over(1)

    for k in range(1, VIEWS):
        part_copy(slot, k - 1, partner, 0).wait_send()

    @pl.when(is_edge)
    def _():
        for k in range(VIEWS):
            outer_copy(0, k, partner, 0).wait_send()

    def sent(ref, semaphore):
        pltpu.make_async_remote_copy(
            src_ref=ref, dst_ref=ref, send_sem=semaphore, recv_sem=face_recv.at[0],
            device_id=partner, device_id_type=MESH,
        ).wait_send()

    for name, (index, (_, there), _) in ways.items():
        relayed = field.at[0:3, 0:2, :, 0:1] if name[0] == "v" else field.at[0:2, 0:2, :, 0:1]

        @pl.when(there)
        def _():
            sent(field.at[1, 1, core], face_send.at[index])
            sent(relayed, face_send.at[4 + index])

    sent(field.at[:, :, core], core_send.at[0])

    start = jnp.where(last, RAD, 0)
    lane = iota((64, LANES), 1)
    keep = is_edge & (lane >= start) & (lane < start + RAD)
    for h in range(2):
        near_swap[h].wait_recv()
        mine = sums[h, slot] + got_core[h, 1]
        over[h].wait_recv()
        mine = mine + got_chip[h]

        pl.when(is_edge)(lambda: rim_came(h))
        edge = got_edge[0, h] + got_edge[1, h] + (got_edge[2, h] + got_edge[3, h])
        for g in range(GROUPS):
            own = pltpu.roll(mine, (8 - g - slot) % 4 * 32, 1)
            sides = []
            for k in range(2):
                rim = pltpu.roll(edge, (start + LANES - 64 * k - RAD * g) % LANES, 1)
                part = own[64 * k : 64 * k + 64] + jnp.where(keep, rim, 0.0)
                sides.append(part.reshape(8, 8, LANES) * (1.0 / (RANK * VIEWS)))
            part = jnp.stack(swap_quads(*sides), axis=1).reshape(16, 8, LANES)
            at = (slice(16 * h, 16 * h + 16), slice(g * 8, g * 8 + 8))
            refined[at] = est[at] * part[:, :, 0:BLOCK]

    for copy in far_swap + near_swap + over:
        copy.wait_send()
    for which in range(2):

        @pl.when((below, above)[which])
        def _():
            for h in range(2):
                rim_copy(h, which).wait_send()


def local(estimate, view_tiles, slot_view, psf_taps):
    vmem = pl.BlockSpec(memory_space=pltpu.VMEM)
    hbm = pl.BlockSpec(memory_space=pltpu.HBM)
    tile = view_tiles[0, 0, 0]
    psf = jnp.transpose(psf_taps, (1, 2, 0, 3))
    scratch = [
        pltpu.VMEM(estimate.shape, F32),
        pltpu.VMEM(tile.shape, BF16),
        pltpu.VMEM(psf.shape, F32),
        pltpu.VMEM(slot_view.shape, jnp.int32),
        pltpu.VMEM((256, LANES), BF16),
        pltpu.VMEM((VIEWS, 128, LANES), BF16),
        pltpu.VMEM((2, 128, LANES), BF16),
        pltpu.VMEM((3, 3, 2, 10, 64, LANES), BF16),
        pltpu.VMEM((RANK, 12, 2, 384, LANES), BF16),
        pltpu.VMEM((RANK, 12, 2, 256, LANES), BF16),
        pltpu.VMEM((16, 256, LANES), BF16),
        pltpu.VMEM((24, 256, LANES), BF16),
        pltpu.VMEM((GROUPS, 2, 128, RANK * LANES), BF16),
        pltpu.VMEM((2, 4, 128, LANES), F32),
        pltpu.VMEM((2, 2, 64, LANES), F32),
        pltpu.VMEM((2, 2, 128, LANES), F32),
        pltpu.VMEM((2, 128, LANES), F32),
        pltpu.VMEM((VIEWS, 2, 64, LANES), F32),
        pltpu.VMEM((2, 24, LANES), F32),
        pltpu.VMEM((RANK, 128, 256), BF16),
        pltpu.VMEM((128, RANK * 256), BF16),
        pltpu.VMEM((256, RANK * LANES), BF16),
        pltpu.VMEM((RANK * 128, 256), BF16),
        pltpu.VMEM((2, RANK, 64, 256), BF16),
        pltpu.VMEM((GROUPS, RANK * LANES, 256), BF16),
        pltpu.SemaphoreType.DMA((4,)),
        pltpu.SemaphoreType.DMA((7,)),
        pltpu.SemaphoreType.DMA((6,)),
        pltpu.SemaphoreType.DMA((8,)),
        pltpu.SemaphoreType.DMA((27,)),
        pltpu.SemaphoreType.DMA((1,)),
        pltpu.SemaphoreType.DMA((9,)),
        pltpu.SemaphoreType.DMA((10,)),
        pltpu.SemaphoreType.DMA((14,)),
        pltpu.SemaphoreType.REGULAR,
    ]
    return pl.pallas_call(
        kernel,
        out_shape=pltpu.VMEM(estimate.shape, F32),
        in_specs=[hbm] * 4,
        out_specs=vmem,
        scratch_shapes=scratch,
        compiler_params=pltpu.CompilerParams(
            collective_id=0, has_side_effects=True, vmem_limit_bytes=56 * 1024 * 1024
        ),
    )(*(pltpu.with_memory_space_constraint(a, pltpu.HBM) for a in (estimate, tile, psf, slot_view)))


def solution(mesh):
    placed = (
        P("bx", "by", "vert"),
        P("bx", "by", "vert", None, None, None),
        P("bx", "by", None),
        P(),
    )
    return jax.shard_map(
        local, mesh=mesh, in_specs=placed, out_specs=P("bx", "by", "vert"), check_vma=False
    )
```

```python
import jax
import jax.numpy as jnp
from jax import lax
from jax.experimental import pallas as pl
from jax.experimental.pallas import tpu as pltpu
from jax.sharding import PartitionSpec as P

BACKGROUND = 0.1
MESH = pl.DeviceIdType.MESH
F32, BF16 = jnp.float32, jnp.bfloat16
BLOCK = 32
RAD = 16
TAPS = 33
RANK = 3
VIEWS = 4
GROUPS = 4
LANES = 128


def iota(shape, axis):
    return lax.broadcasted_iota(jnp.int32, shape, axis)


def dot(a, b):
    return jnp.dot(a, b, preferred_element_type=F32)


def band(line, rows, start):
    line = jnp.broadcast_to(line, (rows, LANES))
    return pltpu.roll(line, start % LANES, 1, stride=1, stride_axis=0)


def swap_quads(a, b):
    low, axis = iota(a.shape, a.ndim - 2) < 4, a.ndim - 2
    return jnp.where(low, a, pltpu.roll(b, 4, axis)), jnp.where(low, pltpu.roll(a, 4, axis), b)


def build_taps(psf, slot_view, slot, taps):
    listed = slot_view[...]
    view = jnp.sum(jnp.where(iota(listed.shape, 2) == slot, listed, 0), axis=2, keepdims=True)
    held = iota((VIEWS, TAPS), 0) == view[0]
    mine = jnp.sum(jnp.where(held[None, None], psf[...], 0.0), axis=2)
    mine = (mine / jnp.sum(mine, axis=-1, keepdims=True)).astype(BF16).astype(F32)
    taps[...] = jnp.zeros_like(taps)
    for a in range(3):
        taps[0, 8 * a : 8 * a + RANK, :TAPS] = mine[a]
    flip = (iota((LANES, LANES), 0) + iota((LANES, LANES), 1) == TAPS - 1).astype(BF16)
    taps[1] = dot(taps[0].astype(BF16), flip)


def build_z(taps, wz, wb):
    z_in, z_out = iota((LANES, LANES), 0), iota((LANES, LANES), 1)
    near = jnp.abs(z_in - z_out) <= RAD
    rim, out = iota((32, LANES), 0), iota((32, LANES), 1)
    rim_ok = ((rim < RAD) & (out <= rim)) | ((rim >= RAD) & (out >= rim + 96))
    lane16 = iota((16, LANES), 1)
    for r in range(RANK):
        forward, backward = taps[1, 16 + r : 17 + r, :], taps[0, 16 + r : 17 + r, :]
        columns = slice(r * LANES, (r + 1) * LANES)
        wz[0:128, columns] = jnp.where(near, band(forward, LANES, -RAD), 0.0).astype(BF16)
        wz[128:160, columns] = jnp.where(rim_ok, band(forward, 32, 96), 0.0).astype(BF16)
        wz[160:256, columns] = jnp.zeros((96, LANES), BF16)
        main = jnp.where(near, band(backward, LANES, -RAD), 0.0)
        low = jnp.where(lane16 < RAD, band(backward, 16, 0), 0.0)
        high = jnp.where(lane16 < RAD, band(backward, 16, 96), 0.0)
        for g in range(GROUPS):
            wb[g, r * 128 : r * 128 + 128, 0:128] = (
                pltpu.roll(main, 32 * g, 1) if g else main
            ).astype(BF16)
            wb[g, r * 128 : r * 128 + 128, 128:256] = jnp.zeros((128, LANES), BF16)
            lo, hi = pltpu.roll(low, RAD * g, 1) if g else low, pltpu.roll(high, 64 + RAD * g, 1)
            wb[g, r * 128 : r * 128 + 16, 128:256] = lo.astype(BF16)
            wb[g, r * 128 + 112 : r * 128 + 128, 128:256] = hi.astype(BF16)


def build_x(taps, bx, tx, txb):
    spread = (iota((LANES, 256), 1) == 4 * iota((LANES, 256), 0)).astype(BF16)
    lane, row = iota((LANES, LANES), 1), iota((LANES, LANES), 0)
    low, high = bx > 0, bx < 3

    def tiles(line):
        turned = [band(line[:, i * LANES : (i + 1) * LANES], LANES, 0) for i in range(2)]
        return jnp.where(lane >= row, turned[0], 0.0), jnp.where(lane >= row, turned[1], turned[0])

    wide = [dot(taps[k, 0:8, :].astype(BF16), spread) for k in range(2)]
    for r in range(RANK):
        left, right = tiles(wide[0][r : r + 1])
        tx[r, :, 0:128] = left.astype(BF16)
        tx[r, :, 128:256] = right.astype(BF16)
        left, right = [m[0:64] for m in tiles(wide[1][r : r + 1])]
        txb[0, r, :, 0:128] = jnp.where((lane[0:64] >= 64) | low, left, 0.0).astype(BF16)
        txb[0, r, :, 128:256] = right.astype(BF16)
        txb[1, r, :, 0:128] = left.astype(BF16)
        txb[1, r, :, 128:256] = jnp.where(high, right, 0.0).astype(BF16)


def build_y(taps, by, ty, tyb):
    place = by * BLOCK - RAD + iota((BLOCK, LANES), 1)
    inside = (place >= 0) & (place < 4 * BLOCK)
    plain = [band(taps[0, 8 + r : 9 + r, :], BLOCK, 0) for r in range(RANK)]
    plain += [
        jnp.where(inside, band(taps[1, 8 + r : 9 + r, :], BLOCK, 0), 0.0) for r in range(RANK)
    ]
    plain = jnp.concatenate(plain, axis=0).astype(BF16)
    y, column = iota((LANES, 256), 0), iota((LANES, 256), 1)
    wide = [
        dot(plain, (column == 16 * (y // 4) + 4 * x + y % 4).astype(BF16)).astype(BF16)
        for x in range(4)
    ]
    row, source = iota((LANES, LANES), 0), iota((LANES, LANES), 1)
    order = (row == 16 * (source % 32 // 4) + 4 * (source // 32) + source % 4).astype(BF16)
    for i in range(2 * RANK):
        done = dot(order, jnp.concatenate([m[i * 32 : i * 32 + 32] for m in wide], axis=0)).astype(BF16)
        if i < RANK:
            ty[:, i * 256 : (i + 1) * 256] = done
        else:
            tyb[(i - RANK) * 128 : (i - RANK + 1) * 128, :] = done


def kernel(
    est_hbm, tile_hbm, psf_hbm, slot_view_hbm, refined,
    est, tile, psf, slot_view,
    packed, parts, outer, field, after_z, after_x, seen, quotient, back_y, back_x, sums, rims,
    got_core, got_chip, got_edge,
    taps, tx, ty, wz, tyb, txb, wb,
    load_sem, part_send, part_recv, face_send, face_recv, core_send, core_recv, sum_send, sum_recv, ready,
):
    bx, by, vert = lax.axis_index("bx"), lax.axis_index("by"), lax.axis_index("vert")
    q, slot = vert // VIEWS, vert % VIEWS
    core, chip = slot % 2, slot // 2

    loads = [
        pltpu.make_async_copy(source, target, load_sem.at[i])
        for i, (source, target) in enumerate(
            ((est_hbm, est), (psf_hbm, psf), (slot_view_hbm, slot_view), (tile_hbm, tile))
        )
    ]
    for copy in loads:
        copy.start()

    def at_vert(index):
        return {"vert": index}

    partner = at_vert(q * 4 + chip * 2 + 1 - core)
    above, below = q < 3, q > 0
    first, last = slot == 0, slot == VIEWS - 1
    is_edge = (first & below) | (last & above)

    straight = core == 0

    def block(ju, jv):
        return jnp.where(straight, jv, ju), jnp.where(straight, ju, jv)

    def link(along_u, step):
        x_step = jnp.where(straight == along_u, step, 0)
        x, y = bx + x_step, by + step - x_step
        return {"bx": x, "by": y}, (x >= 0) & (x < 4) & (y >= 0) & (y < 4)

    u_up, u_down, v_up, v_down = link(True, 1), link(True, -1), link(False, 1), link(False, -1)

    def clear(ref):
        ref[...] = jnp.zeros(ref.shape, BF16)

    pl.when(bx == 0)(lambda: clear(field.at[:, 0, core]))
    pl.when(bx == 3)(lambda: clear(field.at[:, 2, core]))
    pl.when(by == 0)(lambda: clear(field.at[0, :, core]))
    pl.when(by == 3)(lambda: clear(field.at[2, :, core]))
    pl.when(~below)(lambda: clear(outer.at[0]))
    pl.when(~above)(lambda: clear(outer.at[1]))

    got_edge[...] = jnp.zeros_like(got_edge)
    barrier = pltpu.get_barrier_semaphore()

    def greet(device):
        pl.semaphore_signal(barrier, inc=1, device_id=device, device_id_type=MESH)

    for k in range(1, VIEWS):
        greet(at_vert(q * 4 + (slot + k) % VIEWS))
    for device, there in (u_up, u_down, v_up, v_down):
        pl.when(there)(lambda device=device: greet(device))

    @pl.when(above)
    def _():
        greet(at_vert(vert - slot + 4))

        @pl.when(last)
        def _():
            for k in range(2, VIEWS + 1):
                greet(at_vert(vert + k))

    beside = [(there, 1) for _, there in (u_up, u_down, v_up, v_down)]
    beside += [(first & below, VIEWS), (~first & below, 1)]
    pl.semaphore_wait(barrier, 3 + sum(jnp.where(there, n, 0) for there, n in beside))

    def answer(device):
        pl.semaphore_signal(ready, inc=1, device_id=device, device_id_type=MESH)

    @pl.when(first & below)
    def _():
        for k in range(1, VIEWS + 1):
            answer(at_vert(vert - k))

    pl.when(~first & below)(lambda: answer(at_vert(vert - slot - 1)))

    loads[0].wait()
    groups = est[...].reshape(BLOCK, GROUPS, 8, BLOCK)
    line = jnp.concatenate([groups[:, g].reshape(256, BLOCK) for g in range(GROUPS)], axis=1)
    line = pltpu.roll(line, slot * 32, 1).reshape(16, 2, 8, LANES)
    for side, quads in enumerate(swap_quads(line[:, 0], line[:, 1])):
        packed[side * 128 : side * 128 + 128, :] = quads.reshape(128, LANES).astype(BF16)

    def part_copy(source, send, device, side):
        return pltpu.make_async_remote_copy(
            src_ref=packed.at[pl.ds(side * 128, 128), :], dst_ref=parts.at[source],
            send_sem=part_send.at[send], recv_sem=part_recv.at[source],
            device_id=device, device_id_type=MESH,
        )

    for k in range(1, VIEWS):
        other = (slot + k) % VIEWS
        part_copy(slot, k - 1, at_vert(q * 4 + other), other % 2).start()

    def outer_copy(which, send, device, side):
        return pltpu.make_async_remote_copy(
            src_ref=packed.at[pl.ds(side * 128, 128), :], dst_ref=outer.at[which],
            send_sem=part_send.at[3 + send], recv_sem=part_recv.at[4 + which],
            device_id=device, device_id_type=MESH,
        )

    @pl.when(first & below)
    def _():
        for k in range(VIEWS):
            outer_copy(1, k, at_vert(vert - 4 + k), k % 2).start()

    parts[slot] = packed[pl.ds(core * 128, 128), :]
    loads[1].wait()
    loads[2].wait()
    build_taps(psf, slot_view, slot, taps)
    build_z(taps, wz, wb)

    def assemble():
        for k in range(1, VIEWS):
            part_copy((slot + k) % VIEWS, 0, partner, 0).wait_recv()
        chunk = iota((128, LANES), 1) // 32
        have = [parts[k].astype(F32) for k in range(VIEWS)]
        for g in range(GROUPS):
            line = have[(3 - g) % 4]
            for at in range(3):
                line = jnp.where(chunk == at, have[(at - g) % 4], line)
            if g:
                line = pltpu.roll(line, LANES - 32 * g, 1)
            for tp in range(2):
                field[1, 1, core, 4 * tp + g] = line[64 * tp : 64 * tp + 64].astype(BF16)

    def assemble_rims():
        for k, there in enumerate((below, above)):
            pl.when(there)(lambda k=k: outer_copy(k, 0, partner, 0).wait_recv())
        is_above = iota((128, LANES), 1) % 32 < RAD
        line = jnp.where(is_above, outer[1].astype(F32), outer[0].astype(F32))
        field[1, 1, core, 8:10] = pltpu.roll(line, RAD, 1).astype(BF16).reshape(2, 64, LANES)

    def message(ju, jv, which):
        return field.at[(*block(ju, jv), core, slice(4 * which, min(4 * which + 4, 10)))]

    def face_copy(source, target, which, send, device):
        return pltpu.make_async_remote_copy(
            src_ref=message(*source, which), dst_ref=message(*target, which),
            send_sem=face_send.at[send],
            recv_sem=face_recv.at[which * 9 + target[0] * 3 + target[1]],
            device_id=device, device_id_type=MESH,
        )

    ways = {"u_up": (0, u_up, (0, 1)), "u_down": (1, u_down, (2, 1)), "v_up": (2, v_up, (1, 0)), "v_down": (3, v_down, (1, 2))}

    def send_own(name, which):
        index, (device, there), target = ways[name]
        pl.when(there)(face_copy((1, 1), target, which, index, device).start)

    def relay(name, along, which):
        index, (device, there), target = ways[name]
        source = (along, 1) if name[0] == "v" else (1, along)
        target = (along, target[1]) if name[0] == "v" else (target[0], along)
        pl.when(there)(face_copy(source, target, which, 4 + index, device).start)

    def came(ju, jv, which, over):
        there = ways[f"{over}_{'down' if (jv if over == 'v' else ju) == 0 else 'up'}"][1][1]
        copy = face_copy((ju, jv), (ju, jv), which, 0, partner)
        pl.when(there)(copy.wait_recv)

    def core_copy(jy, jx, side):
        return pltpu.make_async_remote_copy(
            src_ref=field.at[jy, jx, side], dst_ref=field.at[jy, jx, side],
            send_sem=core_send.at[0], recv_sem=core_recv.at[jy * 3 + jx],
            device_id=partner, device_id_type=MESH,
        )

    def pass_on(ju, jv):
        core_copy(*block(ju, jv), core).start()

    def swapped(jy, jx):
        core_copy(jy, jx, 1 - core).wait_recv()

    def forward_z(*blocks):
        pieces = [(*b, side) for b in blocks for side in range(2)]
        rim = jnp.concatenate([field[jy, jx, side, 8 + tp] for jy, jx, side in pieces for tp in range(2)])
        for g in range(GROUPS):
            turned = pltpu.roll(rim, LANES - 32 * g, 1) if g else rim
            main = jnp.concatenate(
                [field[jy, jx, side, 4 * tp + g] for jy, jx, side in pieces for tp in range(2)]
            )
            done = dot(jnp.concatenate([main, turned], axis=1), wz[...]).astype(BF16)
            for i, (jy, jx, side) in enumerate(pieces):
                for r in range(RANK):
                    after_z[r, jy * GROUPS + g, side, jx * 128 : jx * 128 + 128, :] = done[
                        i * 128 : (i + 1) * 128, r * 128 : (r + 1) * 128
                    ]

    def forward_x(jy, b):
        for r in range(RANK):
            for group in (jy * GROUPS, jy * GROUPS + 2):
                rows = slice(b * 128, b * 128 + 256)
                both = [after_z[r, group + k // 2, k % 2, rows, :] for k in range(4)]
                done = dot(tx[r], jnp.concatenate(both, axis=1)).astype(BF16)
                for k in range(4):
                    after_x[r, group + k // 2, k % 2, b * 128 : b * 128 + 128, :] = done[
                        :, k * 128 : k * 128 + 128
                    ]

    def forward_y(step, b):
        terms = []
        for r in range(RANK):
            quads = [
                after_x[r, 4 * b : 4 * b + 8, :, 16 * i : 16 * i + 16, :].reshape(256, LANES)
                for i in range(4 * step, 4 * step + 4)
            ]
            terms.append(jnp.concatenate(quads, axis=1))
        blurred = dot(ty[...], jnp.concatenate(terms, axis=0))
        rows = slice(128 * b, 128 * b + 128)
        quads = [seen[i, rows, :] for i in range(4 * step, 4 * step + 4)]
        quads = jnp.concatenate(quads, axis=1).astype(F32)
        quotient[step, rows, :] = (RANK * quads / (blurred + RANK * BACKGROUND)).astype(BF16)

    def backward_y(step):
        for r in range(RANK):
            done = dot(tyb[r * 128 : r * 128 + 128, :], quotient[step]).astype(BF16)
            for k in range(4):
                i = 4 * step + k
                back_y[r * 8 : r * 8 + 8, 16 * i : 16 * i + 16, :] = done[
                    :, k * 128 : k * 128 + 128
                ].reshape(8, 16, LANES)

    assemble()
    for name in ("u_up", "u_down", "v_up", "v_down"):
        send_own(name, 0)
    for name in ("v_up", "v_down", "u_up", "u_down"):
        send_own(name, 1)

    @pl.when(last & above)
    def _():
        pl.semaphore_wait(ready, VIEWS)
        for k in range(VIEWS):
            outer_copy(0, k, at_vert(vert + 1 + k), k % 2).start()

    build_x(taps, bx, tx, txb)
    assemble_rims()
    for name in ("u_up", "u_down", "v_up", "v_down"):
        send_own(name, 2)
    pass_on(1, 1)
    for side in (0, 2):
        came(side, 1, 0, "u")
    for one, other in ((0, 2), (2, 0)):
        relay("v_up", one, 0)
        relay("v_down", other, 0)
    build_y(taps, by, ty, tyb)
    for side in (0, 2):
        came(1, side, 1, "v")
    for one, other in ((0, 2), (2, 0)):
        relay("u_up", one, 1)
        relay("u_down", other, 1)
    loads[3].wait()

    def order_tile(i, carry):
        quad = tile[pl.ds(4 * i, 4)].astype(F32).reshape(2, 2, 8, 8, LANES)
        sides = swap_quads(quad[:, 0], quad[:, 1])
        rows = jnp.stack([m[x] for m in sides for x in range(2)], axis=1)
        seen[i] = rows.reshape(256, LANES).astype(BF16)
        return carry

    lax.fori_loop(0, 16, order_tile, 0, unroll=4)
    swapped(1, 1)
    forward_z((1, 1))
    for side in (0, 2):
        came(side, 1, 2, "u")
    for one, other in ((0, 2), (2, 0)):
        relay("v_up", one, 2)
        relay("v_down", other, 2)
    for side in (0, 2):
        came(side, 1, 1, "u")
        pass_on(side, 1)
        came(1, side, 0, "v")
        came(1, side, 2, "v")
        pass_on(1, side)
    for side in (0, 2):
        swapped(1, side)
        swapped(side, 1)
    forward_z((1, 0), (1, 2))
    forward_z((0, 1), (2, 1))
    waves = (((0, 0), (2, 2)), ((0, 2), (2, 0)))

    def wave_came(wave):
        for corner in wave:
            came(*corner, 0, "v")
            came(*corner, 1, "u")
            came(*corner, 2, "v")
            pass_on(*corner)

    wave_came(waves[0])
    forward_x(1, 0)
    forward_x(1, 1)
    for corner in waves[0]:
        swapped(*corner)
    forward_z(*waves[0])
    forward_x(0, 0)
    forward_x(2, 1)
    wave_came(waves[1])
    for step in range(2):
        forward_y(step, 0)
        forward_y(step + 2, 1)
    for corner in waves[1]:
        swapped(*corner)
    forward_z(*waves[1])
    forward_x(2, 0)
    forward_x(0, 1)

    def backward_x(half):
        within = slice(half * 64, half * 64 + 192)
        for g in (0, 2):
            for r in range(RANK):
                at = (r * GROUPS + g) * 2
                sides = jnp.concatenate([back_y[at + k, within, :] for k in range(4)], axis=1)
                done = dot(txb[half, r, :, 0:192], sides).astype(BF16)
                for k in range(4):
                    rows = slice(k % 2 * 64, k % 2 * 64 + 64)
                    back_x[g + k // 2, half, rows, r * 128 : (r + 1) * 128] = done[
                        :, k * 128 : k * 128 + 128
                    ]

    def backward_z(half):
        parts_z = [dot(back_x[g, half], wb[g]) for g in range(GROUPS)]
        both = (parts_z[0] + parts_z[1] + (parts_z[2] + parts_z[3]))[:, LANES:]
        is_low = iota((64, LANES), 1) < 64
        rims[half, 0] = jnp.where(is_low, both[0:64], pltpu.roll(both[64:128], 64, 1))
        rims[half, 1] = jnp.where(is_low, pltpu.roll(both[0:64], 64, 1), both[64:128])
        for which in range(2):
            pl.when((below, above)[which])(rim_copy(half, which).start)
        for g in range(GROUPS):
            for c in range(4):
                at = (g + c) % 4
                sums[half, c, :, at * 32 : at * 32 + 32] = parts_z[g][:, at * 32 : at * 32 + 32]

    far = (1 - chip) * 2 + core

    def sum_copy(source, target, index, device):
        return pltpu.make_async_remote_copy(
            src_ref=source, dst_ref=target, send_sem=sum_send.at[index],
            recv_sem=sum_recv.at[index], device_id=device, device_id_type=MESH,
        )

    far_swap = [
        sum_copy(sums.at[h, (1 - chip) * 2 + 1 - core], got_core.at[h, 0], h, partner) for h in range(2)
    ]
    near_swap = [
        sum_copy(sums.at[h, chip * 2 + 1 - core], got_core.at[h, 1], 2 + h, partner) for h in range(2)
    ]
    over = [sum_copy(sums.at[h, far], got_chip.at[h], 4 + h, at_vert(q * 4 + far)) for h in range(2)]

    def rim_copy(h, which):
        home = (vert - slot - 1, vert - slot + 4)[which]
        return pltpu.make_async_remote_copy(
            src_ref=rims.at[h, which], dst_ref=got_edge.at[slot, h], send_sem=sum_send.at[6 + 2 * h + which],
            recv_sem=sum_recv.at[6 + 2 * slot + h], device_id=at_vert(home), device_id_type=MESH,
        )

    def rim_came(h):
        for k in range(VIEWS):
            pltpu.make_async_remote_copy(
                src_ref=rims.at[h, 0], dst_ref=got_edge.at[k, h], send_sem=sum_send.at[6],
                recv_sem=sum_recv.at[6 + 2 * k + h], device_id=partner, device_id_type=MESH,
            ).wait_recv()

    def backward(h):
        backward_x(h)
        backward_z(h)
        far_swap[h].start()
        near_swap[h].start()

    def pass_over(h):
        far_swap[h].wait_recv()
        sums[h, far] = sums[h, far] + got_core[h, 0]
        over[h].start()

    pl.when(~last & above)(lambda: pl.semaphore_wait(ready, 1))
    for step in range(3):
        forward_y(step, 1 if step < 2 else 0)
        backward_y(step)
    backward(0)
    forward_y(3, 0)
    backward_y(3)
    pass_over(0)
    backward(1)
    pass_over(1)

    for k in range(1, VIEWS):
        part_copy(slot, k - 1, partner, 0).wait_send()

    @pl.when(is_edge)
    def _():
        for k in range(VIEWS):
            outer_copy(0, k, partner, 0).wait_send()

    def sent(ref, semaphore):
        pltpu.make_async_remote_copy(
            src_ref=ref, dst_ref=ref, send_sem=semaphore, recv_sem=face_recv.at[0],
            device_id=partner, device_id_type=MESH,
        ).wait_send()

    for name, (index, (_, there), _) in ways.items():
        relayed = field.at[0:3, 0:2, :, 0:1] if name[0] == "v" else field.at[0:2, 0:2, :, 0:1]

        @pl.when(there)
        def _():
            sent(field.at[1, 1, core], face_send.at[index])
            sent(relayed, face_send.at[4 + index])

    sent(field.at[:, :, core], core_send.at[0])

    start = jnp.where(last, RAD, 0)
    lane = iota((64, LANES), 1)
    keep = is_edge & (lane >= start) & (lane < start + RAD)
    for h in range(2):
        near_swap[h].wait_recv()
        mine = sums[h, slot] + got_core[h, 1]
        over[h].wait_recv()
        mine = mine + got_chip[h]

        pl.when(is_edge)(lambda: rim_came(h))
        edge = got_edge[0, h] + got_edge[1, h] + (got_edge[2, h] + got_edge[3, h])
        for g in range(GROUPS):
            own = pltpu.roll(mine, (8 - g - slot) % 4 * 32, 1)
            sides = []
            for k in range(2):
                rim = pltpu.roll(edge, (start + LANES - 64 * k - RAD * g) % LANES, 1)
                part = own[64 * k : 64 * k + 64] + jnp.where(keep, rim, 0.0)
                sides.append(part.reshape(8, 8, LANES) * (1.0 / (RANK * VIEWS)))
            part = jnp.stack(swap_quads(*sides), axis=1).reshape(16, 8, LANES)
            at = (slice(16 * h, 16 * h + 16), slice(g * 8, g * 8 + 8))
            refined[at] = est[at] * part[:, :, 0:BLOCK]

    for copy in far_swap + near_swap + over:
        copy.wait_send()
    for which in range(2):

        @pl.when((below, above)[which])
        def _():
            for h in range(2):
                rim_copy(h, which).wait_send()


def local(estimate, view_tiles, slot_view, psf_taps):
    vmem = pl.BlockSpec(memory_space=pltpu.VMEM)
    hbm = pl.BlockSpec(memory_space=pltpu.HBM)
    tile = view_tiles[0, 0, 0]
    psf = jnp.transpose(psf_taps, (1, 2, 0, 3))
    scratch = [
        pltpu.VMEM(estimate.shape, F32),
        pltpu.VMEM(tile.shape, BF16),
        pltpu.VMEM(psf.shape, F32),
        pltpu.VMEM(slot_view.shape, jnp.int32),
        pltpu.VMEM((256, LANES), BF16),
        pltpu.VMEM((VIEWS, 128, LANES), BF16),
        pltpu.VMEM((2, 128, LANES), BF16),
        pltpu.VMEM((3, 3, 2, 10, 64, LANES), BF16),
        pltpu.VMEM((RANK, 12, 2, 384, LANES), BF16),
        pltpu.VMEM((RANK, 12, 2, 256, LANES), BF16),
        pltpu.VMEM((16, 256, LANES), BF16),
        pltpu.VMEM((4, 256, 4 * LANES), BF16),
        pltpu.VMEM((24, 256, LANES), BF16),
        pltpu.VMEM((GROUPS, 2, 128, RANK * LANES), BF16),
        pltpu.VMEM((2, 4, 128, LANES), F32),
        pltpu.VMEM((2, 2, 64, LANES), F32),
        pltpu.VMEM((2, 2, 128, LANES), F32),
        pltpu.VMEM((2, 128, LANES), F32),
        pltpu.VMEM((VIEWS, 2, 64, LANES), F32),
        pltpu.VMEM((2, 24, LANES), F32),
        pltpu.VMEM((RANK, 128, 256), BF16),
        pltpu.VMEM((128, RANK * 256), BF16),
        pltpu.VMEM((256, RANK * LANES), BF16),
        pltpu.VMEM((RANK * 128, 256), BF16),
        pltpu.VMEM((2, RANK, 64, 256), BF16),
        pltpu.VMEM((GROUPS, RANK * LANES, 256), BF16),
        pltpu.SemaphoreType.DMA((4,)),
        pltpu.SemaphoreType.DMA((7,)),
        pltpu.SemaphoreType.DMA((6,)),
        pltpu.SemaphoreType.DMA((8,)),
        pltpu.SemaphoreType.DMA((27,)),
        pltpu.SemaphoreType.DMA((1,)),
        pltpu.SemaphoreType.DMA((9,)),
        pltpu.SemaphoreType.DMA((10,)),
        pltpu.SemaphoreType.DMA((14,)),
        pltpu.SemaphoreType.REGULAR,
    ]
    return pl.pallas_call(
        kernel,
        out_shape=pltpu.VMEM(estimate.shape, F32),
        in_specs=[hbm] * 4,
        out_specs=vmem,
        scratch_shapes=scratch,
        compiler_params=pltpu.CompilerParams(
            collective_id=0, has_side_effects=True, vmem_limit_bytes=56 * 1024 * 1024
        ),
    )(*(pltpu.with_memory_space_constraint(a, pltpu.HBM) for a in (estimate, tile, psf, slot_view)))


def solution(mesh):
    placed = (
        P("bx", "by", "vert"),
        P("bx", "by", "vert", None, None, None),
        P("bx", "by", None),
        P(),
    )
    return jax.shard_map(
        local, mesh=mesh, in_specs=placed, out_specs=P("bx", "by", "vert"), check_vma=False
    )
```

```python
import jax
import jax.numpy as jnp
from jax import lax
from jax.experimental import pallas as pl
from jax.experimental.pallas import tpu as pltpu
from jax.sharding import PartitionSpec as P

BACKGROUND = 0.1
MESH = pl.DeviceIdType.MESH
F32, BF16 = jnp.float32, jnp.bfloat16
BLOCK = 32
RAD = 16
TAPS = 33
RANK = 3
VIEWS = 4
GROUPS = 4
LANES = 128


def iota(shape, axis):
    return lax.broadcasted_iota(jnp.int32, shape, axis)


def dot(a, b):
    return jnp.dot(a, b, preferred_element_type=F32)


def band(line, rows, start):
    line = jnp.broadcast_to(line, (rows, LANES))
    return pltpu.roll(line, start % LANES, 1, stride=1, stride_axis=0)


def swap_quads(a, b):
    low, axis = iota(a.shape, a.ndim - 2) < 4, a.ndim - 2
    return jnp.where(low, a, pltpu.roll(b, 4, axis)), jnp.where(low, pltpu.roll(a, 4, axis), b)


def build_taps(psf, slot_view, slot, taps):
    listed = slot_view[...]
    view = jnp.sum(jnp.where(iota(listed.shape, 2) == slot, listed, 0), axis=2, keepdims=True)
    held = iota((VIEWS, TAPS), 0) == view[0]
    mine = jnp.sum(jnp.where(held[None, None], psf[...], 0.0), axis=2)
    mine = (mine / jnp.sum(mine, axis=-1, keepdims=True)).astype(BF16).astype(F32)
    taps[...] = jnp.zeros_like(taps)
    for a in range(3):
        taps[0, 8 * a : 8 * a + RANK, :TAPS] = mine[a]
    flip = (iota((LANES, LANES), 0) + iota((LANES, LANES), 1) == TAPS - 1).astype(BF16)
    taps[1] = dot(taps[0].astype(BF16), flip)


def build_z(taps, wz, wb):
    z_in, z_out = iota((LANES, LANES), 0), iota((LANES, LANES), 1)
    near = jnp.abs(z_in - z_out) <= RAD
    rim, out = iota((32, LANES), 0), iota((32, LANES), 1)
    rim_ok = ((rim < RAD) & (out <= rim)) | ((rim >= RAD) & (out >= rim + 96))
    lane16 = iota((16, LANES), 1)
    for r in range(RANK):
        forward, backward = taps[1, 16 + r : 17 + r, :], taps[0, 16 + r : 17 + r, :]
        columns = slice(r * LANES, (r + 1) * LANES)
        wz[0:128, columns] = jnp.where(near, band(forward, LANES, -RAD), 0.0).astype(BF16)
        wz[128:160, columns] = jnp.where(rim_ok, band(forward, 32, 96), 0.0).astype(BF16)
        wz[160:256, columns] = jnp.zeros((96, LANES), BF16)
        main = jnp.where(near, band(backward, LANES, -RAD), 0.0)
        low = jnp.where(lane16 < RAD, band(backward, 16, 0), 0.0)
        high = jnp.where(lane16 < RAD, band(backward, 16, 96), 0.0)
        for g in range(GROUPS):
            wb[g, r * 128 : r * 128 + 128, 0:128] = (
                pltpu.roll(main, 32 * g, 1) if g else main
            ).astype(BF16)
            wb[g, r * 128 : r * 128 + 128, 128:256] = jnp.zeros((128, LANES), BF16)
            lo, hi = pltpu.roll(low, RAD * g, 1) if g else low, pltpu.roll(high, 64 + RAD * g, 1)
            wb[g, r * 128 : r * 128 + 16, 128:256] = lo.astype(BF16)
            wb[g, r * 128 + 112 : r * 128 + 128, 128:256] = hi.astype(BF16)


def build_x(taps, bx, tx, txb):
    spread = (iota((LANES, 256), 1) == 4 * iota((LANES, 256), 0)).astype(BF16)
    lane, row = iota((LANES, LANES), 1), iota((LANES, LANES), 0)
    low, high = bx > 0, bx < 3

    def tiles(line):
        turned = [band(line[:, i * LANES : (i + 1) * LANES], LANES, 0) for i in range(2)]
        return jnp.where(lane >= row, turned[0], 0.0), jnp.where(lane >= row, turned[1], turned[0])

    wide = [dot(taps[k, 0:8, :].astype(BF16), spread) for k in range(2)]
    for r in range(RANK):
        left, right = tiles(wide[0][r : r + 1])
        tx[r, :, 0:128] = left.astype(BF16)
        tx[r, :, 128:256] = right.astype(BF16)
        left, right = [m[0:64] for m in tiles(wide[1][r : r + 1])]
        txb[0, r, :, 0:128] = jnp.where((lane[0:64] >= 64) | low, left, 0.0).astype(BF16)
        txb[0, r, :, 128:256] = right.astype(BF16)
        txb[1, r, :, 0:128] = left.astype(BF16)
        txb[1, r, :, 128:256] = jnp.where(high, right, 0.0).astype(BF16)


def build_y(taps, by, ty, tyb):
    place = by * BLOCK - RAD + iota((BLOCK, LANES), 1)
    inside = (place >= 0) & (place < 4 * BLOCK)
    plain = [band(taps[0, 8 + r : 9 + r, :], BLOCK, 0) for r in range(RANK)]
    plain += [
        jnp.where(inside, band(taps[1, 8 + r : 9 + r, :], BLOCK, 0), 0.0) for r in range(RANK)
    ]
    plain = jnp.concatenate(plain, axis=0).astype(BF16)
    y, column = iota((LANES, 256), 0), iota((LANES, 256), 1)
    wide = [
        dot(plain, (column == 16 * (y // 4) + 4 * x + y % 4).astype(BF16)).astype(BF16)
        for x in range(4)
    ]
    row, source = iota((LANES, LANES), 0), iota((LANES, LANES), 1)
    order = (row == 16 * (source % 32 // 4) + 4 * (source // 32) + source % 4).astype(BF16)
    for i in range(2 * RANK):
        done = dot(order, jnp.concatenate([m[i * 32 : i * 32 + 32] for m in wide], axis=0)).astype(BF16)
        if i < RANK:
            ty[:, i * 256 : (i + 1) * 256] = done
        else:
            tyb[(i - RANK) * 128 : (i - RANK + 1) * 128, :] = done


def kernel(
    est_hbm, tile_hbm, psf_hbm, slot_view_hbm, refined,
    est, tile, psf, slot_view,
    packed, parts, outer, field, after_z, after_x, seen, back_y, back_x, sums, rims,
    got_core, got_chip, got_edge,
    taps, tx, ty, wz, tyb, txb, wb,
    load_sem, part_send, part_recv, face_send, face_recv, core_send, core_recv, sum_send, sum_recv, ready,
):
    bx, by, vert = lax.axis_index("bx"), lax.axis_index("by"), lax.axis_index("vert")
    q, slot = vert // VIEWS, vert % VIEWS
    core, chip = slot % 2, slot // 2

    loads = [
        pltpu.make_async_copy(source, target, load_sem.at[i])
        for i, (source, target) in enumerate(
            ((est_hbm, est), (psf_hbm, psf), (slot_view_hbm, slot_view), (tile_hbm, tile))
        )
    ]
    for copy in loads:
        copy.start()

    def at_vert(index):
        return {"vert": index}

    partner = at_vert(q * 4 + chip * 2 + 1 - core)
    above, below = q < 3, q > 0
    first, last = slot == 0, slot == VIEWS - 1
    is_edge = (first & below) | (last & above)

    straight = core == 0

    def block(ju, jv):
        return jnp.where(straight, jv, ju), jnp.where(straight, ju, jv)

    def link(along_u, step):
        x_step = jnp.where(straight == along_u, step, 0)
        x, y = bx + x_step, by + step - x_step
        return {"bx": x, "by": y}, (x >= 0) & (x < 4) & (y >= 0) & (y < 4)

    u_up, u_down, v_up, v_down = link(True, 1), link(True, -1), link(False, 1), link(False, -1)

    def clear(ref):
        ref[...] = jnp.zeros(ref.shape, BF16)

    pl.when(bx == 0)(lambda: clear(field.at[:, 0, core]))
    pl.when(bx == 3)(lambda: clear(field.at[:, 2, core]))
    pl.when(by == 0)(lambda: clear(field.at[0, :, core]))
    pl.when(by == 3)(lambda: clear(field.at[2, :, core]))
    pl.when(~below)(lambda: clear(outer.at[0]))
    pl.when(~above)(lambda: clear(outer.at[1]))

    got_edge[...] = jnp.zeros_like(got_edge)
    barrier = pltpu.get_barrier_semaphore()

    def greet(device):
        pl.semaphore_signal(barrier, inc=1, device_id=device, device_id_type=MESH)

    for k in range(1, VIEWS):
        greet(at_vert(q * 4 + (slot + k) % VIEWS))
    for device, there in (u_up, u_down, v_up, v_down):
        pl.when(there)(lambda device=device: greet(device))

    @pl.when(above)
    def _():
        greet(at_vert(vert - slot + 4))

        @pl.when(last)
        def _():
            for k in range(2, VIEWS + 1):
                greet(at_vert(vert + k))

    beside = [(there, 1) for _, there in (u_up, u_down, v_up, v_down)]
    beside += [(first & below, VIEWS), (~first & below, 1)]
    pl.semaphore_wait(barrier, 3 + sum(jnp.where(there, n, 0) for there, n in beside))

    def answer(device):
        pl.semaphore_signal(ready, inc=1, device_id=device, device_id_type=MESH)

    @pl.when(first & below)
    def _():
        for k in range(1, VIEWS + 1):
            answer(at_vert(vert - k))

    pl.when(~first & below)(lambda: answer(at_vert(vert - slot - 1)))

    loads[0].wait()
    groups = est[...].reshape(BLOCK, GROUPS, 8, BLOCK)
    line = jnp.concatenate([groups[:, g].reshape(256, BLOCK) for g in range(GROUPS)], axis=1)
    line = pltpu.roll(line, slot * 32, 1).reshape(16, 2, 8, LANES)
    for side, quads in enumerate(swap_quads(line[:, 0], line[:, 1])):
        packed[side * 128 : side * 128 + 128, :] = quads.reshape(128, LANES).astype(BF16)

    def part_copy(source, send, device, side):
        return pltpu.make_async_remote_copy(
            src_ref=packed.at[pl.ds(side * 128, 128), :], dst_ref=parts.at[source],
            send_sem=part_send.at[send], recv_sem=part_recv.at[source],
            device_id=device, device_id_type=MESH,
        )

    for k in range(1, VIEWS):
        other = (slot + k) % VIEWS
        part_copy(slot, k - 1, at_vert(q * 4 + other), other % 2).start()

    def outer_copy(which, send, device, side):
        return pltpu.make_async_remote_copy(
            src_ref=packed.at[pl.ds(side * 128, 128), :], dst_ref=outer.at[which],
            send_sem=part_send.at[3 + send], recv_sem=part_recv.at[4 + which],
            device_id=device, device_id_type=MESH,
        )

    @pl.when(first & below)
    def _():
        for k in range(VIEWS):
            outer_copy(1, k, at_vert(vert - 4 + k), k % 2).start()

    parts[slot] = packed[pl.ds(core * 128, 128), :]
    loads[1].wait()
    loads[2].wait()
    build_taps(psf, slot_view, slot, taps)
    build_z(taps, wz, wb)

    def assemble():
        for k in range(1, VIEWS):
            part_copy((slot + k) % VIEWS, 0, partner, 0).wait_recv()
        chunk = iota((128, LANES), 1) // 32
        have = [parts[k].astype(F32) for k in range(VIEWS)]
        for g in range(GROUPS):
            line = have[(3 - g) % 4]
            for at in range(3):
                line = jnp.where(chunk == at, have[(at - g) % 4], line)
            if g:
                line = pltpu.roll(line, LANES - 32 * g, 1)
            for tp in range(2):
                field[1, 1, core, 4 * tp + g] = line[64 * tp : 64 * tp + 64].astype(BF16)

    def assemble_rims():
        for k, there in enumerate((below, above)):
            pl.when(there)(lambda k=k: outer_copy(k, 0, partner, 0).wait_recv())
        is_above = iota((128, LANES), 1) % 32 < RAD
        line = jnp.where(is_above, outer[1].astype(F32), outer[0].astype(F32))
        field[1, 1, core, 8:10] = pltpu.roll(line, RAD, 1).astype(BF16).reshape(2, 64, LANES)

    def message(ju, jv, which):
        return field.at[(*block(ju, jv), core, slice(4 * which, min(4 * which + 4, 10)))]

    def face_copy(source, target, which, send, device):
        return pltpu.make_async_remote_copy(
            src_ref=message(*source, which), dst_ref=message(*target, which),
            send_sem=face_send.at[send],
            recv_sem=face_recv.at[which * 9 + target[0] * 3 + target[1]],
            device_id=device, device_id_type=MESH,
        )

    ways = {"u_up": (0, u_up, (0, 1)), "u_down": (1, u_down, (2, 1)), "v_up": (2, v_up, (1, 0)), "v_down": (3, v_down, (1, 2))}

    def send_own(name, which):
        index, (device, there), target = ways[name]
        pl.when(there)(face_copy((1, 1), target, which, index, device).start)

    def relay(name, along, which):
        index, (device, there), target = ways[name]
        source = (along, 1) if name[0] == "v" else (1, along)
        target = (along, target[1]) if name[0] == "v" else (target[0], along)
        pl.when(there)(face_copy(source, target, which, 4 + index, device).start)

    def came(ju, jv, which, over):
        there = ways[f"{over}_{'down' if (jv if over == 'v' else ju) == 0 else 'up'}"][1][1]
        copy = face_copy((ju, jv), (ju, jv), which, 0, partner)
        pl.when(there)(copy.wait_recv)

    def core_copy(jy, jx, side):
        return pltpu.make_async_remote_copy(
            src_ref=field.at[jy, jx, side], dst_ref=field.at[jy, jx, side],
            send_sem=core_send.at[0], recv_sem=core_recv.at[jy * 3 + jx],
            device_id=partner, device_id_type=MESH,
        )

    def pass_on(ju, jv):
        core_copy(*block(ju, jv), core).start()

    def swapped(jy, jx):
        core_copy(jy, jx, 1 - core).wait_recv()

    def forward_z(*blocks):
        pieces = [(*b, side) for b in blocks for side in range(2)]
        rim = jnp.concatenate([field[jy, jx, side, 8 + tp] for jy, jx, side in pieces for tp in range(2)])
        for g in range(GROUPS):
            turned = pltpu.roll(rim, LANES - 32 * g, 1) if g else rim
            main = jnp.concatenate(
                [field[jy, jx, side, 4 * tp + g] for jy, jx, side in pieces for tp in range(2)]
            )
            done = dot(jnp.concatenate([main, turned], axis=1), wz[...]).astype(BF16)
            for i, (jy, jx, side) in enumerate(pieces):
                for r in range(RANK):
                    after_z[r, jy * GROUPS + g, side, jx * 128 : jx * 128 + 128, :] = done[
                        i * 128 : (i + 1) * 128, r * 128 : (r + 1) * 128
                    ]

    def forward_x(jy):
        for r in range(RANK):
            for group in (jy * GROUPS, jy * GROUPS + 2):
                for b in range(2):
                    rows = slice(b * 128, b * 128 + 256)
                    both = [after_z[r, group + k // 2, k % 2, rows, :] for k in range(4)]
                    done = dot(tx[r], jnp.concatenate(both, axis=1)).astype(BF16)
                    for k in range(4):
                        after_x[r, group + k // 2, k % 2, b * 128 : b * 128 + 128, :] = done[
                            :, k * 128 : k * 128 + 128
                        ]

    assemble()
    for name in ("u_up", "u_down", "v_up", "v_down"):
        send_own(name, 0)
    for name in ("v_up", "v_down", "u_up", "u_down"):
        send_own(name, 1)

    @pl.when(last & above)
    def _():
        pl.semaphore_wait(ready, VIEWS)
        for k in range(VIEWS):
            outer_copy(0, k, at_vert(vert + 1 + k), k % 2).start()

    build_x(taps, bx, tx, txb)
    assemble_rims()
    for name in ("u_up", "u_down", "v_up", "v_down"):
        send_own(name, 2)
    pass_on(1, 1)
    for side in (0, 2):
        came(side, 1, 0, "u")
    for one, other in ((0, 2), (2, 0)):
        relay("v_up", one, 0)
        relay("v_down", other, 0)
    build_y(taps, by, ty, tyb)
    for side in (0, 2):
        came(1, side, 1, "v")
    for one, other in ((0, 2), (2, 0)):
        relay("u_up", one, 1)
        relay("u_down", other, 1)
    loads[3].wait()

    def order_tile(i, carry):
        quad = tile[pl.ds(4 * i, 4)].astype(F32).reshape(2, 2, 8, 8, LANES)
        sides = swap_quads(quad[:, 0], quad[:, 1])
        rows = jnp.stack([m[x] for m in sides for x in range(2)], axis=1)
        seen[i] = rows.reshape(256, LANES).astype(BF16)
        return carry

    lax.fori_loop(0, 16, order_tile, 0, unroll=4)
    swapped(1, 1)
    forward_z((1, 1))
    for side in (0, 2):
        came(side, 1, 2, "u")
    for one, other in ((0, 2), (2, 0)):
        relay("v_up", one, 2)
        relay("v_down", other, 2)
    for side in (0, 2):
        came(side, 1, 1, "u")
        pass_on(side, 1)
        came(1, side, 0, "v")
        came(1, side, 2, "v")
        pass_on(1, side)
    for side in (0, 2):
        swapped(1, side)
        swapped(side, 1)
    forward_z((1, 0), (1, 2))
    forward_z((0, 1), (2, 1))
    waves = (((0, 0), (2, 2)), ((0, 2), (2, 0)))
    for corner in waves[0]:
        came(*corner, 0, "v")
        came(*corner, 1, "u")
        came(*corner, 2, "v")
        pass_on(*corner)
    forward_x(1)
    for corner in waves[1]:
        came(*corner, 0, "v")
        came(*corner, 1, "u")
        came(*corner, 2, "v")
        pass_on(*corner)
    for wave in waves:
        for corner in wave:
            swapped(*corner)
        forward_z(*wave)
    for jy in (0, 2):
        forward_x(jy)

    def along_y(step):
        quotient = []
        for b in range(2):
            terms = []
            for r in range(RANK):
                quads = [
                    after_x[r, 4 * b : 4 * b + 8, :, 16 * i : 16 * i + 16, :].reshape(256, LANES)
                    for i in range(4 * step, 4 * step + 4)
                ]
                terms.append(jnp.concatenate(quads, axis=1))
            blurred = dot(ty[...], jnp.concatenate(terms, axis=0))
            rows = slice(128 * b, 128 * b + 128)
            quads = [seen[i, rows, :] for i in range(4 * step, 4 * step + 4)]
            quads = jnp.concatenate(quads, axis=1).astype(F32)
            quotient.append((RANK * quads / (blurred + RANK * BACKGROUND)).astype(BF16))
        quotient = jnp.concatenate(quotient, axis=0)
        for r in range(RANK):
            done = dot(tyb[r * 128 : r * 128 + 128, :], quotient).astype(BF16)
            for k in range(4):
                i = 4 * step + k
                back_y[r * 8 : r * 8 + 8, 16 * i : 16 * i + 16, :] = done[
                    :, k * 128 : k * 128 + 128
                ].reshape(8, 16, LANES)

    def backward_x(half):
        within = slice(half * 64, half * 64 + 192)
        for g in (0, 2):
            for r in range(RANK):
                at = (r * GROUPS + g) * 2
                sides = jnp.concatenate([back_y[at + k, within, :] for k in range(4)], axis=1)
                done = dot(txb[half, r, :, 0:192], sides).astype(BF16)
                for k in range(4):
                    rows = slice(k % 2 * 64, k % 2 * 64 + 64)
                    back_x[g + k // 2, half, rows, r * 128 : (r + 1) * 128] = done[
                        :, k * 128 : k * 128 + 128
                    ]

    def backward_z(half):
        parts_z = [dot(back_x[g, half], wb[g]) for g in range(GROUPS)]
        both = (parts_z[0] + parts_z[1] + (parts_z[2] + parts_z[3]))[:, LANES:]
        is_low = iota((64, LANES), 1) < 64
        rims[half, 0] = jnp.where(is_low, both[0:64], pltpu.roll(both[64:128], 64, 1))
        rims[half, 1] = jnp.where(is_low, pltpu.roll(both[0:64], 64, 1), both[64:128])
        for which in range(2):
            pl.when((below, above)[which])(rim_copy(half, which).start)
        for g in range(GROUPS):
            for c in range(4):
                at = (g + c) % 4
                sums[half, c, :, at * 32 : at * 32 + 32] = parts_z[g][:, at * 32 : at * 32 + 32]

    far = (1 - chip) * 2 + core

    def sum_copy(source, target, index, device):
        return pltpu.make_async_remote_copy(
            src_ref=source, dst_ref=target, send_sem=sum_send.at[index],
            recv_sem=sum_recv.at[index], device_id=device, device_id_type=MESH,
        )

    far_swap = [
        sum_copy(sums.at[h, (1 - chip) * 2 + 1 - core], got_core.at[h, 0], h, partner) for h in range(2)
    ]
    near_swap = [
        sum_copy(sums.at[h, chip * 2 + 1 - core], got_core.at[h, 1], 2 + h, partner) for h in range(2)
    ]
    over = [sum_copy(sums.at[h, far], got_chip.at[h], 4 + h, at_vert(q * 4 + far)) for h in range(2)]

    def rim_copy(h, which):
        home = (vert - slot - 1, vert - slot + 4)[which]
        return pltpu.make_async_remote_copy(
            src_ref=rims.at[h, which], dst_ref=got_edge.at[slot, h], send_sem=sum_send.at[6 + 2 * h + which],
            recv_sem=sum_recv.at[6 + 2 * slot + h], device_id=at_vert(home), device_id_type=MESH,
        )

    def rim_came(h):
        for k in range(VIEWS):
            pltpu.make_async_remote_copy(
                src_ref=rims.at[h, 0], dst_ref=got_edge.at[k, h], send_sem=sum_send.at[6],
                recv_sem=sum_recv.at[6 + 2 * k + h], device_id=partner, device_id_type=MESH,
            ).wait_recv()

    def backward(h):
        backward_z(h)
        far_swap[h].start()
        near_swap[h].start()

    def pass_over(h):
        far_swap[h].wait_recv()
        sums[h, far] = sums[h, far] + got_core[h, 0]
        over[h].start()

    pl.when(~last & above)(lambda: pl.semaphore_wait(ready, 1))
    for step in range(4):
        along_y(step)
    backward_x(0)
    backward(0)
    backward_x(1)
    pass_over(0)
    backward(1)
    pass_over(1)

    for k in range(1, VIEWS):
        part_copy(slot, k - 1, partner, 0).wait_send()

    @pl.when(is_edge)
    def _():
        for k in range(VIEWS):
            outer_copy(0, k, partner, 0).wait_send()

    def sent(ref, semaphore):
        pltpu.make_async_remote_copy(
            src_ref=ref, dst_ref=ref, send_sem=semaphore, recv_sem=face_recv.at[0],
            device_id=partner, device_id_type=MESH,
        ).wait_send()

    for name, (index, (_, there), _) in ways.items():
        relayed = field.at[0:3, 0:2, :, 0:1] if name[0] == "v" else field.at[0:2, 0:2, :, 0:1]

        @pl.when(there)
        def _():
            sent(field.at[1, 1, core], face_send.at[index])
            sent(relayed, face_send.at[4 + index])

    sent(field.at[:, :, core], core_send.at[0])

    start = jnp.where(last, RAD, 0)
    lane = iota((64, LANES), 1)
    keep = is_edge & (lane >= start) & (lane < start + RAD)
    for h in range(2):
        near_swap[h].wait_recv()
        mine = sums[h, slot] + got_core[h, 1]
        over[h].wait_recv()
        mine = mine + got_chip[h]

        pl.when(is_edge)(lambda: rim_came(h))
        edge = got_edge[0, h] + got_edge[1, h] + (got_edge[2, h] + got_edge[3, h])
        for g in range(GROUPS):
            own = pltpu.roll(mine, (8 - g - slot) % 4 * 32, 1)
            sides = []
            for k in range(2):
                rim = pltpu.roll(edge, (start + LANES - 64 * k - RAD * g) % LANES, 1)
                part = own[64 * k : 64 * k + 64] + jnp.where(keep, rim, 0.0)
                sides.append(part.reshape(8, 8, LANES) * (1.0 / (RANK * VIEWS)))
            part = jnp.stack(swap_quads(*sides), axis=1).reshape(16, 8, LANES)
            at = (slice(16 * h, 16 * h + 16), slice(g * 8, g * 8 + 8))
            refined[at] = est[at] * part[:, :, 0:BLOCK]

    for copy in far_swap + near_swap + over:
        copy.wait_send()
    for which in range(2):

        @pl.when((below, above)[which])
        def _():
            for h in range(2):
                rim_copy(h, which).wait_send()


def local(estimate, view_tiles, slot_view, psf_taps):
    vmem = pl.BlockSpec(memory_space=pltpu.VMEM)
    hbm = pl.BlockSpec(memory_space=pltpu.HBM)
    tile = view_tiles[0, 0, 0]
    psf = jnp.transpose(psf_taps, (1, 2, 0, 3))
    scratch = [
        pltpu.VMEM(estimate.shape, F32),
        pltpu.VMEM(tile.shape, BF16),
        pltpu.VMEM(psf.shape, F32),
        pltpu.VMEM(slot_view.shape, jnp.int32),
        pltpu.VMEM((256, LANES), BF16),
        pltpu.VMEM((VIEWS, 128, LANES), BF16),
        pltpu.VMEM((2, 128, LANES), BF16),
        pltpu.VMEM((3, 3, 2, 10, 64, LANES), BF16),
        pltpu.VMEM((RANK, 12, 2, 384, LANES), BF16),
        pltpu.VMEM((RANK, 12, 2, 256, LANES), BF16),
        pltpu.VMEM((16, 256, LANES), BF16),
        pltpu.VMEM((24, 256, LANES), BF16),
        pltpu.VMEM((GROUPS, 2, 128, RANK * LANES), BF16),
        pltpu.VMEM((2, 4, 128, LANES), F32),
        pltpu.VMEM((2, 2, 64, LANES), F32),
        pltpu.VMEM((2, 2, 128, LANES), F32),
        pltpu.VMEM((2, 128, LANES), F32),
        pltpu.VMEM((VIEWS, 2, 64, LANES), F32),
        pltpu.VMEM((2, 24, LANES), F32),
        pltpu.VMEM((RANK, 128, 256), BF16),
        pltpu.VMEM((128, RANK * 256), BF16),
        pltpu.VMEM((256, RANK * LANES), BF16),
        pltpu.VMEM((RANK * 128, 256), BF16),
        pltpu.VMEM((2, RANK, 64, 256), BF16),
        pltpu.VMEM((GROUPS, RANK * LANES, 256), BF16),
        pltpu.SemaphoreType.DMA((4,)),
        pltpu.SemaphoreType.DMA((7,)),
        pltpu.SemaphoreType.DMA((6,)),
        pltpu.SemaphoreType.DMA((8,)),
        pltpu.SemaphoreType.DMA((27,)),
        pltpu.SemaphoreType.DMA((1,)),
        pltpu.SemaphoreType.DMA((9,)),
        pltpu.SemaphoreType.DMA((10,)),
        pltpu.SemaphoreType.DMA((14,)),
        pltpu.SemaphoreType.REGULAR,
    ]
    return pl.pallas_call(
        kernel,
        out_shape=pltpu.VMEM(estimate.shape, F32),
        in_specs=[hbm] * 4,
        out_specs=vmem,
        scratch_shapes=scratch,
        compiler_params=pltpu.CompilerParams(
            collective_id=0, has_side_effects=True, vmem_limit_bytes=56 * 1024 * 1024
        ),
    )(*(pltpu.with_memory_space_constraint(a, pltpu.HBM) for a in (estimate, tile, psf, slot_view)))


def solution(mesh):
    placed = (
        P("bx", "by", "vert"),
        P("bx", "by", "vert", None, None, None),
        P("bx", "by", None),
        P(),
    )
    return jax.shard_map(
        local, mesh=mesh, in_specs=placed, out_specs=P("bx", "by", "vert"), check_vma=False
    )
```

```python
import jax
import jax.numpy as jnp
from jax import lax
from jax.experimental import pallas as pl
from jax.experimental.pallas import tpu as pltpu
from jax.sharding import PartitionSpec as P

BACKGROUND = 0.1
MESH = pl.DeviceIdType.MESH
F32, BF16 = jnp.float32, jnp.bfloat16
BLOCK = 32
RAD = 16
TAPS = 33
RANK = 3
VIEWS = 4
GROUPS = 4
LANES = 128


def iota(shape, axis):
    return lax.broadcasted_iota(jnp.int32, shape, axis)


def dot(a, b):
    return jnp.dot(a, b, preferred_element_type=F32)


def band(line, rows, start):
    line = jnp.broadcast_to(line, (rows, LANES))
    return pltpu.roll(line, start % LANES, 1, stride=1, stride_axis=0)


def swap_quads(a, b):
    low, axis = iota(a.shape, a.ndim - 2) < 4, a.ndim - 2
    return jnp.where(low, a, pltpu.roll(b, 4, axis)), jnp.where(low, pltpu.roll(a, 4, axis), b)


def build_taps(psf, slot_view, slot, taps):
    listed = slot_view[...]
    view = jnp.sum(jnp.where(iota(listed.shape, 2) == slot, listed, 0), axis=2, keepdims=True)
    held = iota((VIEWS, TAPS), 0) == view[0]
    mine = jnp.sum(jnp.where(held[None, None], psf[...], 0.0), axis=2)
    mine = (mine / jnp.sum(mine, axis=-1, keepdims=True)).astype(BF16).astype(F32)
    taps[...] = jnp.zeros_like(taps)
    for a in range(3):
        taps[0, 8 * a : 8 * a + RANK, :TAPS] = mine[a]
    flip = (iota((LANES, LANES), 0) + iota((LANES, LANES), 1) == TAPS - 1).astype(BF16)
    taps[1] = dot(taps[0].astype(BF16), flip)


def build_z(taps, wz, wb):
    z_in, z_out = iota((LANES, LANES), 0), iota((LANES, LANES), 1)
    near = jnp.abs(z_in - z_out) <= RAD
    rim, out = iota((32, LANES), 0), iota((32, LANES), 1)
    rim_ok = ((rim < RAD) & (out <= rim)) | ((rim >= RAD) & (out >= rim + 96))
    lane16 = iota((16, LANES), 1)
    for r in range(RANK):
        forward, backward = taps[1, 16 + r : 17 + r, :], taps[0, 16 + r : 17 + r, :]
        columns = slice(r * LANES, (r + 1) * LANES)
        wz[0:128, columns] = jnp.where(near, band(forward, LANES, -RAD), 0.0).astype(BF16)
        wz[128:160, columns] = jnp.where(rim_ok, band(forward, 32, 96), 0.0).astype(BF16)
        wz[160:256, columns] = jnp.zeros((96, LANES), BF16)
        main = jnp.where(near, band(backward, LANES, -RAD), 0.0)
        low = jnp.where(lane16 < RAD, band(backward, 16, 0), 0.0)
        high = jnp.where(lane16 < RAD, band(backward, 16, 96), 0.0)
        for g in range(GROUPS):
            wb[g, r * 128 : r * 128 + 128, 0:128] = (
                pltpu.roll(main, 32 * g, 1) if g else main
            ).astype(BF16)
            wb[g, r * 128 : r * 128 + 128, 128:256] = jnp.zeros((128, LANES), BF16)
            lo, hi = pltpu.roll(low, RAD * g, 1) if g else low, pltpu.roll(high, 64 + RAD * g, 1)
            wb[g, r * 128 : r * 128 + 16, 128:256] = lo.astype(BF16)
            wb[g, r * 128 + 112 : r * 128 + 128, 128:256] = hi.astype(BF16)


def build_x(taps, bx, tx, txb):
    spread = (iota((LANES, 256), 1) == 4 * iota((LANES, 256), 0)).astype(BF16)
    lane, row = iota((LANES, LANES), 1), iota((LANES, LANES), 0)
    low, high = bx > 0, bx < 3

    def tiles(line):
        turned = [band(line[:, i * LANES : (i + 1) * LANES], LANES, 0) for i in range(2)]
        return jnp.where(lane >= row, turned[0], 0.0), jnp.where(lane >= row, turned[1], turned[0])

    wide = [dot(taps[k, 0:8, :].astype(BF16), spread) for k in range(2)]
    for r in range(RANK):
        left, right = tiles(wide[0][r : r + 1])
        tx[r, :, 0:128] = left.astype(BF16)
        tx[r, :, 128:256] = right.astype(BF16)
        left, right = [m[0:64] for m in tiles(wide[1][r : r + 1])]
        txb[0, r, :, 0:128] = jnp.where((lane[0:64] >= 64) | low, left, 0.0).astype(BF16)
        txb[0, r, :, 128:256] = right.astype(BF16)
        txb[1, r, :, 0:128] = left.astype(BF16)
        txb[1, r, :, 128:256] = jnp.where(high, right, 0.0).astype(BF16)


def build_y(taps, by, ty, tyb):
    place = by * BLOCK - RAD + iota((BLOCK, LANES), 1)
    inside = (place >= 0) & (place < 4 * BLOCK)
    plain = [band(taps[0, 8 + r : 9 + r, :], BLOCK, 0) for r in range(RANK)]
    plain += [
        jnp.where(inside, band(taps[1, 8 + r : 9 + r, :], BLOCK, 0), 0.0) for r in range(RANK)
    ]
    plain = jnp.concatenate(plain, axis=0).astype(BF16)
    y, column = iota((LANES, 256), 0), iota((LANES, 256), 1)
    wide = [
        dot(plain, (column == 16 * (y // 4) + 4 * x + y % 4).astype(BF16)).astype(BF16)
        for x in range(4)
    ]
    row, source = iota((LANES, LANES), 0), iota((LANES, LANES), 1)
    order = (row == 16 * (source % 32 // 4) + 4 * (source // 32) + source % 4).astype(BF16)
    for i in range(2 * RANK):
        done = dot(order, jnp.concatenate([m[i * 32 : i * 32 + 32] for m in wide], axis=0)).astype(BF16)
        if i < RANK:
            ty[:, i * 256 : (i + 1) * 256] = done
        else:
            tyb[(i - RANK) * 128 : (i - RANK + 1) * 128, :] = done


def kernel(
    est_hbm, tile_hbm, psf_hbm, slot_view_hbm, refined,
    est, tile, psf, slot_view,
    packed, parts, outer, field, after_z, after_x, seen, back_y, back_x, sums, rims,
    got_core, got_chip, got_edge,
    taps, tx, ty, wz, tyb, txb, wb,
    load_sem, part_send, part_recv, face_send, face_recv, core_send, core_recv, sum_send, sum_recv, ready,
):
    bx, by, vert = lax.axis_index("bx"), lax.axis_index("by"), lax.axis_index("vert")
    q, slot = vert // VIEWS, vert % VIEWS
    core, chip = slot % 2, slot // 2

    loads = [
        pltpu.make_async_copy(source, target, load_sem.at[i])
        for i, (source, target) in enumerate(
            ((est_hbm, est), (psf_hbm, psf), (slot_view_hbm, slot_view), (tile_hbm, tile))
        )
    ]
    for copy in loads:
        copy.start()

    def at_vert(index):
        return {"vert": index}

    partner = at_vert(q * 4 + chip * 2 + 1 - core)
    above, below = q < 3, q > 0
    first, last = slot == 0, slot == VIEWS - 1
    is_edge = (first & below) | (last & above)

    straight = core == 0

    def block(ju, jv):
        return jnp.where(straight, jv, ju), jnp.where(straight, ju, jv)

    def link(along_u, step):
        x_step = jnp.where(straight == along_u, step, 0)
        x, y = bx + x_step, by + step - x_step
        return {"bx": x, "by": y}, (x >= 0) & (x < 4) & (y >= 0) & (y < 4)

    u_up, u_down, v_up, v_down = link(True, 1), link(True, -1), link(False, 1), link(False, -1)

    def clear(ref):
        ref[...] = jnp.zeros(ref.shape, BF16)

    pl.when(bx == 0)(lambda: clear(field.at[:, 0, core]))
    pl.when(bx == 3)(lambda: clear(field.at[:, 2, core]))
    pl.when(by == 0)(lambda: clear(field.at[0, :, core]))
    pl.when(by == 3)(lambda: clear(field.at[2, :, core]))
    pl.when(~below)(lambda: clear(outer.at[0]))
    pl.when(~above)(lambda: clear(outer.at[1]))

    got_edge[...] = jnp.zeros_like(got_edge)
    barrier = pltpu.get_barrier_semaphore()

    def greet(device):
        pl.semaphore_signal(barrier, inc=1, device_id=device, device_id_type=MESH)

    for k in range(1, VIEWS):
        greet(at_vert(q * 4 + (slot + k) % VIEWS))
    for device, there in (u_up, u_down, v_up, v_down):
        pl.when(there)(lambda device=device: greet(device))

    @pl.when(above)
    def _():
        greet(at_vert(vert - slot + 4))

        @pl.when(last)
        def _():
            for k in range(2, VIEWS + 1):
                greet(at_vert(vert + k))

    beside = [(there, 1) for _, there in (u_up, u_down, v_up, v_down)]
    beside += [(first & below, VIEWS), (~first & below, 1)]
    pl.semaphore_wait(barrier, 3 + sum(jnp.where(there, n, 0) for there, n in beside))

    def answer(device):
        pl.semaphore_signal(ready, inc=1, device_id=device, device_id_type=MESH)

    @pl.when(first & below)
    def _():
        for k in range(1, VIEWS + 1):
            answer(at_vert(vert - k))

    pl.when(~first & below)(lambda: answer(at_vert(vert - slot - 1)))

    loads[0].wait()
    groups = est[...].reshape(BLOCK, GROUPS, 8, BLOCK)
    line = jnp.concatenate([groups[:, g].reshape(256, BLOCK) for g in range(GROUPS)], axis=1)
    line = pltpu.roll(line, slot * 32, 1).reshape(16, 2, 8, LANES)
    for side, quads in enumerate(swap_quads(line[:, 0], line[:, 1])):
        packed[side * 128 : side * 128 + 128, :] = quads.reshape(128, LANES).astype(BF16)

    def part_copy(source, send, device, side):
        return pltpu.make_async_remote_copy(
            src_ref=packed.at[pl.ds(side * 128, 128), :], dst_ref=parts.at[source],
            send_sem=part_send.at[send], recv_sem=part_recv.at[source],
            device_id=device, device_id_type=MESH,
        )

    for k in range(1, VIEWS):
        other = (slot + k) % VIEWS
        part_copy(slot, k - 1, at_vert(q * 4 + other), other % 2).start()

    def outer_copy(which, send, device, side):
        return pltpu.make_async_remote_copy(
            src_ref=packed.at[pl.ds(side * 128, 128), :], dst_ref=outer.at[which],
            send_sem=part_send.at[3 + send], recv_sem=part_recv.at[4 + which],
            device_id=device, device_id_type=MESH,
        )

    @pl.when(first & below)
    def _():
        for k in range(VIEWS):
            outer_copy(1, k, at_vert(vert - 4 + k), k % 2).start()

    parts[slot] = packed[pl.ds(core * 128, 128), :]
    loads[1].wait()
    loads[2].wait()
    build_taps(psf, slot_view, slot, taps)

    def assemble():
        for k in range(1, VIEWS):
            part_copy((slot + k) % VIEWS, 0, partner, 0).wait_recv()
        chunk = iota((128, LANES), 1) // 32
        have = [parts[k].astype(F32) for k in range(VIEWS)]
        for g in range(GROUPS):
            line = have[(3 - g) % 4]
            for at in range(3):
                line = jnp.where(chunk == at, have[(at - g) % 4], line)
            if g:
                line = pltpu.roll(line, LANES - 32 * g, 1)
            for tp in range(2):
                field[1, 1, core, 4 * tp + g] = line[64 * tp : 64 * tp + 64].astype(BF16)

    def assemble_rims():
        for k, there in enumerate((below, above)):
            pl.when(there)(lambda k=k: outer_copy(k, 0, partner, 0).wait_recv())
        is_above = iota((128, LANES), 1) % 32 < RAD
        line = jnp.where(is_above, outer[1].astype(F32), outer[0].astype(F32))
        field[1, 1, core, 8:10] = pltpu.roll(line, RAD, 1).astype(BF16).reshape(2, 64, LANES)

    def message(ju, jv, which):
        return field.at[(*block(ju, jv), core, slice(4 * which, min(4 * which + 4, 10)))]

    def face_copy(source, target, which, send, device):
        return pltpu.make_async_remote_copy(
            src_ref=message(*source, which), dst_ref=message(*target, which),
            send_sem=face_send.at[send],
            recv_sem=face_recv.at[which * 9 + target[0] * 3 + target[1]],
            device_id=device, device_id_type=MESH,
        )

    ways = {"u_up": (0, u_up, (0, 1)), "u_down": (1, u_down, (2, 1)), "v_up": (2, v_up, (1, 0)), "v_down": (3, v_down, (1, 2))}

    def send_own(name, which):
        index, (device, there), target = ways[name]
        pl.when(there)(face_copy((1, 1), target, which, index, device).start)

    def relay(name, along, which):
        index, (device, there), target = ways[name]
        source = (along, 1) if name[0] == "v" else (1, along)
        target = (along, target[1]) if name[0] == "v" else (target[0], along)
        pl.when(there)(face_copy(source, target, which, 4 + index, device).start)

    def came(ju, jv, which, over):
        there = ways[f"{over}_{'down' if (jv if over == 'v' else ju) == 0 else 'up'}"][1][1]
        copy = face_copy((ju, jv), (ju, jv), which, 0, partner)
        pl.when(there)(copy.wait_recv)

    def core_copy(jy, jx, side):
        return pltpu.make_async_remote_copy(
            src_ref=field.at[jy, jx, side], dst_ref=field.at[jy, jx, side],
            send_sem=core_send.at[0], recv_sem=core_recv.at[jy * 3 + jx],
            device_id=partner, device_id_type=MESH,
        )

    def pass_on(ju, jv):
        core_copy(*block(ju, jv), core).start()

    def swapped(jy, jx):
        core_copy(jy, jx, 1 - core).wait_recv()

    def forward_z(*blocks):
        pieces = [(*b, side) for b in blocks for side in range(2)]
        rim = jnp.concatenate([field[jy, jx, side, 8 + tp] for jy, jx, side in pieces for tp in range(2)])
        for g in range(GROUPS):
            turned = pltpu.roll(rim, LANES - 32 * g, 1) if g else rim
            main = jnp.concatenate(
                [field[jy, jx, side, 4 * tp + g] for jy, jx, side in pieces for tp in range(2)]
            )
            done = dot(jnp.concatenate([main, turned], axis=1), wz[...]).astype(BF16)
            for i, (jy, jx, side) in enumerate(pieces):
                for r in range(RANK):
                    after_z[r, jy * GROUPS + g, side, jx * 128 : jx * 128 + 128, :] = done[
                        i * 128 : (i + 1) * 128, r * 128 : (r + 1) * 128
                    ]

    def forward_x(jy):
        for r in range(RANK):
            for group in (jy * GROUPS, jy * GROUPS + 2):
                for b in range(2):
                    rows = slice(b * 128, b * 128 + 256)
                    both = [after_z[r, group + k // 2, k % 2, rows, :] for k in range(4)]
                    done = dot(tx[r], jnp.concatenate(both, axis=1)).astype(BF16)
                    for k in range(4):
                        after_x[r, group + k // 2, k % 2, b * 128 : b * 128 + 128, :] = done[
                            :, k * 128 : k * 128 + 128
                        ]

    assemble()
    for name in ("u_up", "u_down", "v_up", "v_down"):
        send_own(name, 0)
    for name in ("v_up", "v_down", "u_up", "u_down"):
        send_own(name, 1)

    @pl.when(last & above)
    def _():
        pl.semaphore_wait(ready, VIEWS)
        for k in range(VIEWS):
            outer_copy(0, k, at_vert(vert + 1 + k), k % 2).start()

    build_z(taps, wz, wb)
    assemble_rims()
    for name in ("u_up", "u_down", "v_up", "v_down"):
        send_own(name, 2)
    pass_on(1, 1)
    build_x(taps, bx, tx, txb)
    for side in (0, 2):
        came(side, 1, 0, "u")
    for one, other in ((0, 2), (2, 0)):
        relay("v_up", one, 0)
        relay("v_down", other, 0)
    build_y(taps, by, ty, tyb)
    for side in (0, 2):
        came(1, side, 1, "v")
    for one, other in ((0, 2), (2, 0)):
        relay("u_up", one, 1)
        relay("u_down", other, 1)
    loads[3].wait()

    def order_tile(i, carry):
        quad = tile[pl.ds(4 * i, 4)].astype(F32).reshape(2, 2, 8, 8, LANES)
        sides = swap_quads(quad[:, 0], quad[:, 1])
        rows = jnp.stack([m[x] for m in sides for x in range(2)], axis=1)
        seen[i] = rows.reshape(256, LANES).astype(BF16)
        return carry

    lax.fori_loop(0, 16, order_tile, 0, unroll=4)
    swapped(1, 1)
    forward_z((1, 1))
    for side in (0, 2):
        came(side, 1, 2, "u")
    for one, other in ((0, 2), (2, 0)):
        relay("v_up", one, 2)
        relay("v_down", other, 2)
    for side in (0, 2):
        came(side, 1, 1, "u")
        pass_on(side, 1)
        came(1, side, 0, "v")
        came(1, side, 2, "v")
        pass_on(1, side)
    for side in (0, 2):
        swapped(1, side)
        swapped(side, 1)
    forward_z((1, 0), (1, 2))
    forward_z((0, 1), (2, 1))
    waves = (((0, 0), (2, 2)), ((0, 2), (2, 0)))
    for corner in waves[0]:
        came(*corner, 0, "v")
        came(*corner, 1, "u")
        came(*corner, 2, "v")
        pass_on(*corner)
    forward_x(1)
    for corner in waves[1]:
        came(*corner, 0, "v")
        came(*corner, 1, "u")
        came(*corner, 2, "v")
        pass_on(*corner)
    for wave in waves:
        for corner in wave:
            swapped(*corner)
        forward_z(*wave)
    for jy in (0, 2):
        forward_x(jy)

    def along_y(step):
        quotient = []
        for b in range(2):
            terms = []
            for r in range(RANK):
                quads = [
                    after_x[r, 4 * b : 4 * b + 8, :, 16 * i : 16 * i + 16, :].reshape(256, LANES)
                    for i in range(4 * step, 4 * step + 4)
                ]
                terms.append(jnp.concatenate(quads, axis=1))
            blurred = dot(ty[...], jnp.concatenate(terms, axis=0))
            rows = slice(128 * b, 128 * b + 128)
            quads = [seen[i, rows, :] for i in range(4 * step, 4 * step + 4)]
            quads = jnp.concatenate(quads, axis=1).astype(F32)
            quotient.append((RANK * quads / (blurred + RANK * BACKGROUND)).astype(BF16))
        quotient = jnp.concatenate(quotient, axis=0)
        for r in range(RANK):
            done = dot(tyb[r * 128 : r * 128 + 128, :], quotient).astype(BF16)
            for k in range(4):
                i = 4 * step + k
                back_y[r * 8 : r * 8 + 8, 16 * i : 16 * i + 16, :] = done[
                    :, k * 128 : k * 128 + 128
                ].reshape(8, 16, LANES)

    def backward_x(half):
        within = slice(half * 64, half * 64 + 192)
        for g in (0, 2):
            for r in range(RANK):
                at = (r * GROUPS + g) * 2
                sides = jnp.concatenate([back_y[at + k, within, :] for k in range(4)], axis=1)
                done = dot(txb[half, r, :, 0:192], sides).astype(BF16)
                for k in range(4):
                    rows = slice(k % 2 * 64, k % 2 * 64 + 64)
                    back_x[g + k // 2, half, rows, r * 128 : (r + 1) * 128] = done[
                        :, k * 128 : k * 128 + 128
                    ]

    def backward_z(half):
        parts_z = [dot(back_x[g, half], wb[g]) for g in range(GROUPS)]
        both = (parts_z[0] + parts_z[1] + (parts_z[2] + parts_z[3]))[:, LANES:]
        is_low = iota((64, LANES), 1) < 64
        rims[half, 0] = jnp.where(is_low, both[0:64], pltpu.roll(both[64:128], 64, 1))
        rims[half, 1] = jnp.where(is_low, pltpu.roll(both[0:64], 64, 1), both[64:128])
        for which in range(2):
            pl.when((below, above)[which])(rim_copy(half, which).start)
        for g in range(GROUPS):
            for c in range(4):
                at = (g + c) % 4
                sums[half, c, :, at * 32 : at * 32 + 32] = parts_z[g][:, at * 32 : at * 32 + 32]

    far = (1 - chip) * 2 + core

    def sum_copy(source, target, index, device):
        return pltpu.make_async_remote_copy(
            src_ref=source, dst_ref=target, send_sem=sum_send.at[index],
            recv_sem=sum_recv.at[index], device_id=device, device_id_type=MESH,
        )

    far_swap = [
        sum_copy(sums.at[h, (1 - chip) * 2 + 1 - core], got_core.at[h, 0], h, partner) for h in range(2)
    ]
    near_swap = [
        sum_copy(sums.at[h, chip * 2 + 1 - core], got_core.at[h, 1], 2 + h, partner) for h in range(2)
    ]
    over = [sum_copy(sums.at[h, far], got_chip.at[h], 4 + h, at_vert(q * 4 + far)) for h in range(2)]

    def rim_copy(h, which):
        home = (vert - slot - 1, vert - slot + 4)[which]
        return pltpu.make_async_remote_copy(
            src_ref=rims.at[h, which], dst_ref=got_edge.at[slot, h], send_sem=sum_send.at[6 + 2 * h + which],
            recv_sem=sum_recv.at[6 + 2 * slot + h], device_id=at_vert(home), device_id_type=MESH,
        )

    def rim_came(h):
        for k in range(VIEWS):
            pltpu.make_async_remote_copy(
                src_ref=rims.at[h, 0], dst_ref=got_edge.at[k, h], send_sem=sum_send.at[6],
                recv_sem=sum_recv.at[6 + 2 * k + h], device_id=partner, device_id_type=MESH,
            ).wait_recv()

    def backward(h):
        backward_x(h)
        backward_z(h)
        far_swap[h].start()
        near_swap[h].start()

    def pass_over(h):
        far_swap[h].wait_recv()
        sums[h, far] = sums[h, far] + got_core[h, 0]
        over[h].start()

    pl.when(~last & above)(lambda: pl.semaphore_wait(ready, 1))
    for step in range(3):
        along_y(step)
    backward(0)
    along_y(3)
    pass_over(0)
    backward(1)
    pass_over(1)

    for k in range(1, VIEWS):
        part_copy(slot, k - 1, partner, 0).wait_send()

    @pl.when(is_edge)
    def _():
        for k in range(VIEWS):
            outer_copy(0, k, partner, 0).wait_send()

    def sent(ref, semaphore):
        pltpu.make_async_remote_copy(
            src_ref=ref, dst_ref=ref, send_sem=semaphore, recv_sem=face_recv.at[0],
            device_id=partner, device_id_type=MESH,
        ).wait_send()

    for name, (index, (_, there), _) in ways.items():
        relayed = field.at[0:3, 0:2, :, 0:1] if name[0] == "v" else field.at[0:2, 0:2, :, 0:1]

        @pl.when(there)
        def _():
            sent(field.at[1, 1, core], face_send.at[index])
            sent(relayed, face_send.at[4 + index])

    sent(field.at[:, :, core], core_send.at[0])

    start = jnp.where(last, RAD, 0)
    lane = iota((64, LANES), 1)
    keep = is_edge & (lane >= start) & (lane < start + RAD)
    for h in range(2):
        near_swap[h].wait_recv()
        mine = sums[h, slot] + got_core[h, 1]
        over[h].wait_recv()
        mine = mine + got_chip[h]

        pl.when(is_edge)(lambda: rim_came(h))
        edge = got_edge[0, h] + got_edge[1, h] + (got_edge[2, h] + got_edge[3, h])
        for g in range(GROUPS):
            own = pltpu.roll(mine, (8 - g - slot) % 4 * 32, 1)
            sides = []
            for k in range(2):
                rim = pltpu.roll(edge, (start + LANES - 64 * k - RAD * g) % LANES, 1)
                part = own[64 * k : 64 * k + 64] + jnp.where(keep, rim, 0.0)
                sides.append(part.reshape(8, 8, LANES) * (1.0 / (RANK * VIEWS)))
            part = jnp.stack(swap_quads(*sides), axis=1).reshape(16, 8, LANES)
            at = (slice(16 * h, 16 * h + 16), slice(g * 8, g * 8 + 8))
            refined[at] = est[at] * part[:, :, 0:BLOCK]

    for copy in far_swap + near_swap + over:
        copy.wait_send()
    for which in range(2):

        @pl.when((below, above)[which])
        def _():
            for h in range(2):
                rim_copy(h, which).wait_send()


def local(estimate, view_tiles, slot_view, psf_taps):
    vmem = pl.BlockSpec(memory_space=pltpu.VMEM)
    hbm = pl.BlockSpec(memory_space=pltpu.HBM)
    tile = view_tiles[0, 0, 0]
    psf = jnp.transpose(psf_taps, (1, 2, 0, 3))
    scratch = [
        pltpu.VMEM(estimate.shape, F32),
        pltpu.VMEM(tile.shape, BF16),
        pltpu.VMEM(psf.shape, F32),
        pltpu.VMEM(slot_view.shape, jnp.int32),
        pltpu.VMEM((256, LANES), BF16),
        pltpu.VMEM((VIEWS, 128, LANES), BF16),
        pltpu.VMEM((2, 128, LANES), BF16),
        pltpu.VMEM((3, 3, 2, 10, 64, LANES), BF16),
        pltpu.VMEM((RANK, 12, 2, 384, LANES), BF16),
        pltpu.VMEM((RANK, 12, 2, 256, LANES), BF16),
        pltpu.VMEM((16, 256, LANES), BF16),
        pltpu.VMEM((24, 256, LANES), BF16),
        pltpu.VMEM((GROUPS, 2, 128, RANK * LANES), BF16),
        pltpu.VMEM((2, 4, 128, LANES), F32),
        pltpu.VMEM((2, 2, 64, LANES), F32),
        pltpu.VMEM((2, 2, 128, LANES), F32),
        pltpu.VMEM((2, 128, LANES), F32),
        pltpu.VMEM((VIEWS, 2, 64, LANES), F32),
        pltpu.VMEM((2, 24, LANES), F32),
        pltpu.VMEM((RANK, 128, 256), BF16),
        pltpu.VMEM((128, RANK * 256), BF16),
        pltpu.VMEM((256, RANK * LANES), BF16),
        pltpu.VMEM((RANK * 128, 256), BF16),
        pltpu.VMEM((2, RANK, 64, 256), BF16),
        pltpu.VMEM((GROUPS, RANK * LANES, 256), BF16),
        pltpu.SemaphoreType.DMA((4,)),
        pltpu.SemaphoreType.DMA((7,)),
        pltpu.SemaphoreType.DMA((6,)),
        pltpu.SemaphoreType.DMA((8,)),
        pltpu.SemaphoreType.DMA((27,)),
        pltpu.SemaphoreType.DMA((1,)),
        pltpu.SemaphoreType.DMA((9,)),
        pltpu.SemaphoreType.DMA((10,)),
        pltpu.SemaphoreType.DMA((14,)),
        pltpu.SemaphoreType.REGULAR,
    ]
    return pl.pallas_call(
        kernel,
        out_shape=pltpu.VMEM(estimate.shape, F32),
        in_specs=[hbm] * 4,
        out_specs=vmem,
        scratch_shapes=scratch,
        compiler_params=pltpu.CompilerParams(
            collective_id=0, has_side_effects=True, vmem_limit_bytes=56 * 1024 * 1024
        ),
    )(*(pltpu.with_memory_space_constraint(a, pltpu.HBM) for a in (estimate, tile, psf, slot_view)))


def solution(mesh):
    placed = (
        P("bx", "by", "vert"),
        P("bx", "by", "vert", None, None, None),
        P("bx", "by", None),
        P(),
    )
    return jax.shard_map(
        local, mesh=mesh, in_specs=placed, out_specs=P("bx", "by", "vert"), check_vma=False
    )
```

```python
import jax
import jax.numpy as jnp
from jax import lax
from jax.experimental import pallas as pl
from jax.experimental.pallas import tpu as pltpu
from jax.sharding import PartitionSpec as P

BACKGROUND = 0.1
MESH = pl.DeviceIdType.MESH
F32, BF16 = jnp.float32, jnp.bfloat16
BLOCK = 32
RAD = 16
TAPS = 33
RANK = 3
VIEWS = 4
GROUPS = 4
LANES = 128


def iota(shape, axis):
    return lax.broadcasted_iota(jnp.int32, shape, axis)


def dot(a, b):
    return jnp.dot(a, b, preferred_element_type=F32)


def band(line, rows, start):
    line = jnp.broadcast_to(line, (rows, LANES))
    return pltpu.roll(line, start % LANES, 1, stride=1, stride_axis=0)


def swap_quads(a, b):
    low, axis = iota(a.shape, a.ndim - 2) < 4, a.ndim - 2
    return jnp.where(low, a, pltpu.roll(b, 4, axis)), jnp.where(low, pltpu.roll(a, 4, axis), b)


def build_taps(psf, slot_view, slot, taps):
    listed = slot_view[...]
    view = jnp.sum(jnp.where(iota(listed.shape, 2) == slot, listed, 0), axis=2, keepdims=True)
    held = iota((VIEWS, TAPS), 0) == view[0]
    mine = jnp.sum(jnp.where(held[None, None], psf[...], 0.0), axis=2)
    mine = (mine / jnp.sum(mine, axis=-1, keepdims=True)).astype(BF16).astype(F32)
    taps[...] = jnp.zeros_like(taps)
    for a in range(3):
        taps[0, 8 * a : 8 * a + RANK, :TAPS] = mine[a]
    flip = (iota((LANES, LANES), 0) + iota((LANES, LANES), 1) == TAPS - 1).astype(BF16)
    taps[1] = dot(taps[0].astype(BF16), flip)


def build_z(taps, wz, wb):
    z_in, z_out = iota((LANES, LANES), 0), iota((LANES, LANES), 1)
    near = jnp.abs(z_in - z_out) <= RAD
    rim, out = iota((32, LANES), 0), iota((32, LANES), 1)
    rim_ok = ((rim < RAD) & (out <= rim)) | ((rim >= RAD) & (out >= rim + 96))
    lane16 = iota((16, LANES), 1)
    for r in range(RANK):
        forward, backward = taps[1, 16 + r : 17 + r, :], taps[0, 16 + r : 17 + r, :]
        columns = slice(r * LANES, (r + 1) * LANES)
        wz[0:128, columns] = jnp.where(near, band(forward, LANES, -RAD), 0.0).astype(BF16)
        wz[128:160, columns] = jnp.where(rim_ok, band(forward, 32, 96), 0.0).astype(BF16)
        wz[160:256, columns] = jnp.zeros((96, LANES), BF16)
        main = jnp.where(near, band(backward, LANES, -RAD), 0.0)
        low = jnp.where(lane16 < RAD, band(backward, 16, 0), 0.0)
        high = jnp.where(lane16 < RAD, band(backward, 16, 96), 0.0)
        for g in range(GROUPS):
            wb[g, r * 128 : r * 128 + 128, 0:128] = (
                pltpu.roll(main, 32 * g, 1) if g else main
            ).astype(BF16)
            wb[g, r * 128 : r * 128 + 128, 128:256] = jnp.zeros((128, LANES), BF16)
            lo, hi = pltpu.roll(low, RAD * g, 1) if g else low, pltpu.roll(high, 64 + RAD * g, 1)
            wb[g, r * 128 : r * 128 + 16, 128:256] = lo.astype(BF16)
            wb[g, r * 128 + 112 : r * 128 + 128, 128:256] = hi.astype(BF16)


def build_x(taps, bx, tx, txb):
    spread = (iota((LANES, 256), 1) == 4 * iota((LANES, 256), 0)).astype(BF16)
    lane, row = iota((LANES, LANES), 1), iota((LANES, LANES), 0)
    low, high = bx > 0, bx < 3

    def tiles(line):
        turned = [band(line[:, i * LANES : (i + 1) * LANES], LANES, 0) for i in range(2)]
        return jnp.where(lane >= row, turned[0], 0.0), jnp.where(lane >= row, turned[1], turned[0])

    wide = [dot(taps[k, 0:8, :].astype(BF16), spread) for k in range(2)]
    for r in range(RANK):
        left, right = tiles(wide[0][r : r + 1])
        tx[r, :, 0:128] = left.astype(BF16)
        tx[r, :, 128:256] = right.astype(BF16)
        left, right = [m[0:64] for m in tiles(wide[1][r : r + 1])]
        txb[0, r, :, 0:128] = jnp.where((lane[0:64] >= 64) | low, left, 0.0).astype(BF16)
        txb[0, r, :, 128:256] = right.astype(BF16)
        txb[1, r, :, 0:128] = left.astype(BF16)
        txb[1, r, :, 128:256] = jnp.where(high, right, 0.0).astype(BF16)


def build_y(taps, by, ty, tyb):
    place = by * BLOCK - RAD + iota((BLOCK, LANES), 1)
    inside = (place >= 0) & (place < 4 * BLOCK)
    plain = [band(taps[0, 8 + r : 9 + r, :], BLOCK, 0) for r in range(RANK)]
    plain += [
        jnp.where(inside, band(taps[1, 8 + r : 9 + r, :], BLOCK, 0), 0.0) for r in range(RANK)
    ]
    plain = jnp.concatenate(plain, axis=0).astype(BF16)
    y, column = iota((LANES, 256), 0), iota((LANES, 256), 1)
    wide = [
        dot(plain, (column == 16 * (y // 4) + 4 * x + y % 4).astype(BF16)).astype(BF16)
        for x in range(4)
    ]
    row, source = iota((LANES, LANES), 0), iota((LANES, LANES), 1)
    order = (row == 16 * (source % 32 // 4) + 4 * (source // 32) + source % 4).astype(BF16)
    for i in range(2 * RANK):
        done = dot(order, jnp.concatenate([m[i * 32 : i * 32 + 32] for m in wide], axis=0)).astype(BF16)
        if i < RANK:
            ty[:, i * 256 : (i + 1) * 256] = done
        else:
            tyb[(i - RANK) * 128 : (i - RANK + 1) * 128, :] = done


def kernel(
    est_hbm, tile_hbm, psf_hbm, slot_view_hbm, refined,
    est, tile, psf, slot_view,
    packed, parts, outer, field, after_z, after_x, seen, back_y, back_x, sums, rims,
    got_core, got_chip, got_edge,
    taps, tx, ty, wz, tyb, txb, wb,
    load_sem, part_send, part_recv, face_send, face_recv, core_send, core_recv, sum_send, sum_recv, ready,
):
    bx, by, vert = lax.axis_index("bx"), lax.axis_index("by"), lax.axis_index("vert")
    q, slot = vert // VIEWS, vert % VIEWS
    core, chip = slot % 2, slot // 2

    loads = [
        pltpu.make_async_copy(source, target, load_sem.at[i])
        for i, (source, target) in enumerate(
            ((est_hbm, est), (psf_hbm, psf), (slot_view_hbm, slot_view), (tile_hbm, tile))
        )
    ]
    for copy in loads:
        copy.start()

    def at_vert(index):
        return {"vert": index}

    partner = at_vert(q * 4 + chip * 2 + 1 - core)
    above, below = q < 3, q > 0
    first, last = slot == 0, slot == VIEWS - 1
    is_edge = (first & below) | (last & above)

    straight = core == 0

    def block(ju, jv):
        return jnp.where(straight, jv, ju), jnp.where(straight, ju, jv)

    def link(along_u, step):
        x_step = jnp.where(straight == along_u, step, 0)
        x, y = bx + x_step, by + step - x_step
        return {"bx": x, "by": y}, (x >= 0) & (x < 4) & (y >= 0) & (y < 4)

    u_up, u_down, v_up, v_down = link(True, 1), link(True, -1), link(False, 1), link(False, -1)

    def clear(ref):
        ref[...] = jnp.zeros(ref.shape, BF16)

    pl.when(bx == 0)(lambda: clear(field.at[:, 0, core]))
    pl.when(bx == 3)(lambda: clear(field.at[:, 2, core]))
    pl.when(by == 0)(lambda: clear(field.at[0, :, core]))
    pl.when(by == 3)(lambda: clear(field.at[2, :, core]))
    pl.when(~below)(lambda: clear(outer.at[0]))
    pl.when(~above)(lambda: clear(outer.at[1]))

    got_edge[...] = jnp.zeros_like(got_edge)
    barrier = pltpu.get_barrier_semaphore()

    def greet(device):
        pl.semaphore_signal(barrier, inc=1, device_id=device, device_id_type=MESH)

    for k in range(1, VIEWS):
        greet(at_vert(q * 4 + (slot + k) % VIEWS))
    for device, there in (u_up, u_down, v_up, v_down):
        pl.when(there)(lambda device=device: greet(device))

    @pl.when(above)
    def _():
        greet(at_vert(vert - slot + 4))

        @pl.when(last)
        def _():
            for k in range(2, VIEWS + 1):
                greet(at_vert(vert + k))

    beside = [(there, 1) for _, there in (u_up, u_down, v_up, v_down)]
    beside += [(first & below, VIEWS), (~first & below, 1)]
    pl.semaphore_wait(barrier, 3 + sum(jnp.where(there, n, 0) for there, n in beside))

    def answer(device):
        pl.semaphore_signal(ready, inc=1, device_id=device, device_id_type=MESH)

    @pl.when(first & below)
    def _():
        for k in range(1, VIEWS + 1):
            answer(at_vert(vert - k))

    pl.when(~first & below)(lambda: answer(at_vert(vert - slot - 1)))

    loads[0].wait()
    groups = est[...].reshape(BLOCK, GROUPS, 8, BLOCK)
    line = jnp.concatenate([groups[:, g].reshape(256, BLOCK) for g in range(GROUPS)], axis=1)
    line = pltpu.roll(line, slot * 32, 1).reshape(16, 2, 8, LANES)
    for side, quads in enumerate(swap_quads(line[:, 0], line[:, 1])):
        packed[side * 128 : side * 128 + 128, :] = quads.reshape(128, LANES).astype(BF16)

    def part_copy(source, send, device, side):
        return pltpu.make_async_remote_copy(
            src_ref=packed.at[pl.ds(side * 128, 128), :], dst_ref=parts.at[source],
            send_sem=part_send.at[send], recv_sem=part_recv.at[source],
            device_id=device, device_id_type=MESH,
        )

    for k in range(1, VIEWS):
        other = (slot + k) % VIEWS
        part_copy(slot, k - 1, at_vert(q * 4 + other), other % 2).start()

    def outer_copy(which, send, device, side):
        return pltpu.make_async_remote_copy(
            src_ref=packed.at[pl.ds(side * 128, 128), :], dst_ref=outer.at[which],
            send_sem=part_send.at[3 + send], recv_sem=part_recv.at[4 + which],
            device_id=device, device_id_type=MESH,
        )

    @pl.when(first & below)
    def _():
        for k in range(VIEWS):
            outer_copy(1, k, at_vert(vert - 4 + k), k % 2).start()

    parts[slot] = packed[pl.ds(core * 128, 128), :]
    loads[1].wait()
    loads[2].wait()
    build_taps(psf, slot_view, slot, taps)
    build_z(taps, wz, wb)

    def assemble():
        for k in range(1, VIEWS):
            part_copy((slot + k) % VIEWS, 0, partner, 0).wait_recv()
        chunk = iota((128, LANES), 1) // 32
        have = [parts[k].astype(F32) for k in range(VIEWS)]
        for g in range(GROUPS):
            line = have[(3 - g) % 4]
            for at in range(3):
                line = jnp.where(chunk == at, have[(at - g) % 4], line)
            if g:
                line = pltpu.roll(line, LANES - 32 * g, 1)
            for tp in range(2):
                field[1, 1, core, 4 * tp + g] = line[64 * tp : 64 * tp + 64].astype(BF16)

    def assemble_rims():
        for k, there in enumerate((below, above)):
            pl.when(there)(lambda k=k: outer_copy(k, 0, partner, 0).wait_recv())
        is_above = iota((128, LANES), 1) % 32 < RAD
        line = jnp.where(is_above, outer[1].astype(F32), outer[0].astype(F32))
        field[1, 1, core, 8:10] = pltpu.roll(line, RAD, 1).astype(BF16).reshape(2, 64, LANES)

    def message(ju, jv, which):
        return field.at[(*block(ju, jv), core, slice(4 * which, min(4 * which + 4, 10)))]

    def face_copy(source, target, which, send, device):
        return pltpu.make_async_remote_copy(
            src_ref=message(*source, which), dst_ref=message(*target, which),
            send_sem=face_send.at[send],
            recv_sem=face_recv.at[which * 9 + target[0] * 3 + target[1]],
            device_id=device, device_id_type=MESH,
        )

    ways = {"u_up": (0, u_up, (0, 1)), "u_down": (1, u_down, (2, 1)), "v_up": (2, v_up, (1, 0)), "v_down": (3, v_down, (1, 2))}

    def send_own(name, which):
        index, (device, there), target = ways[name]
        pl.when(there)(face_copy((1, 1), target, which, index, device).start)

    def relay(name, along, which):
        index, (device, there), target = ways[name]
        source = (along, 1) if name[0] == "v" else (1, along)
        target = (along, target[1]) if name[0] == "v" else (target[0], along)
        pl.when(there)(face_copy(source, target, which, 4 + index, device).start)

    def came(ju, jv, which, over):
        there = ways[f"{over}_{'down' if (jv if over == 'v' else ju) == 0 else 'up'}"][1][1]
        copy = face_copy((ju, jv), (ju, jv), which, 0, partner)
        pl.when(there)(copy.wait_recv)

    def core_copy(jy, jx, side):
        return pltpu.make_async_remote_copy(
            src_ref=field.at[jy, jx, side], dst_ref=field.at[jy, jx, side],
            send_sem=core_send.at[0], recv_sem=core_recv.at[jy * 3 + jx],
            device_id=partner, device_id_type=MESH,
        )

    def pass_on(ju, jv):
        core_copy(*block(ju, jv), core).start()

    def swapped(jy, jx):
        core_copy(jy, jx, 1 - core).wait_recv()

    def forward_z(*blocks):
        pieces = [(*b, side) for b in blocks for side in range(2)]
        rim = jnp.concatenate([field[jy, jx, side, 8 + tp] for jy, jx, side in pieces for tp in range(2)])
        for g in range(GROUPS):
            turned = pltpu.roll(rim, LANES - 32 * g, 1) if g else rim
            main = jnp.concatenate(
                [field[jy, jx, side, 4 * tp + g] for jy, jx, side in pieces for tp in range(2)]
            )
            done = dot(jnp.concatenate([main, turned], axis=1), wz[...]).astype(BF16)
            for i, (jy, jx, side) in enumerate(pieces):
                for r in range(RANK):
                    after_z[r, jy * GROUPS + g, side, jx * 128 : jx * 128 + 128, :] = done[
                        i * 128 : (i + 1) * 128, r * 128 : (r + 1) * 128
                    ]

    def forward_x(jy):
        for r in range(RANK):
            for group in (jy * GROUPS, jy * GROUPS + 2):
                for b in range(2):
                    rows = slice(b * 128, b * 128 + 256)
                    both = [after_z[r, group + k // 2, k % 2, rows, :] for k in range(4)]
                    done = dot(tx[r], jnp.concatenate(both, axis=1)).astype(BF16)
                    for k in range(4):
                        after_x[r, group + k // 2, k % 2, b * 128 : b * 128 + 128, :] = done[
                            :, k * 128 : k * 128 + 128
                        ]

    assemble()
    for name, which in (("u_up", 0), ("u_down", 0), ("v_up", 1), ("v_down", 1)):
        send_own(name, which)
    for name, which in (("u_up", 1), ("u_down", 1), ("v_up", 0), ("v_down", 0)):
        send_own(name, which)

    @pl.when(last & above)
    def _():
        pl.semaphore_wait(ready, VIEWS)
        for k in range(VIEWS):
            outer_copy(0, k, at_vert(vert + 1 + k), k % 2).start()

    build_x(taps, bx, tx, txb)
    assemble_rims()
    for name in ("u_up", "u_down", "v_up", "v_down"):
        send_own(name, 2)
    pass_on(1, 1)
    for side in (0, 2):
        came(side, 1, 0, "u")
    for one, other in ((0, 2), (2, 0)):
        relay("v_up", one, 0)
        relay("v_down", other, 0)
    build_y(taps, by, ty, tyb)
    for side in (0, 2):
        came(1, side, 1, "v")
    for one, other in ((0, 2), (2, 0)):
        relay("u_up", one, 1)
        relay("u_down", other, 1)
    loads[3].wait()

    def order_tile(i, carry):
        quad = tile[pl.ds(4 * i, 4)].astype(F32).reshape(2, 2, 8, 8, LANES)
        sides = swap_quads(quad[:, 0], quad[:, 1])
        rows = jnp.stack([m[x] for m in sides for x in range(2)], axis=1)
        seen[i] = rows.reshape(256, LANES).astype(BF16)
        return carry

    lax.fori_loop(0, 16, order_tile, 0, unroll=4)
    swapped(1, 1)
    forward_z((1, 1))
    for side in (0, 2):
        came(side, 1, 2, "u")
    for one, other in ((0, 2), (2, 0)):
        relay("v_up", one, 2)
        relay("v_down", other, 2)
    for side in (0, 2):
        came(side, 1, 1, "u")
        pass_on(side, 1)
        came(1, side, 0, "v")
        came(1, side, 2, "v")
        pass_on(1, side)
    for side in (0, 2):
        swapped(1, side)
        swapped(side, 1)
    forward_z((1, 0), (1, 2))
    forward_z((0, 1), (2, 1))
    waves = (((0, 0), (2, 2)), ((0, 2), (2, 0)))
    for corner in waves[0]:
        came(*corner, 0, "v")
        came(*corner, 1, "u")
        came(*corner, 2, "v")
        pass_on(*corner)
    forward_x(1)
    for corner in waves[1]:
        came(*corner, 0, "v")
        came(*corner, 1, "u")
        came(*corner, 2, "v")
        pass_on(*corner)
    for wave in waves:
        for corner in wave:
            swapped(*corner)
        forward_z(*wave)
    for jy in (0, 2):
        forward_x(jy)

    def along_y(step):
        quotient = []
        for b in range(2):
            terms = []
            for r in range(RANK):
                quads = [
                    after_x[r, 4 * b : 4 * b + 8, :, 16 * i : 16 * i + 16, :].reshape(256, LANES)
                    for i in range(4 * step, 4 * step + 4)
                ]
                terms.append(jnp.concatenate(quads, axis=1))
            blurred = dot(ty[...], jnp.concatenate(terms, axis=0))
            rows = slice(128 * b, 128 * b + 128)
            quads = [seen[i, rows, :] for i in range(4 * step, 4 * step + 4)]
            quads = jnp.concatenate(quads, axis=1).astype(F32)
            quotient.append((RANK * quads / (blurred + RANK * BACKGROUND)).astype(BF16))
        quotient = jnp.concatenate(quotient, axis=0)
        for r in range(RANK):
            done = dot(tyb[r * 128 : r * 128 + 128, :], quotient).astype(BF16)
            for k in range(4):
                i = 4 * step + k
                back_y[r * 8 : r * 8 + 8, 16 * i : 16 * i + 16, :] = done[
                    :, k * 128 : k * 128 + 128
                ].reshape(8, 16, LANES)

    def backward_x(half):
        within = slice(half * 64, half * 64 + 192)
        for g in (0, 2):
            for r in range(RANK):
                at = (r * GROUPS + g) * 2
                sides = jnp.concatenate([back_y[at + k, within, :] for k in range(4)], axis=1)
                done = dot(txb[half, r, :, 0:192], sides).astype(BF16)
                for k in range(4):
                    rows = slice(k % 2 * 64, k % 2 * 64 + 64)
                    back_x[g + k // 2, half, rows, r * 128 : (r + 1) * 128] = done[
                        :, k * 128 : k * 128 + 128
                    ]

    def backward_z(half):
        parts_z = [dot(back_x[g, half], wb[g]) for g in range(GROUPS)]
        both = (parts_z[0] + parts_z[1] + (parts_z[2] + parts_z[3]))[:, LANES:]
        is_low = iota((64, LANES), 1) < 64
        rims[half, 0] = jnp.where(is_low, both[0:64], pltpu.roll(both[64:128], 64, 1))
        rims[half, 1] = jnp.where(is_low, pltpu.roll(both[0:64], 64, 1), both[64:128])
        for which in range(2):
            pl.when((below, above)[which])(rim_copy(half, which).start)
        for g in range(GROUPS):
            for c in range(4):
                at = (g + c) % 4
                sums[half, c, :, at * 32 : at * 32 + 32] = parts_z[g][:, at * 32 : at * 32 + 32]

    far = (1 - chip) * 2 + core

    def sum_copy(source, target, index, device):
        return pltpu.make_async_remote_copy(
            src_ref=source, dst_ref=target, send_sem=sum_send.at[index],
            recv_sem=sum_recv.at[index], device_id=device, device_id_type=MESH,
        )

    far_swap = [
        sum_copy(sums.at[h, (1 - chip) * 2 + 1 - core], got_core.at[h, 0], h, partner) for h in range(2)
    ]
    near_swap = [
        sum_copy(sums.at[h, chip * 2 + 1 - core], got_core.at[h, 1], 2 + h, partner) for h in range(2)
    ]
    over = [sum_copy(sums.at[h, far], got_chip.at[h], 4 + h, at_vert(q * 4 + far)) for h in range(2)]

    def rim_copy(h, which):
        home = (vert - slot - 1, vert - slot + 4)[which]
        return pltpu.make_async_remote_copy(
            src_ref=rims.at[h, which], dst_ref=got_edge.at[slot, h], send_sem=sum_send.at[6 + 2 * h + which],
            recv_sem=sum_recv.at[6 + 2 * slot + h], device_id=at_vert(home), device_id_type=MESH,
        )

    def rim_came(h):
        for k in range(VIEWS):
            pltpu.make_async_remote_copy(
                src_ref=rims.at[h, 0], dst_ref=got_edge.at[k, h], send_sem=sum_send.at[6],
                recv_sem=sum_recv.at[6 + 2 * k + h], device_id=partner, device_id_type=MESH,
            ).wait_recv()

    def backward(h):
        backward_x(h)
        backward_z(h)
        far_swap[h].start()
        near_swap[h].start()

    def pass_over(h):
        far_swap[h].wait_recv()
        sums[h, far] = sums[h, far] + got_core[h, 0]
        over[h].start()

    pl.when(~last & above)(lambda: pl.semaphore_wait(ready, 1))
    for step in range(3):
        along_y(step)
    backward(0)
    along_y(3)
    pass_over(0)
    backward(1)
    pass_over(1)

    for k in range(1, VIEWS):
        part_copy(slot, k - 1, partner, 0).wait_send()

    @pl.when(is_edge)
    def _():
        for k in range(VIEWS):
            outer_copy(0, k, partner, 0).wait_send()

    def sent(ref, semaphore):
        pltpu.make_async_remote_copy(
            src_ref=ref, dst_ref=ref, send_sem=semaphore, recv_sem=face_recv.at[0],
            device_id=partner, device_id_type=MESH,
        ).wait_send()

    for name, (index, (_, there), _) in ways.items():
        relayed = field.at[0:3, 0:2, :, 0:1] if name[0] == "v" else field.at[0:2, 0:2, :, 0:1]

        @pl.when(there)
        def _():
            sent(field.at[1, 1, core], face_send.at[index])
            sent(relayed, face_send.at[4 + index])

    sent(field.at[:, :, core], core_send.at[0])

    start = jnp.where(last, RAD, 0)
    lane = iota((64, LANES), 1)
    keep = is_edge & (lane >= start) & (lane < start + RAD)
    for h in range(2):
        near_swap[h].wait_recv()
        mine = sums[h, slot] + got_core[h, 1]
        over[h].wait_recv()
        mine = mine + got_chip[h]

        pl.when(is_edge)(lambda: rim_came(h))
        edge = got_edge[0, h] + got_edge[1, h] + (got_edge[2, h] + got_edge[3, h])
        for g in range(GROUPS):
            own = pltpu.roll(mine, (8 - g - slot) % 4 * 32, 1)
            sides = []
            for k in range(2):
                rim = pltpu.roll(edge, (start + LANES - 64 * k - RAD * g) % LANES, 1)
                part = own[64 * k : 64 * k + 64] + jnp.where(keep, rim, 0.0)
                sides.append(part.reshape(8, 8, LANES) * (1.0 / (RANK * VIEWS)))
            part = jnp.stack(swap_quads(*sides), axis=1).reshape(16, 8, LANES)
            at = (slice(16 * h, 16 * h + 16), slice(g * 8, g * 8 + 8))
            refined[at] = est[at] * part[:, :, 0:BLOCK]

    for copy in far_swap + near_swap + over:
        copy.wait_send()
    for which in range(2):

        @pl.when((below, above)[which])
        def _():
            for h in range(2):
                rim_copy(h, which).wait_send()


def local(estimate, view_tiles, slot_view, psf_taps):
    vmem = pl.BlockSpec(memory_space=pltpu.VMEM)
    hbm = pl.BlockSpec(memory_space=pltpu.HBM)
    tile = view_tiles[0, 0, 0]
    psf = jnp.transpose(psf_taps, (1, 2, 0, 3))
    scratch = [
        pltpu.VMEM(estimate.shape, F32),
        pltpu.VMEM(tile.shape, BF16),
        pltpu.VMEM(psf.shape, F32),
        pltpu.VMEM(slot_view.shape, jnp.int32),
        pltpu.VMEM((256, LANES), BF16),
        pltpu.VMEM((VIEWS, 128, LANES), BF16),
        pltpu.VMEM((2, 128, LANES), BF16),
        pltpu.VMEM((3, 3, 2, 10, 64, LANES), BF16),
        pltpu.VMEM((RANK, 12, 2, 384, LANES), BF16),
        pltpu.VMEM((RANK, 12, 2, 256, LANES), BF16),
        pltpu.VMEM((16, 256, LANES), BF16),
        pltpu.VMEM((24, 256, LANES), BF16),
        pltpu.VMEM((GROUPS, 2, 128, RANK * LANES), BF16),
        pltpu.VMEM((2, 4, 128, LANES), F32),
        pltpu.VMEM((2, 2, 64, LANES), F32),
        pltpu.VMEM((2, 2, 128, LANES), F32),
        pltpu.VMEM((2, 128, LANES), F32),
        pltpu.VMEM((VIEWS, 2, 64, LANES), F32),
        pltpu.VMEM((2, 24, LANES), F32),
        pltpu.VMEM((RANK, 128, 256), BF16),
        pltpu.VMEM((128, RANK * 256), BF16),
        pltpu.VMEM((256, RANK * LANES), BF16),
        pltpu.VMEM((RANK * 128, 256), BF16),
        pltpu.VMEM((2, RANK, 64, 256), BF16),
        pltpu.VMEM((GROUPS, RANK * LANES, 256), BF16),
        pltpu.SemaphoreType.DMA((4,)),
        pltpu.SemaphoreType.DMA((7,)),
        pltpu.SemaphoreType.DMA((6,)),
        pltpu.SemaphoreType.DMA((8,)),
        pltpu.SemaphoreType.DMA((27,)),
        pltpu.SemaphoreType.DMA((1,)),
        pltpu.SemaphoreType.DMA((9,)),
        pltpu.SemaphoreType.DMA((10,)),
        pltpu.SemaphoreType.DMA((14,)),
        pltpu.SemaphoreType.REGULAR,
    ]
    return pl.pallas_call(
        kernel,
        out_shape=pltpu.VMEM(estimate.shape, F32),
        in_specs=[hbm] * 4,
        out_specs=vmem,
        scratch_shapes=scratch,
        compiler_params=pltpu.CompilerParams(
            collective_id=0, has_side_effects=True, vmem_limit_bytes=56 * 1024 * 1024
        ),
    )(*(pltpu.with_memory_space_constraint(a, pltpu.HBM) for a in (estimate, tile, psf, slot_view)))


def solution(mesh):
    placed = (
        P("bx", "by", "vert"),
        P("bx", "by", "vert", None, None, None),
        P("bx", "by", None),
        P(),
    )
    return jax.shard_map(
        local, mesh=mesh, in_specs=placed, out_specs=P("bx", "by", "vert"), check_vma=False
    )
```

```python
import jax
import jax.numpy as jnp
from jax import lax
from jax.experimental import pallas as pl
from jax.experimental.pallas import tpu as pltpu
from jax.sharding import PartitionSpec as P

BACKGROUND = 0.1
MESH = pl.DeviceIdType.MESH
F32, BF16 = jnp.float32, jnp.bfloat16
BLOCK = 32
RAD = 16
TAPS = 33
RANK = 3
VIEWS = 4
GROUPS = 4
LANES = 128


def iota(shape, axis):
    return lax.broadcasted_iota(jnp.int32, shape, axis)


def dot(a, b):
    return jnp.dot(a, b, preferred_element_type=F32)


def band(line, rows, start):
    line = jnp.broadcast_to(line, (rows, LANES))
    return pltpu.roll(line, start % LANES, 1, stride=1, stride_axis=0)


def swap_quads(a, b):
    low, axis = iota(a.shape, a.ndim - 2) < 4, a.ndim - 2
    return jnp.where(low, a, pltpu.roll(b, 4, axis)), jnp.where(low, pltpu.roll(a, 4, axis), b)


def build_taps(psf, slot_view, slot, taps):
    listed = slot_view[...]
    view = jnp.sum(jnp.where(iota(listed.shape, 2) == slot, listed, 0), axis=2, keepdims=True)
    held = iota((VIEWS, TAPS), 0) == view[0]
    mine = jnp.sum(jnp.where(held[None, None], psf[...], 0.0), axis=2)
    mine = (mine / jnp.sum(mine, axis=-1, keepdims=True)).astype(BF16).astype(F32)
    taps[...] = jnp.zeros_like(taps)
    for a in range(3):
        taps[0, 8 * a : 8 * a + RANK, :TAPS] = mine[a]
    flip = (iota((LANES, LANES), 0) + iota((LANES, LANES), 1) == TAPS - 1).astype(BF16)
    taps[1] = dot(taps[0].astype(BF16), flip)


def build_z(taps, wz, wb):
    z_in, z_out = iota((LANES, LANES), 0), iota((LANES, LANES), 1)
    near = jnp.abs(z_in - z_out) <= RAD
    rim, out = iota((32, LANES), 0), iota((32, LANES), 1)
    rim_ok = ((rim < RAD) & (out <= rim)) | ((rim >= RAD) & (out >= rim + 96))
    lane16 = iota((16, LANES), 1)
    for r in range(RANK):
        forward, backward = taps[1, 16 + r : 17 + r, :], taps[0, 16 + r : 17 + r, :]
        columns = slice(r * LANES, (r + 1) * LANES)
        wz[0:128, columns] = jnp.where(near, band(forward, LANES, -RAD), 0.0).astype(BF16)
        wz[128:160, columns] = jnp.where(rim_ok, band(forward, 32, 96), 0.0).astype(BF16)
        wz[160:256, columns] = jnp.zeros((96, LANES), BF16)
        main = jnp.where(near, band(backward, LANES, -RAD), 0.0)
        low = jnp.where(lane16 < RAD, band(backward, 16, 0), 0.0)
        high = jnp.where(lane16 < RAD, band(backward, 16, 96), 0.0)
        for g in range(GROUPS):
            wb[g, r * 128 : r * 128 + 128, 0:128] = (
                pltpu.roll(main, 32 * g, 1) if g else main
            ).astype(BF16)
            wb[g, r * 128 : r * 128 + 128, 128:256] = jnp.zeros((128, LANES), BF16)
            lo, hi = pltpu.roll(low, RAD * g, 1) if g else low, pltpu.roll(high, 64 + RAD * g, 1)
            wb[g, r * 128 : r * 128 + 16, 128:256] = lo.astype(BF16)
            wb[g, r * 128 + 112 : r * 128 + 128, 128:256] = hi.astype(BF16)


def build_x(taps, bx, tx, txb):
    spread = (iota((LANES, 256), 1) == 4 * iota((LANES, 256), 0)).astype(BF16)
    lane, row = iota((LANES, LANES), 1), iota((LANES, LANES), 0)
    low, high = bx > 0, bx < 3

    def tiles(line):
        turned = [band(line[:, i * LANES : (i + 1) * LANES], LANES, 0) for i in range(2)]
        return jnp.where(lane >= row, turned[0], 0.0), jnp.where(lane >= row, turned[1], turned[0])

    wide = [dot(taps[k, 0:8, :].astype(BF16), spread) for k in range(2)]
    for r in range(RANK):
        left, right = tiles(wide[0][r : r + 1])
        tx[r, :, 0:128] = left.astype(BF16)
        tx[r, :, 128:256] = right.astype(BF16)
        left, right = [m[0:64] for m in tiles(wide[1][r : r + 1])]
        txb[0, r, :, 0:128] = jnp.where((lane[0:64] >= 64) | low, left, 0.0).astype(BF16)
        txb[0, r, :, 128:256] = right.astype(BF16)
        txb[1, r, :, 0:128] = left.astype(BF16)
        txb[1, r, :, 128:256] = jnp.where(high, right, 0.0).astype(BF16)


def build_y(taps, by, ty, tyb):
    place = by * BLOCK - RAD + iota((BLOCK, LANES), 1)
    inside = (place >= 0) & (place < 4 * BLOCK)
    plain = [band(taps[0, 8 + r : 9 + r, :], BLOCK, 0) for r in range(RANK)]
    plain += [
        jnp.where(inside, band(taps[1, 8 + r : 9 + r, :], BLOCK, 0), 0.0) for r in range(RANK)
    ]
    plain = jnp.concatenate(plain, axis=0).astype(BF16)
    y, column = iota((LANES, 256), 0), iota((LANES, 256), 1)
    wide = [
        dot(plain, (column == 16 * (y // 4) + 4 * x + y % 4).astype(BF16)).astype(BF16)
        for x in range(4)
    ]
    row, source = iota((LANES, LANES), 0), iota((LANES, LANES), 1)
    order = (row == 16 * (source % 32 // 4) + 4 * (source // 32) + source % 4).astype(BF16)
    for i in range(2 * RANK):
        done = dot(order, jnp.concatenate([m[i * 32 : i * 32 + 32] for m in wide], axis=0)).astype(BF16)
        if i < RANK:
            ty[:, i * 256 : (i + 1) * 256] = done
        else:
            tyb[(i - RANK) * 128 : (i - RANK + 1) * 128, :] = done


def kernel(
    est_hbm, tile_hbm, psf_hbm, slot_view_hbm, refined,
    est, tile, psf, slot_view,
    packed, parts, outer, field, after_z, after_x, seen, back_y, back_x, sums, rims,
    got_core, got_chip, got_edge,
    taps, tx, ty, wz, tyb, txb, wb,
    load_sem, part_send, part_recv, face_send, face_recv, core_send, core_recv, sum_send, sum_recv, ready,
):
    bx, by, vert = lax.axis_index("bx"), lax.axis_index("by"), lax.axis_index("vert")
    q, slot = vert // VIEWS, vert % VIEWS
    core, chip = slot % 2, slot // 2

    loads = [
        pltpu.make_async_copy(source, target, load_sem.at[i])
        for i, (source, target) in enumerate(
            ((est_hbm, est), (psf_hbm, psf), (slot_view_hbm, slot_view), (tile_hbm, tile))
        )
    ]
    for copy in loads:
        copy.start()

    def at_vert(index):
        return {"vert": index}

    partner = at_vert(q * 4 + chip * 2 + 1 - core)
    above, below = q < 3, q > 0
    first, last = slot == 0, slot == VIEWS - 1
    is_edge = (first & below) | (last & above)

    straight = core == 0

    def block(ju, jv):
        return jnp.where(straight, jv, ju), jnp.where(straight, ju, jv)

    def link(along_u, step):
        x_step = jnp.where(straight == along_u, step, 0)
        x, y = bx + x_step, by + step - x_step
        return {"bx": x, "by": y}, (x >= 0) & (x < 4) & (y >= 0) & (y < 4)

    u_up, u_down, v_up, v_down = link(True, 1), link(True, -1), link(False, 1), link(False, -1)

    def clear(ref):
        ref[...] = jnp.zeros(ref.shape, BF16)

    pl.when(bx == 0)(lambda: clear(field.at[:, 0, core]))
    pl.when(bx == 3)(lambda: clear(field.at[:, 2, core]))
    pl.when(by == 0)(lambda: clear(field.at[0, :, core]))
    pl.when(by == 3)(lambda: clear(field.at[2, :, core]))
    pl.when(~below)(lambda: clear(outer.at[0]))
    pl.when(~above)(lambda: clear(outer.at[1]))

    got_edge[...] = jnp.zeros_like(got_edge)
    barrier = pltpu.get_barrier_semaphore()

    def greet(device):
        pl.semaphore_signal(barrier, inc=1, device_id=device, device_id_type=MESH)

    for k in range(1, VIEWS):
        greet(at_vert(q * 4 + (slot + k) % VIEWS))
    for device, there in (u_up, u_down, v_up, v_down):
        pl.when(there)(lambda device=device: greet(device))

    @pl.when(above)
    def _():
        greet(at_vert(vert - slot + 4))

        @pl.when(last)
        def _():
            for k in range(2, VIEWS + 1):
                greet(at_vert(vert + k))

    beside = [(there, 1) for _, there in (u_up, u_down, v_up, v_down)]
    beside += [(first & below, VIEWS), (~first & below, 1)]
    pl.semaphore_wait(barrier, 3 + sum(jnp.where(there, n, 0) for there, n in beside))

    def answer(device):
        pl.semaphore_signal(ready, inc=1, device_id=device, device_id_type=MESH)

    @pl.when(first & below)
    def _():
        for k in range(1, VIEWS + 1):
            answer(at_vert(vert - k))

    pl.when(~first & below)(lambda: answer(at_vert(vert - slot - 1)))

    loads[0].wait()
    groups = est[...].reshape(BLOCK, GROUPS, 8, BLOCK)
    line = jnp.concatenate([groups[:, g].reshape(256, BLOCK) for g in range(GROUPS)], axis=1)
    line = pltpu.roll(line, slot * 32, 1).reshape(16, 2, 8, LANES)
    for side, quads in enumerate(swap_quads(line[:, 0], line[:, 1])):
        packed[side * 128 : side * 128 + 128, :] = quads.reshape(128, LANES).astype(BF16)

    def part_copy(source, send, device, side):
        return pltpu.make_async_remote_copy(
            src_ref=packed.at[pl.ds(side * 128, 128), :], dst_ref=parts.at[source],
            send_sem=part_send.at[send], recv_sem=part_recv.at[source],
            device_id=device, device_id_type=MESH,
        )

    for k in range(1, VIEWS):
        other = (slot + k) % VIEWS
        part_copy(slot, k - 1, at_vert(q * 4 + other), other % 2).start()

    def outer_copy(which, send, device, side):
        return pltpu.make_async_remote_copy(
            src_ref=packed.at[pl.ds(side * 128, 128), :], dst_ref=outer.at[which],
            send_sem=part_send.at[3 + send], recv_sem=part_recv.at[4 + which],
            device_id=device, device_id_type=MESH,
        )

    @pl.when(first & below)
    def _():
        for k in range(VIEWS):
            outer_copy(1, k, at_vert(vert - 4 + k), k % 2).start()

    parts[slot] = packed[pl.ds(core * 128, 128), :]
    loads[1].wait()
    loads[2].wait()
    build_taps(psf, slot_view, slot, taps)
    build_z(taps, wz, wb)

    def assemble():
        for k in range(1, VIEWS):
            part_copy((slot + k) % VIEWS, 0, partner, 0).wait_recv()
        chunk = iota((128, LANES), 1) // 32
        have = [parts[k].astype(F32) for k in range(VIEWS)]
        for g in range(GROUPS):
            line = have[(3 - g) % 4]
            for at in range(3):
                line = jnp.where(chunk == at, have[(at - g) % 4], line)
            if g:
                line = pltpu.roll(line, LANES - 32 * g, 1)
            for tp in range(2):
                field[1, 1, core, 4 * tp + g] = line[64 * tp : 64 * tp + 64].astype(BF16)

    def assemble_rims():
        for k, there in enumerate((below, above)):
            pl.when(there)(lambda k=k: outer_copy(k, 0, partner, 0).wait_recv())
        is_above = iota((128, LANES), 1) % 32 < RAD
        line = jnp.where(is_above, outer[1].astype(F32), outer[0].astype(F32))
        field[1, 1, core, 8:10] = pltpu.roll(line, RAD, 1).astype(BF16).reshape(2, 64, LANES)

    def message(ju, jv, which):
        return field.at[(*block(ju, jv), core, slice(4 * which, min(4 * which + 4, 10)))]

    def face_copy(source, target, which, send, device):
        return pltpu.make_async_remote_copy(
            src_ref=message(*source, which), dst_ref=message(*target, which),
            send_sem=face_send.at[send],
            recv_sem=face_recv.at[which * 9 + target[0] * 3 + target[1]],
            device_id=device, device_id_type=MESH,
        )

    ways = {"u_up": (0, u_up, (0, 1)), "u_down": (1, u_down, (2, 1)), "v_up": (2, v_up, (1, 0)), "v_down": (3, v_down, (1, 2))}

    def send_own(name, which):
        index, (device, there), target = ways[name]
        pl.when(there)(face_copy((1, 1), target, which, index, device).start)

    def relay(name, along, which):
        index, (device, there), target = ways[name]
        source = (along, 1) if name[0] == "v" else (1, along)
        target = (along, target[1]) if name[0] == "v" else (target[0], along)
        pl.when(there)(face_copy(source, target, which, 4 + index, device).start)

    def came(ju, jv, which, over):
        there = ways[f"{over}_{'down' if (jv if over == 'v' else ju) == 0 else 'up'}"][1][1]
        copy = face_copy((ju, jv), (ju, jv), which, 0, partner)
        pl.when(there)(copy.wait_recv)

    def core_copy(jy, jx, side):
        return pltpu.make_async_remote_copy(
            src_ref=field.at[jy, jx, side], dst_ref=field.at[jy, jx, side],
            send_sem=core_send.at[0], recv_sem=core_recv.at[jy * 3 + jx],
            device_id=partner, device_id_type=MESH,
        )

    def pass_on(ju, jv):
        core_copy(*block(ju, jv), core).start()

    def swapped(jy, jx):
        core_copy(jy, jx, 1 - core).wait_recv()

    def forward_z(*blocks):
        pieces = [(*b, side) for b in blocks for side in range(2)]
        rim = jnp.concatenate([field[jy, jx, side, 8 + tp] for jy, jx, side in pieces for tp in range(2)])
        for g in range(GROUPS):
            turned = pltpu.roll(rim, LANES - 32 * g, 1) if g else rim
            main = jnp.concatenate(
                [field[jy, jx, side, 4 * tp + g] for jy, jx, side in pieces for tp in range(2)]
            )
            done = dot(jnp.concatenate([main, turned], axis=1), wz[...]).astype(BF16)
            for i, (jy, jx, side) in enumerate(pieces):
                for r in range(RANK):
                    after_z[r, jy * GROUPS + g, side, jx * 128 : jx * 128 + 128, :] = done[
                        i * 128 : (i + 1) * 128, r * 128 : (r + 1) * 128
                    ]

    def forward_x(jy):
        for r in range(RANK):
            for group in (jy * GROUPS, jy * GROUPS + 2):
                for b in range(2):
                    rows = slice(b * 128, b * 128 + 256)
                    both = [after_z[r, group + k // 2, k % 2, rows, :] for k in range(4)]
                    done = dot(tx[r], jnp.concatenate(both, axis=1)).astype(BF16)
                    for k in range(4):
                        after_x[r, group + k // 2, k % 2, b * 128 : b * 128 + 128, :] = done[
                            :, k * 128 : k * 128 + 128
                        ]

    assemble()
    for name, which in (("u_up", 0), ("u_down", 0), ("v_up", 1), ("v_down", 1)):
        send_own(name, which)
    for name, which in (("u_up", 1), ("u_down", 1), ("v_up", 0), ("v_down", 0)):
        send_own(name, which)

    @pl.when(last & above)
    def _():
        pl.semaphore_wait(ready, VIEWS)
        for k in range(VIEWS):
            outer_copy(0, k, at_vert(vert + 1 + k), k % 2).start()

    build_x(taps, bx, tx, txb)
    assemble_rims()
    for name in ("u_up", "u_down", "v_up", "v_down"):
        send_own(name, 2)
    pass_on(1, 1)
    for side in (0, 2):
        came(side, 1, 0, "u")
    for one, other in ((0, 2), (2, 0)):
        relay("v_up", one, 0)
        relay("v_down", other, 0)
    build_y(taps, by, ty, tyb)
    for side in (0, 2):
        came(1, side, 1, "v")
    for one, other in ((0, 2), (2, 0)):
        relay("u_up", one, 1)
        relay("u_down", other, 1)
    loads[3].wait()

    def order_tile(i, carry):
        quad = tile[pl.ds(4 * i, 4)].astype(F32).reshape(2, 2, 8, 8, LANES)
        sides = swap_quads(quad[:, 0], quad[:, 1])
        rows = jnp.stack([m[x] for m in sides for x in range(2)], axis=1)
        seen[i] = rows.reshape(256, LANES).astype(BF16)
        return carry

    lax.fori_loop(0, 16, order_tile, 0, unroll=4)
    swapped(1, 1)
    forward_z((1, 1))
    for side in (0, 2):
        came(side, 1, 2, "u")
    for one, other in ((0, 2), (2, 0)):
        relay("v_up", one, 2)
        relay("v_down", other, 2)
    for side in (0, 2):
        came(side, 1, 1, "u")
        pass_on(side, 1)
        came(1, side, 0, "v")
        came(1, side, 2, "v")
        pass_on(1, side)
    for side in (0, 2):
        swapped(1, side)
        swapped(side, 1)
    forward_z((1, 0), (1, 2))
    forward_z((0, 1), (2, 1))
    waves = (((0, 0), (2, 2)), ((0, 2), (2, 0)))
    for corner in waves[0]:
        came(*corner, 0, "v")
        came(*corner, 1, "u")
        came(*corner, 2, "v")
        pass_on(*corner)
    forward_x(1)
    for corner in waves[1]:
        came(*corner, 0, "v")
        came(*corner, 1, "u")
        came(*corner, 2, "v")
        pass_on(*corner)
    for corner in waves[0] + waves[1]:
        swapped(*corner)
    for wave in waves:
        forward_z(*wave)
    for jy in (0, 2):
        forward_x(jy)

    def along_y(step):
        quotient = []
        for b in range(2):
            terms = []
            for r in range(RANK):
                quads = [
                    after_x[r, 4 * b : 4 * b + 8, :, 16 * i : 16 * i + 16, :].reshape(256, LANES)
                    for i in range(4 * step, 4 * step + 4)
                ]
                terms.append(jnp.concatenate(quads, axis=1))
            blurred = dot(ty[...], jnp.concatenate(terms, axis=0))
            rows = slice(128 * b, 128 * b + 128)
            quads = [seen[i, rows, :] for i in range(4 * step, 4 * step + 4)]
            quads = jnp.concatenate(quads, axis=1).astype(F32)
            quotient.append((RANK * quads / (blurred + RANK * BACKGROUND)).astype(BF16))
        quotient = jnp.concatenate(quotient, axis=0)
        for r in range(RANK):
            done = dot(tyb[r * 128 : r * 128 + 128, :], quotient).astype(BF16)
            for k in range(4):
                i = 4 * step + k
                back_y[r * 8 : r * 8 + 8, 16 * i : 16 * i + 16, :] = done[
                    :, k * 128 : k * 128 + 128
                ].reshape(8, 16, LANES)

    def backward_x(half):
        within = slice(half * 64, half * 64 + 192)
        for g in (0, 2):
            for r in range(RANK):
                at = (r * GROUPS + g) * 2
                sides = jnp.concatenate([back_y[at + k, within, :] for k in range(4)], axis=1)
                done = dot(txb[half, r, :, 0:192], sides).astype(BF16)
                for k in range(4):
                    rows = slice(k % 2 * 64, k % 2 * 64 + 64)
                    back_x[g + k // 2, half, rows, r * 128 : (r + 1) * 128] = done[
                        :, k * 128 : k * 128 + 128
                    ]

    def backward_z(half):
        parts_z = [dot(back_x[g, half], wb[g]) for g in range(GROUPS)]
        both = (parts_z[0] + parts_z[1] + (parts_z[2] + parts_z[3]))[:, LANES:]
        is_low = iota((64, LANES), 1) < 64
        rims[half, 0] = jnp.where(is_low, both[0:64], pltpu.roll(both[64:128], 64, 1))
        rims[half, 1] = jnp.where(is_low, pltpu.roll(both[0:64], 64, 1), both[64:128])
        for which in range(2):
            pl.when((below, above)[which])(rim_copy(half, which).start)
        for g in range(GROUPS):
            for c in range(4):
                at = (g + c) % 4
                sums[half, c, :, at * 32 : at * 32 + 32] = parts_z[g][:, at * 32 : at * 32 + 32]

    far = (1 - chip) * 2 + core

    def sum_copy(source, target, index, device):
        return pltpu.make_async_remote_copy(
            src_ref=source, dst_ref=target, send_sem=sum_send.at[index],
            recv_sem=sum_recv.at[index], device_id=device, device_id_type=MESH,
        )

    far_swap = [
        sum_copy(sums.at[h, (1 - chip) * 2 + 1 - core], got_core.at[h, 0], h, partner) for h in range(2)
    ]
    near_swap = [
        sum_copy(sums.at[h, chip * 2 + 1 - core], got_core.at[h, 1], 2 + h, partner) for h in range(2)
    ]
    over = [sum_copy(sums.at[h, far], got_chip.at[h], 4 + h, at_vert(q * 4 + far)) for h in range(2)]

    def rim_copy(h, which):
        home = (vert - slot - 1, vert - slot + 4)[which]
        return pltpu.make_async_remote_copy(
            src_ref=rims.at[h, which], dst_ref=got_edge.at[slot, h], send_sem=sum_send.at[6 + 2 * h + which],
            recv_sem=sum_recv.at[6 + 2 * slot + h], device_id=at_vert(home), device_id_type=MESH,
        )

    def rim_came(h):
        for k in range(VIEWS):
            pltpu.make_async_remote_copy(
                src_ref=rims.at[h, 0], dst_ref=got_edge.at[k, h], send_sem=sum_send.at[6],
                recv_sem=sum_recv.at[6 + 2 * k + h], device_id=partner, device_id_type=MESH,
            ).wait_recv()

    def backward(h):
        backward_x(h)
        backward_z(h)
        far_swap[h].start()
        near_swap[h].start()

    def pass_over(h):
        far_swap[h].wait_recv()
        sums[h, far] = sums[h, far] + got_core[h, 0]
        over[h].start()

    pl.when(~last & above)(lambda: pl.semaphore_wait(ready, 1))
    for step in range(3):
        along_y(step)
    backward(0)
    along_y(3)
    pass_over(0)
    backward(1)
    pass_over(1)

    for k in range(1, VIEWS):
        part_copy(slot, k - 1, partner, 0).wait_send()

    @pl.when(is_edge)
    def _():
        for k in range(VIEWS):
            outer_copy(0, k, partner, 0).wait_send()

    def sent(ref, semaphore):
        pltpu.make_async_remote_copy(
            src_ref=ref, dst_ref=ref, send_sem=semaphore, recv_sem=face_recv.at[0],
            device_id=partner, device_id_type=MESH,
        ).wait_send()

    for name, (index, (_, there), _) in ways.items():
        relayed = field.at[0:3, 0:2, :, 0:1] if name[0] == "v" else field.at[0:2, 0:2, :, 0:1]

        @pl.when(there)
        def _():
            sent(field.at[1, 1, core], face_send.at[index])
            sent(relayed, face_send.at[4 + index])

    sent(field.at[:, :, core], core_send.at[0])

    start = jnp.where(last, RAD, 0)
    lane = iota((64, LANES), 1)
    keep = is_edge & (lane >= start) & (lane < start + RAD)
    for h in range(2):
        near_swap[h].wait_recv()
        mine = sums[h, slot] + got_core[h, 1]
        over[h].wait_recv()
        mine = mine + got_chip[h]

        pl.when(is_edge)(lambda: rim_came(h))
        edge = got_edge[0, h] + got_edge[1, h] + (got_edge[2, h] + got_edge[3, h])
        for g in range(GROUPS):
            own = pltpu.roll(mine, (8 - g - slot) % 4 * 32, 1)
            sides = []
            for k in range(2):
                rim = pltpu.roll(edge, (start + LANES - 64 * k - RAD * g) % LANES, 1)
                part = own[64 * k : 64 * k + 64] + jnp.where(keep, rim, 0.0)
                sides.append(part.reshape(8, 8, LANES) * (1.0 / (RANK * VIEWS)))
            part = jnp.stack(swap_quads(*sides), axis=1).reshape(16, 8, LANES)
            at = (slice(16 * h, 16 * h + 16), slice(g * 8, g * 8 + 8))
            refined[at] = est[at] * part[:, :, 0:BLOCK]

    for copy in far_swap + near_swap + over:
        copy.wait_send()
    for which in range(2):

        @pl.when((below, above)[which])
        def _():
            for h in range(2):
                rim_copy(h, which).wait_send()


def local(estimate, view_tiles, slot_view, psf_taps):
    vmem = pl.BlockSpec(memory_space=pltpu.VMEM)
    hbm = pl.BlockSpec(memory_space=pltpu.HBM)
    tile = view_tiles[0, 0, 0]
    psf = jnp.transpose(psf_taps, (1, 2, 0, 3))
    scratch = [
        pltpu.VMEM(estimate.shape, F32),
        pltpu.VMEM(tile.shape, BF16),
        pltpu.VMEM(psf.shape, F32),
        pltpu.VMEM(slot_view.shape, jnp.int32),
        pltpu.VMEM((256, LANES), BF16),
        pltpu.VMEM((VIEWS, 128, LANES), BF16),
        pltpu.VMEM((2, 128, LANES), BF16),
        pltpu.VMEM((3, 3, 2, 10, 64, LANES), BF16),
        pltpu.VMEM((RANK, 12, 2, 384, LANES), BF16),
        pltpu.VMEM((RANK, 12, 2, 256, LANES), BF16),
        pltpu.VMEM((16, 256, LANES), BF16),
        pltpu.VMEM((24, 256, LANES), BF16),
        pltpu.VMEM((GROUPS, 2, 128, RANK * LANES), BF16),
        pltpu.VMEM((2, 4, 128, LANES), F32),
        pltpu.VMEM((2, 2, 64, LANES), F32),
        pltpu.VMEM((2, 2, 128, LANES), F32),
        pltpu.VMEM((2, 128, LANES), F32),
        pltpu.VMEM((VIEWS, 2, 64, LANES), F32),
        pltpu.VMEM((2, 24, LANES), F32),
        pltpu.VMEM((RANK, 128, 256), BF16),
        pltpu.VMEM((128, RANK * 256), BF16),
        pltpu.VMEM((256, RANK * LANES), BF16),
        pltpu.VMEM((RANK * 128, 256), BF16),
        pltpu.VMEM((2, RANK, 64, 256), BF16),
        pltpu.VMEM((GROUPS, RANK * LANES, 256), BF16),
        pltpu.SemaphoreType.DMA((4,)),
        pltpu.SemaphoreType.DMA((7,)),
        pltpu.SemaphoreType.DMA((6,)),
        pltpu.SemaphoreType.DMA((8,)),
        pltpu.SemaphoreType.DMA((27,)),
        pltpu.SemaphoreType.DMA((1,)),
        pltpu.SemaphoreType.DMA((9,)),
        pltpu.SemaphoreType.DMA((10,)),
        pltpu.SemaphoreType.DMA((14,)),
        pltpu.SemaphoreType.REGULAR,
    ]
    return pl.pallas_call(
        kernel,
        out_shape=pltpu.VMEM(estimate.shape, F32),
        in_specs=[hbm] * 4,
        out_specs=vmem,
        scratch_shapes=scratch,
        compiler_params=pltpu.CompilerParams(
            collective_id=0, has_side_effects=True, vmem_limit_bytes=56 * 1024 * 1024
        ),
    )(*(pltpu.with_memory_space_constraint(a, pltpu.HBM) for a in (estimate, tile, psf, slot_view)))


def solution(mesh):
    placed = (
        P("bx", "by", "vert"),
        P("bx", "by", "vert", None, None, None),
        P("bx", "by", None),
        P(),
    )
    return jax.shard_map(
        local, mesh=mesh, in_specs=placed, out_specs=P("bx", "by", "vert"), check_vma=False
    )
```
